128 devices in a mesh: seq: 32 (over y, z, core), tile: 4 (over x).
Axes of the slice: x: 4, y: 4, z: 4, core: 2. Of those that a mesh axis runs over, the one named last changes fastest.
Arguments:
- tile_features: bfloat16 [16384, 1536], P(('seq', 'tile')), may hold values from -36 to 36
- gate_weight: bfloat16 [1536, 2048], replicated, may hold values from -0.15625 to 0.15625
- up_weight: bfloat16 [1536, 2048], replicated, may hold values from -0.15625 to 0.15625
- down_weight: bfloat16 [2048, 1536], replicated, may hold values from -0.125 to 0.125
- input_projection_weight: bfloat16 [1536, 768], replicated
- query_key_value_weight: bfloat16 [768, 2304], replicated
- positions: int32 [16384], replicated, may hold values from 0 to 16383, as said below
- dilation_shift: int32 [2, 16], replicated, may hold values from 0 to 15, as said below
- slide_output_gradient: bfloat16 [16384, 768], P('seq', 'tile'), may hold values from -6 to 6
Outputs:
- slide_out: bfloat16 [16384, 768], P('seq', 'tile')
- tile_grad: bfloat16 [16384, 1536], P(('seq', 'tile'))
The draws below stay inside these ranges and needn't reach their ends.
Inputs may be any that keep to these rules, and one draw needn't show every extreme that they name: Each slide position belongs to exactly one tile. Of one device's tiles at most 8 fall in one block of 512 positions, and in every draw some device reaches 8. `dilation_shift`: row 0 lies below 4, row 1 below 16.
All inputs are finite; a program needn't handle non-finite values.
Results may differ from the reference program's by a relative error of at most 0.039.
Values may be sent and summed in bfloat16 or wider, within the bound.
No kernel may reach another device: no remote copies, remote signals or barrier semaphores. Data moves between devices by JAX's collectives and lax.ppermute only.
A program may use at most 128 MiB of HBM per device.

```python
import math
import jax
import jax.numpy as jnp
from jax import lax

E = 1536
FF = 2048
D = 768
SLIDE_HEADS = 16
HEAD_DIM = 48
TILE_DEV = 128
MIDDLE_DILATION = 4
SEQ_ROWS = 512
TILES = 16384
WIDEST_DILATION = 16
N_SEQ = 32
N_TILE = 4
DEVICES = 128


def spread_scales(key, shape):
    return jnp.exp(jax.random.uniform(key, shape, minval=math.log(0.3), maxval=math.log(3.0)))


def draw_tile_features(key, part):
    key = jax.random.fold_in(key, 11)
    key_base, key_rows, key_cols = jax.random.split(key, 3)
    scales = spread_scales(key_rows, (TILES, 1)) * spread_scales(key_cols, (1, E))
    values = jnp.clip(jax.random.normal(key_base, (TILES, E)), -4.0, 4.0) * scales
    return values.astype(jnp.bfloat16)


def draw_input_projection_weight(key, part):
    key = jax.random.fold_in(key, 13)
    key_base, key_cols = jax.random.split(key, 2)
    scales = spread_scales(key_cols, (1, D)) * (0.5 * E ** (-0.5))
    base = jnp.clip(jax.random.normal(key_base, (E, D)), -4.0, 4.0)
    return (base * scales).astype(jnp.bfloat16)


def draw_query_key_value_weight(key, part):
    key = jax.random.fold_in(key, 17)
    factor = 2.0 * D ** (-0.5)
    base = jnp.clip(jax.random.normal(key, (D, 3 * D)), -4.0, 4.0)
    return (base * factor).astype(jnp.bfloat16)


def draw_positions(key, part):
    key = jax.random.fold_in(key, 21)
    key_pairs, key_order, key_rows, key_mix = jax.random.split(key, 4)
    per_group = TILE_DEV // N_SEQ
    spread_half = jax.random.randint(key_pairs, (N_TILE, N_SEQ // 2), 0, per_group + 1)
    spread_half = spread_half.at[:, 0].set(per_group)
    signed = jnp.concatenate([spread_half, -spread_half], axis=1)
    signed = jax.vmap(lambda sub_key, row_vals: jax.random.permutation(sub_key, row_vals))(jax.random.split(key_order, N_TILE), signed)
    tile_counts = per_group + signed
    device_iota = jnp.arange(DEVICES)
    seq_of = device_iota // N_TILE
    tile_of = device_iota % N_TILE
    shifted = (jnp.arange(N_SEQ)[None, :] - seq_of[:, None]) % N_SEQ
    counts = tile_counts[tile_of[:, None], shifted]
    before = jnp.cumsum(counts, axis=0) - counts
    ends = jnp.cumsum(counts, axis=1)
    starts = ends - counts
    slot_iota = jnp.arange(TILE_DEV)
    group_of = jnp.sum((slot_iota[None, :, None] >= ends[:, None, :]).astype(jnp.int32), axis=2)
    within = slot_iota[None, :] - jnp.take_along_axis(starts, group_of, axis=1)
    incoming = jnp.take_along_axis(before, group_of, axis=1) + within
    row_orders = jax.vmap(lambda sub_key: jax.random.permutation(sub_key, SEQ_ROWS))(jax.random.split(key_rows, N_SEQ))
    placed = group_of * SEQ_ROWS + row_orders[group_of, incoming]
    mixing = jax.vmap(lambda sub_key: jax.random.permutation(sub_key, TILE_DEV))(jax.random.split(key_mix, DEVICES))
    placed = jnp.take_along_axis(placed, mixing, axis=1)
    return placed.reshape(TILES).astype(jnp.int32)


def draw_dilation_shift(key, part):
    key = jax.random.fold_in(key, 31)
    key_mid, key_wide, key_pick = jax.random.split(key, 3)
    middle = jax.random.randint(key_mid, (SLIDE_HEADS,), 0, MIDDLE_DILATION)
    widest = jax.random.randint(key_wide, (SLIDE_HEADS,), 0, WIDEST_DILATION)
    chosen = jax.random.randint(key_pick, (2,), 0, SLIDE_HEADS)
    middle = middle.at[chosen[0]].set(MIDDLE_DILATION - 1)
    widest = widest.at[chosen[1]].set(WIDEST_DILATION - 1)
    return jnp.stack([middle, widest]).astype(jnp.int32)


def steps_of(own_key, extent, pieces, least, largest):
    level, own = 1.0, jax.random.fold_in(own_key, 6)
    for axis_at, shards_of in pieces:
        draws = jnp.exp(jax.random.uniform(jax.random.fold_in(own, axis_at), (shards_of,), jnp.float32, least / len(pieces), largest / len(pieces)))
        level = level * jnp.repeat(draws, extent[axis_at] // shards_of).reshape([-1 if axis == axis_at else 1 for axis in range(len(extent))])
    return level


def gaussian(rng, dims, scale, most, cuts=(), kind=jnp.bfloat16):
    drawn = jax.random.normal(rng, dims, jnp.float32) * scale
    if len(cuts) > 0:
        drawn = steps_of(rng, dims, cuts, -0.22, 0.18) * drawn
    return jnp.clip(drawn, min=-most, max=most).astype(kind)


def setup_inputs(seed: int = 0) -> dict:
    splits = jax.random.split(jax.random.key(seed), 10)
    return {
        "tile_features": draw_tile_features(jax.random.fold_in(splits[9], 71), 0),
        "gate_weight": gaussian(splits[1], (E, FF), E ** -0.5, 0.15625),
        "up_weight": gaussian(splits[2], (E, FF), E ** -0.5, 0.15625),
        "down_weight": gaussian(splits[3], (FF, E), FF ** -0.5, 0.125),
        "input_projection_weight": draw_input_projection_weight(jax.random.fold_in(splits[9], 71), 0),
        "query_key_value_weight": draw_query_key_value_weight(jax.random.fold_in(splits[9], 71), 0),
        "positions": draw_positions(jax.random.fold_in(splits[9], 71), 0),
        "dilation_shift": draw_dilation_shift(jax.random.fold_in(splits[9], 71), 0),
        "slide_output_gradient": gaussian(splits[8], (TILES, D), 1.0, 6.0, ((0, 32), (1, 4))),
    }


EPSILON = 1e-06
SOFT_CAP = 50.0

def normalize(values):
    centred = values - lax.optimization_barrier(jnp.mean(values, axis=-1, keepdims=True))
    inv_std = lax.rsqrt(lax.optimization_barrier(jnp.mean(centred * centred, axis=-1, keepdims=True)) + EPSILON)
    return (centred * inv_std, inv_std)

def norm_back(normed, inv_std, grads):
    mean_grad = lax.optimization_barrier(jnp.mean(grads, axis=-1, keepdims=True))
    mean_cross = lax.optimization_barrier(jnp.mean(grads * normed, axis=-1, keepdims=True))
    return (grads - mean_grad - normed * mean_cross) * inv_std

def select_rows(values, dilation, offsets):
    shaped = values.reshape(values.shape[0] // dilation, dilation, values.shape[1], values.shape[2])
    picker = jnp.arange(dilation, dtype=jnp.int32)[:, None] == offsets[None, :]
    return lax.optimization_barrier(jnp.sum(jnp.where(picker[None, :, :, None], shaped, jnp.zeros((), values.dtype)), axis=1))

def spread_rows(sparse, dilation, offsets):
    picker = jnp.arange(dilation, dtype=jnp.int32)[:, None] == offsets[None, :]
    spread_out = jnp.where(picker[None, :, :, None], sparse[:, None], jnp.zeros((), sparse.dtype))
    return spread_out.reshape(sparse.shape[0] * dilation, sparse.shape[1], sparse.shape[2])

def rounded(values):
    return lax.optimization_barrier(values.astype(jnp.bfloat16)).astype(jnp.float32)

def attend(queries, key_rows, value_rows):
    raw_scores = jnp.einsum('qhd,khd->hqk', queries.astype(jnp.float32), key_rows.astype(jnp.float32)) * HEAD_DIM ** (-0.5)
    capped = SOFT_CAP * jnp.tanh(raw_scores / SOFT_CAP)
    log_total = jnp.log(lax.optimization_barrier(jnp.sum(jnp.exp(capped), axis=-1)))
    probs = jnp.exp(capped - log_total[:, :, None])
    outputs = jnp.einsum('hqk,khd->qhd', rounded(probs), value_rows.astype(jnp.float32))
    return (outputs, log_total.T)

def attend_back(queries, key_rows, value_rows, log_total, grad_out, shift_term):
    query32 = queries.astype(jnp.float32)
    key32 = key_rows.astype(jnp.float32)
    grad_out32 = grad_out.astype(jnp.float32)
    raw_scores = jnp.einsum('qhd,khd->hqk', query32, key32) * HEAD_DIM ** (-0.5)
    tangent = jnp.tanh(raw_scores / SOFT_CAP)
    probs = jnp.exp(SOFT_CAP * tangent - log_total.T[:, :, None])
    grad_probs = jnp.einsum('qhd,khd->hqk', grad_out32, value_rows.astype(jnp.float32))
    grad_scores = probs * (grad_probs + shift_term.T[:, :, None])
    grad_raw = rounded(grad_scores * (1.0 - tangent * tangent) * HEAD_DIM ** (-0.5))
    grad_query = jnp.einsum('hqk,khd->qhd', grad_raw, key32)
    grad_key = jnp.einsum('hqk,qhd->khd', grad_raw, query32)
    grad_value = jnp.einsum('hqk,qhd->khd', rounded(probs), grad_out32)
    return (grad_query, grad_key, grad_value)

def reference(tile_features, gate_weight, up_weight, down_weight, input_projection_weight, query_key_value_weight, positions, dilation_shift, slide_output_gradient):
    feats32 = tile_features.astype(jnp.float32)
    feat_norm, feat_inv = normalize(feats32)
    feat_bf = feat_norm.astype(jnp.bfloat16)
    gate_proj = jnp.dot(feat_bf, gate_weight, preferred_element_type=jnp.float32)
    up_proj = jnp.dot(feat_bf, up_weight, preferred_element_type=jnp.float32)
    gate_sigmoid = jax.nn.sigmoid(gate_proj)
    hidden = (gate_proj * gate_sigmoid * up_proj).astype(jnp.bfloat16)
    embedding = (feats32 + jnp.dot(hidden, down_weight, preferred_element_type=jnp.float32)).astype(jnp.bfloat16)
    tile_proj = jnp.dot(embedding, input_projection_weight, preferred_element_type=jnp.float32).astype(jnp.bfloat16)
    slide_in = jnp.zeros((TILES, D), jnp.bfloat16).at[positions].set(tile_proj)
    slide32 = slide_in.astype(jnp.float32)
    slide_norm, slide_inv = normalize(slide32)
    qkv_rows = jnp.dot(slide_norm.astype(jnp.bfloat16), query_key_value_weight, preferred_element_type=jnp.float32)
    qkv_rows = qkv_rows.astype(jnp.bfloat16).reshape(TILES, 3, SLIDE_HEADS, HEAD_DIM)
    query_all = qkv_rows[:, 0]
    key_all = qkv_rows[:, 1]
    value_all = qkv_rows[:, 2]
    run_options = ((1, jnp.zeros((SLIDE_HEADS,), jnp.int32)), (MIDDLE_DILATION, dilation_shift[0]), (WIDEST_DILATION, dilation_shift[1]))
    weight_sum = jnp.zeros((TILES, SLIDE_HEADS), jnp.float32)
    weighted = jnp.zeros((TILES, SLIDE_HEADS, HEAD_DIM), jnp.float32)
    saved = []
    for dilation, offsets in run_options:
        segments = TILES // (dilation * SEQ_ROWS)
        seg_shape = (segments, SEQ_ROWS, SLIDE_HEADS, HEAD_DIM)
        query_sel = select_rows(query_all, dilation, offsets).reshape(seg_shape)
        key_sel = select_rows(key_all, dilation, offsets).reshape(seg_shape)
        value_sel = select_rows(value_all, dilation, offsets).reshape(seg_shape)
        out_sel, lse_sel = lax.map(lambda seg_data: attend(*seg_data), (query_sel, key_sel, value_sel))
        sparse_rows = TILES // dilation
        out_full = spread_rows(out_sel.reshape(sparse_rows, SLIDE_HEADS, HEAD_DIM), dilation, offsets)
        lse_full = spread_rows(lse_sel.reshape(sparse_rows, SLIDE_HEADS, 1), dilation, offsets)[..., 0]
        valid = spread_rows(jnp.ones((sparse_rows, SLIDE_HEADS, 1), jnp.float32), dilation, offsets)[..., 0]
        branch_weight = valid * jnp.exp(lse_full)
        weight_sum = weight_sum + branch_weight
        weighted = weighted + branch_weight[..., None] * out_full
        saved.append((query_sel, key_sel, value_sel, lse_sel, out_full, branch_weight))
    attention = weighted / weight_sum[..., None]
    slide_out = (slide32 + attention.reshape(TILES, D)).astype(jnp.bfloat16)
    grad_attn = slide_output_gradient.astype(jnp.float32).reshape(TILES, SLIDE_HEADS, HEAD_DIM)
    grad_qkv = jnp.zeros((TILES, 3, SLIDE_HEADS, HEAD_DIM), jnp.float32)
    for (dilation, offsets), (query_sel, key_sel, value_sel, lse_sel, out_full, branch_weight) in zip(run_options, saved):
        segments = TILES // (dilation * SEQ_ROWS)
        sparse_rows = TILES // dilation
        branch_share = branch_weight / weight_sum
        grad_out = (branch_share[..., None] * grad_attn).astype(jnp.bfloat16)
        grad_lse = branch_share * lax.optimization_barrier(jnp.sum(grad_attn * (out_full - attention), axis=-1))
        shift_term = grad_lse - lax.optimization_barrier(jnp.sum(lax.optimization_barrier(grad_out).astype(jnp.float32) * out_full, axis=-1))
        grad_out_sel = select_rows(grad_out, dilation, offsets).reshape(segments, SEQ_ROWS, SLIDE_HEADS, HEAD_DIM)
        shift_sel = select_rows(shift_term[..., None], dilation, offsets).reshape(segments, SEQ_ROWS, SLIDE_HEADS)
        grad_query, grad_key, grad_value = lax.map(lambda seg_data: attend_back(*seg_data), (query_sel, key_sel, value_sel, lse_sel, grad_out_sel, shift_sel))
        grad_qkv = grad_qkv + jnp.stack([spread_rows(grad_query.reshape(sparse_rows, SLIDE_HEADS, HEAD_DIM), dilation, offsets), spread_rows(grad_key.reshape(sparse_rows, SLIDE_HEADS, HEAD_DIM), dilation, offsets), spread_rows(grad_value.reshape(sparse_rows, SLIDE_HEADS, HEAD_DIM), dilation, offsets)], axis=1)
    qkv_grad_bf = grad_qkv.astype(jnp.bfloat16).reshape(TILES, 3 * D)
    grad_norm = jnp.dot(qkv_grad_bf, query_key_value_weight.T, preferred_element_type=jnp.float32)
    grad_slide = slide_output_gradient.astype(jnp.float32) + norm_back(slide_norm, slide_inv, grad_norm)
    grad_tile_proj = grad_slide[positions].astype(jnp.bfloat16)
    grad_embed = jnp.dot(grad_tile_proj, input_projection_weight.T, preferred_element_type=jnp.float32).astype(jnp.bfloat16)
    grad_hidden = jnp.dot(grad_embed, down_weight.T, preferred_element_type=jnp.float32)
    grad_gate = (grad_hidden * up_proj * gate_sigmoid * (1.0 + gate_proj * (1.0 - gate_sigmoid))).astype(jnp.bfloat16)
    grad_up = (grad_hidden * gate_proj * gate_sigmoid).astype(jnp.bfloat16)
    grad_feat = jnp.dot(grad_gate, gate_weight.T, preferred_element_type=jnp.float32) + jnp.dot(grad_up, up_weight.T, preferred_element_type=jnp.float32)
    embed32 = lax.optimization_barrier(grad_embed).astype(jnp.float32)
    tile_grad = (embed32 + norm_back(feat_norm, feat_inv, grad_feat)).astype(jnp.bfloat16)
    return (slide_out, tile_grad)
```

```python
import jax
import jax.numpy as jnp
from jax import lax
from jax.experimental import pallas as pl
from jax.experimental.pallas import tpu as pltpu
from jax.sharding import PartitionSpec as P

HEADS = 16
HD = 48
EPSILON = 1e-06
SOFT_CAP = 50.0
SCALE = HD**-0.5
BLK = 512
SLOTS = 8
BF = jnp.bfloat16
F32 = jnp.float32
I32 = jnp.int32

NN = (((1,), (0,)), ((), ()))
NT = (((1,), (1,)), ((), ()))
TN = (((0,), (0,)), ((), ()))


def mm(a, b, dims=NN):
    return lax.dot_general(a, b, dims, preferred_element_type=F32)


def iota(shape, dim):
    return lax.broadcasted_iota(I32, shape, dim)


def class_order(row):
    return (row & 3) * 128 + ((row >> 2) & 3) * 32 + (row >> 4)


def order_matrix():
    return jnp.where(class_order(iota((BLK, BLK), 0)) == iota((BLK, BLK), 1), 1.0, 0.0).astype(BF)


def normalize(values):
    centred = values - jnp.mean(values, axis=-1, keepdims=True)
    inv_std = lax.rsqrt(jnp.mean(centred * centred, axis=-1, keepdims=True) + EPSILON)
    return (centred * inv_std, inv_std)


def norm_back(normed, inv_std, grads):
    mean_grad = jnp.mean(grads, axis=-1, keepdims=True)
    mean_cross = jnp.mean(grads * normed, axis=-1, keepdims=True)
    return (grads - mean_grad - normed * mean_cross) * inv_std


def call(kernel, outs, scratch=(), n_smem=0, limit=40):
    def run(*args):
        specs = [pl.BlockSpec(memory_space=pltpu.SMEM)] * n_smem
        specs += [pl.BlockSpec(memory_space=pltpu.VMEM)] * (len(args) - n_smem)
        shapes = [jax.ShapeDtypeStruct(s, d) for s, d in outs]
        out_specs = [pl.BlockSpec(memory_space=pltpu.VMEM)] * len(outs)
        return pl.pallas_call(
            kernel,
            out_shape=shapes,
            in_specs=specs,
            out_specs=out_specs,
            scratch_shapes=list(scratch),
            compiler_params=pltpu.CompilerParams(vmem_limit_bytes=limit * 1024 * 1024),
        )(*args)

    return run


def order_kernel(grad_ref, out_ref):
    out_ref[...] = mm(grad_ref[...], order_matrix(), TN).astype(BF)


def pack_kernel(qkv_ref, x_ref, prow_ref, pcol_ref, out_ref, heads_ref, wide_ref):
    brow = prow_ref[...] >> 9
    bcol = pcol_ref[...] >> 9
    n = prow_ref.shape[1]
    before = iota((n, n), 0) < iota((n, n), 1)
    rank = jnp.sum(jnp.where((bcol == brow) & before, 1, 0), axis=0, keepdims=True)
    code = brow * SLOTS + rank
    width = HEADS * HD
    for h in range(HEADS):
        for part in range(3):
            heads_ref[:, 192 * h + HD * part : 192 * h + HD * part + HD] = qkv_ref[
                :, part * width + h * HD : part * width + h * HD + HD
            ]
        heads_ref[:, 192 * h + 144 : 192 * h + 192] = x_ref[:, h * HD : h * HD + HD]
    seat = iota((64, n), 0)
    heads = heads_ref[...]
    for block in range(4):
        want = ((seat >> 3) * 4 + block) * SLOTS + (seat & 7)
        picker = jnp.where(code == want, 1.0, 0.0).astype(BF)
        rows = mm(picker, heads)
        for h in range(HEADS):
            t, j = h // 4, h % 4
            lane = (j ^ block) * 192
            wide_ref[:, j * 4 + t, :, lane : lane + 192] = rows[:, 192 * h : 192 * h + 192].reshape(
                8, SLOTS, 192
            )
    out_ref[...] = wide_ref[...].reshape(8 * 16 * SLOTS, 768).astype(BF)


def place_kernel(off_ref, recv_ref, tab_ref, y_ref, yt_ref, y2_ref):
    o2 = pl.multiple_of(off_ref[1], 32)
    for d in range(4):
        tab = tab_ref[d : d + 1, :]
        onehot = jnp.where(iota((BLK, tab.shape[1]), 0) == tab, 1.0, 0.0).astype(BF)
        y = mm(onehot, recv_ref[:, 192 * d : 192 * d + 192])
        y_ref[d] = y.astype(BF)
        yt_ref[d] = y.T.astype(BF)
        y2_ref[32 * d : 32 * d + 32, :] = y_ref[d, pl.ds(o2, 32), :]


def score_rows(keys, queries_t, e_store, m_store):
    scores = mm(keys, queries_t)
    count, width = scores.shape
    total = jnp.zeros((8, width), F32)
    step = 64
    for c in range(0, count, step):
        t = jnp.tanh(scores[c : c + step] * (SCALE / SOFT_CAP))
        e = jnp.exp(SOFT_CAP * t)
        total = total + jnp.sum(e.reshape(step // 8, 8, width), axis=0)
        e_store(c, step, e.astype(BF))
        m_store(c, step, (e * (1.0 - t * t) * SCALE).astype(BF))
    return jnp.sum(total, axis=0, keepdims=True)


def forward_kernel(off_ref, y_ref, yt_ref, e0_ref, m0_ref, e1_ref, m1_ref, u_ref, l_ref):
    o1 = pl.multiple_of(off_ref[0], 128)

    def block(d, carry):
        def e_store(c, n, v):
            e0_ref[d, c : c + n, :] = v

        def m_store(c, n, v):
            m0_ref[d, c : c + n, :] = v

        l_ref[d] = score_rows(y_ref[d, :, 48:96], yt_ref[d, 0:48, :], e_store, m_store)
        u_ref[d] = mm(yt_ref[d, 96:144, :], e0_ref[d])
        return carry

    lax.fori_loop(0, 4, block, 0)

    def e_store(c, n, v):
        e1_ref[c : c + n, :] = v

    def m_store(c, n, v):
        m1_ref[c : c + n, :] = v

    keys = jnp.concatenate([y_ref[d, pl.ds(o1, 128), 48:96] for d in range(4)], axis=0)
    queries = jnp.concatenate([yt_ref[d, 0:48, pl.ds(o1, 128)] for d in range(4)], axis=1)
    values = jnp.concatenate([yt_ref[d, 96:144, pl.ds(o1, 128)] for d in range(4)], axis=1)
    l1 = score_rows(keys, queries, e_store, m_store)
    u1 = mm(values, e1_ref[...])
    for d in range(4):
        u_ref[d, :, pl.ds(o1, 128)] += u1[:, 128 * d : 128 * d + 128]
        l_ref[d, :, pl.ds(o1, 128)] += l1[:, 128 * d : 128 * d + 128]


def turned(value, shift):
    return pltpu.roll(value, shift & 127, 1)


def wide_kernel(
    off_ref,
    yt_ref,
    a0_ref,
    a1_ref,
    a2_ref,
    a3_ref,
    u_ref,
    l_ref,
    g0_ref,
    g1_ref,
    g2_ref,
    g3_ref,
    so_ref,
    gs_ref,
    ds_ref,
    own_ref,
    send_ref,
    dq_ref,
    e2_ref,
    m2_ref,
    usum_ref,
    lsum_ref,
):
    o2 = off_ref[1]
    base = pl.multiple_of((o2 >> 7) << 7, 128)
    part = (o2 >> 5) & 3
    y2 = jnp.concatenate([a0_ref[...], a1_ref[...], a2_ref[...], a3_ref[...]], axis=0)
    keys, values = y2[:, 48:96], y2[:, 96:144]
    both_t = y2[:, 48:144].astype(F32).T.astype(BF)
    query_t = a0_ref[:, 0:48].astype(F32).T.astype(BF)

    def e_store(c, n, v):
        e2_ref[c : c + n, :] = v

    def m_store(c, n, v):
        m2_ref[c : c + n, :] = v

    l2 = score_rows(keys, query_t, e_store, m_store)
    u2 = mm(both_t[48:96], e2_ref[...])
    l2w = jnp.broadcast_to(l2, (8, 128))
    lane = iota((1, 128), 1) >> 5
    gs2 = jnp.zeros((48, 128), F32)
    ds2 = jnp.zeros((8, 128), F32)
    for d in range(4):
        grad_ref = (g0_ref, g1_ref, g2_ref, g3_ref)[d]
        here = lane == part
        shift = 32 * (part - d)
        usum_ref[...] = u_ref[d]
        lsum_ref[...] = l_ref[d]
        usum_ref[:, pl.ds(base, 128)] += jnp.where(here, turned(u2, shift), 0.0)
        lsum_ref[:, pl.ds(base, 128)] += jnp.where(here, turned(l2w, shift), 0.0)[0:1]
        inv = 1.0 / lsum_ref[...]
        att = usum_ref[...] * inv
        so_ref[d] = (yt_ref[d, 144:192, :].astype(F32) + att).astype(BF)
        gs = (grad_ref[...].astype(F32) * inv).astype(BF)
        gs_ref[d] = gs
        ds_ref[d] = jnp.sum(gs.astype(F32) * att, axis=0, keepdims=True)
        gs_wide = gs_ref[d, :, pl.ds(base, 128)].astype(F32)
        ds_wide = jnp.broadcast_to(ds_ref[d, :, pl.ds(base, 128)], (8, 128))
        gs2 = jnp.where(lane == d, turned(gs_wide, -shift), gs2)
        ds2 = jnp.where(lane == d, turned(ds_wide, -shift), ds2)
    gs2 = gs2.astype(BF)
    dp = mm(values, gs2)
    dscore = (m2_ref[...].astype(F32) * (dp - ds2[0:1])).astype(BF)
    dq_ref[...] = mm(both_t[0:48], dscore)
    dk = mm(query_t, dscore, NT)
    dv = mm(gs2, e2_ref[...], NT)
    dkv = jnp.concatenate([dk, dv], axis=0)
    own_ref[...] = dkv[:, 0:128]
    for e in range(3):
        send_ref[e] = dkv[:, 128 * e + 128 : 128 * e + 256].astype(BF)


def dscores(values, gs, ds, m_load, store):
    dp = mm(values, gs)
    step = 64
    for c in range(0, dp.shape[0], step):
        store(c, step, (m_load(c, step).astype(F32) * (dp[c : c + step] - ds)).astype(BF))


def backward_kernel(
    off_ref, y_ref, yt_ref, e0_ref, m0_ref, e1_ref, m1_ref, gs_ref, ds_ref, out_ref, tmp_ref
):
    o1 = pl.multiple_of(off_ref[0], 128)

    def store(c, n, v):
        tmp_ref[c : c + n, :] = v

    def block(d, carry):
        gs = gs_ref[d]
        dscores(y_ref[d, :, 96:144], gs, ds_ref[d], lambda c, n: m0_ref[d, c : c + n, :], store)
        dscore = tmp_ref[...]
        out_ref[d, 0:48, :] = mm(yt_ref[d, 48:96, :], dscore)
        out_ref[d, 48:96, :] = mm(yt_ref[d, 0:48, :], dscore, NT)
        out_ref[d, 96:144, :] = mm(gs, e0_ref[d], NT)
        return carry

    lax.fori_loop(0, 4, block, 0)
    values = jnp.concatenate([y_ref[d, pl.ds(o1, 128), 96:144] for d in range(4)], axis=0)
    queries = jnp.concatenate([yt_ref[d, 0:48, pl.ds(o1, 128)] for d in range(4)], axis=1)
    keys = jnp.concatenate([yt_ref[d, 48:96, pl.ds(o1, 128)] for d in range(4)], axis=1)
    gs = jnp.concatenate([gs_ref[d, :, pl.ds(o1, 128)] for d in range(4)], axis=1)
    ds = jnp.concatenate([ds_ref[d, :, pl.ds(o1, 128)] for d in range(4)], axis=1)
    dscores(values, gs, ds, lambda c, n: m1_ref[c : c + n, :], store)
    dscore = tmp_ref[...]
    dq = mm(keys, dscore)
    dk = mm(queries, dscore, NT)
    dv = mm(gs, e1_ref[...], NT)
    dall = jnp.concatenate([dq, dk, dv], axis=0)
    for d in range(4):
        out_ref[d, :, pl.ds(o1, 128)] += dall[:, 128 * d : 128 * d + 128]


def return_kernel(
    off_ref,
    dall_ref,
    own_ref,
    dq_ref,
    r1_ref,
    r2_ref,
    r3_ref,
    g0_ref,
    g1_ref,
    g2_ref,
    g3_ref,
    tab_ref,
    out_ref,
    sum_ref,
):
    o2 = off_ref[1]
    base = pl.multiple_of((o2 >> 7) << 7, 128)
    part = (o2 >> 5) & 3
    dkv = (
        own_ref[...]
        + r1_ref[...].astype(F32)
        + r2_ref[...].astype(F32)
        + r3_ref[...].astype(F32)
    )
    extra = jnp.concatenate([dq_ref[...], dkv], axis=0)
    lane = iota((1, 128), 1) >> 5
    rows = tab_ref.shape[0]
    for d in range(4):
        grad_ref = (g0_ref, g1_ref, g2_ref, g3_ref)[d]
        sum_ref[...] = dall_ref[d]
        sum_ref[:, pl.ds(base, 128)] += jnp.where(
            lane == part, turned(extra, 32 * (part - d)), 0.0
        )
        both = jnp.concatenate([sum_ref[...].astype(BF), grad_ref[...]], axis=0)
        onehot = jnp.where(tab_ref[:, d : d + 1] == iota((rows, BLK), 1), 1.0, 0.0).astype(BF)
        out_ref[:, 192 * d : 192 * d + 192] = mm(onehot, both, NT).astype(BF)


def out_kernel(j_ref, s0_ref, s1_ref, s2_ref, s3_ref, out_ref, tmp_ref):
    j = j_ref[0]
    for d in range(4):
        at = pl.multiple_of((j ^ d) * HD, 16)
        tmp_ref[pl.ds(at, HD), :] = (s0_ref, s1_ref, s2_ref, s3_ref)[d][...]
    out_ref[...] = mm(order_matrix(), tmp_ref[...], NT).astype(BF)


def unpack_kernel(ret_ref, prow_ref, pcol_ref, dqkv_ref, grad_ref, wide_ref):
    brow = prow_ref[...] >> 9
    bcol = pcol_ref[...] >> 9
    n = prow_ref.shape[1]
    before = iota((n, n), 1) < iota((n, n), 0)
    rank = jnp.sum(jnp.where((bcol == brow) & before, 1, 0), axis=1, keepdims=True)
    code = bcol * SLOTS + rank
    seat = iota((n, 256), 1)
    want = (((seat >> 3) & 7) * 4 + (seat >> 6)) * SLOTS + (seat & 7)
    picker = jnp.where(code == want, 1.0, 0.0).astype(BF)
    wide_ref[...] = ret_ref[...].astype(F32).reshape(8, 16, SLOTS, 768)
    width = HEADS * HD
    for h in range(HEADS):
        t, j = h // 4, h % 4
        rows = wide_ref[:, j * 4 + t, :, :].reshape(64, 768)
        stacked = jnp.concatenate(
            [rows[:, (j ^ b) * 192 : (j ^ b) * 192 + 192] for b in range(4)], axis=0
        ).astype(BF)
        got = mm(picker, stacked).astype(BF)
        for part in range(3):
            dqkv_ref[:, part * width + h * HD : part * width + h * HD + HD] = got[
                :, HD * part : HD * part + HD
            ]
        grad_ref[:, h * HD : h * HD + HD] = got[:, 144:192]


def swap(value, distance, count):
    return lax.ppermute(value, "seq", [(i, i ^ distance) for i in range(count)])


def on_device(
    tile_features,
    gate_weight,
    up_weight,
    down_weight,
    input_projection_weight,
    query_key_value_weight,
    positions,
    dilation_shift,
    slide_output_gradient,
):
    seq_count = lax.axis_size("seq")
    tile_count = lax.axis_size("tile")
    s = lax.axis_index("seq")
    t = lax.axis_index("tile")
    j = s % 4
    g = s // 4
    device_count = seq_count * tile_count
    my_device = s * tile_count + t
    tile_rows = tile_features.shape[0]
    head = 4 * t + j
    o1 = dilation_shift[0, head]
    o2 = dilation_shift[1, head]
    offs = jnp.stack([o1 * 128, (o2 & 3) * 128 + (o2 >> 2) * 32]).astype(I32)

    (ordered,) = call(order_kernel, [((192, BLK), BF)])(slide_output_gradient)
    pieces = ordered.reshape(4, HD, BLK)
    grads = [lax.dynamic_index_in_dim(pieces, j ^ d, 0, keepdims=False) for d in range(4)]
    grads = [grads[0]] + [swap(grads[d], d, seq_count) for d in range(1, 4)]

    feats32 = tile_features.astype(F32)
    feat_norm, feat_inv = normalize(feats32)
    feat_bf = feat_norm.astype(BF)
    gate_proj = jnp.dot(feat_bf, gate_weight, preferred_element_type=F32)
    up_proj = jnp.dot(feat_bf, up_weight, preferred_element_type=F32)
    gate_sigmoid = jax.nn.sigmoid(gate_proj)
    hidden = (gate_proj * gate_sigmoid * up_proj).astype(BF)
    embedding = (feats32 + jnp.dot(hidden, down_weight, preferred_element_type=F32)).astype(BF)
    tile_proj = jnp.dot(embedding, input_projection_weight, preferred_element_type=F32).astype(BF)
    slide32 = lax.optimization_barrier(tile_proj).astype(F32)
    slide_norm, slide_inv = normalize(slide32)
    qkv = jnp.dot(
        slide_norm.astype(BF), query_key_value_weight, preferred_element_type=F32
    ).astype(BF)

    all_pos = positions.reshape(device_count, tile_rows)
    own_pos = lax.dynamic_slice_in_dim(all_pos, my_device, 1, 0)
    own_col = own_pos.reshape(tile_rows, 1)
    (outgoing,) = call(
        pack_kernel,
        [((device_count * SLOTS, 768), BF)],
        [pltpu.VMEM((tile_rows, 192 * HEADS), BF), pltpu.VMEM((8, 16, SLOTS, 768), F32)],
    )(qkv, tile_proj, own_pos, own_col)
    arrived = lax.all_to_all(
        outgoing.reshape(device_count, SLOTS, 768),
        ("seq", "tile"),
        split_axis=0,
        concat_axis=0,
        tiled=True,
    ).reshape(device_count * SLOTS, 768)

    block_of = all_pos >> 9
    same = block_of[:, :, None] == block_of[:, None, :]
    before = jnp.arange(tile_rows)[:, None] < jnp.arange(tile_rows)[None, :]
    rank = jnp.sum((same & before[None]).astype(I32), axis=1)
    code = block_of * SLOTS + rank
    place = class_order(all_pos & 511) + 1
    blocks = 4 * g + (j ^ jnp.arange(4, dtype=I32))
    want = (blocks[:, None] * SLOTS + jnp.arange(SLOTS, dtype=I32)[None, :])[:, None, :, None]
    table = (
        jnp.sum(jnp.where(code[None, :, None, :] == want, place[None, :, None, :], 0), axis=3) - 1
    )
    table = table.reshape(4, device_count * SLOTS)
    table_col = table.T

    y, yt, y2 = call(
        place_kernel,
        [((4, BLK, 192), BF), ((4, 192, BLK), BF), ((128, 192), BF)],
        n_smem=1,
    )(offs, arrived, table)
    y2_in = [swap(y2, 4 * e, seq_count) for e in range(1, 4)]
    e0, m0, e1, m1, u, l = call(
        forward_kernel,
        [
            ((4, BLK, BLK), BF),
            ((4, BLK, BLK), BF),
            ((BLK, BLK), BF),
            ((BLK, BLK), BF),
            ((4, HD, BLK), F32),
            ((4, 1, BLK), F32),
        ],
        n_smem=1,
    )(offs, y, yt)
    so, gs, ds, own, send, dq2 = call(
        wide_kernel,
        [
            ((4, HD, BLK), BF),
            ((4, HD, BLK), BF),
            ((4, 1, BLK), F32),
            ((96, 128), F32),
            ((3, 96, 128), BF),
            ((HD, 128), F32),
        ],
        [
            pltpu.VMEM((BLK, 128), BF),
            pltpu.VMEM((BLK, 128), BF),
            pltpu.VMEM((HD, BLK), F32),
            pltpu.VMEM((1, BLK), F32),
        ],
        n_smem=1,
    )(offs, yt, y2, *y2_in, u, l, *grads)
    back = [swap(send[e - 1], 4 * e, seq_count) for e in range(1, 4)]
    (dall,) = call(
        backward_kernel,
        [((4, 144, BLK), F32)],
        [pltpu.VMEM((BLK, BLK), BF)],
        n_smem=1,
    )(offs, y, yt, e0, m0, e1, m1, gs, ds)
    (returning,) = call(
        return_kernel,
        [((device_count * SLOTS, 768), BF)],
        [pltpu.VMEM((144, BLK), F32)],
        n_smem=1,
    )(
        offs, dall, own, dq2, *back, *grads, table_col
    )
    returned = lax.all_to_all(
        returning.reshape(device_count, SLOTS, 768),
        ("seq", "tile"),
        split_axis=0,
        concat_axis=0,
        tiled=True,
    ).reshape(device_count * SLOTS, 768)

    parts = [so[0]] + [swap(so[d], d, seq_count) for d in range(1, 4)]
    (slide_out,) = call(
        out_kernel, [((BLK, 192), BF)], [pltpu.VMEM((192, BLK), BF)], n_smem=1
    )(j.reshape(1).astype(I32), *parts)

    dqkv, grad_rows = call(
        unpack_kernel,
        [((tile_rows, 3 * HEADS * HD), BF), ((tile_rows, HEADS * HD), BF)],
        [pltpu.VMEM((8, 16, SLOTS, 768), F32)],
    )(returned, own_pos, own_col)
    grad_norm = jnp.dot(dqkv, query_key_value_weight.T, preferred_element_type=F32)
    grad_slide = grad_rows.astype(F32) + norm_back(slide_norm, slide_inv, grad_norm)
    grad_embed = jnp.dot(
        grad_slide.astype(BF), input_projection_weight.T, preferred_element_type=F32
    ).astype(BF)
    grad_hidden = jnp.dot(grad_embed, down_weight.T, preferred_element_type=F32)
    grad_gate = (
        grad_hidden * up_proj * gate_sigmoid * (1.0 + gate_proj * (1.0 - gate_sigmoid))
    ).astype(BF)
    grad_up = (grad_hidden * gate_proj * gate_sigmoid).astype(BF)
    grad_feat = jnp.dot(grad_gate, gate_weight.T, preferred_element_type=F32) + jnp.dot(
        grad_up, up_weight.T, preferred_element_type=F32
    )
    embed32 = lax.optimization_barrier(grad_embed).astype(F32)
    tile_grad = (embed32 + norm_back(feat_norm, feat_inv, grad_feat)).astype(BF)
    return (slide_out, tile_grad)


def solution(mesh):
    placed = (P(("seq", "tile"), None), P(), P(), P(), P(), P(), P(), P(), P("seq", "tile"))
    return jax.shard_map(
        on_device,
        mesh=mesh,
        in_specs=placed,
        out_specs=(P("seq", "tile"), P(("seq", "tile"), None)),
        check_vma=False,
    )
```

```python
import jax
import jax.numpy as jnp
from jax import lax
from jax.experimental import pallas as pl
from jax.experimental.pallas import tpu as pltpu
from jax.sharding import PartitionSpec as P

HEADS = 16
HD = 48
EPSILON = 1e-06
SOFT_CAP = 50.0
SCALE = HD**-0.5
BLK = 512
SLOTS = 8
BF = jnp.bfloat16
F32 = jnp.float32
I32 = jnp.int32

NN = (((1,), (0,)), ((), ()))
NT = (((1,), (1,)), ((), ()))
TN = (((0,), (0,)), ((), ()))


def mm(a, b, dims=NN):
    return lax.dot_general(a, b, dims, preferred_element_type=F32)


def iota(shape, dim):
    return lax.broadcasted_iota(I32, shape, dim)


def class_order(row):
    return (row & 3) * 128 + ((row >> 2) & 3) * 32 + (row >> 4)


def order_matrix():
    return jnp.where(class_order(iota((BLK, BLK), 0)) == iota((BLK, BLK), 1), 1.0, 0.0).astype(BF)


def normalize(values):
    centred = values - jnp.mean(values, axis=-1, keepdims=True)
    inv_std = lax.rsqrt(jnp.mean(centred * centred, axis=-1, keepdims=True) + EPSILON)
    return (centred * inv_std, inv_std)


def norm_back(normed, inv_std, grads):
    mean_grad = jnp.mean(grads, axis=-1, keepdims=True)
    mean_cross = jnp.mean(grads * normed, axis=-1, keepdims=True)
    return (grads - mean_grad - normed * mean_cross) * inv_std


def call(kernel, outs, scratch=(), n_smem=0, n_any=0, limit=24):
    def run(*args):
        specs = [pl.BlockSpec(memory_space=pltpu.SMEM)] * n_smem
        specs += [pl.BlockSpec(memory_space=pltpu.VMEM)] * (len(args) - n_smem - n_any)
        specs += [pl.BlockSpec(memory_space=pl.ANY)] * n_any
        shapes = [jax.ShapeDtypeStruct(s, d) for s, d in outs]
        out_specs = [pl.BlockSpec(memory_space=pltpu.VMEM)] * len(outs)
        return pl.pallas_call(
            kernel,
            out_shape=shapes,
            in_specs=specs,
            out_specs=out_specs,
            scratch_shapes=list(scratch),
            compiler_params=pltpu.CompilerParams(vmem_limit_bytes=limit * 1024 * 1024),
        )(*args)

    return run


def order_kernel(grad_ref, g0_ref, g1_ref, g2_ref, g3_ref, tmp_ref):
    j = lax.axis_index("seq") & 3
    tmp_ref[...] = mm(grad_ref[...], order_matrix(), TN).astype(BF)
    for d, out_ref in enumerate((g0_ref, g1_ref, g2_ref, g3_ref)):
        out_ref[...] = tmp_ref[pl.ds(pl.multiple_of((j ^ d) * HD, 16), HD), :]


def offsets(shift_ref):
    head = 4 * lax.axis_index("tile") + (lax.axis_index("seq") & 3)
    o1 = shift_ref[0, head]
    o2 = shift_ref[1, head]
    return (o1 * 128, (o2 & 3) * 128, o2 >> 2)


def table_kernel(pos_ref, row_ref, col_ref):
    s = lax.axis_index("seq")
    pos = pos_ref[...].T
    n = pos.shape[0]
    block = pos >> 9
    seat = class_order(pos & (BLK - 1)) + 1
    lower = jnp.where(iota((n, n), 1) < iota((n, n), 0), 1.0, 0.0).astype(BF)
    high, low = [], []
    for d in range(4):
        owned = block == (s ^ d)
        rank = mm(lower, jnp.where(owned, 1.0, 0.0).astype(BF)).astype(I32)
        held = jnp.where(owned, seat, 0)
        for k in range(SLOTS):
            found = jnp.sum(jnp.where(rank == k, held, 0), axis=0, keepdims=True)
            high.append(found >> 4)
            low.append(found & 15)
    digits = jnp.concatenate(high + low, axis=0).astype(F32).astype(BF)
    lanes = n * SLOTS
    spread = jnp.where(iota((n, lanes), 0) == iota((n, lanes), 1) >> 3, 1.0, 0.0).astype(BF)
    wide = mm(digits, spread)
    wide = 16.0 * wide[0:32] + wide[32:64]
    own = iota((8, lanes), 0) == (iota((8, lanes), 1) & 7)
    rows = [
        jnp.sum(jnp.where(own, wide[8 * d : 8 * d + 8], 0.0), axis=0, keepdims=True)
        for d in range(4)
    ]
    table = jnp.concatenate(rows + rows, axis=0) - 1.0
    row_ref[...] = table.astype(I32)
    col_ref[...] = table.T.astype(I32)


def forward_mlp_kernel(
    feat_ref,
    pos_ref,
    gate_hbm,
    up_hbm,
    down_hbm,
    proj_hbm,
    qkvw_hbm,
    out_ref,
    x_ref,
    gate_ref,
    up_ref,
    wg_ref,
    wu_ref,
    wd_ref,
    wp_ref,
    wq_ref,
    qkv_ref,
    heads_ref,
    wide_ref,
    sems,
):
    ff = gate_hbm.shape[1]
    step = 512
    chunks = ff // step
    waits = []
    for c in range(chunks):
        at = pl.ds(c * step, step)
        trio = [
            pltpu.make_async_copy(gate_hbm.at[:, at], wg_ref.at[:, at], sems.at[3 * c]),
            pltpu.make_async_copy(up_hbm.at[:, at], wu_ref.at[:, at], sems.at[3 * c + 1]),
            pltpu.make_async_copy(down_hbm.at[at, :], wd_ref.at[at, :], sems.at[3 * c + 2]),
        ]
        for copy in trio:
            copy.start()
        waits.append(trio)
    last = [
        pltpu.make_async_copy(proj_hbm, wp_ref, sems.at[3 * chunks]),
        pltpu.make_async_copy(qkvw_hbm, wq_ref, sems.at[3 * chunks + 1]),
    ]
    for copy in last:
        copy.start()

    me = lax.axis_index("seq") * 4 + lax.axis_index("tile")
    brow = pos_ref[pl.ds(me, 1), :] >> 9
    n = brow.shape[1]
    bcol = jnp.broadcast_to(brow, (n, n)).T
    before = iota((n, n), 0) < iota((n, n), 1)
    rank = jnp.sum(jnp.where((bcol == brow) & before, 1, 0), axis=0, keepdims=True)
    code = brow * SLOTS + rank

    feats = feat_ref[...].astype(F32)
    normed = normalize(feats)[0].astype(BF)
    total = feats
    for c in range(chunks):
        at = slice(c * step, c * step + step)
        waits[c][0].wait()
        gate = mm(normed, wg_ref[:, at])
        gate_ref[:, at] = gate
        waits[c][1].wait()
        up = mm(normed, wu_ref[:, at])
        up_ref[:, at] = up
        hidden = (gate * jax.nn.sigmoid(gate) * up).astype(BF)
        waits[c][2].wait()
        total = total + mm(hidden, wd_ref[at, :])
    last[0].wait()
    x = mm(total.astype(BF), wp_ref[...]).astype(BF)
    x_ref[...] = x
    slide_norm = normalize(x.astype(F32))[0].astype(BF)
    last[1].wait()
    qkv_ref[...] = mm(slide_norm, wq_ref[...]).astype(BF)

    width = HEADS * HD
    for h in range(HEADS):
        for part in range(3):
            heads_ref[:, 192 * h + HD * part : 192 * h + HD * part + HD] = qkv_ref[
                :, part * width + h * HD : part * width + h * HD + HD
            ]
        heads_ref[:, 192 * h + 144 : 192 * h + 192] = x_ref[:, h * HD : h * HD + HD]
    seat = iota((64, n), 0)
    heads = heads_ref[...]
    for block in range(4):
        want = ((seat >> 3) * 4 + block) * SLOTS + (seat & 7)
        picker = jnp.where(code == want, 1.0, 0.0).astype(BF)
        rows = mm(picker, heads)
        for h in range(HEADS):
            t, j = h // 4, h % 4
            lane = (j ^ block) * 192
            wide_ref[:, j * 4 + t, :, lane : lane + 192] = rows[:, 192 * h : 192 * h + 192].reshape(
                8, SLOTS, 192
            )
    out_ref[...] = wide_ref[...].reshape(8 * 16 * SLOTS, 768).astype(BF)


def backward_mlp_kernel(
    ret_ref,
    pos_ref,
    feat_ref,
    x_ref,
    gate_ref,
    up_ref,
    wg_ref,
    wu_ref,
    wd_ref,
    wp_ref,
    wq_ref,
    out_ref,
    dqkv_ref,
    grad_ref,
    wide_ref,
):
    me = lax.axis_index("seq") * 4 + lax.axis_index("tile")
    brow = pos_ref[pl.ds(me, 1), :] >> 9
    n = brow.shape[1]
    bcol = jnp.broadcast_to(brow, (n, n)).T
    before = iota((n, n), 1) < iota((n, n), 0)
    rank = jnp.sum(jnp.where((bcol == brow) & before, 1, 0), axis=1, keepdims=True)
    code = bcol[:, 0:1] * SLOTS + rank
    seat = iota((n, 256), 1)
    want = (((seat >> 3) & 7) * 4 + (seat >> 6)) * SLOTS + (seat & 7)
    picker = jnp.where(code == want, 1.0, 0.0).astype(BF)
    wide_ref[...] = ret_ref[...].astype(F32).reshape(8, 16, SLOTS, 768)
    width = HEADS * HD
    for h in range(HEADS):
        t, j = h // 4, h % 4
        rows = wide_ref[:, j * 4 + t, :, :].reshape(64, 768)
        stacked = jnp.concatenate(
            [rows[:, (j ^ b) * 192 : (j ^ b) * 192 + 192] for b in range(4)], axis=0
        ).astype(BF)
        got = mm(picker, stacked)
        for part in range(3):
            dqkv_ref[:, part * width + h * HD : part * width + h * HD + HD] = got[
                :, HD * part : HD * part + HD
            ].astype(BF)
        grad_ref[:, h * HD : h * HD + HD] = got[:, 144:192]
    dnorm = mm(dqkv_ref[...], wq_ref[...], NT)
    slide_norm, slide_inv = normalize(x_ref[...].astype(F32))
    dslide = (grad_ref[...] + norm_back(slide_norm, slide_inv, dnorm)).astype(BF)
    dembed = mm(dslide, wp_ref[...], NT).astype(BF)
    ff = gate_ref.shape[1]
    step = 512
    dfeat = jnp.zeros(feat_ref.shape, F32)
    for c in range(ff // step):
        at = slice(c * step, c * step + step)
        dhidden = mm(dembed, wd_ref[at, :], NT)
        gate = gate_ref[:, at]
        sig = jax.nn.sigmoid(gate)
        dgate = (dhidden * up_ref[:, at] * sig * (1.0 + gate * (1.0 - sig))).astype(BF)
        dup = (dhidden * gate * sig).astype(BF)
        dfeat = dfeat + mm(dgate, wg_ref[:, at], NT) + mm(dup, wu_ref[:, at], NT)
    normed, inv = normalize(feat_ref[...].astype(F32))
    out_ref[...] = (dembed.astype(F32) + norm_back(normed, inv, dfeat)).astype(BF)


def place_kernel(shift_ref, recv_ref, tab_ref, y_ref, yt_ref, y2_ref):
    _, base, part = offsets(shift_ref)
    o2 = pl.multiple_of(base + 32 * part, 32)
    for d in range(4):
        tab = tab_ref[d : d + 1, :]
        onehot = jnp.where(iota((BLK, tab.shape[1]), 0) == tab, 1.0, 0.0).astype(BF)
        y = mm(onehot, recv_ref[:, 192 * d : 192 * d + 192])
        y_ref[d] = y.astype(BF)
        yt_ref[d] = y.T.astype(BF)
        y2_ref[32 * d : 32 * d + 32, :] = y_ref[d, pl.ds(o2, 32), :]


def score_rows(keys, queries_t, e_store, m_store):
    scores = mm(keys, queries_t)
    count, width = scores.shape
    total = jnp.zeros((8, width), F32)
    step = 64
    for c in range(0, count, step):
        t = jnp.tanh(scores[c : c + step] * (SCALE / SOFT_CAP))
        e = jnp.exp(SOFT_CAP * t)
        total = total + jnp.sum(e.reshape(step // 8, 8, width), axis=0)
        e_store(c, step, e.astype(BF))
        m_store(c, step, (e * (1.0 - t * t) * SCALE).astype(BF))
    return jnp.sum(total, axis=0, keepdims=True)


def forward_kernel(shift_ref, y_ref, yt_ref, e0_ref, m0_ref, e1_ref, m1_ref, u_ref, l_ref):
    o1 = pl.multiple_of(offsets(shift_ref)[0], 128)

    def block(d, carry):
        def e_store(c, n, v):
            e0_ref[d, c : c + n, :] = v

        def m_store(c, n, v):
            m0_ref[d, c : c + n, :] = v

        l_ref[d] = score_rows(y_ref[d, :, 48:96], yt_ref[d, 0:48, :], e_store, m_store)
        u_ref[d] = mm(yt_ref[d, 96:144, :], e0_ref[d])
        return carry

    lax.fori_loop(0, 4, block, 0)

    def e_store(c, n, v):
        e1_ref[c : c + n, :] = v

    def m_store(c, n, v):
        m1_ref[c : c + n, :] = v

    keys = jnp.concatenate([y_ref[d, pl.ds(o1, 128), 48:96] for d in range(4)], axis=0)
    queries = jnp.concatenate([yt_ref[d, 0:48, pl.ds(o1, 128)] for d in range(4)], axis=1)
    values = jnp.concatenate([yt_ref[d, 96:144, pl.ds(o1, 128)] for d in range(4)], axis=1)
    l1 = score_rows(keys, queries, e_store, m_store)
    u1 = mm(values, e1_ref[...])
    for d in range(4):
        u_ref[d, :, pl.ds(o1, 128)] += u1[:, 128 * d : 128 * d + 128]
        l_ref[d, :, pl.ds(o1, 128)] += l1[:, 128 * d : 128 * d + 128]


def turned(value, shift):
    return pltpu.roll(value, shift & 127, 1)


def wide_kernel(
    shift_ref,
    yt_ref,
    a0_ref,
    a1_ref,
    a2_ref,
    a3_ref,
    u_ref,
    l_ref,
    g0_ref,
    g1_ref,
    g2_ref,
    g3_ref,
    so0_ref,
    so1_ref,
    so2_ref,
    so3_ref,
    gs_ref,
    ds_ref,
    own_ref,
    send_ref,
    dq_ref,
    e2_ref,
    m2_ref,
    usum_ref,
    lsum_ref,
):
    _, base, part = offsets(shift_ref)
    base = pl.multiple_of(base, 128)
    y2 = jnp.concatenate([a0_ref[...], a1_ref[...], a2_ref[...], a3_ref[...]], axis=0)
    keys, values = y2[:, 48:96], y2[:, 96:144]
    both_t = y2[:, 48:144].astype(F32).T.astype(BF)
    query_t = a0_ref[:, 0:48].astype(F32).T.astype(BF)

    def e_store(c, n, v):
        e2_ref[c : c + n, :] = v

    def m_store(c, n, v):
        m2_ref[c : c + n, :] = v

    l2 = score_rows(keys, query_t, e_store, m_store)
    u2 = mm(both_t[48:96], e2_ref[...])
    l2w = jnp.broadcast_to(l2, (8, 128))
    lane = iota((1, 128), 1) >> 5
    gs2 = jnp.zeros((48, 128), F32)
    ds2 = jnp.zeros((8, 128), F32)
    for d in range(4):
        grad_ref = (g0_ref, g1_ref, g2_ref, g3_ref)[d]
        here = lane == part
        shift = 32 * (part - d)
        usum_ref[...] = u_ref[d]
        lsum_ref[...] = l_ref[d]
        usum_ref[:, pl.ds(base, 128)] += jnp.where(here, turned(u2, shift), 0.0)
        lsum_ref[:, pl.ds(base, 128)] += jnp.where(here, turned(l2w, shift), 0.0)[0:1]
        inv = 1.0 / lsum_ref[...]
        att = usum_ref[...] * inv
        (so0_ref, so1_ref, so2_ref, so3_ref)[d][...] = (yt_ref[d, 144:192, :].astype(F32) + att).astype(BF)
        gs = (grad_ref[...].astype(F32) * inv).astype(BF)
        gs_ref[d] = gs
        ds_ref[d] = jnp.sum(gs.astype(F32) * att, axis=0, keepdims=True)
        gs_wide = gs_ref[d, :, pl.ds(base, 128)].astype(F32)
        ds_wide = jnp.broadcast_to(ds_ref[d, :, pl.ds(base, 128)], (8, 128))
        gs2 = jnp.where(lane == d, turned(gs_wide, -shift), gs2)
        ds2 = jnp.where(lane == d, turned(ds_wide, -shift), ds2)
    gs2 = gs2.astype(BF)
    dp = mm(values, gs2)
    dscore = (m2_ref[...].astype(F32) * (dp - ds2[0:1])).astype(BF)
    dq_ref[...] = mm(both_t[0:48], dscore)
    dk = mm(query_t, dscore, NT)
    dv = mm(gs2, e2_ref[...], NT)
    dkv = jnp.concatenate([dk, dv], axis=0)
    own_ref[...] = dkv[:, 0:128]
    for e in range(3):
        send_ref[e] = dkv[:, 128 * e + 128 : 128 * e + 256].astype(BF)


def dscores(values, gs, ds, m_load, store):
    dp = mm(values, gs)
    step = 64
    for c in range(0, dp.shape[0], step):
        store(c, step, (m_load(c, step).astype(F32) * (dp[c : c + step] - ds)).astype(BF))


def backward_kernel(
    shift_ref, y_ref, yt_ref, e0_ref, m0_ref, e1_ref, m1_ref, gs_ref, ds_ref, out_ref, tmp_ref
):
    o1 = pl.multiple_of(offsets(shift_ref)[0], 128)

    def store(c, n, v):
        tmp_ref[c : c + n, :] = v

    def block(d, carry):
        gs = gs_ref[d]
        dscores(y_ref[d, :, 96:144], gs, ds_ref[d], lambda c, n: m0_ref[d, c : c + n, :], store)
        dscore = tmp_ref[...]
        out_ref[d, 0:48, :] = mm(yt_ref[d, 48:96, :], dscore)
        out_ref[d, 48:96, :] = mm(yt_ref[d, 0:48, :], dscore, NT)
        out_ref[d, 96:144, :] = mm(gs, e0_ref[d], NT)
        return carry

    lax.fori_loop(0, 4, block, 0)
    values = jnp.concatenate([y_ref[d, pl.ds(o1, 128), 96:144] for d in range(4)], axis=0)
    queries = jnp.concatenate([yt_ref[d, 0:48, pl.ds(o1, 128)] for d in range(4)], axis=1)
    keys = jnp.concatenate([yt_ref[d, 48:96, pl.ds(o1, 128)] for d in range(4)], axis=1)
    gs = jnp.concatenate([gs_ref[d, :, pl.ds(o1, 128)] for d in range(4)], axis=1)
    ds = jnp.concatenate([ds_ref[d, :, pl.ds(o1, 128)] for d in range(4)], axis=1)
    dscores(values, gs, ds, lambda c, n: m1_ref[c : c + n, :], store)
    dscore = tmp_ref[...]
    dq = mm(keys, dscore)
    dk = mm(queries, dscore, NT)
    dv = mm(gs, e1_ref[...], NT)
    dall = jnp.concatenate([dq, dk, dv], axis=0)
    for d in range(4):
        out_ref[d, :, pl.ds(o1, 128)] += dall[:, 128 * d : 128 * d + 128]


def return_kernel(
    shift_ref,
    dall_ref,
    own_ref,
    dq_ref,
    r1_ref,
    r2_ref,
    r3_ref,
    g0_ref,
    g1_ref,
    g2_ref,
    g3_ref,
    tab_ref,
    out_ref,
    sum_ref,
):
    _, base, part = offsets(shift_ref)
    base = pl.multiple_of(base, 128)
    dkv = (
        own_ref[...]
        + r1_ref[...].astype(F32)
        + r2_ref[...].astype(F32)
        + r3_ref[...].astype(F32)
    )
    extra = jnp.concatenate([dq_ref[...], dkv], axis=0)
    lane = iota((1, 128), 1) >> 5
    rows = tab_ref.shape[0]
    for d in range(4):
        grad_ref = (g0_ref, g1_ref, g2_ref, g3_ref)[d]
        sum_ref[...] = dall_ref[d]
        sum_ref[:, pl.ds(base, 128)] += jnp.where(
            lane == part, turned(extra, 32 * (part - d)), 0.0
        )
        both = jnp.concatenate([sum_ref[...].astype(BF), grad_ref[...]], axis=0)
        onehot = jnp.where(tab_ref[:, d : d + 1] == iota((rows, BLK), 1), 1.0, 0.0).astype(BF)
        out_ref[:, 192 * d : 192 * d + 192] = mm(onehot, both, NT).astype(BF)


def out_kernel(s0_ref, s1_ref, s2_ref, s3_ref, out_ref, tmp_ref):
    j = lax.axis_index("seq") & 3
    for d in range(4):
        at = pl.multiple_of((j ^ d) * HD, 16)
        tmp_ref[pl.ds(at, HD), :] = (s0_ref, s1_ref, s2_ref, s3_ref)[d][...]
    out_ref[...] = mm(order_matrix(), tmp_ref[...], NT).astype(BF)


def swap(value, distance, count):
    return lax.ppermute(value, "seq", [(i, i ^ distance) for i in range(count)])


def on_device(
    tile_features,
    gate_weight,
    up_weight,
    down_weight,
    input_projection_weight,
    query_key_value_weight,
    positions,
    dilation_shift,
    slide_output_gradient,
):
    seq_count = lax.axis_size("seq")
    device_count = seq_count * lax.axis_size("tile")
    rows, width = tile_features.shape
    ff = gate_weight.shape[1]
    slide_width = input_projection_weight.shape[1]
    all_pos = positions.reshape(device_count, rows)
    routed = ((device_count * SLOTS, slide_width), BF)
    weights = (gate_weight, up_weight, down_weight, input_projection_weight, query_key_value_weight)

    def exchange(block):
        return lax.all_to_all(
            block.reshape(device_count, SLOTS, slide_width),
            ("seq", "tile"),
            split_axis=0,
            concat_axis=0,
            tiled=True,
        ).reshape(device_count * SLOTS, slide_width)

    outgoing, x, gate_proj, up_proj = call(
        forward_mlp_kernel,
        [routed, ((rows, slide_width), BF), ((rows, ff), F32), ((rows, ff), F32)],
        [
            pltpu.VMEM((width, ff), BF),
            pltpu.VMEM((width, ff), BF),
            pltpu.VMEM((ff, width), BF),
            pltpu.VMEM((width, slide_width), BF),
            pltpu.VMEM((slide_width, 3 * slide_width), BF),
            pltpu.VMEM((rows, 3 * slide_width), BF),
            pltpu.VMEM((rows, 4 * slide_width), BF),
            pltpu.VMEM((8, 16, SLOTS, slide_width), F32),
            pltpu.SemaphoreType.DMA((14,)),
        ],
        n_any=5,
        limit=48,
    )(tile_features, all_pos, *weights)
    arrived = exchange(outgoing)

    grads = call(order_kernel, [((HD, BLK), BF)] * 4, [pltpu.VMEM((192, BLK), BF)])(
        slide_output_gradient
    )
    grads = [grads[0]] + [swap(grads[d], d, seq_count) for d in range(1, 4)]
    table, table_col = call(
        table_kernel,
        [((8, device_count * SLOTS), I32), ((device_count * SLOTS, 8), I32)],
    )(all_pos)

    y, yt, y2 = call(
        place_kernel,
        [((4, BLK, 192), BF), ((4, 192, BLK), BF), ((128, 192), BF)],
        n_smem=1,
    )(dilation_shift, arrived, table)
    y2_in = [swap(y2, 4 * e, seq_count) for e in range(1, 4)]
    e0, m0, e1, m1, u, l = call(
        forward_kernel,
        [
            ((4, BLK, BLK), BF),
            ((4, BLK, BLK), BF),
            ((BLK, BLK), BF),
            ((BLK, BLK), BF),
            ((4, HD, BLK), F32),
            ((4, 1, BLK), F32),
        ],
        n_smem=1,
    )(dilation_shift, y, yt)
    *parts, gs, ds, own, send, dq2 = call(
        wide_kernel,
        [((HD, BLK), BF)] * 4
        + [
            ((4, HD, BLK), BF),
            ((4, 1, BLK), F32),
            ((96, 128), F32),
            ((3, 96, 128), BF),
            ((HD, 128), F32),
        ],
        [
            pltpu.VMEM((BLK, 128), BF),
            pltpu.VMEM((BLK, 128), BF),
            pltpu.VMEM((HD, BLK), F32),
            pltpu.VMEM((1, BLK), F32),
        ],
        n_smem=1,
    )(dilation_shift, yt, y2, *y2_in, u, l, *grads)
    back = [swap(send[e - 1], 4 * e, seq_count) for e in range(1, 4)]
    parts = [parts[0]] + [swap(parts[d], d, seq_count) for d in range(1, 4)]
    (dall,) = call(
        backward_kernel,
        [((4, 144, BLK), F32)],
        [pltpu.VMEM((BLK, BLK), BF)],
        n_smem=1,
    )(dilation_shift, y, yt, e0, m0, e1, m1, gs, ds)
    dall, parts = lax.optimization_barrier((dall, parts))
    (returning,) = call(
        return_kernel,
        [routed],
        [pltpu.VMEM((144, BLK), F32)],
        n_smem=1,
    )(dilation_shift, dall, own, dq2, *back, *grads, table_col)
    returned = exchange(returning)
    (slide_out,) = call(out_kernel, [((BLK, 192), BF)], [pltpu.VMEM((192, BLK), BF)])(*parts)
    (tile_grad,) = call(
        backward_mlp_kernel,
        [((rows, width), BF)],
        [
            pltpu.VMEM((rows, 3 * slide_width), BF),
            pltpu.VMEM((rows, slide_width), F32),
            pltpu.VMEM((8, 16, SLOTS, slide_width), F32),
        ],
        limit=40,
    )(returned, all_pos, tile_features, x, gate_proj, up_proj, *weights)
    return (slide_out, tile_grad)


def solution(mesh):
    placed = (P(("seq", "tile"), None), P(), P(), P(), P(), P(), P(), P(), P("seq", "tile"))
    return jax.shard_map(
        on_device,
        mesh=mesh,
        in_specs=placed,
        out_specs=(P("seq", "tile"), P(("seq", "tile"), None)),
        check_vma=False,
    )
```

```python
import jax
import jax.numpy as jnp
from jax import lax
from jax.experimental import pallas as pl
from jax.experimental.pallas import tpu as pltpu
from jax.sharding import PartitionSpec as P

HEADS = 16
HD = 48
EPSILON = 1e-06
SOFT_CAP = 50.0
SCALE = HD**-0.5
BLK = 512
SLOTS = 8
BF = jnp.bfloat16
F32 = jnp.float32
I32 = jnp.int32

NN = (((1,), (0,)), ((), ()))
NT = (((1,), (1,)), ((), ()))
TN = (((0,), (0,)), ((), ()))


def mm(a, b, dims=NN):
    return lax.dot_general(a, b, dims, preferred_element_type=F32)


def iota(shape, dim):
    return lax.broadcasted_iota(I32, shape, dim)


def class_order(row):
    return (row & 3) * 128 + ((row >> 2) & 3) * 32 + (row >> 4)


def order_matrix():
    return jnp.where(class_order(iota((BLK, BLK), 0)) == iota((BLK, BLK), 1), 1.0, 0.0).astype(BF)


def normalize(values):
    centred = values - jnp.mean(values, axis=-1, keepdims=True)
    inv_std = lax.rsqrt(jnp.mean(centred * centred, axis=-1, keepdims=True) + EPSILON)
    return (centred * inv_std, inv_std)


def norm_back(normed, inv_std, grads):
    mean_grad = jnp.mean(grads, axis=-1, keepdims=True)
    mean_cross = jnp.mean(grads * normed, axis=-1, keepdims=True)
    return (grads - mean_grad - normed * mean_cross) * inv_std


def call(kernel, outs, scratch=(), n_smem=0, n_any=0, n_any_out=0, n_after=0, limit=4):
    def run(*args):
        specs = [pl.BlockSpec(memory_space=pltpu.SMEM)] * n_smem
        specs += [pl.BlockSpec(memory_space=pltpu.VMEM)] * (len(args) - n_smem - n_any - n_after)
        specs += [pl.BlockSpec(memory_space=pltpu.HBM)] * n_any
        specs += [pl.BlockSpec(memory_space=pl.ANY)] * n_after
        shapes = [jax.ShapeDtypeStruct(s, d) for s, d in outs]
        out_specs = [pl.BlockSpec(memory_space=pltpu.HBM)] * n_any_out
        out_specs += [pl.BlockSpec(memory_space=pltpu.VMEM)] * (len(outs) - n_any_out)
        return pl.pallas_call(
            kernel,
            out_shape=shapes,
            in_specs=specs,
            out_specs=out_specs,
            scratch_shapes=list(scratch),
            compiler_params=pltpu.CompilerParams(vmem_limit_bytes=limit * 1024 * 1024),
        )(*args)

    return run


def order_kernel(grad_ref, g0_ref, g1_ref, g2_ref, g3_ref, tmp_ref):
    j = lax.axis_index("seq") & 3
    tmp_ref[...] = mm(grad_ref[...], order_matrix()).astype(BF)
    for d, out_ref in enumerate((g0_ref, g1_ref, g2_ref, g3_ref)):
        out_ref[...] = tmp_ref[pl.ds(pl.multiple_of((j ^ d) * HD, 16), HD), :]


def offsets(shift_ref):
    head = 4 * lax.axis_index("tile") + (lax.axis_index("seq") & 3)
    o1 = shift_ref[0, head]
    o2 = shift_ref[1, head]
    return (o1 * 128, (o2 & 3) * 128, o2 >> 2)


def table_kernel(pos_ref, row_ref, col_ref):
    s = lax.axis_index("seq")
    pos = pos_ref[...].T
    n = pos.shape[0]
    block = pos >> 9
    seat = class_order(pos & (BLK - 1)) + 1
    lower = jnp.where(iota((n, n), 1) < iota((n, n), 0), 1.0, 0.0).astype(BF)
    high, low = [], []
    for d in range(4):
        owned = block == (s ^ d)
        rank = mm(lower, jnp.where(owned, 1.0, 0.0).astype(BF)).astype(I32)
        held = jnp.where(owned, seat, 0)
        for k in range(SLOTS):
            found = jnp.sum(jnp.where(rank == k, held, 0), axis=0, keepdims=True)
            high.append(found >> 4)
            low.append(found & 15)
    digits = jnp.concatenate(high + low, axis=0).astype(F32).astype(BF)
    lanes = n * SLOTS
    spread = jnp.where(iota((n, lanes), 0) == iota((n, lanes), 1) >> 3, 1.0, 0.0).astype(BF)
    wide = mm(digits, spread)
    wide = 16.0 * wide[0:32] + wide[32:64]
    own = iota((8, lanes), 0) == (iota((8, lanes), 1) & 7)
    rows = [
        jnp.sum(jnp.where(own, wide[8 * d : 8 * d + 8], 0.0), axis=0, keepdims=True)
        for d in range(4)
    ]
    table = jnp.concatenate(rows + rows, axis=0) - 1.0
    row_ref[...] = table.astype(I32)
    col_ref[...] = table.T.astype(I32)


def forward_mlp_kernel(
    feat_ref,
    pos_ref,
    gate_hbm,
    up_hbm,
    down_hbm,
    proj_hbm,
    qkvw_hbm,
    out_hbm,
    x_ref,
    gate_ref,
    up_ref,
    wg_ref,
    wu_ref,
    wd_ref,
    wp_ref,
    wq_ref,
    qkv_ref,
    heads_ref,
    picker_ref,
    tmp_ref,
    sems,
):
    ff = gate_hbm.shape[1]
    step = 512
    chunks = ff // step
    waits = []
    for c in range(chunks):
        at = pl.ds(c * step, step)
        trio = [
            pltpu.make_async_copy(gate_hbm.at[:, at], wg_ref.at[:, at], sems.at[3 * c]),
            pltpu.make_async_copy(up_hbm.at[:, at], wu_ref.at[:, at], sems.at[3 * c + 1]),
            pltpu.make_async_copy(down_hbm.at[at, :], wd_ref.at[at, :], sems.at[3 * c + 2]),
        ]
        for copy in trio:
            copy.start()
        waits.append(trio)
    last = [
        pltpu.make_async_copy(proj_hbm, wp_ref, sems.at[3 * chunks]),
        pltpu.make_async_copy(qkvw_hbm, wq_ref, sems.at[3 * chunks + 1]),
    ]
    for copy in last:
        copy.start()

    me = lax.axis_index("seq") * 4 + lax.axis_index("tile")
    brow = pos_ref[pl.ds(me, 1), :] >> 9
    n = brow.shape[1]
    bcol = jnp.broadcast_to(brow, (n, n)).T
    before = iota((n, n), 0) < iota((n, n), 1)
    rank = jnp.sum(jnp.where((bcol == brow) & before, 1, 0), axis=0, keepdims=True)
    code = brow * SLOTS + rank
    code = jnp.concatenate([code, code + 4096], axis=1)
    seat = iota((BLK, 2 * n), 0)
    want = (((seat >> 4) & 7) * 4 + (seat >> 7)) * SLOTS + (seat & 7) + 4096 * ((seat >> 3) & 1)
    picker_ref[...] = jnp.where(code == want, 1.0, 0.0).astype(BF)

    feats = feat_ref[...].astype(F32)
    normed = normalize(feats)[0].astype(BF)
    total = feats
    for c in range(chunks):
        at = slice(c * step, c * step + step)
        waits[c][0].wait()
        gate = mm(normed, wg_ref[:, at])
        gate_ref[:, at] = gate
        waits[c][1].wait()
        up = mm(normed, wu_ref[:, at])
        up_ref[:, at] = up
        hidden = (gate * jax.nn.sigmoid(gate) * up).astype(BF)
        waits[c][2].wait()
        total = total + mm(hidden, wd_ref[at, :])
    last[0].wait()
    x = mm(total.astype(BF), wp_ref[...]).astype(BF)
    x_ref[...] = x
    slide_norm = normalize(x.astype(F32))[0].astype(BF)
    last[1].wait()
    qkv_ref[...] = mm(slide_norm, wq_ref[...]).astype(BF)

    width = HEADS * HD
    outs = []
    for pair in range(HEADS // 2):
        j, t = pair // 2, 2 * (pair % 2)
        for tp in range(2):
            h = 4 * (t + tp) + j
            for part in range(3):
                heads_ref[n * tp : n * tp + n, HD * part : HD * part + HD] = qkv_ref[
                    :, part * width + h * HD : part * width + h * HD + HD
                ]
            heads_ref[n * tp : n * tp + n, 144:192] = x_ref[:, h * HD : h * HD + HD]
        rows = mm(picker_ref[...], heads_ref[...]).astype(BF)
        at = slice(16 * pair, 16 * pair + 16)
        for block in range(4):
            lane = (j ^ block) * 192
            tmp_ref[:, at, lane : lane + 192] = rows[128 * block : 128 * block + 128].reshape(
                8, 16, 192
            )
        copy = pltpu.make_async_copy(tmp_ref.at[:, at, :], out_hbm.at[:, at, :], sems.at[14 + pair])
        copy.start()
        outs.append(copy)
    for copy in outs:
        copy.wait()


def between_kernel(gate_ref, up_ref, wq_ref, a1_ref, a2_ref, wqp_ref):
    gate = gate_ref[...]
    sig = jax.nn.sigmoid(gate)
    a1_ref[...] = up_ref[...] * sig * (1.0 + gate * (1.0 - sig))
    a2_ref[...] = gate * sig
    width = HEADS * HD
    zeros = jnp.zeros((width, HD), BF)
    for h in range(HEADS):
        for part in range(3):
            wqp_ref[:, 192 * h + HD * part : 192 * h + HD * part + HD] = wq_ref[
                :, part * width + h * HD : part * width + h * HD + HD
            ]
        wqp_ref[:, 192 * h + 144 : 192 * h + 192] = zeros


def backward_mlp_kernel(
    ret_ref,
    pos_ref,
    feat_ref,
    x_ref,
    a1_ref,
    a2_ref,
    wqp_ref,
    gate_hbm,
    up_hbm,
    down_hbm,
    proj_hbm,
    out_ref,
    wg_ref,
    wu_ref,
    wd_ref,
    wp_ref,
    got_ref,
    grad_ref,
    sems,
):
    ff = a1_ref.shape[1]
    step = 512
    chunks = ff // step
    first = pltpu.make_async_copy(proj_hbm, wp_ref, sems.at[3 * chunks])
    first.start()
    waits = []
    for c in range(chunks):
        at = pl.ds(c * step, step)
        trio = [
            pltpu.make_async_copy(down_hbm.at[at, :], wd_ref.at[at, :], sems.at[3 * c]),
            pltpu.make_async_copy(gate_hbm.at[:, at], wg_ref.at[:, at], sems.at[3 * c + 1]),
            pltpu.make_async_copy(up_hbm.at[:, at], wu_ref.at[:, at], sems.at[3 * c + 2]),
        ]
        for copy in trio:
            copy.start()
        waits.append(trio)
    me = lax.axis_index("seq") * 4 + lax.axis_index("tile")
    brow = pos_ref[pl.ds(me, 1), :] >> 9
    n = brow.shape[1]
    bcol = jnp.broadcast_to(brow, (n, n)).T
    before = iota((n, n), 1) < iota((n, n), 0)
    rank = jnp.sum(jnp.where((bcol == brow) & before, 1, 0), axis=1, keepdims=True)
    code = bcol[:, 0:1] * SLOTS + rank
    code = jnp.concatenate([code, code + 4096], axis=0)
    seat = iota((2 * n, BLK), 1)
    want = (((seat >> 4) & 7) * 4 + (seat >> 7)) * SLOTS + (seat & 7) + 4096 * ((seat >> 3) & 1)
    picker = jnp.where(code == want, 1.0, 0.0).astype(BF)
    for pair in range(HEADS // 2):
        j, t = pair // 2, 2 * (pair % 2)
        tile = ret_ref[:, 16 * pair : 16 * pair + 16, :].reshape(128, 768)
        stacked = jnp.concatenate(
            [tile[:, (j ^ b) * 192 : (j ^ b) * 192 + 192] for b in range(4)], axis=0
        )
        got = mm(picker, stacked).astype(BF)
        for tp in range(2):
            h = 4 * (t + tp) + j
            got_ref[:, 192 * h : 192 * h + 192] = got[n * tp : n * tp + n]
            grad_ref[:, h * HD : h * HD + HD] = got[n * tp : n * tp + n, 144:192]
    dnorm = mm(got_ref[...], wqp_ref[...], NT)
    slide_norm, slide_inv = normalize(x_ref[...].astype(F32))
    dslide = (grad_ref[...].astype(F32) + norm_back(slide_norm, slide_inv, dnorm)).astype(BF)
    first.wait()
    dembed = mm(dslide, wp_ref[...], NT).astype(BF)
    dfeat = jnp.zeros(feat_ref.shape, F32)
    for c in range(chunks):
        at = slice(c * step, c * step + step)
        waits[c][0].wait()
        dhidden = mm(dembed, wd_ref[at, :], NT)
        dgate = (dhidden * a1_ref[:, at]).astype(BF)
        dup = (dhidden * a2_ref[:, at]).astype(BF)
        waits[c][1].wait()
        dfeat = dfeat + mm(dgate, wg_ref[:, at], NT)
        waits[c][2].wait()
        dfeat = dfeat + mm(dup, wu_ref[:, at], NT)
    normed, inv = normalize(feat_ref[...].astype(F32))
    out_ref[...] = (dembed.astype(F32) + norm_back(normed, inv, dfeat)).astype(BF)


def place_kernel(shift_ref, recv_ref, tab_ref, _after_ref, y_ref, yt_ref, y2_ref):
    _, base, part = offsets(shift_ref)
    o2 = pl.multiple_of(base + 32 * part, 32)
    for d in range(4):
        tab = tab_ref[d : d + 1, :]
        onehot = jnp.where(iota((BLK, tab.shape[1]), 0) == tab, 1.0, 0.0).astype(BF)
        y = mm(onehot, recv_ref[:, 192 * d : 192 * d + 192])
        y_ref[d] = y.astype(BF)
        yt_ref[d] = y.T.astype(BF)
        y2_ref[32 * d : 32 * d + 32, :] = y_ref[d, pl.ds(o2, 32), :]


def score_rows(keys, queries_t, e_store, m_store):
    scores = mm(keys, queries_t)
    count, width = scores.shape
    total = jnp.zeros((8, width), F32)
    step = 64
    for c in range(0, count, step):
        t = jnp.tanh(scores[c : c + step] * (SCALE / SOFT_CAP))
        e = jnp.exp(SOFT_CAP * t)
        total = total + jnp.sum(e.reshape(step // 8, 8, width), axis=0)
        e_store(c, step, e.astype(BF))
        m_store(c, step, (e * (1.0 - t * t) * SCALE).astype(BF))
    return jnp.sum(total, axis=0, keepdims=True)


def forward_kernel(shift_ref, y_ref, yt_ref, e0_ref, m0_ref, e1_ref, m1_ref, u_ref, l_ref):
    o1 = pl.multiple_of(offsets(shift_ref)[0], 128)

    def block(d, carry):
        def e_store(c, n, v):
            e0_ref[d, c : c + n, :] = v

        def m_store(c, n, v):
            m0_ref[d, c : c + n, :] = v

        l_ref[d] = score_rows(y_ref[d, :, 48:96], yt_ref[d, 0:48, :], e_store, m_store)
        u_ref[d] = mm(yt_ref[d, 96:144, :], e0_ref[d])
        return carry

    lax.fori_loop(0, 4, block, 0)

    def e_store(c, n, v):
        e1_ref[c : c + n, :] = v

    def m_store(c, n, v):
        m1_ref[c : c + n, :] = v

    keys = jnp.concatenate([y_ref[d, pl.ds(o1, 128), 48:96] for d in range(4)], axis=0)
    queries = jnp.concatenate([yt_ref[d, 0:48, pl.ds(o1, 128)] for d in range(4)], axis=1)
    values = jnp.concatenate([yt_ref[d, 96:144, pl.ds(o1, 128)] for d in range(4)], axis=1)
    l1 = score_rows(keys, queries, e_store, m_store)
    u1 = mm(values, e1_ref[...])
    for d in range(4):
        u_ref[d, :, pl.ds(o1, 128)] += u1[:, 128 * d : 128 * d + 128]
        l_ref[d, :, pl.ds(o1, 128)] += l1[:, 128 * d : 128 * d + 128]


def turned(value, shift):
    return pltpu.roll(value, shift & 127, 1)


def wide_kernel(
    shift_ref,
    yt_ref,
    a0_ref,
    a1_ref,
    a2_ref,
    a3_ref,
    u_ref,
    l_ref,
    g0_ref,
    g1_ref,
    g2_ref,
    g3_ref,
    so0_ref,
    so1_ref,
    so2_ref,
    so3_ref,
    gs_ref,
    ds_ref,
    own_ref,
    send_ref,
    dq_ref,
    e2_ref,
    m2_ref,
    usum_ref,
    lsum_ref,
):
    _, base, part = offsets(shift_ref)
    base = pl.multiple_of(base, 128)
    y2 = jnp.concatenate([a0_ref[...], a1_ref[...], a2_ref[...], a3_ref[...]], axis=0)
    keys, values = y2[:, 48:96], y2[:, 96:144]
    both_t = y2[:, 48:144].astype(F32).T.astype(BF)
    query_t = a0_ref[:, 0:48].astype(F32).T.astype(BF)

    def e_store(c, n, v):
        e2_ref[c : c + n, :] = v

    def m_store(c, n, v):
        m2_ref[c : c + n, :] = v

    l2 = score_rows(keys, query_t, e_store, m_store)
    u2 = mm(both_t[48:96], e2_ref[...])
    l2w = jnp.broadcast_to(l2, (8, 128))
    lane = iota((1, 128), 1) >> 5
    gs2 = jnp.zeros((48, 128), F32)
    ds2 = jnp.zeros((8, 128), F32)
    for d in range(4):
        grad_ref = (g0_ref, g1_ref, g2_ref, g3_ref)[d]
        here = lane == part
        shift = 32 * (part - d)
        usum_ref[...] = u_ref[d]
        lsum_ref[...] = l_ref[d]
        usum_ref[:, pl.ds(base, 128)] += jnp.where(here, turned(u2, shift), 0.0)
        lsum_ref[:, pl.ds(base, 128)] += jnp.where(here, turned(l2w, shift), 0.0)[0:1]
        inv = 1.0 / lsum_ref[...]
        att = usum_ref[...] * inv
        (so0_ref, so1_ref, so2_ref, so3_ref)[d][...] = (yt_ref[d, 144:192, :].astype(F32) + att).astype(BF)
        gs = (grad_ref[...].astype(F32) * inv).astype(BF)
        gs_ref[d] = gs
        ds_ref[d] = jnp.sum(gs.astype(F32) * att, axis=0, keepdims=True)
        gs_wide = gs_ref[d, :, pl.ds(base, 128)].astype(F32)
        ds_wide = jnp.broadcast_to(ds_ref[d, :, pl.ds(base, 128)], (8, 128))
        gs2 = jnp.where(lane == d, turned(gs_wide, -shift), gs2)
        ds2 = jnp.where(lane == d, turned(ds_wide, -shift), ds2)
    gs2 = gs2.astype(BF)
    dp = mm(values, gs2)
    dscore = (m2_ref[...].astype(F32) * (dp - ds2[0:1])).astype(BF)
    dq_ref[...] = mm(both_t[0:48], dscore)
    dk = mm(query_t, dscore, NT)
    dv = mm(gs2, e2_ref[...], NT)
    dkv = jnp.concatenate([dk, dv], axis=0)
    own_ref[...] = dkv[:, 0:128]
    for e in range(3):
        send_ref[e] = dkv[:, 128 * e + 128 : 128 * e + 256].astype(BF)


def dscores(values, gs, ds, m_load, store):
    dp = mm(values, gs)
    step = 64
    for c in range(0, dp.shape[0], step):
        store(c, step, (m_load(c, step).astype(F32) * (dp[c : c + step] - ds)).astype(BF))


def backward_kernel(
    shift_ref, y_ref, yt_ref, e0_ref, m0_ref, e1_ref, m1_ref, gs_ref, ds_ref, out_ref, tmp_ref
):
    o1 = pl.multiple_of(offsets(shift_ref)[0], 128)

    def store(c, n, v):
        tmp_ref[c : c + n, :] = v

    def block(d, carry):
        gs = gs_ref[d]
        dscores(y_ref[d, :, 96:144], gs, ds_ref[d], lambda c, n: m0_ref[d, c : c + n, :], store)
        dscore = tmp_ref[...]
        out_ref[d, 0:48, :] = mm(yt_ref[d, 48:96, :], dscore)
        out_ref[d, 48:96, :] = mm(yt_ref[d, 0:48, :], dscore, NT)
        out_ref[d, 96:144, :] = mm(gs, e0_ref[d], NT)
        return carry

    lax.fori_loop(0, 4, block, 0)
    values = jnp.concatenate([y_ref[d, pl.ds(o1, 128), 96:144] for d in range(4)], axis=0)
    queries = jnp.concatenate([yt_ref[d, 0:48, pl.ds(o1, 128)] for d in range(4)], axis=1)
    keys = jnp.concatenate([yt_ref[d, 48:96, pl.ds(o1, 128)] for d in range(4)], axis=1)
    gs = jnp.concatenate([gs_ref[d, :, pl.ds(o1, 128)] for d in range(4)], axis=1)
    ds = jnp.concatenate([ds_ref[d, :, pl.ds(o1, 128)] for d in range(4)], axis=1)
    dscores(values, gs, ds, lambda c, n: m1_ref[c : c + n, :], store)
    dscore = tmp_ref[...]
    dq = mm(keys, dscore)
    dk = mm(queries, dscore, NT)
    dv = mm(gs, e1_ref[...], NT)
    dall = jnp.concatenate([dq, dk, dv], axis=0)
    for d in range(4):
        out_ref[d, :, pl.ds(o1, 128)] += dall[:, 128 * d : 128 * d + 128]


def return_kernel(
    shift_ref,
    dall_ref,
    own_ref,
    dq_ref,
    r1_ref,
    r2_ref,
    r3_ref,
    g0_ref,
    g1_ref,
    g2_ref,
    g3_ref,
    tab_ref,
    out_hbm,
    sum_ref,
    out_ref,
    sems,
):
    _, base, part = offsets(shift_ref)
    base = pl.multiple_of(base, 128)
    dkv = (
        own_ref[...]
        + r1_ref[...].astype(F32)
        + r2_ref[...].astype(F32)
        + r3_ref[...].astype(F32)
    )
    extra = jnp.concatenate([dq_ref[...], dkv], axis=0)
    lane = iota((1, 128), 1) >> 5
    rows = tab_ref.shape[0]
    outs = []
    for d in range(4):
        grad_ref = (g0_ref, g1_ref, g2_ref, g3_ref)[d]
        sum_ref[...] = dall_ref[d]
        sum_ref[:, pl.ds(base, 128)] += jnp.where(
            lane == part, turned(extra, 32 * (part - d)), 0.0
        )
        both = jnp.concatenate([sum_ref[...].astype(BF), grad_ref[...]], axis=0)
        onehot = jnp.where(tab_ref[:, d : d + 1] == iota((rows, BLK), 1), 1.0, 0.0).astype(BF)
        out_ref[:, 192 * d : 192 * d + 192] = mm(onehot, both, NT).astype(BF)
        if d % 2:
            at = pl.ds(384 * (d // 2), 384)
            copy = pltpu.make_async_copy(out_ref.at[:, at], out_hbm.at[:, at], sems.at[d // 2])
            copy.start()
            outs.append(copy)
    for copy in outs:
        copy.wait()


def out_kernel(s0_ref, s1_ref, s2_ref, s3_ref, _after_ref, out_ref, tmp_ref):
    j = lax.axis_index("seq") & 3
    for d in range(4):
        at = pl.multiple_of((j ^ d) * HD, 16)
        tmp_ref[pl.ds(at, HD), :] = (s0_ref, s1_ref, s2_ref, s3_ref)[d][...]
    out_ref[...] = mm(tmp_ref[...], order_matrix(), NT).astype(BF)


def swap(value, distance, count):
    return lax.ppermute(value, "seq", [(i, i ^ distance) for i in range(count)])


def on_device(
    tile_features,
    gate_weight,
    up_weight,
    down_weight,
    input_projection_weight,
    query_key_value_weight,
    positions,
    dilation_shift,
    slide_output_gradient,
):
    seq_count = lax.axis_size("seq")
    device_count = seq_count * lax.axis_size("tile")
    rows, width = tile_features.shape
    ff = gate_weight.shape[1]
    slide_width = input_projection_weight.shape[1]
    all_pos = positions.reshape(device_count, rows)
    routed = ((8, 16 * SLOTS, slide_width), BF)
    weights = (gate_weight, up_weight, down_weight, input_projection_weight, query_key_value_weight)

    def exchange(block):
        return lax.all_to_all(
            block.reshape(device_count, SLOTS, slide_width),
            ("seq", "tile"),
            split_axis=0,
            concat_axis=0,
            tiled=True,
        ).reshape(device_count * SLOTS, slide_width)

    outgoing, x, gate_proj, up_proj = call(
        forward_mlp_kernel,
        [routed, ((rows, slide_width), BF), ((rows, ff), F32), ((rows, ff), F32)],
        [
            pltpu.VMEM((width, ff), BF),
            pltpu.VMEM((width, ff), BF),
            pltpu.VMEM((ff, width), BF),
            pltpu.VMEM((width, slide_width), BF),
            pltpu.VMEM((slide_width, 3 * slide_width), BF),
            pltpu.VMEM((rows, 3 * slide_width), BF),
            pltpu.VMEM((2 * rows, 192), BF),
            pltpu.VMEM((BLK, 2 * rows), BF),
            pltpu.VMEM((8, 16 * SLOTS, slide_width), BF),
            pltpu.SemaphoreType.DMA((14 + HEADS // 2,)),
        ],
        n_any=5,
        n_any_out=1,
        limit=34,
    )(tile_features, all_pos, *weights)
    arrived = exchange(outgoing)

    grads = call(order_kernel, [((HD, BLK), BF)] * 4, [pltpu.VMEM((192, BLK), BF)])(
        slide_output_gradient.T
    )
    grads = [grads[0]] + [swap(grads[d], d, seq_count) for d in range(1, 4)]
    table, table_col = call(
        table_kernel,
        [((8, device_count * SLOTS), I32), ((device_count * SLOTS, 8), I32)],
    )(all_pos)

    a1, a2, wqp = call(
        between_kernel,
        [((rows, ff), F32), ((rows, ff), F32), ((slide_width, 4 * slide_width), BF)],
    )(gate_proj, up_proj, query_key_value_weight)

    y, yt, y2 = call(
        place_kernel,
        [((4, BLK, 192), BF), ((4, 192, BLK), BF), ((128, 192), BF)],
        n_smem=1,
        n_after=1,
    )(dilation_shift, arrived, table, a1)
    y2_in = [swap(y2, 4 * e, seq_count) for e in range(1, 4)]
    e0, m0, e1, m1, u, l = call(
        forward_kernel,
        [
            ((4, BLK, BLK), BF),
            ((4, BLK, BLK), BF),
            ((BLK, BLK), BF),
            ((BLK, BLK), BF),
            ((4, HD, BLK), F32),
            ((4, 1, BLK), F32),
        ],
        n_smem=1,
    )(dilation_shift, y, yt)
    *parts, gs, ds, own, send, dq2 = call(
        wide_kernel,
        [((HD, BLK), BF)] * 4
        + [
            ((4, HD, BLK), BF),
            ((4, 1, BLK), F32),
            ((96, 128), F32),
            ((3, 96, 128), BF),
            ((HD, 128), F32),
        ],
        [
            pltpu.VMEM((BLK, 128), BF),
            pltpu.VMEM((BLK, 128), BF),
            pltpu.VMEM((HD, BLK), F32),
            pltpu.VMEM((1, BLK), F32),
        ],
        n_smem=1,
    )(dilation_shift, yt, y2, *y2_in, u, l, *grads)
    back = [swap(send[e - 1], 4 * e, seq_count) for e in range(1, 4)]
    parts = [parts[0]] + [swap(parts[d], d, seq_count) for d in range(1, 4)]
    (dall,) = call(
        backward_kernel,
        [((4, 144, BLK), F32)],
        [pltpu.VMEM((BLK, BLK), BF)],
        n_smem=1,
    )(dilation_shift, y, yt, e0, m0, e1, m1, gs, ds)
    (returning,) = call(
        return_kernel,
        [((device_count * SLOTS, slide_width), BF)],
        [
            pltpu.VMEM((144, BLK), F32),
            pltpu.VMEM((device_count * SLOTS, slide_width), BF),
            pltpu.SemaphoreType.DMA((2,)),
        ],
        n_smem=1,
        n_any_out=1,
        limit=6,
    )(dilation_shift, dall, own, dq2, *back, *grads, table_col)
    returned = exchange(returning)
    (tile_grad,) = call(
        backward_mlp_kernel,
        [((rows, width), BF)],
        [
            pltpu.VMEM((width, ff), BF),
            pltpu.VMEM((width, ff), BF),
            pltpu.VMEM((ff, width), BF),
            pltpu.VMEM((width, slide_width), BF),
            pltpu.VMEM((rows, 4 * slide_width), BF),
            pltpu.VMEM((rows, slide_width), BF),
            pltpu.SemaphoreType.DMA((13,)),
        ],
        n_any=4,
        limit=32,
    )(
        returned.reshape(8, 16 * SLOTS, slide_width),
        all_pos,
        tile_features,
        x,
        a1,
        a2,
        wqp,
        *weights[:4],
    )
    (slide_out,) = call(
        out_kernel, [((192, BLK), BF)], [pltpu.VMEM((192, BLK), BF)], n_after=1
    )(*parts, tile_grad)
    return (slide_out.T, tile_grad)


def solution(mesh):
    placed = (P(("seq", "tile"), None), P(), P(), P(), P(), P(), P(), P(), P("seq", "tile"))
    return jax.shard_map(
        on_device,
        mesh=mesh,
        in_specs=placed,
        out_specs=(P("seq", "tile"), P(("seq", "tile"), None)),
        check_vma=False,
    )
```

```python
import jax
import jax.numpy as jnp
from jax import lax
from jax.experimental import pallas as pl
from jax.experimental.pallas import tpu as pltpu
from jax.sharding import PartitionSpec as P

HEADS = 16
HD = 48
EPSILON = 1e-06
SOFT_CAP = 50.0
SCALE = HD**-0.5
BLK = 512
SLOTS = 8
BF = jnp.bfloat16
F32 = jnp.float32
I32 = jnp.int32

NN = (((1,), (0,)), ((), ()))
NT = (((1,), (1,)), ((), ()))
TN = (((0,), (0,)), ((), ()))


def mm(a, b, dims=NN):
    return lax.dot_general(a, b, dims, preferred_element_type=F32)


def iota(shape, dim):
    return lax.broadcasted_iota(I32, shape, dim)


def class_order(row):
    return (row & 3) * 128 + ((row >> 2) & 3) * 32 + (row >> 4)


def order_matrix():
    return jnp.where(class_order(iota((BLK, BLK), 0)) == iota((BLK, BLK), 1), 1.0, 0.0).astype(BF)


def normalize(values):
    centred = values - jnp.mean(values, axis=-1, keepdims=True)
    inv_std = lax.rsqrt(jnp.mean(centred * centred, axis=-1, keepdims=True) + EPSILON)
    return (centred * inv_std, inv_std)


def norm_back(normed, inv_std, grads):
    mean_grad = jnp.mean(grads, axis=-1, keepdims=True)
    mean_cross = jnp.mean(grads * normed, axis=-1, keepdims=True)
    return (grads - mean_grad - normed * mean_cross) * inv_std


def call(kernel, outs, scratch=(), n_smem=0, n_any=0, n_hbm=0, n_hbm_out=0, limit=4):
    def run(*args):
        n_vmem = len(args) - n_smem - n_any - n_hbm
        specs = [pl.BlockSpec(memory_space=pltpu.SMEM)] * n_smem
        specs += [pl.BlockSpec(memory_space=pltpu.VMEM)] * n_vmem
        specs += [pl.BlockSpec(memory_space=pl.ANY)] * n_any
        specs += [pl.BlockSpec(memory_space=pltpu.HBM)] * n_hbm
        out_specs = [pl.BlockSpec(memory_space=pltpu.HBM)] * n_hbm_out
        out_specs += [pl.BlockSpec(memory_space=pltpu.VMEM)] * (len(outs) - n_hbm_out)
        shapes = [pltpu.HBM(shape, kind) for shape, kind in outs[:n_hbm_out]]
        shapes += [jax.ShapeDtypeStruct(shape, kind) for shape, kind in outs[n_hbm_out:]]
        cut = len(args) - n_hbm
        held = [pltpu.with_memory_space_constraint(x, pltpu.HBM) for x in args[cut:]]
        return pl.pallas_call(
            kernel,
            out_shape=shapes,
            in_specs=specs,
            out_specs=out_specs,
            scratch_shapes=list(scratch),
            compiler_params=pltpu.CompilerParams(vmem_limit_bytes=limit * 1024 * 1024),
        )(*args[:cut], *held)

    return run


def started(copies):
    for copy in copies:
        copy.start()
    return copies


def finish(copies):
    for copy in copies:
        copy.wait()


def order_kernel(grad_ref, g0_hbm, g1_hbm, g2_hbm, g3_hbm, tmp_ref, sems):
    j = lax.axis_index("seq") & 3
    tmp_ref[...] = mm(grad_ref[...], order_matrix()).astype(BF)
    finish(
        started(
            [
                pltpu.make_async_copy(
                    tmp_ref.at[pl.ds(pl.multiple_of((j ^ d) * HD, 16), HD), :], out, sems.at[d]
                )
                for d, out in enumerate((g0_hbm, g1_hbm, g2_hbm, g3_hbm))
            ]
        )
    )


def offsets(shift_ref):
    head = 4 * lax.axis_index("tile") + (lax.axis_index("seq") & 3)
    o1 = shift_ref[0, head]
    o2 = shift_ref[1, head]
    return (o1 * 128, (o2 & 3) * 128, o2 >> 2)


def table_kernel(pos_ref, row_hbm, col_hbm, row_ref, col_ref, sems):
    s = lax.axis_index("seq")
    pos = pos_ref[...].T
    n = pos.shape[0]
    block = pos >> 9
    seat = class_order(pos & (BLK - 1)) + 1
    lower = jnp.where(iota((n, n), 1) < iota((n, n), 0), 1.0, 0.0).astype(BF)
    high, low = [], []
    for d in range(4):
        owned = block == (s ^ d)
        rank = mm(lower, jnp.where(owned, 1.0, 0.0).astype(BF)).astype(I32)
        held = jnp.where(owned, seat, 0)
        for k in range(SLOTS):
            found = jnp.sum(jnp.where(rank == k, held, 0), axis=0, keepdims=True)
            high.append(found >> 4)
            low.append(found & 15)
    digits = jnp.concatenate(high + low, axis=0).astype(F32).astype(BF)
    lanes = n * SLOTS
    spread = jnp.where(iota((n, lanes), 0) == iota((n, lanes), 1) >> 3, 1.0, 0.0).astype(BF)
    wide = mm(digits, spread)
    wide = 16.0 * wide[0:32] + wide[32:64]
    own = iota((8, lanes), 0) == (iota((8, lanes), 1) & 7)
    rows = [
        jnp.sum(jnp.where(own, wide[8 * d : 8 * d + 8], 0.0), axis=0, keepdims=True)
        for d in range(4)
    ]
    table = jnp.concatenate(rows + rows, axis=0) - 1.0
    row_ref[...] = table.astype(I32)
    col_ref[...] = table.T.astype(I32)
    finish(
        started(
            [
                pltpu.make_async_copy(row_ref, row_hbm, sems.at[0]),
                pltpu.make_async_copy(col_ref, col_hbm, sems.at[1]),
            ]
        )
    )


def forward_mlp_kernel(
    feat_hbm,
    pos_hbm,
    gate_hbm,
    up_hbm,
    down_hbm,
    proj_hbm,
    qkvw_hbm,
    out_hbm,
    x_hbm,
    a1_hbm,
    a2_hbm,
    feat_ref,
    pos_ref,
    wg_ref,
    wu_ref,
    wd_ref,
    wp_ref,
    wq_ref,
    x_ref,
    a1_ref,
    a2_ref,
    qkv_ref,
    heads_ref,
    picker_ref,
    tmp_ref,
    sems,
    out_sems,
):
    ff = gate_hbm.shape[1]
    step = 512
    chunks = ff // step
    first = started(
        [
            pltpu.make_async_copy(feat_hbm, feat_ref, sems.at[3 * chunks]),
            pltpu.make_async_copy(pos_hbm, pos_ref, sems.at[3 * chunks + 1]),
        ]
    )
    waits = []
    for c in range(chunks):
        at = pl.ds(c * step, step)
        waits.append(
            started(
                [
                    pltpu.make_async_copy(gate_hbm.at[:, at], wg_ref.at[:, at], sems.at[3 * c]),
                    pltpu.make_async_copy(up_hbm.at[:, at], wu_ref.at[:, at], sems.at[3 * c + 1]),
                    pltpu.make_async_copy(down_hbm.at[at, :], wd_ref.at[at, :], sems.at[3 * c + 2]),
                ]
            )
        )
    last = started(
        [
            pltpu.make_async_copy(proj_hbm, wp_ref, sems.at[3 * chunks + 2]),
            pltpu.make_async_copy(qkvw_hbm, wq_ref, sems.at[3 * chunks + 3]),
        ]
    )
    finish(first)

    me = lax.axis_index("seq") * 4 + lax.axis_index("tile")
    brow = pos_ref[pl.ds(me, 1), :] >> 9
    n = brow.shape[1]
    bcol = jnp.broadcast_to(brow, (n, n)).T
    before = iota((n, n), 0) < iota((n, n), 1)
    rank = jnp.sum(jnp.where((bcol == brow) & before, 1, 0), axis=0, keepdims=True)
    code = brow * SLOTS + rank
    code = jnp.concatenate([code, code + 4096], axis=1)
    seat = iota((BLK, 2 * n), 0)
    want = (((seat >> 4) & 7) * 4 + (seat >> 7)) * SLOTS + (seat & 7) + 4096 * ((seat >> 3) & 1)
    picker_ref[...] = jnp.where(code == want, 1.0, 0.0).astype(BF)

    feats = feat_ref[...].astype(F32)
    normed = normalize(feats)[0].astype(BF)
    total = feats
    outs = []
    for c in range(chunks):
        at = slice(c * step, c * step + step)
        waits[c][0].wait()
        gate = mm(normed, wg_ref[:, at])
        waits[c][1].wait()
        up = mm(normed, wu_ref[:, at])
        sig = jax.nn.sigmoid(gate)
        silu = gate * sig
        hidden = (silu * up).astype(BF)
        a1_ref[:, at] = (up * (sig + silu * (1.0 - sig))).astype(BF)
        a2_ref[:, at] = silu.astype(BF)
        waits[c][2].wait()
        total = total + mm(hidden, wd_ref[at, :])
    outs += started(
        [
            pltpu.make_async_copy(a1_ref, a1_hbm, out_sems.at[0]),
            pltpu.make_async_copy(a2_ref, a2_hbm, out_sems.at[1]),
        ]
    )
    last[0].wait()
    x = mm(total.astype(BF), wp_ref[...]).astype(BF)
    x_ref[...] = x
    outs += started([pltpu.make_async_copy(x_ref, x_hbm, out_sems.at[2])])
    slide_norm = normalize(x.astype(F32))[0].astype(BF)
    last[1].wait()
    qkv_ref[...] = mm(slide_norm, wq_ref[...]).astype(BF)

    width = HEADS * HD
    for pair in range(HEADS // 2):
        j, t = pair // 2, 2 * (pair % 2)
        for tp in range(2):
            h = 4 * (t + tp) + j
            for part in range(3):
                heads_ref[n * tp : n * tp + n, HD * part : HD * part + HD] = qkv_ref[
                    :, part * width + h * HD : part * width + h * HD + HD
                ]
            heads_ref[n * tp : n * tp + n, 144:192] = x_ref[:, h * HD : h * HD + HD]
        rows = mm(picker_ref[...], heads_ref[...]).astype(BF)
        at = slice(16 * pair, 16 * pair + 16)
        for block in range(4):
            lane = (j ^ block) * 192
            tmp_ref[:, at, lane : lane + 192] = rows[128 * block : 128 * block + 128].reshape(
                8, 16, 192
            )
        outs += started(
            [
                pltpu.make_async_copy(
                    tmp_ref.at[:, at, :], out_hbm.at[:, at, :], out_sems.at[3 + pair]
                )
            ]
        )
    finish(outs)


def backward_mlp_kernel(
    ret_ref,
    pos_hbm,
    feat_hbm,
    x_hbm,
    a1_hbm,
    a2_hbm,
    gate_hbm,
    up_hbm,
    down_hbm,
    proj_hbm,
    qkvw_hbm,
    out_ref,
    pos_ref,
    feat_ref,
    x_ref,
    a1_ref,
    a2_ref,
    wg_ref,
    wu_ref,
    wd_ref,
    wp_ref,
    wq_ref,
    dqkv_ref,
    grad_ref,
    sems,
):
    ff = gate_hbm.shape[1]
    step = 512
    chunks = ff // step
    pairs = (
        (pos_hbm, pos_ref),
        (x_hbm, x_ref),
        (qkvw_hbm, wq_ref),
        (proj_hbm, wp_ref),
        (a1_hbm, a1_ref),
        (a2_hbm, a2_ref),
        (feat_hbm, feat_ref),
    )
    first = started(
        [
            pltpu.make_async_copy(here, there, sems.at[3 * chunks + i])
            for i, (here, there) in enumerate(pairs)
        ]
    )
    waits = []
    for c in range(chunks):
        at = pl.ds(c * step, step)
        waits.append(
            started(
                [
                    pltpu.make_async_copy(down_hbm.at[at, :], wd_ref.at[at, :], sems.at[3 * c]),
                    pltpu.make_async_copy(gate_hbm.at[:, at], wg_ref.at[:, at], sems.at[3 * c + 1]),
                    pltpu.make_async_copy(up_hbm.at[:, at], wu_ref.at[:, at], sems.at[3 * c + 2]),
                ]
            )
        )
    first[0].wait()
    me = lax.axis_index("seq") * 4 + lax.axis_index("tile")
    brow = pos_ref[pl.ds(me, 1), :] >> 9
    n = brow.shape[1]
    bcol = jnp.broadcast_to(brow, (n, n)).T
    before = iota((n, n), 1) < iota((n, n), 0)
    rank = jnp.sum(jnp.where((bcol == brow) & before, 1, 0), axis=1, keepdims=True)
    code = bcol[:, 0:1] * SLOTS + rank
    code = jnp.concatenate([code, code + 4096], axis=0)
    seat = iota((2 * n, BLK), 1)
    want = (((seat >> 4) & 7) * 4 + (seat >> 7)) * SLOTS + (seat & 7) + 4096 * ((seat >> 3) & 1)
    picker = jnp.where(code == want, 1.0, 0.0).astype(BF)
    width = HEADS * HD
    for pair in range(HEADS // 2):
        j, t = pair // 2, 2 * (pair % 2)
        tile = ret_ref[:, 16 * pair : 16 * pair + 16, :].reshape(128, 768)
        stacked = jnp.concatenate(
            [tile[:, (j ^ b) * 192 : (j ^ b) * 192 + 192] for b in range(4)], axis=0
        )
        got = mm(picker, stacked).astype(BF)
        for tp in range(2):
            h = 4 * (t + tp) + j
            mine = got[n * tp : n * tp + n]
            for part in range(3):
                dqkv_ref[:, part * width + h * HD : part * width + h * HD + HD] = mine[
                    :, HD * part : HD * part + HD
                ]
            grad_ref[:, h * HD : h * HD + HD] = mine[:, 144:192]
    first[1].wait()
    slide_norm, slide_inv = normalize(x_ref[...].astype(F32))
    first[2].wait()
    dnorm = mm(dqkv_ref[...], wq_ref[...], NT)
    dslide = (grad_ref[...].astype(F32) + norm_back(slide_norm, slide_inv, dnorm)).astype(BF)
    first[3].wait()
    dembed = mm(dslide, wp_ref[...], NT).astype(BF)
    finish(first[4:])
    normed, inv = normalize(feat_ref[...].astype(F32))
    dfeat = jnp.zeros(feat_ref.shape, F32)
    for c in range(chunks):
        at = slice(c * step, c * step + step)
        waits[c][0].wait()
        dhidden = mm(dembed, wd_ref[at, :], NT)
        dgate = (dhidden * a1_ref[:, at].astype(F32)).astype(BF)
        dup = (dhidden * a2_ref[:, at].astype(F32)).astype(BF)
        waits[c][1].wait()
        dfeat = dfeat + mm(dgate, wg_ref[:, at], NT)
        waits[c][2].wait()
        dfeat = dfeat + mm(dup, wu_ref[:, at], NT)
    out_ref[...] = (dembed.astype(F32) + norm_back(normed, inv, dfeat)).astype(BF)


def place_kernel(shift_ref, recv_ref, tab_hbm, y_ref, yt_ref, y2_ref, tab_ref, sem):
    copy = pltpu.make_async_copy(tab_hbm, tab_ref, sem)
    copy.start()
    copy.wait()
    _, base, part = offsets(shift_ref)
    o2 = pl.multiple_of(base + 32 * part, 32)
    for d in range(4):
        tab = tab_ref[d : d + 1, :]
        onehot = jnp.where(iota((BLK, tab.shape[1]), 0) == tab, 1.0, 0.0).astype(BF)
        y = mm(onehot, recv_ref[:, 192 * d : 192 * d + 192])
        y_ref[d] = y.astype(BF)
        yt_ref[d] = y.T.astype(BF)
        y2_ref[32 * d : 32 * d + 32, :] = y_ref[d, pl.ds(o2, 32), :]


def score_rows(keys, queries_t, e_store, m_store):
    scores = mm(keys, queries_t)
    count, width = scores.shape
    total = jnp.zeros((8, width), F32)
    step = 64
    for c in range(0, count, step):
        t = jnp.tanh(scores[c : c + step] * (SCALE / SOFT_CAP))
        e = jnp.exp(SOFT_CAP * t)
        total = total + jnp.sum(e.reshape(step // 8, 8, width), axis=0)
        e_store(c, step, e.astype(BF))
        m_store(c, step, (e * (1.0 - t * t) * SCALE).astype(BF))
    return jnp.sum(total, axis=0, keepdims=True)


def forward_kernel(shift_ref, y_ref, yt_ref, e0_ref, m0_ref, e1_ref, m1_ref, u_ref, l_ref):
    o1 = pl.multiple_of(offsets(shift_ref)[0], 128)

    def block(d, carry):
        def e_store(c, n, v):
            e0_ref[d, c : c + n, :] = v

        def m_store(c, n, v):
            m0_ref[d, c : c + n, :] = v

        l_ref[d] = score_rows(y_ref[d, :, 48:96], yt_ref[d, 0:48, :], e_store, m_store)
        u_ref[d] = mm(yt_ref[d, 96:144, :], e0_ref[d])
        return carry

    lax.fori_loop(0, 4, block, 0)

    def e_store(c, n, v):
        e1_ref[c : c + n, :] = v

    def m_store(c, n, v):
        m1_ref[c : c + n, :] = v

    keys = jnp.concatenate([y_ref[d, pl.ds(o1, 128), 48:96] for d in range(4)], axis=0)
    queries = jnp.concatenate([yt_ref[d, 0:48, pl.ds(o1, 128)] for d in range(4)], axis=1)
    values = jnp.concatenate([yt_ref[d, 96:144, pl.ds(o1, 128)] for d in range(4)], axis=1)
    l1 = score_rows(keys, queries, e_store, m_store)
    u1 = mm(values, e1_ref[...])
    for d in range(4):
        u_ref[d, :, pl.ds(o1, 128)] += u1[:, 128 * d : 128 * d + 128]
        l_ref[d, :, pl.ds(o1, 128)] += l1[:, 128 * d : 128 * d + 128]


def turned(value, shift):
    return pltpu.roll(value, shift & 127, 1)


def wide_kernel(
    shift_ref,
    yt_ref,
    a0_ref,
    a1_ref,
    a2_ref,
    a3_ref,
    u_ref,
    l_ref,
    g0_hbm,
    g1_hbm,
    g2_hbm,
    g3_hbm,
    so0_hbm,
    so1_hbm,
    so2_hbm,
    so3_hbm,
    gs_ref,
    ds_ref,
    own_ref,
    send1_ref,
    send2_ref,
    send3_ref,
    dq_ref,
    e2_ref,
    m2_ref,
    usum_ref,
    lsum_ref,
    g_ref,
    so_ref,
    sems,
    so_sems,
):
    grads = started(
        [
            pltpu.make_async_copy(g, g_ref.at[d], sems.at[d])
            for d, g in enumerate((g0_hbm, g1_hbm, g2_hbm, g3_hbm))
        ]
    )
    outs = []
    _, base, part = offsets(shift_ref)
    base = pl.multiple_of(base, 128)
    y2 = jnp.concatenate([a0_ref[...], a1_ref[...], a2_ref[...], a3_ref[...]], axis=0)
    keys, values = y2[:, 48:96], y2[:, 96:144]
    both_t = y2[:, 48:144].astype(F32).T.astype(BF)
    query_t = a0_ref[:, 0:48].astype(F32).T.astype(BF)

    def e_store(c, n, v):
        e2_ref[c : c + n, :] = v

    def m_store(c, n, v):
        m2_ref[c : c + n, :] = v

    l2 = score_rows(keys, query_t, e_store, m_store)
    u2 = mm(both_t[48:96], e2_ref[...])
    l2w = jnp.broadcast_to(l2, (8, 128))
    lane = iota((1, 128), 1) >> 5
    gs2 = jnp.zeros((48, 128), F32)
    ds2 = jnp.zeros((8, 128), F32)
    for d in range(4):
        here = lane == part
        shift = 32 * (part - d)
        usum_ref[...] = u_ref[d]
        lsum_ref[...] = l_ref[d]
        usum_ref[:, pl.ds(base, 128)] += jnp.where(here, turned(u2, shift), 0.0)
        lsum_ref[:, pl.ds(base, 128)] += jnp.where(here, turned(l2w, shift), 0.0)[0:1]
        inv = 1.0 / lsum_ref[...]
        att = usum_ref[...] * inv
        so_ref[d] = (yt_ref[d, 144:192, :].astype(F32) + att).astype(BF)
        so = (so0_hbm, so1_hbm, so2_hbm, so3_hbm)[d]
        outs += started([pltpu.make_async_copy(so_ref.at[d], so, so_sems.at[d])])
        grads[d].wait()
        gs = (g_ref[d].astype(F32) * inv).astype(BF)
        gs_ref[d] = gs
        ds_ref[d] = jnp.sum(gs.astype(F32) * att, axis=0, keepdims=True)
        gs_wide = gs_ref[d, :, pl.ds(base, 128)].astype(F32)
        ds_wide = jnp.broadcast_to(ds_ref[d, :, pl.ds(base, 128)], (8, 128))
        gs2 = jnp.where(lane == d, turned(gs_wide, -shift), gs2)
        ds2 = jnp.where(lane == d, turned(ds_wide, -shift), ds2)
    gs2 = gs2.astype(BF)
    dp = mm(values, gs2)
    dscore = (m2_ref[...].astype(F32) * (dp - ds2[0:1])).astype(BF)
    dq_ref[...] = mm(both_t[0:48], dscore)
    dk = mm(query_t, dscore, NT)
    dv = mm(gs2, e2_ref[...], NT)
    dkv = jnp.concatenate([dk, dv], axis=0)
    own_ref[...] = dkv[:, 0:128]
    for e, send_ref in enumerate((send1_ref, send2_ref, send3_ref)):
        send_ref[...] = dkv[:, 128 * e + 128 : 128 * e + 256].astype(BF)
    finish(outs)


def dscores(values, gs, ds, m_load, store):
    dp = mm(values, gs)
    step = 64
    for c in range(0, dp.shape[0], step):
        store(c, step, (m_load(c, step).astype(F32) * (dp[c : c + step] - ds)).astype(BF))


def backward_kernel(
    shift_ref, y_ref, yt_ref, e0_ref, m0_ref, e1_ref, m1_ref, gs_ref, ds_ref, out_ref, tmp_ref
):
    o1 = pl.multiple_of(offsets(shift_ref)[0], 128)

    def store(c, n, v):
        tmp_ref[c : c + n, :] = v

    def block(d, carry):
        gs = gs_ref[d]
        dscores(y_ref[d, :, 96:144], gs, ds_ref[d], lambda c, n: m0_ref[d, c : c + n, :], store)
        dscore = tmp_ref[...]
        out_ref[d, 0:48, :] = mm(yt_ref[d, 48:96, :], dscore)
        out_ref[d, 48:96, :] = mm(yt_ref[d, 0:48, :], dscore, NT)
        out_ref[d, 96:144, :] = mm(gs, e0_ref[d], NT)
        return carry

    lax.fori_loop(0, 4, block, 0)
    values = jnp.concatenate([y_ref[d, pl.ds(o1, 128), 96:144] for d in range(4)], axis=0)
    queries = jnp.concatenate([yt_ref[d, 0:48, pl.ds(o1, 128)] for d in range(4)], axis=1)
    keys = jnp.concatenate([yt_ref[d, 48:96, pl.ds(o1, 128)] for d in range(4)], axis=1)
    gs = jnp.concatenate([gs_ref[d, :, pl.ds(o1, 128)] for d in range(4)], axis=1)
    ds = jnp.concatenate([ds_ref[d, :, pl.ds(o1, 128)] for d in range(4)], axis=1)
    dscores(values, gs, ds, lambda c, n: m1_ref[c : c + n, :], store)
    dscore = tmp_ref[...]
    dq = mm(keys, dscore)
    dk = mm(queries, dscore, NT)
    dv = mm(gs, e1_ref[...], NT)
    dall = jnp.concatenate([dq, dk, dv], axis=0)
    for d in range(4):
        out_ref[d, :, pl.ds(o1, 128)] += dall[:, 128 * d : 128 * d + 128]


def return_kernel(
    shift_ref,
    dall_ref,
    own_ref,
    dq_ref,
    r1_ref,
    r2_ref,
    r3_ref,
    g0_hbm,
    g1_hbm,
    g2_hbm,
    g3_hbm,
    tab_hbm,
    out_hbm,
    sum_ref,
    out_ref,
    g_ref,
    tab_ref,
    sems,
    in_sems,
):
    loads = started(
        [pltpu.make_async_copy(tab_hbm, tab_ref, in_sems.at[4])]
        + [
            pltpu.make_async_copy(g, g_ref.at[d], in_sems.at[d])
            for d, g in enumerate((g0_hbm, g1_hbm, g2_hbm, g3_hbm))
        ]
    )
    _, base, part = offsets(shift_ref)
    base = pl.multiple_of(base, 128)
    dkv = (
        own_ref[...]
        + r1_ref[...].astype(F32)
        + r2_ref[...].astype(F32)
        + r3_ref[...].astype(F32)
    )
    extra = jnp.concatenate([dq_ref[...], dkv], axis=0)
    lane = iota((1, 128), 1) >> 5
    rows = tab_ref.shape[0]
    outs = []
    finish(loads)
    for d in range(4):
        sum_ref[...] = dall_ref[d]
        sum_ref[:, pl.ds(base, 128)] += jnp.where(
            lane == part, turned(extra, 32 * (part - d)), 0.0
        )
        both = jnp.concatenate([sum_ref[...].astype(BF), g_ref[d]], axis=0)
        onehot = jnp.where(tab_ref[:, d : d + 1] == iota((rows, BLK), 1), 1.0, 0.0).astype(BF)
        out_ref[:, 192 * d : 192 * d + 192] = mm(onehot, both, NT).astype(BF)
        if d % 2:
            at = pl.ds(384 * (d // 2), 384)
            outs += started(
                [pltpu.make_async_copy(out_ref.at[:, at], out_hbm.at[:, at], sems.at[d // 2])]
            )
    finish(outs)


def out_kernel(s0_hbm, s1_hbm, s2_hbm, s3_hbm, _after_hbm, out_ref, tmp_ref, sems):
    j = lax.axis_index("seq") & 3
    finish(
        started(
            [
                pltpu.make_async_copy(
                    so, tmp_ref.at[pl.ds(pl.multiple_of((j ^ d) * HD, 16), HD), :], sems.at[d]
                )
                for d, so in enumerate((s0_hbm, s1_hbm, s2_hbm, s3_hbm))
            ]
        )
    )
    out_ref[...] = mm(tmp_ref[...], order_matrix(), NT).astype(BF)


def swap(value, distance, count):
    return lax.ppermute(value, "seq", [(i, i ^ distance) for i in range(count)])


def on_device(
    tile_features,
    gate_weight,
    up_weight,
    down_weight,
    input_projection_weight,
    query_key_value_weight,
    positions,
    dilation_shift,
    slide_output_gradient,
):
    seq_count = lax.axis_size("seq")
    device_count = seq_count * lax.axis_size("tile")
    rows, width = tile_features.shape
    ff = gate_weight.shape[1]
    slide_width = input_projection_weight.shape[1]
    all_pos = positions.reshape(device_count, rows)
    routed = ((8, 16 * SLOTS, slide_width), BF)
    weights = (gate_weight, up_weight, down_weight, input_projection_weight, query_key_value_weight)

    def exchange(block):
        return lax.all_to_all(
            block.reshape(device_count, SLOTS, slide_width),
            ("seq", "tile"),
            split_axis=0,
            concat_axis=0,
            tiled=True,
        ).reshape(device_count * SLOTS, slide_width)

    stored = [
        pltpu.VMEM((width, ff), BF),
        pltpu.VMEM((width, ff), BF),
        pltpu.VMEM((ff, width), BF),
        pltpu.VMEM((width, slide_width), BF),
        pltpu.VMEM((slide_width, 3 * slide_width), BF),
    ]
    dma = pltpu.SemaphoreType.DMA
    outgoing, x, a1, a2 = call(
        forward_mlp_kernel,
        [routed, ((rows, slide_width), BF), ((rows, ff), BF), ((rows, ff), BF)],
        [pltpu.VMEM((rows, width), BF), pltpu.VMEM((device_count, rows), I32)]
        + stored
        + [
            pltpu.VMEM((rows, slide_width), BF),
            pltpu.VMEM((rows, ff), BF),
            pltpu.VMEM((rows, ff), BF),
            pltpu.VMEM((rows, 3 * slide_width), BF),
            pltpu.VMEM((2 * rows, 192), BF),
            pltpu.VMEM((BLK, 2 * rows), BF),
            pltpu.VMEM((8, 16 * SLOTS, slide_width), BF),
            dma((16,)),
            dma((3 + HEADS // 2,)),
        ],
        n_hbm=7,
        n_hbm_out=4,
        limit=48,
    )(tile_features, all_pos, *weights)
    arrived = exchange(outgoing)

    grads = call(
        order_kernel,
        [((HD, BLK), BF)] * 4,
        [pltpu.VMEM((192, BLK), BF), dma((4,))],
        n_hbm_out=4,
    )(slide_output_gradient.T)
    grads = [grads[0]] + [swap(grads[d], d, seq_count) for d in range(1, 4)]
    slots = device_count * SLOTS
    table, table_col = call(
        table_kernel,
        [((8, slots), I32), ((slots, 8), I32)],
        [pltpu.VMEM((8, slots), I32), pltpu.VMEM((slots, 8), I32), dma((2,))],
        n_hbm_out=2,
    )(all_pos)

    y, yt, y2 = call(
        place_kernel,
        [((4, BLK, 192), BF), ((4, 192, BLK), BF), ((128, 192), BF)],
        [pltpu.VMEM((8, slots), I32), dma],
        n_smem=1,
        n_hbm=1,
    )(dilation_shift, arrived, table)
    y2_in = [swap(y2, 4 * e, seq_count) for e in range(1, 4)]
    e0, m0, e1, m1, u, l = call(
        forward_kernel,
        [
            ((4, BLK, BLK), BF),
            ((4, BLK, BLK), BF),
            ((BLK, BLK), BF),
            ((BLK, BLK), BF),
            ((4, HD, BLK), F32),
            ((4, 1, BLK), F32),
        ],
        n_smem=1,
    )(dilation_shift, y, yt)
    *parts, gs, ds, own, send1, send2, send3, dq2 = call(
        wide_kernel,
        [((HD, BLK), BF)] * 4
        + [((4, HD, BLK), BF), ((4, 1, BLK), F32), ((96, 128), F32)]
        + [((96, 128), BF)] * 3
        + [((HD, 128), F32)],
        [
            pltpu.VMEM((BLK, 128), BF),
            pltpu.VMEM((BLK, 128), BF),
            pltpu.VMEM((HD, BLK), F32),
            pltpu.VMEM((1, BLK), F32),
            pltpu.VMEM((4, HD, BLK), BF),
            pltpu.VMEM((4, HD, BLK), BF),
            dma((4,)),
            dma((4,)),
        ],
        n_smem=1,
        n_any=4,
        n_hbm_out=4,
    )(dilation_shift, yt, y2, *y2_in, u, l, *grads)
    back = [swap(send, 4 * e, seq_count) for e, send in ((1, send1), (2, send2), (3, send3))]
    (dall,) = call(
        backward_kernel,
        [((4, 144, BLK), F32)],
        [pltpu.VMEM((BLK, BLK), BF)],
        n_smem=1,
    )(dilation_shift, y, yt, e0, m0, e1, m1, gs, ds)
    (returning,) = call(
        return_kernel,
        [((slots, slide_width), BF)],
        [
            pltpu.VMEM((144, BLK), F32),
            pltpu.VMEM((slots, slide_width), BF),
            pltpu.VMEM((4, HD, BLK), BF),
            pltpu.VMEM((slots, 8), I32),
            dma((2,)),
            dma((5,)),
        ],
        n_smem=1,
        n_any=4,
        n_hbm=1,
        n_hbm_out=1,
        limit=6,
    )(dilation_shift, dall, own, dq2, *back, *grads, table_col)
    returned = exchange(returning)
    parts = [parts[0]] + [swap(parts[d], d, seq_count) for d in range(1, 4)]

    (tile_grad,) = call(
        backward_mlp_kernel,
        [((rows, width), BF)],
        [
            pltpu.VMEM((device_count, rows), I32),
            pltpu.VMEM((rows, width), BF),
            pltpu.VMEM((rows, slide_width), BF),
            pltpu.VMEM((rows, ff), BF),
            pltpu.VMEM((rows, ff), BF),
        ]
        + stored
        + [
            pltpu.VMEM((rows, 3 * slide_width), BF),
            pltpu.VMEM((rows, slide_width), BF),
            dma((19,)),
        ],
        n_hbm=10,
        limit=48,
    )(returned.reshape(8, 16 * SLOTS, slide_width), all_pos, tile_features, x, a1, a2, *weights)
    (slide_out,) = call(
        out_kernel,
        [((192, BLK), BF)],
        [pltpu.VMEM((192, BLK), BF), dma((4,))],
        n_any=4,
        n_hbm=1,
    )(*parts, tile_grad)
    return (slide_out.T, tile_grad)


def solution(mesh):
    placed = (P(("seq", "tile"), None), P(), P(), P(), P(), P(), P(), P(), P("seq", "tile"))
    return jax.shard_map(
        on_device,
        mesh=mesh,
        in_specs=placed,
        out_specs=(P("seq", "tile"), P(("seq", "tile"), None)),
        check_vma=False,
    )
```

```python
import functools

import jax
import jax.numpy as jnp
from jax import lax
from jax.experimental import pallas as pl
from jax.experimental.pallas import tpu as pltpu
from jax.sharding import PartitionSpec as P

HEADS = 16
HD = 48
EPSILON = 1e-06
SOFT_CAP = 50.0
SCALE = HD**-0.5
BLK = 512
SLOTS = 8
BF = jnp.bfloat16
F32 = jnp.float32
I32 = jnp.int32

NN = (((1,), (0,)), ((), ()))
NT = (((1,), (1,)), ((), ()))
TN = (((0,), (0,)), ((), ()))


def mm(a, b, dims=NN):
    return lax.dot_general(a, b, dims, preferred_element_type=F32)


def iota(shape, dim):
    return lax.broadcasted_iota(I32, shape, dim)


def class_order(row):
    return (row & 3) * 128 + ((row >> 2) & 3) * 32 + (row >> 4)


def order_matrix():
    return jnp.where(class_order(iota((BLK, BLK), 0)) == iota((BLK, BLK), 1), 1.0, 0.0).astype(BF)


def normalize(values):
    centred = values - jnp.mean(values, axis=-1, keepdims=True)
    inv_std = lax.rsqrt(jnp.mean(centred * centred, axis=-1, keepdims=True) + EPSILON)
    return (centred * inv_std, inv_std)


def norm_back(normed, inv_std, grads):
    mean_grad = jnp.mean(grads, axis=-1, keepdims=True)
    mean_cross = jnp.mean(grads * normed, axis=-1, keepdims=True)
    return (grads - mean_grad - normed * mean_cross) * inv_std


def call(kernel, outs, scratch=(), n_smem=0, n_any=0, n_hbm=0, n_hbm_out=0, limit=4):
    def run(*args):
        n_vmem = len(args) - n_smem - n_any - n_hbm
        specs = [pl.BlockSpec(memory_space=pltpu.SMEM)] * n_smem
        specs += [pl.BlockSpec(memory_space=pltpu.VMEM)] * n_vmem
        specs += [pl.BlockSpec(memory_space=pl.ANY)] * n_any
        specs += [pl.BlockSpec(memory_space=pltpu.HBM)] * n_hbm
        out_specs = [pl.BlockSpec(memory_space=pltpu.HBM)] * n_hbm_out
        out_specs += [pl.BlockSpec(memory_space=pltpu.VMEM)] * (len(outs) - n_hbm_out)
        shapes = [pltpu.HBM(shape, kind) for shape, kind in outs[:n_hbm_out]]
        shapes += [jax.ShapeDtypeStruct(shape, kind) for shape, kind in outs[n_hbm_out:]]
        cut = len(args) - n_hbm
        held = [pltpu.with_memory_space_constraint(x, pltpu.HBM) for x in args[cut:]]
        return pl.pallas_call(
            kernel,
            out_shape=shapes,
            in_specs=specs,
            out_specs=out_specs,
            scratch_shapes=list(scratch),
            compiler_params=pltpu.CompilerParams(vmem_limit_bytes=limit * 1024 * 1024),
        )(*args[:cut], *held)

    return run


def started(copies):
    for copy in copies:
        copy.start()
    return copies


def finish(copies):
    for copy in copies:
        copy.wait()


def order_kernel(grad_ref, g0_ref, g1_ref, g2_ref, g3_ref, tmp_ref):
    j = lax.axis_index("seq") & 3
    tmp_ref[...] = mm(grad_ref[...], order_matrix()).astype(BF)
    for d, out_ref in enumerate((g0_ref, g1_ref, g2_ref, g3_ref)):
        out_ref[...] = tmp_ref[pl.ds(pl.multiple_of((j ^ d) * HD, 16), HD), :]


def offsets(shift_ref):
    head = 4 * lax.axis_index("tile") + (lax.axis_index("seq") & 3)
    o1 = shift_ref[0, head]
    o2 = shift_ref[1, head]
    return (o1 * 128, (o2 & 3) * 128, o2 >> 2)


def table_kernel(pos_ref, row_ref, col_ref):
    s = lax.axis_index("seq")
    pos = pos_ref[...].T
    n = pos.shape[0]
    block = pos >> 9
    seat = class_order(pos & (BLK - 1)) + 1
    lower = jnp.where(iota((n, n), 1) < iota((n, n), 0), 1.0, 0.0).astype(BF)
    high, low = [], []
    for d in range(4):
        owned = block == (s ^ d)
        rank = mm(lower, jnp.where(owned, 1.0, 0.0).astype(BF)).astype(I32)
        held = jnp.where(owned, seat, 0)
        for k in range(SLOTS):
            found = jnp.sum(jnp.where(rank == k, held, 0), axis=0, keepdims=True)
            high.append(found >> 4)
            low.append(found & 15)
    digits = jnp.concatenate(high + low, axis=0).astype(F32).astype(BF)
    lanes = n * SLOTS
    spread = jnp.where(iota((n, lanes), 0) == iota((n, lanes), 1) >> 3, 1.0, 0.0).astype(BF)
    wide = mm(digits, spread)
    wide = 16.0 * wide[0:32] + wide[32:64]
    own = iota((8, lanes), 0) == (iota((8, lanes), 1) & 7)
    rows = [
        jnp.sum(jnp.where(own, wide[8 * d : 8 * d + 8], 0.0), axis=0, keepdims=True)
        for d in range(4)
    ]
    table = jnp.concatenate(rows + rows, axis=0) - 1.0
    row_ref[...] = table.astype(I32)
    col_ref[...] = table.T.astype(I32)


def forward_mlp_kernel(
    feat_hbm,
    pos_hbm,
    gate_hbm,
    up_hbm,
    down_hbm,
    proj_hbm,
    qkvw_hbm,
    out_hbm,
    x_hbm,
    a1_hbm,
    a2_hbm,
    feat_ref,
    pos_ref,
    wg_ref,
    wu_ref,
    wd_ref,
    wp_ref,
    wq_ref,
    x_ref,
    a1_ref,
    a2_ref,
    qkv_ref,
    heads_ref,
    picker_ref,
    tmp_ref,
    sems,
    out_sems,
):
    ff = gate_hbm.shape[1]
    step = 512
    chunks = ff // step
    first = started(
        [
            pltpu.make_async_copy(feat_hbm, feat_ref, sems.at[3 * chunks]),
            pltpu.make_async_copy(pos_hbm, pos_ref, sems.at[3 * chunks + 1]),
        ]
    )
    waits = []
    for c in range(chunks):
        at = pl.ds(c * step, step)
        waits.append(
            started(
                [
                    pltpu.make_async_copy(gate_hbm.at[:, at], wg_ref.at[:, at], sems.at[3 * c]),
                    pltpu.make_async_copy(up_hbm.at[:, at], wu_ref.at[:, at], sems.at[3 * c + 1]),
                    pltpu.make_async_copy(down_hbm.at[at, :], wd_ref.at[at, :], sems.at[3 * c + 2]),
                ]
            )
        )
    last = started(
        [
            pltpu.make_async_copy(proj_hbm, wp_ref, sems.at[3 * chunks + 2]),
            pltpu.make_async_copy(qkvw_hbm, wq_ref, sems.at[3 * chunks + 3]),
        ]
    )
    finish(first)

    me = lax.axis_index("seq") * 4 + lax.axis_index("tile")
    brow = pos_ref[pl.ds(me, 1), :] >> 9
    n = brow.shape[1]
    bcol = jnp.broadcast_to(brow, (n, n)).T
    before = iota((n, n), 0) < iota((n, n), 1)
    rank = jnp.sum(jnp.where((bcol == brow) & before, 1, 0), axis=0, keepdims=True)
    code = brow * SLOTS + rank
    code = jnp.concatenate([code, code + 4096], axis=1)
    seat = iota((BLK, 2 * n), 0)
    want = (((seat >> 4) & 7) * 4 + (seat >> 7)) * SLOTS + (seat & 7) + 4096 * ((seat >> 3) & 1)
    picker_ref[...] = jnp.where(code == want, 1.0, 0.0).astype(BF)

    feats = feat_ref[...].astype(F32)
    normed = normalize(feats)[0].astype(BF)
    total = feats
    outs = []
    for c in range(chunks):
        at = slice(c * step, c * step + step)
        waits[c][0].wait()
        gate = mm(normed, wg_ref[:, at])
        waits[c][1].wait()
        up = mm(normed, wu_ref[:, at])
        sig = jax.nn.sigmoid(gate)
        silu = gate * sig
        hidden = (silu * up).astype(BF)
        a1_ref[:, at] = (up * (sig + silu * (1.0 - sig))).astype(BF)
        a2_ref[:, at] = silu.astype(BF)
        waits[c][2].wait()
        total = total + mm(hidden, wd_ref[at, :])
    outs += started(
        [
            pltpu.make_async_copy(a1_ref, a1_hbm, out_sems.at[0]),
            pltpu.make_async_copy(a2_ref, a2_hbm, out_sems.at[1]),
        ]
    )
    last[0].wait()
    x = mm(total.astype(BF), wp_ref[...]).astype(BF)
    x_ref[...] = x
    outs += started([pltpu.make_async_copy(x_ref, x_hbm, out_sems.at[2])])
    slide_norm = normalize(x.astype(F32))[0].astype(BF)
    last[1].wait()
    qkv_ref[...] = mm(slide_norm, wq_ref[...]).astype(BF)

    width = HEADS * HD
    for pair in range(HEADS // 2):
        j, t = pair // 2, 2 * (pair % 2)
        for tp in range(2):
            h = 4 * (t + tp) + j
            for part in range(3):
                heads_ref[n * tp : n * tp + n, HD * part : HD * part + HD] = qkv_ref[
                    :, part * width + h * HD : part * width + h * HD + HD
                ]
            heads_ref[n * tp : n * tp + n, 144:192] = x_ref[:, h * HD : h * HD + HD]
        rows = mm(picker_ref[...], heads_ref[...]).astype(BF)
        at = slice(16 * pair, 16 * pair + 16)
        for block in range(4):
            lane = (j ^ block) * 192
            tmp_ref[:, at, lane : lane + 192] = rows[128 * block : 128 * block + 128].reshape(
                8, 16, 192
            )
        outs += started(
            [
                pltpu.make_async_copy(
                    tmp_ref.at[:, at, :], out_hbm.at[:, at, :], out_sems.at[3 + pair]
                )
            ]
        )
    finish(outs)


def turn_steps(shapes):
    steps = []
    for which, (rows, columns) in enumerate(shapes):
        band = 384 if columns == 2048 else 512 if columns == 1536 else 256 if columns == 2304 else 768
        steps += [(which, at, band) for at in range(0, rows, band)]
    return steps


def turn_kernel(shapes, *refs):
    count = len(shapes)
    given = refs[:count]
    made = refs[count + 1 : 2 * count + 1]
    in_ref, out_ref, in_sems, out_sems = refs[2 * count + 1 :]
    steps = turn_steps(shapes)

    def load(i):
        which, at, band = steps[i]
        columns = shapes[which][1]
        return pltpu.make_async_copy(
            given[which].at[pl.ds(at, band), :],
            in_ref.at[i % 2, pl.ds(0, band), pl.ds(0, columns)],
            in_sems.at[i % 2],
        )

    def store(i):
        which, at, band = steps[i]
        columns = shapes[which][1]
        return pltpu.make_async_copy(
            out_ref.at[i % 2, pl.ds(0, columns), pl.ds(0, band)],
            made[which].at[:, pl.ds(at, band)],
            out_sems.at[i % 2],
        )

    load(0).start()
    for i, (which, _, band) in enumerate(steps):
        columns = shapes[which][1]
        if i + 1 < len(steps):
            load(i + 1).start()
        load(i).wait()
        if i >= 2:
            store(i - 2).wait()
        out_ref[i % 2, 0:columns, 0:band] = in_ref[i % 2, 0:band, 0:columns].T
        store(i).start()
    for i in range(max(len(steps) - 2, 0), len(steps)):
        store(i).wait()


def turned_weights(weights, after):
    shapes = [w.shape for w in weights]
    bands = [band for _, _, band in turn_steps(shapes)]
    widest = max(columns for _, columns in shapes)
    return call(
        functools.partial(turn_kernel, shapes),
        [((columns, rows), BF) for rows, columns in shapes],
        [
            pltpu.VMEM((2, max(bands), widest), BF),
            pltpu.VMEM((2, widest, max(bands)), BF),
            pltpu.SemaphoreType.DMA((2,)),
            pltpu.SemaphoreType.DMA((2,)),
        ],
        n_hbm=len(shapes) + 1,
        n_hbm_out=len(shapes),
        limit=20,
    )(*weights, after)


def backward_mlp_kernel(
    ret_ref,
    pos_hbm,
    feat_hbm,
    x_hbm,
    a1_hbm,
    a2_hbm,
    gate_hbm,
    up_hbm,
    down_hbm,
    proj_hbm,
    qkvw_hbm,
    out_ref,
    pos_ref,
    feat_ref,
    x_ref,
    a1_ref,
    a2_ref,
    wg_ref,
    wu_ref,
    wd_ref,
    wp_ref,
    wq_ref,
    dqkv_ref,
    grad_ref,
    sems,
):
    ff = gate_hbm.shape[0]
    cuts = [(at, 512) for at in range(0, ff - 512, 512)] + [(ff - 512, 256), (ff - 256, 256)]
    chunks = len(cuts)
    pairs = (
        (pos_hbm, pos_ref),
        (x_hbm, x_ref),
        (qkvw_hbm, wq_ref),
        (proj_hbm, wp_ref),
        (a1_hbm, a1_ref),
        (a2_hbm, a2_ref),
        (feat_hbm, feat_ref),
    )
    first = started(
        [
            pltpu.make_async_copy(here, there, sems.at[3 * chunks + i])
            for i, (here, there) in enumerate(pairs)
        ]
    )
    waits = []
    for c, (start, size) in enumerate(cuts):
        at = pl.ds(start, size)
        waits.append(
            started(
                [
                    pltpu.make_async_copy(down_hbm.at[:, at], wd_ref.at[:, at], sems.at[3 * c]),
                    pltpu.make_async_copy(gate_hbm.at[at, :], wg_ref.at[at, :], sems.at[3 * c + 1]),
                    pltpu.make_async_copy(up_hbm.at[at, :], wu_ref.at[at, :], sems.at[3 * c + 2]),
                ]
            )
        )
    first[0].wait()
    me = lax.axis_index("seq") * 4 + lax.axis_index("tile")
    brow = pos_ref[pl.ds(me, 1), :] >> 9
    n = brow.shape[1]
    bcol = jnp.broadcast_to(brow, (n, n)).T
    before = iota((n, n), 1) < iota((n, n), 0)
    rank = jnp.sum(jnp.where((bcol == brow) & before, 1, 0), axis=1, keepdims=True)
    code = bcol[:, 0:1] * SLOTS + rank
    code = jnp.concatenate([code, code + 4096], axis=0)
    seat = iota((2 * n, BLK), 1)
    want = (((seat >> 4) & 7) * 4 + (seat >> 7)) * SLOTS + (seat & 7) + 4096 * ((seat >> 3) & 1)
    picker = jnp.where(code == want, 1.0, 0.0).astype(BF)
    width = HEADS * HD
    for pair in range(HEADS // 2):
        j, t = pair // 2, 2 * (pair % 2)
        tile = ret_ref[:, 16 * pair : 16 * pair + 16, :].reshape(128, 768)
        stacked = jnp.concatenate(
            [tile[:, (j ^ b) * 192 : (j ^ b) * 192 + 192] for b in range(4)], axis=0
        )
        got = mm(picker, stacked).astype(BF)
        for tp in range(2):
            h = 4 * (t + tp) + j
            mine = got[n * tp : n * tp + n]
            for part in range(3):
                dqkv_ref[:, part * width + h * HD : part * width + h * HD + HD] = mine[
                    :, HD * part : HD * part + HD
                ]
            grad_ref[:, h * HD : h * HD + HD] = mine[:, 144:192]
    first[1].wait()
    slide_norm, slide_inv = normalize(x_ref[...].astype(F32))
    first[2].wait()
    dnorm = mm(dqkv_ref[...], wq_ref[...])
    dslide = (grad_ref[...].astype(F32) + norm_back(slide_norm, slide_inv, dnorm)).astype(BF)
    first[3].wait()
    dembed = mm(dslide, wp_ref[...]).astype(BF)
    finish(first[4:])
    normed, inv = normalize(feat_ref[...].astype(F32))
    dfeat = jnp.zeros(feat_ref.shape, F32)
    for c, (start, size) in enumerate(cuts):
        at = slice(start, start + size)
        waits[c][0].wait()
        dhidden = mm(dembed, wd_ref[:, at])
        dgate = (dhidden * a1_ref[:, at].astype(F32)).astype(BF)
        dup = (dhidden * a2_ref[:, at].astype(F32)).astype(BF)
        waits[c][1].wait()
        dfeat = dfeat + mm(dgate, wg_ref[at, :])
        waits[c][2].wait()
        dfeat = dfeat + mm(dup, wu_ref[at, :])
    out_ref[...] = (dembed.astype(F32) + norm_back(normed, inv, dfeat)).astype(BF)


def place_kernel(shift_ref, recv_ref, tab_ref, _after_hbm, y_ref, yt_ref, y2_ref):
    _, base, part = offsets(shift_ref)
    o2 = pl.multiple_of(base + 32 * part, 32)
    for d in range(4):
        tab = tab_ref[d : d + 1, :]
        onehot = jnp.where(iota((BLK, tab.shape[1]), 0) == tab, 1.0, 0.0).astype(BF)
        y = mm(onehot, recv_ref[:, 192 * d : 192 * d + 192])
        y_ref[d] = y.astype(BF)
        yt_ref[d] = y.T.astype(BF)
        y2_ref[32 * d : 32 * d + 32, :] = y_ref[d, pl.ds(o2, 32), :]


def score_rows(keys, queries_t, e_store, m_store):
    scores = mm(keys, queries_t)
    count, width = scores.shape
    total = jnp.zeros((8, width), F32)
    step = 64
    for c in range(0, count, step):
        t = jnp.tanh(scores[c : c + step] * (SCALE / SOFT_CAP))
        e = jnp.exp(SOFT_CAP * t)
        total = total + jnp.sum(e.reshape(step // 8, 8, width), axis=0)
        e_store(c, step, e.astype(BF))
        m_store(c, step, (e * (1.0 - t * t) * SCALE).astype(BF))
    return jnp.sum(total, axis=0, keepdims=True)


def forward_kernel(shift_ref, y_ref, yt_ref, e0_ref, m0_ref, e1_ref, m1_ref, u_ref, l_ref):
    o1 = pl.multiple_of(offsets(shift_ref)[0], 128)

    def block(d, carry):
        def e_store(c, n, v):
            e0_ref[d, c : c + n, :] = v

        def m_store(c, n, v):
            m0_ref[d, c : c + n, :] = v

        l_ref[d] = score_rows(y_ref[d, :, 48:96], yt_ref[d, 0:48, :], e_store, m_store)
        u_ref[d] = mm(yt_ref[d, 96:144, :], e0_ref[d])
        return carry

    lax.fori_loop(0, 4, block, 0)

    def e_store(c, n, v):
        e1_ref[c : c + n, :] = v

    def m_store(c, n, v):
        m1_ref[c : c + n, :] = v

    keys = jnp.concatenate([y_ref[d, pl.ds(o1, 128), 48:96] for d in range(4)], axis=0)
    queries = jnp.concatenate([yt_ref[d, 0:48, pl.ds(o1, 128)] for d in range(4)], axis=1)
    values = jnp.concatenate([yt_ref[d, 96:144, pl.ds(o1, 128)] for d in range(4)], axis=1)
    l1 = score_rows(keys, queries, e_store, m_store)
    u1 = mm(values, e1_ref[...])
    for d in range(4):
        u_ref[d, :, pl.ds(o1, 128)] += u1[:, 128 * d : 128 * d + 128]
        l_ref[d, :, pl.ds(o1, 128)] += l1[:, 128 * d : 128 * d + 128]


def turned(value, shift):
    return pltpu.roll(value, shift & 127, 1)


def wide_kernel(
    shift_ref,
    yt_ref,
    a0_ref,
    a1_ref,
    a2_ref,
    a3_ref,
    u_ref,
    l_ref,
    g0_ref,
    g1_ref,
    g2_ref,
    g3_ref,
    so0_hbm,
    so1_hbm,
    so2_hbm,
    so3_hbm,
    gs_ref,
    ds_ref,
    own_ref,
    send1_ref,
    send2_ref,
    send3_ref,
    dq_ref,
    e2_ref,
    m2_ref,
    usum_ref,
    lsum_ref,
    so_ref,
    so_sems,
):
    outs = []
    _, base, part = offsets(shift_ref)
    base = pl.multiple_of(base, 128)
    y2 = jnp.concatenate([a0_ref[...], a1_ref[...], a2_ref[...], a3_ref[...]], axis=0)
    keys, values = y2[:, 48:96], y2[:, 96:144]
    both_t = y2[:, 48:144].astype(F32).T.astype(BF)
    query_t = a0_ref[:, 0:48].astype(F32).T.astype(BF)

    def e_store(c, n, v):
        e2_ref[c : c + n, :] = v

    def m_store(c, n, v):
        m2_ref[c : c + n, :] = v

    l2 = score_rows(keys, query_t, e_store, m_store)
    u2 = mm(both_t[48:96], e2_ref[...])
    l2w = jnp.broadcast_to(l2, (8, 128))
    lane = iota((1, 128), 1) >> 5
    gs2 = jnp.zeros((48, 128), F32)
    ds2 = jnp.zeros((8, 128), F32)
    for d in range(4):
        here = lane == part
        shift = 32 * (part - d)
        usum_ref[...] = u_ref[d]
        lsum_ref[...] = l_ref[d]
        usum_ref[:, pl.ds(base, 128)] += jnp.where(here, turned(u2, shift), 0.0)
        lsum_ref[:, pl.ds(base, 128)] += jnp.where(here, turned(l2w, shift), 0.0)[0:1]
        inv = 1.0 / lsum_ref[...]
        att = usum_ref[...] * inv
        so_ref[d] = (yt_ref[d, 144:192, :].astype(F32) + att).astype(BF)
        so = (so0_hbm, so1_hbm, so2_hbm, so3_hbm)[d]
        outs += started([pltpu.make_async_copy(so_ref.at[d], so, so_sems.at[d])])
        grad_ref = (g0_ref, g1_ref, g2_ref, g3_ref)[d]
        gs = (grad_ref[...].astype(F32) * inv).astype(BF)
        gs_ref[d] = gs
        ds_ref[d] = jnp.sum(gs.astype(F32) * att, axis=0, keepdims=True)
        gs_wide = gs_ref[d, :, pl.ds(base, 128)].astype(F32)
        ds_wide = jnp.broadcast_to(ds_ref[d, :, pl.ds(base, 128)], (8, 128))
        gs2 = jnp.where(lane == d, turned(gs_wide, -shift), gs2)
        ds2 = jnp.where(lane == d, turned(ds_wide, -shift), ds2)
    gs2 = gs2.astype(BF)
    dp = mm(values, gs2)
    dscore = (m2_ref[...].astype(F32) * (dp - ds2[0:1])).astype(BF)
    dq_ref[...] = mm(both_t[0:48], dscore)
    dk = mm(query_t, dscore, NT)
    dv = mm(gs2, e2_ref[...], NT)
    dkv = jnp.concatenate([dk, dv], axis=0)
    own_ref[...] = dkv[:, 0:128]
    for e, send_ref in enumerate((send1_ref, send2_ref, send3_ref)):
        send_ref[...] = dkv[:, 128 * e + 128 : 128 * e + 256].astype(BF)
    finish(outs)


def dscores(values, gs, ds, m_load, store):
    dp = mm(values, gs)
    step = 64
    for c in range(0, dp.shape[0], step):
        store(c, step, (m_load(c, step).astype(F32) * (dp[c : c + step] - ds)).astype(BF))


def backward_kernel(
    shift_ref, y_ref, yt_ref, e0_ref, m0_ref, e1_ref, m1_ref, gs_ref, ds_ref, out_ref, tmp_ref
):
    o1 = pl.multiple_of(offsets(shift_ref)[0], 128)

    def store(c, n, v):
        tmp_ref[c : c + n, :] = v

    def block(d, carry):
        gs = gs_ref[d]
        dscores(y_ref[d, :, 96:144], gs, ds_ref[d], lambda c, n: m0_ref[d, c : c + n, :], store)
        dscore = tmp_ref[...]
        out_ref[d, 0:48, :] = mm(yt_ref[d, 48:96, :], dscore)
        out_ref[d, 48:96, :] = mm(yt_ref[d, 0:48, :], dscore, NT)
        out_ref[d, 96:144, :] = mm(gs, e0_ref[d], NT)
        return carry

    lax.fori_loop(0, 4, block, 0)
    values = jnp.concatenate([y_ref[d, pl.ds(o1, 128), 96:144] for d in range(4)], axis=0)
    queries = jnp.concatenate([yt_ref[d, 0:48, pl.ds(o1, 128)] for d in range(4)], axis=1)
    keys = jnp.concatenate([yt_ref[d, 48:96, pl.ds(o1, 128)] for d in range(4)], axis=1)
    gs = jnp.concatenate([gs_ref[d, :, pl.ds(o1, 128)] for d in range(4)], axis=1)
    ds = jnp.concatenate([ds_ref[d, :, pl.ds(o1, 128)] for d in range(4)], axis=1)
    dscores(values, gs, ds, lambda c, n: m1_ref[c : c + n, :], store)
    dscore = tmp_ref[...]
    dq = mm(keys, dscore)
    dk = mm(queries, dscore, NT)
    dv = mm(gs, e1_ref[...], NT)
    dall = jnp.concatenate([dq, dk, dv], axis=0)
    for d in range(4):
        out_ref[d, :, pl.ds(o1, 128)] += dall[:, 128 * d : 128 * d + 128]


def return_kernel(
    shift_ref,
    dall_ref,
    own_ref,
    dq_ref,
    r1_ref,
    r2_ref,
    r3_ref,
    g0_ref,
    g1_ref,
    g2_ref,
    g3_ref,
    tab_ref,
    out_hbm,
    sum_ref,
    out_ref,
    sems,
):
    _, base, part = offsets(shift_ref)
    base = pl.multiple_of(base, 128)
    dkv = (
        own_ref[...]
        + r1_ref[...].astype(F32)
        + r2_ref[...].astype(F32)
        + r3_ref[...].astype(F32)
    )
    extra = jnp.concatenate([dq_ref[...], dkv], axis=0)
    lane = iota((1, 128), 1) >> 5
    rows = tab_ref.shape[0]
    outs = []
    for d in range(4):
        grad_ref = (g0_ref, g1_ref, g2_ref, g3_ref)[d]
        sum_ref[...] = dall_ref[d]
        sum_ref[:, pl.ds(base, 128)] += jnp.where(
            lane == part, turned(extra, 32 * (part - d)), 0.0
        )
        both = jnp.concatenate([sum_ref[...].astype(BF), grad_ref[...]], axis=0)
        onehot = jnp.where(tab_ref[:, d : d + 1] == iota((rows, BLK), 1), 1.0, 0.0).astype(BF)
        out_ref[:, 192 * d : 192 * d + 192] = mm(onehot, both, NT).astype(BF)
        if d % 2:
            at = pl.ds(384 * (d // 2), 384)
            outs += started(
                [pltpu.make_async_copy(out_ref.at[:, at], out_hbm.at[:, at], sems.at[d // 2])]
            )
    finish(outs)


def out_kernel(s0_hbm, s1_hbm, s2_hbm, s3_hbm, _after_hbm, out_ref, tmp_ref, sems):
    j = lax.axis_index("seq") & 3
    finish(
        started(
            [
                pltpu.make_async_copy(
                    so, tmp_ref.at[pl.ds(pl.multiple_of((j ^ d) * HD, 16), HD), :], sems.at[d]
                )
                for d, so in enumerate((s0_hbm, s1_hbm, s2_hbm, s3_hbm))
            ]
        )
    )
    out_ref[...] = mm(tmp_ref[...], order_matrix(), NT).astype(BF)


def swap(value, distance, count):
    return lax.ppermute(value, "seq", [(i, i ^ distance) for i in range(count)])


def on_device(
    tile_features,
    gate_weight,
    up_weight,
    down_weight,
    input_projection_weight,
    query_key_value_weight,
    positions,
    dilation_shift,
    slide_output_gradient,
):
    seq_count = lax.axis_size("seq")
    device_count = seq_count * lax.axis_size("tile")
    rows, width = tile_features.shape
    ff = gate_weight.shape[1]
    slide_width = input_projection_weight.shape[1]
    all_pos = positions.reshape(device_count, rows)
    routed = ((8, 16 * SLOTS, slide_width), BF)
    weights = (gate_weight, up_weight, down_weight, input_projection_weight, query_key_value_weight)

    def exchange(block):
        return lax.all_to_all(
            block.reshape(device_count, SLOTS, slide_width),
            ("seq", "tile"),
            split_axis=0,
            concat_axis=0,
            tiled=True,
        ).reshape(device_count * SLOTS, slide_width)

    stored = [
        pltpu.VMEM((width, ff), BF),
        pltpu.VMEM((width, ff), BF),
        pltpu.VMEM((ff, width), BF),
        pltpu.VMEM((width, slide_width), BF),
        pltpu.VMEM((slide_width, 3 * slide_width), BF),
    ]
    dma = pltpu.SemaphoreType.DMA
    outgoing, x, a1, a2 = call(
        forward_mlp_kernel,
        [routed, ((rows, slide_width), BF), ((rows, ff), BF), ((rows, ff), BF)],
        [pltpu.VMEM((rows, width), BF), pltpu.VMEM((device_count, rows), I32)]
        + stored
        + [
            pltpu.VMEM((rows, slide_width), BF),
            pltpu.VMEM((rows, ff), BF),
            pltpu.VMEM((rows, ff), BF),
            pltpu.VMEM((rows, 3 * slide_width), BF),
            pltpu.VMEM((2 * rows, 192), BF),
            pltpu.VMEM((BLK, 2 * rows), BF),
            pltpu.VMEM((8, 16 * SLOTS, slide_width), BF),
            dma((16,)),
            dma((3 + HEADS // 2,)),
        ],
        n_hbm=7,
        n_hbm_out=4,
        limit=48,
    )(tile_features, all_pos, *weights)
    arrived = exchange(outgoing)
    turned_ff = turned_weights(weights[:3], x)

    grads = call(
        order_kernel,
        [((HD, BLK), BF)] * 4,
        [pltpu.VMEM((192, BLK), BF)],
    )(slide_output_gradient.T)
    grads = [grads[0]] + [swap(grads[d], d, seq_count) for d in range(1, 4)]
    slots = device_count * SLOTS
    table, table_col = call(
        table_kernel,
        [((8, slots), I32), ((slots, 8), I32)],
    )(all_pos)

    y, yt, y2 = call(
        place_kernel,
        [((4, BLK, 192), BF), ((4, 192, BLK), BF), ((128, 192), BF)],
        n_smem=1,
        n_hbm=1,
    )(dilation_shift, arrived, table, turned_ff[0])
    y2_in = [swap(y2, 4 * e, seq_count) for e in range(1, 4)]
    e0, m0, e1, m1, u, l = call(
        forward_kernel,
        [
            ((4, BLK, BLK), BF),
            ((4, BLK, BLK), BF),
            ((BLK, BLK), BF),
            ((BLK, BLK), BF),
            ((4, HD, BLK), F32),
            ((4, 1, BLK), F32),
        ],
        n_smem=1,
    )(dilation_shift, y, yt)
    *parts, gs, ds, own, send1, send2, send3, dq2 = call(
        wide_kernel,
        [((HD, BLK), BF)] * 4
        + [((4, HD, BLK), BF), ((4, 1, BLK), F32), ((96, 128), F32)]
        + [((96, 128), BF)] * 3
        + [((HD, 128), F32)],
        [
            pltpu.VMEM((BLK, 128), BF),
            pltpu.VMEM((BLK, 128), BF),
            pltpu.VMEM((HD, BLK), F32),
            pltpu.VMEM((1, BLK), F32),
            pltpu.VMEM((4, HD, BLK), BF),
            dma((4,)),
        ],
        n_smem=1,
        n_hbm_out=4,
    )(dilation_shift, yt, y2, *y2_in, u, l, *grads)
    back = [swap(send, 4 * e, seq_count) for e, send in ((1, send1), (2, send2), (3, send3))]
    (dall,) = call(
        backward_kernel,
        [((4, 144, BLK), F32)],
        [pltpu.VMEM((BLK, BLK), BF)],
        n_smem=1,
    )(dilation_shift, y, yt, e0, m0, e1, m1, gs, ds)
    (returning,) = call(
        return_kernel,
        [((slots, slide_width), BF)],
        [
            pltpu.VMEM((144, BLK), F32),
            pltpu.VMEM((slots, slide_width), BF),
            dma((2,)),
        ],
        n_smem=1,
        n_hbm_out=1,
        limit=6,
    )(dilation_shift, dall, own, dq2, *back, *grads, table_col)
    returned = exchange(returning)
    turned_rest = turned_weights(weights[3:], returning)
    parts = [parts[0]] + [swap(parts[d], d, seq_count) for d in range(1, 4)]

    (tile_grad,) = call(
        backward_mlp_kernel,
        [((rows, width), BF)],
        [
            pltpu.VMEM((device_count, rows), I32),
            pltpu.VMEM((rows, width), BF),
            pltpu.VMEM((rows, slide_width), BF),
            pltpu.VMEM((rows, ff), BF),
            pltpu.VMEM((rows, ff), BF),
        ]
        + [pltpu.VMEM(w.shape[::-1], BF) for w in weights]
        + [
            pltpu.VMEM((rows, 3 * slide_width), BF),
            pltpu.VMEM((rows, slide_width), BF),
            dma((22,)),
        ],
        n_hbm=10,
        limit=48,
    )(
        returned.reshape(8, 16 * SLOTS, slide_width),
        all_pos,
        tile_features,
        x,
        a1,
        a2,
        *turned_ff,
        *turned_rest,
    )
    (slide_out,) = call(
        out_kernel,
        [((192, BLK), BF)],
        [pltpu.VMEM((192, BLK), BF), dma((4,))],
        n_any=4,
        n_hbm=1,
    )(*parts, tile_grad)
    return (slide_out.T, tile_grad)


def solution(mesh):
    placed = (P(("seq", "tile"), None), P(), P(), P(), P(), P(), P(), P(), P("seq", "tile"))
    return jax.shard_map(
        on_device,
        mesh=mesh,
        in_specs=placed,
        out_specs=(P("seq", "tile"), P(("seq", "tile"), None)),
        check_vma=False,
    )
```

```python
import functools

import jax
import jax.numpy as jnp
from jax import lax
from jax.experimental import pallas as pl
from jax.experimental.pallas import tpu as pltpu
from jax.sharding import PartitionSpec as P

HEADS = 16
HD = 48
EPSILON = 1e-06
SOFT_CAP = 50.0
SCALE = HD**-0.5
LOG2_E = 1.4426950408889634
BLK = 512
SLOTS = 8
BF = jnp.bfloat16
F32 = jnp.float32
I32 = jnp.int32

NN = (((1,), (0,)), ((), ()))
NT = (((1,), (1,)), ((), ()))
TN = (((0,), (0,)), ((), ()))


def mm(a, b, dims=NN):
    return lax.dot_general(a, b, dims, preferred_element_type=F32)


def iota(shape, dim):
    return lax.broadcasted_iota(I32, shape, dim)


def class_order(row):
    return (row & 3) * 128 + ((row >> 2) & 3) * 32 + (row >> 4)


def order_matrix():
    return jnp.where(class_order(iota((BLK, BLK), 0)) == iota((BLK, BLK), 1), 1.0, 0.0).astype(BF)


def normalize(values):
    centred = values - jnp.mean(values, axis=-1, keepdims=True)
    inv_std = lax.rsqrt(jnp.mean(centred * centred, axis=-1, keepdims=True) + EPSILON)
    return (centred * inv_std, inv_std)


def norm_back(normed, inv_std, grads):
    mean_grad = jnp.mean(grads, axis=-1, keepdims=True)
    mean_cross = jnp.mean(grads * normed, axis=-1, keepdims=True)
    return (grads - mean_grad - normed * mean_cross) * inv_std


def call(kernel, outs, scratch=(), n_smem=0, n_any=0, n_hbm=0, n_hbm_out=0, limit=4):
    def run(*args):
        n_vmem = len(args) - n_smem - n_any - n_hbm
        specs = [pl.BlockSpec(memory_space=pltpu.SMEM)] * n_smem
        specs += [pl.BlockSpec(memory_space=pltpu.VMEM)] * n_vmem
        specs += [pl.BlockSpec(memory_space=pl.ANY)] * n_any
        specs += [pl.BlockSpec(memory_space=pltpu.HBM)] * n_hbm
        out_specs = [pl.BlockSpec(memory_space=pltpu.HBM)] * n_hbm_out
        out_specs += [pl.BlockSpec(memory_space=pltpu.VMEM)] * (len(outs) - n_hbm_out)
        shapes = [pltpu.HBM(shape, kind) for shape, kind in outs[:n_hbm_out]]
        shapes += [jax.ShapeDtypeStruct(shape, kind) for shape, kind in outs[n_hbm_out:]]
        cut = len(args) - n_hbm
        held = [pltpu.with_memory_space_constraint(x, pltpu.HBM) for x in args[cut:]]
        return pl.pallas_call(
            kernel,
            out_shape=shapes,
            in_specs=specs,
            out_specs=out_specs,
            scratch_shapes=list(scratch),
            compiler_params=pltpu.CompilerParams(vmem_limit_bytes=limit * 1024 * 1024),
        )(*args[:cut], *held)

    return run


def started(copies):
    for copy in copies:
        copy.start()
    return copies


def finish(copies):
    for copy in copies:
        copy.wait()


def order_kernel(grad_ref, g0_ref, g1_ref, g2_ref, g3_ref, tmp_ref):
    j = lax.axis_index("seq") & 3
    tmp_ref[...] = mm(grad_ref[...], order_matrix()).astype(BF)
    for d, out_ref in enumerate((g0_ref, g1_ref, g2_ref, g3_ref)):
        out_ref[...] = tmp_ref[pl.ds(pl.multiple_of((j ^ d) * HD, 16), HD), :]


def offsets(shift_ref):
    head = 4 * lax.axis_index("tile") + (lax.axis_index("seq") & 3)
    o1 = shift_ref[0, head]
    o2 = shift_ref[1, head]
    return (o1 * 128, (o2 & 3) * 128, o2 >> 2)


def table_kernel(pos_ref, row_ref, col_ref):
    s = lax.axis_index("seq")
    pos = pos_ref[...].T
    n = pos.shape[0]
    block = pos >> 9
    seat = class_order(pos & (BLK - 1)) + 1
    lower = jnp.where(iota((n, n), 1) < iota((n, n), 0), 1.0, 0.0).astype(BF)
    high, low = [], []
    for d in range(4):
        owned = block == (s ^ d)
        rank = mm(lower, jnp.where(owned, 1.0, 0.0).astype(BF)).astype(I32)
        held = jnp.where(owned, seat, 0)
        for k in range(SLOTS):
            found = jnp.sum(jnp.where(rank == k, held, 0), axis=0, keepdims=True)
            high.append(found >> 4)
            low.append(found & 15)
    digits = jnp.concatenate(high + low, axis=0).astype(F32).astype(BF)
    lanes = n * SLOTS
    spread = jnp.where(iota((n, lanes), 0) == iota((n, lanes), 1) >> 3, 1.0, 0.0).astype(BF)
    wide = mm(digits, spread)
    wide = 16.0 * wide[0:32] + wide[32:64]
    own = iota((8, lanes), 0) == (iota((8, lanes), 1) & 7)
    rows = [
        jnp.sum(jnp.where(own, wide[8 * d : 8 * d + 8], 0.0), axis=0, keepdims=True)
        for d in range(4)
    ]
    table = jnp.concatenate(rows + rows, axis=0) - 1.0
    row_ref[...] = table.astype(I32)
    col_ref[...] = table.T.astype(I32)


def forward_mlp_kernel(
    feat_hbm,
    pos_hbm,
    gate_hbm,
    up_hbm,
    down_hbm,
    proj_hbm,
    qkvw_hbm,
    out_hbm,
    x_hbm,
    a1_hbm,
    a2_hbm,
    feat_ref,
    pos_ref,
    wg_ref,
    wu_ref,
    wd_ref,
    wp_ref,
    wq_ref,
    x_ref,
    a1_ref,
    a2_ref,
    heads_ref,
    picker_ref,
    tmp_ref,
    sems,
    out_sems,
):
    ff = gate_hbm.shape[1]
    width = HEADS * HD
    step = 512
    chunks = ff // step
    first = started(
        [
            pltpu.make_async_copy(feat_hbm, feat_ref, sems.at[3 * chunks]),
            pltpu.make_async_copy(pos_hbm, pos_ref, sems.at[3 * chunks + 1]),
        ]
    )
    waits = []
    for c in range(chunks):
        at = pl.ds(c * step, step)
        waits.append(
            started(
                [
                    pltpu.make_async_copy(gate_hbm.at[:, at], wg_ref.at[:, at], sems.at[3 * c]),
                    pltpu.make_async_copy(up_hbm.at[:, at], wu_ref.at[:, at], sems.at[3 * c + 1]),
                    pltpu.make_async_copy(down_hbm.at[at, :], wd_ref.at[at, :], sems.at[3 * c + 2]),
                ]
            )
        )
    last = started(
        [
            pltpu.make_async_copy(proj_hbm, wp_ref, sems.at[3 * chunks + 2]),
        ]
        + [
            pltpu.make_async_copy(qkvw_hbm.at[:, at], wq_ref.at[:, at], sems.at[3 * chunks + 3 + i])
            for i, at in enumerate(pl.ds(width * part, width) for part in range(3))
        ]
    )
    finish(first)

    me = lax.axis_index("seq") * 4 + lax.axis_index("tile")
    brow = pos_ref[pl.ds(me, 1), :] >> 9
    n = brow.shape[1]
    bcol = jnp.broadcast_to(brow, (n, n)).T
    before = iota((n, n), 0) < iota((n, n), 1)
    rank = jnp.sum(jnp.where((bcol == brow) & before, 1, 0), axis=0, keepdims=True)
    code = brow * SLOTS + rank
    code = jnp.concatenate([code, code + 4096], axis=1)
    seat = iota((BLK, 2 * n), 0)
    want = (((seat >> 4) & 7) * 4 + (seat >> 7)) * SLOTS + (seat & 7) + 4096 * ((seat >> 3) & 1)
    picker_ref[...] = jnp.where(code == want, 1.0, 0.0).astype(BF)

    feats = feat_ref[...].astype(F32)
    normed = normalize(feats)[0].astype(BF)
    total = feats
    outs = []
    for c in range(chunks):
        at = slice(c * step, c * step + step)
        waits[c][0].wait()
        gate = mm(normed, wg_ref[:, at])
        waits[c][1].wait()
        up = mm(normed, wu_ref[:, at])
        sig = jax.nn.sigmoid(gate)
        silu = gate * sig
        hidden = (silu * up).astype(BF)
        a1_ref[:, at] = (up * (sig + silu * (1.0 - sig))).astype(BF)
        a2_ref[:, at] = silu.astype(BF)
        waits[c][2].wait()
        total = total + mm(hidden, wd_ref[at, :])
    outs += started(
        [
            pltpu.make_async_copy(a1_ref, a1_hbm, out_sems.at[0]),
            pltpu.make_async_copy(a2_ref, a2_hbm, out_sems.at[1]),
        ]
    )
    last[0].wait()
    x = mm(total.astype(BF), wp_ref[...]).astype(BF)
    x_ref[...] = x
    outs += started([pltpu.make_async_copy(x_ref, x_hbm, out_sems.at[2])])
    slide_norm = normalize(x.astype(F32))[0].astype(BF)

    def deal(values, part):
        for h in range(HEADS):
            t, j = h // 4, h % 4
            heads_ref[2 * j + t // 2, n * (t % 2) : n * (t % 2) + n, HD * part : HD * part + HD] = (
                values[:, h * HD : h * HD + HD]
            )

    deal(x, 3)
    for part in range(3):
        last[1 + part].wait()
        at = slice(width * part, width * part + width)
        deal(mm(slide_norm, wq_ref[:, at]).astype(BF), part)
    for pair in range(HEADS // 2):
        j = pair // 2
        rows = mm(picker_ref[...], heads_ref[pair]).astype(BF)
        at = slice(16 * pair, 16 * pair + 16)
        for block in range(4):
            lane = (j ^ block) * 192
            tmp_ref[:, at, lane : lane + 192] = rows[128 * block : 128 * block + 128].reshape(
                8, 16, 192
            )
        outs += started(
            [
                pltpu.make_async_copy(
                    tmp_ref.at[:, at, :], out_hbm.at[:, at, :], out_sems.at[3 + pair]
                )
            ]
        )
    finish(outs)


def turn_steps(shapes):
    steps = []
    for which, (rows, columns) in enumerate(shapes):
        band = 384 if columns == 2048 else 512 if columns == 1536 else 256 if columns == 2304 else 768
        steps += [(which, at, band) for at in range(0, rows, band)]
    return steps


def turn_kernel(shapes, *refs):
    count = len(shapes)
    given = refs[:count]
    made = refs[count + 1 : 2 * count + 1]
    in_ref, out_ref, in_sems, out_sems = refs[2 * count + 1 :]
    steps = turn_steps(shapes)

    def load(i):
        which, at, band = steps[i]
        columns = shapes[which][1]
        return pltpu.make_async_copy(
            given[which].at[pl.ds(at, band), :],
            in_ref.at[i % 2, pl.ds(0, band), pl.ds(0, columns)],
            in_sems.at[i % 2],
        )

    def store(i):
        which, at, band = steps[i]
        columns = shapes[which][1]
        return pltpu.make_async_copy(
            out_ref.at[i % 2, pl.ds(0, columns), pl.ds(0, band)],
            made[which].at[:, pl.ds(at, band)],
            out_sems.at[i % 2],
        )

    load(0).start()
    for i, (which, _, band) in enumerate(steps):
        columns = shapes[which][1]
        if i + 1 < len(steps):
            load(i + 1).start()
        load(i).wait()
        if i >= 2:
            store(i - 2).wait()
        out_ref[i % 2, 0:columns, 0:band] = in_ref[i % 2, 0:band, 0:columns].T
        store(i).start()
    for i in range(max(len(steps) - 2, 0), len(steps)):
        store(i).wait()


def turned_weights(weights, after):
    shapes = [w.shape for w in weights]
    bands = [band for _, _, band in turn_steps(shapes)]
    widest = max(columns for _, columns in shapes)
    return call(
        functools.partial(turn_kernel, shapes),
        [((columns, rows), BF) for rows, columns in shapes],
        [
            pltpu.VMEM((2, max(bands), widest), BF),
            pltpu.VMEM((2, widest, max(bands)), BF),
            pltpu.SemaphoreType.DMA((2,)),
            pltpu.SemaphoreType.DMA((2,)),
        ],
        n_hbm=len(shapes) + 1,
        n_hbm_out=len(shapes),
        limit=20,
    )(*weights, after)


def backward_mlp_kernel(
    ret_ref,
    s0_any,
    s1_any,
    s2_any,
    s3_any,
    pos_hbm,
    feat_hbm,
    x_hbm,
    a1_hbm,
    a2_hbm,
    gate_hbm,
    up_hbm,
    down_hbm,
    proj_hbm,
    qkvw_hbm,
    out_ref,
    slide_ref,
    pos_ref,
    feat_ref,
    x_ref,
    a1_ref,
    a2_ref,
    wg_ref,
    wu_ref,
    wd_ref,
    wp_ref,
    wq_ref,
    dqkv_ref,
    grad_ref,
    tmp_ref,
    sems,
):
    ff = gate_hbm.shape[0]
    cuts = [(at, 512) for at in range(0, ff - 512, 512)] + [(ff - 512, 256), (ff - 256, 256)]
    chunks = len(cuts)
    pairs = (
        (pos_hbm, pos_ref),
        (x_hbm, x_ref),
        (qkvw_hbm, wq_ref),
        (proj_hbm, wp_ref),
        (a1_hbm, a1_ref),
        (a2_hbm, a2_ref),
        (feat_hbm, feat_ref),
    )
    first = started(
        [
            pltpu.make_async_copy(here, there, sems.at[3 * chunks + i])
            for i, (here, there) in enumerate(pairs)
        ]
    )
    waits = []
    for c, (start, size) in enumerate(cuts):
        at = pl.ds(start, size)
        waits.append(
            started(
                [
                    pltpu.make_async_copy(down_hbm.at[:, at], wd_ref.at[:, at], sems.at[3 * c]),
                    pltpu.make_async_copy(gate_hbm.at[at, :], wg_ref.at[at, :], sems.at[3 * c + 1]),
                    pltpu.make_async_copy(up_hbm.at[at, :], wu_ref.at[at, :], sems.at[3 * c + 2]),
                ]
            )
        )
    j = lax.axis_index("seq") & 3
    pieces = started(
        [
            pltpu.make_async_copy(
                so,
                tmp_ref.at[pl.ds(pl.multiple_of((j ^ d) * HD, 16), HD), :],
                sems.at[3 * chunks + len(pairs) + d],
            )
            for d, so in enumerate((s0_any, s1_any, s2_any, s3_any))
        ]
    )
    first[0].wait()
    me = lax.axis_index("seq") * 4 + lax.axis_index("tile")
    brow = pos_ref[pl.ds(me, 1), :] >> 9
    n = brow.shape[1]
    bcol = jnp.broadcast_to(brow, (n, n)).T
    before = iota((n, n), 1) < iota((n, n), 0)
    rank = jnp.sum(jnp.where((bcol == brow) & before, 1, 0), axis=1, keepdims=True)
    code = bcol[:, 0:1] * SLOTS + rank
    code = jnp.concatenate([code, code + 4096], axis=0)
    seat = iota((2 * n, BLK), 1)
    want = (((seat >> 4) & 7) * 4 + (seat >> 7)) * SLOTS + (seat & 7) + 4096 * ((seat >> 3) & 1)
    picker = jnp.where(code == want, 1.0, 0.0).astype(BF)
    width = HEADS * HD
    for pair in range(HEADS // 2):
        j, t = pair // 2, 2 * (pair % 2)
        tile = ret_ref[:, 16 * pair : 16 * pair + 16, :].reshape(128, 768)
        stacked = jnp.concatenate(
            [tile[:, (j ^ b) * 192 : (j ^ b) * 192 + 192] for b in range(4)], axis=0
        )
        got = mm(picker, stacked).astype(BF)
        for tp in range(2):
            h = 4 * (t + tp) + j
            mine = got[n * tp : n * tp + n]
            for part in range(3):
                dqkv_ref[:, part * width + h * HD : part * width + h * HD + HD] = mine[
                    :, HD * part : HD * part + HD
                ]
            grad_ref[:, h * HD : h * HD + HD] = mine[:, 144:192]
    first[1].wait()
    slide_norm, slide_inv = normalize(x_ref[...].astype(F32))
    first[2].wait()
    dnorm = mm(dqkv_ref[...], wq_ref[...])
    dslide = (grad_ref[...].astype(F32) + norm_back(slide_norm, slide_inv, dnorm)).astype(BF)
    first[3].wait()
    dembed = mm(dslide, wp_ref[...]).astype(BF)
    finish(first[4:])
    normed, inv = normalize(feat_ref[...].astype(F32))
    finish(pieces)
    slide_ref[...] = mm(tmp_ref[...], order_matrix(), NT).astype(BF)
    dfeat = jnp.zeros(feat_ref.shape, F32)
    for c, (start, size) in enumerate(cuts):
        at = slice(start, start + size)
        waits[c][0].wait()
        dhidden = mm(dembed, wd_ref[:, at])
        dgate = (dhidden * a1_ref[:, at].astype(F32)).astype(BF)
        dup = (dhidden * a2_ref[:, at].astype(F32)).astype(BF)
        waits[c][1].wait()
        dfeat = dfeat + mm(dgate, wg_ref[at, :])
        waits[c][2].wait()
        dfeat = dfeat + mm(dup, wu_ref[at, :])
    out_ref[...] = (dembed.astype(F32) + norm_back(normed, inv, dfeat)).astype(BF)


def place_kernel(shift_ref, recv_ref, tab_ref, _after_hbm, y_ref, yt_ref, y2_ref):
    _, base, part = offsets(shift_ref)
    o2 = pl.multiple_of(base + 32 * part, 32)
    for d in range(4):
        tab = tab_ref[d : d + 1, :]
        onehot = jnp.where(iota((BLK, tab.shape[1]), 0) == tab, 1.0, 0.0).astype(BF)
        y = mm(onehot, recv_ref[:, 192 * d : 192 * d + 192])
        y_ref[d] = y.astype(BF)
        yt_ref[d] = y.T.astype(BF)
        y2_ref[32 * d : 32 * d + 32, :] = y_ref[d, pl.ds(o2, 32), :]


def score_rows(keys, queries_t, e_store, m_store):
    count, width = keys.shape[0], queries_t.shape[1]
    total = jnp.zeros((8, width), F32)
    step = 128
    for c in range(0, count, step):
        t = jnp.tanh(mm(keys[c : c + step], queries_t) * (SCALE / SOFT_CAP))
        e = jnp.exp2((SOFT_CAP * LOG2_E) * t)
        total = total + jnp.sum(e.reshape(step // 8, 8, width), axis=0)
        e_store(c, step, e.astype(BF))
        m_store(c, step, (e - e * (t * t)).astype(BF))
    return jnp.sum(total, axis=0, keepdims=True)


def forward_kernel(shift_ref, y_ref, yt_ref, e0_ref, m0_ref, e1_ref, m1_ref, u_ref, l_ref):
    o1 = pl.multiple_of(offsets(shift_ref)[0], 128)

    def block(d):
        def e_store(c, n, v):
            e0_ref[d, c : c + n, :] = v

        def m_store(c, n, v):
            m0_ref[d, c : c + n, :] = v

        l_ref[d] = score_rows(y_ref[d, :, 48:96], yt_ref[d, 0:48, :], e_store, m_store)
        u_ref[d] = mm(yt_ref[d, 96:144, :], e0_ref[d])

    for d in range(4):
        block(d)

    def e_store(c, n, v):
        e1_ref[c : c + n, :] = v

    def m_store(c, n, v):
        m1_ref[c : c + n, :] = v

    keys = jnp.concatenate([y_ref[d, pl.ds(o1, 128), 48:96] for d in range(4)], axis=0)
    queries = jnp.concatenate([yt_ref[d, 0:48, pl.ds(o1, 128)] for d in range(4)], axis=1)
    values = jnp.concatenate([yt_ref[d, 96:144, pl.ds(o1, 128)] for d in range(4)], axis=1)
    l1 = score_rows(keys, queries, e_store, m_store)
    u1 = mm(values, e1_ref[...])
    for d in range(4):
        u_ref[d, :, pl.ds(o1, 128)] += u1[:, 128 * d : 128 * d + 128]
        l_ref[d, :, pl.ds(o1, 128)] += l1[:, 128 * d : 128 * d + 128]


def turned(value, shift):
    return pltpu.roll(value, shift & 127, 1)


def wide_kernel(
    shift_ref,
    yt_ref,
    a0_ref,
    a1_ref,
    a2_ref,
    a3_ref,
    u_ref,
    l_ref,
    g0_ref,
    g1_ref,
    g2_ref,
    g3_ref,
    so0_hbm,
    so1_hbm,
    so2_hbm,
    so3_hbm,
    gs_ref,
    ds_ref,
    own_ref,
    send1_ref,
    send2_ref,
    send3_ref,
    dq_ref,
    e2_ref,
    m2_ref,
    usum_ref,
    lsum_ref,
    so_ref,
    so_sems,
):
    outs = []
    _, base, part = offsets(shift_ref)
    base = pl.multiple_of(base, 128)
    y2 = jnp.concatenate([a0_ref[...], a1_ref[...], a2_ref[...], a3_ref[...]], axis=0)
    keys, values = y2[:, 48:96], y2[:, 96:144]
    both_t = y2[:, 48:144].astype(F32).T.astype(BF)
    query_t = a0_ref[:, 0:48].astype(F32).T.astype(BF)

    def e_store(c, n, v):
        e2_ref[c : c + n, :] = v

    def m_store(c, n, v):
        m2_ref[c : c + n, :] = v

    l2 = score_rows(keys, query_t, e_store, m_store)
    u2 = mm(both_t[48:96], e2_ref[...])
    l2w = jnp.broadcast_to(l2, (8, 128))
    lane = iota((1, 128), 1) >> 5
    gs2 = jnp.zeros((48, 128), F32)
    ds2 = jnp.zeros((8, 128), F32)
    for d in range(4):
        here = lane == part
        shift = 32 * (part - d)
        usum_ref[...] = u_ref[d]
        lsum_ref[...] = l_ref[d]
        usum_ref[:, pl.ds(base, 128)] += jnp.where(here, turned(u2, shift), 0.0)
        lsum_ref[:, pl.ds(base, 128)] += jnp.where(here, turned(l2w, shift), 0.0)[0:1]
        inv = 1.0 / lsum_ref[...]
        att = usum_ref[...] * inv
        so_ref[d] = (yt_ref[d, 144:192, :].astype(F32) + att).astype(BF)
        so = (so0_hbm, so1_hbm, so2_hbm, so3_hbm)[d]
        outs += started([pltpu.make_async_copy(so_ref.at[d], so, so_sems.at[d])])
        grad_ref = (g0_ref, g1_ref, g2_ref, g3_ref)[d]
        gs = (grad_ref[...].astype(F32) * inv).astype(BF)
        gs_ref[d] = gs
        ds_ref[d] = jnp.sum(gs.astype(F32) * att, axis=0, keepdims=True)
        gs_wide = gs_ref[d, :, pl.ds(base, 128)].astype(F32)
        ds_wide = jnp.broadcast_to(ds_ref[d, :, pl.ds(base, 128)], (8, 128))
        gs2 = jnp.where(lane == d, turned(gs_wide, -shift), gs2)
        ds2 = jnp.where(lane == d, turned(ds_wide, -shift), ds2)
    gs2 = gs2.astype(BF)
    dp = mm(values, gs2)
    dscore = (m2_ref[...].astype(F32) * (dp - ds2[0:1])).astype(BF)
    dq_ref[...] = mm(both_t[0:48], dscore) * SCALE
    dk = mm(query_t, dscore, NT) * SCALE
    dv = mm(gs2, e2_ref[...], NT)
    dkv = jnp.concatenate([dk, dv], axis=0)
    own_ref[...] = dkv[:, 0:128]
    for e, send_ref in enumerate((send1_ref, send2_ref, send3_ref)):
        send_ref[...] = dkv[:, 128 * e + 128 : 128 * e + 256].astype(BF)
    finish(outs)


def dscores(values, gs, ds, m_load, store):
    dp = mm(values, gs)
    step = 64
    for c in range(0, dp.shape[0], step):
        store(c, step, (m_load(c, step).astype(F32) * (dp[c : c + step] - ds)).astype(BF))


def backward_kernel(
    shift_ref, y_ref, yt_ref, e0_ref, m0_ref, e1_ref, m1_ref, gs_ref, ds_ref, out_ref, tmp_ref
):
    o1 = pl.multiple_of(offsets(shift_ref)[0], 128)

    def store(c, n, v):
        tmp_ref[c : c + n, :] = v

    def block(d):
        gs = gs_ref[d]
        dscores(y_ref[d, :, 96:144], gs, ds_ref[d], lambda c, n: m0_ref[d, c : c + n, :], store)
        dscore = tmp_ref[...]
        out_ref[d, 0:48, :] = mm(yt_ref[d, 48:96, :], dscore) * SCALE
        out_ref[d, 48:96, :] = mm(yt_ref[d, 0:48, :], dscore, NT) * SCALE
        out_ref[d, 96:144, :] = mm(gs, e0_ref[d], NT)

    for d in range(4):
        block(d)
    values = jnp.concatenate([y_ref[d, pl.ds(o1, 128), 96:144] for d in range(4)], axis=0)
    queries = jnp.concatenate([yt_ref[d, 0:48, pl.ds(o1, 128)] for d in range(4)], axis=1)
    keys = jnp.concatenate([yt_ref[d, 48:96, pl.ds(o1, 128)] for d in range(4)], axis=1)
    gs = jnp.concatenate([gs_ref[d, :, pl.ds(o1, 128)] for d in range(4)], axis=1)
    ds = jnp.concatenate([ds_ref[d, :, pl.ds(o1, 128)] for d in range(4)], axis=1)
    dscores(values, gs, ds, lambda c, n: m1_ref[c : c + n, :], store)
    dscore = tmp_ref[...]
    dq = mm(keys, dscore) * SCALE
    dk = mm(queries, dscore, NT) * SCALE
    dv = mm(gs, e1_ref[...], NT)
    dall = jnp.concatenate([dq, dk, dv], axis=0)
    for d in range(4):
        out_ref[d, :, pl.ds(o1, 128)] += dall[:, 128 * d : 128 * d + 128]


def return_kernel(
    shift_ref,
    dall_ref,
    own_ref,
    dq_ref,
    r1_ref,
    r2_ref,
    r3_ref,
    g0_ref,
    g1_ref,
    g2_ref,
    g3_ref,
    tab_ref,
    out_hbm,
    sum_ref,
    out_ref,
    sems,
):
    _, base, part = offsets(shift_ref)
    base = pl.multiple_of(base, 128)
    dkv = (
        own_ref[...]
        + r1_ref[...].astype(F32)
        + r2_ref[...].astype(F32)
        + r3_ref[...].astype(F32)
    )
    extra = jnp.concatenate([dq_ref[...], dkv], axis=0)
    lane = iota((1, 128), 1) >> 5
    rows = tab_ref.shape[0]
    step = rows // 4
    outs, parts = [], []
    for d in range(4):
        grad_ref = (g0_ref, g1_ref, g2_ref, g3_ref)[d]
        sum_ref[...] = dall_ref[d]
        sum_ref[:, pl.ds(base, 128)] += jnp.where(
            lane == part, turned(extra, 32 * (part - d)), 0.0
        )
        parts.append(jnp.concatenate([sum_ref[...].astype(BF), grad_ref[...]], axis=0).T)
    for c in range(4):
        at = slice(step * c, step * c + step)
        for d in range(4):
            onehot = jnp.where(tab_ref[at, d : d + 1] == iota((step, BLK), 1), 1.0, 0.0)
            out_ref[at, 192 * d : 192 * d + 192] = mm(onehot.astype(BF), parts[d]).astype(BF)
        outs += started([pltpu.make_async_copy(out_ref.at[at, :], out_hbm.at[at, :], sems.at[c])])
    finish(outs)


def swap(value, distance, count):
    return lax.ppermute(value, "seq", [(i, i ^ distance) for i in range(count)])


def on_device(
    tile_features,
    gate_weight,
    up_weight,
    down_weight,
    input_projection_weight,
    query_key_value_weight,
    positions,
    dilation_shift,
    slide_output_gradient,
):
    seq_count = lax.axis_size("seq")
    device_count = seq_count * lax.axis_size("tile")
    rows, width = tile_features.shape
    ff = gate_weight.shape[1]
    slide_width = input_projection_weight.shape[1]
    all_pos = positions.reshape(device_count, rows)
    routed = ((8, 16 * SLOTS, slide_width), BF)
    weights = (gate_weight, up_weight, down_weight, input_projection_weight, query_key_value_weight)

    def exchange(block):
        return lax.all_to_all(
            block.reshape(device_count, SLOTS, slide_width),
            ("seq", "tile"),
            split_axis=0,
            concat_axis=0,
            tiled=True,
        ).reshape(device_count * SLOTS, slide_width)

    stored = [
        pltpu.VMEM((width, ff), BF),
        pltpu.VMEM((width, ff), BF),
        pltpu.VMEM((ff, width), BF),
        pltpu.VMEM((width, slide_width), BF),
        pltpu.VMEM((slide_width, 3 * slide_width), BF),
    ]
    dma = pltpu.SemaphoreType.DMA
    outgoing, x, a1, a2 = call(
        forward_mlp_kernel,
        [routed, ((rows, slide_width), BF), ((rows, ff), BF), ((rows, ff), BF)],
        [pltpu.VMEM((rows, width), BF), pltpu.VMEM((device_count, rows), I32)]
        + stored
        + [
            pltpu.VMEM((rows, slide_width), BF),
            pltpu.VMEM((rows, ff), BF),
            pltpu.VMEM((rows, ff), BF),
            pltpu.VMEM((HEADS // 2, 2 * rows, 192), BF),
            pltpu.VMEM((BLK, 2 * rows), BF),
            pltpu.VMEM((8, 16 * SLOTS, slide_width), BF),
            dma((18,)),
            dma((3 + HEADS // 2,)),
        ],
        n_hbm=7,
        n_hbm_out=4,
        limit=48,
    )(tile_features, all_pos, *weights)
    arrived = exchange(outgoing)
    turned_ff = turned_weights(weights[:2], x)

    grads = call(
        order_kernel,
        [((HD, BLK), BF)] * 4,
        [pltpu.VMEM((192, BLK), BF)],
    )(slide_output_gradient.T)
    grads = [grads[0]] + [swap(grads[d], d, seq_count) for d in range(1, 4)]
    slots = device_count * SLOTS
    table, table_col = call(
        table_kernel,
        [((8, slots), I32), ((slots, 8), I32)],
    )(all_pos)

    y, yt, y2 = call(
        place_kernel,
        [((4, BLK, 192), BF), ((4, 192, BLK), BF), ((128, 192), BF)],
        n_smem=1,
        n_hbm=1,
    )(dilation_shift, arrived, table, turned_ff[0])
    y2_in = [swap(y2, 4 * e, seq_count) for e in range(1, 4)]
    e0, m0, e1, m1, u, l = call(
        forward_kernel,
        [
            ((4, BLK, BLK), BF),
            ((4, BLK, BLK), BF),
            ((BLK, BLK), BF),
            ((BLK, BLK), BF),
            ((4, HD, BLK), F32),
            ((4, 1, BLK), F32),
        ],
        n_smem=1,
    )(dilation_shift, y, yt)
    *parts, gs, ds, own, send1, send2, send3, dq2 = call(
        wide_kernel,
        [((HD, BLK), BF)] * 4
        + [((4, HD, BLK), BF), ((4, 1, BLK), F32), ((96, 128), F32)]
        + [((96, 128), BF)] * 3
        + [((HD, 128), F32)],
        [
            pltpu.VMEM((BLK, 128), BF),
            pltpu.VMEM((BLK, 128), BF),
            pltpu.VMEM((HD, BLK), F32),
            pltpu.VMEM((1, BLK), F32),
            pltpu.VMEM((4, HD, BLK), BF),
            dma((4,)),
        ],
        n_smem=1,
        n_hbm_out=4,
    )(dilation_shift, yt, y2, *y2_in, u, l, *grads)
    back = [swap(send, 4 * e, seq_count) for e, send in ((1, send1), (2, send2), (3, send3))]
    (dall,) = call(
        backward_kernel,
        [((4, 144, BLK), F32)],
        [pltpu.VMEM((BLK, BLK), BF)],
        n_smem=1,
    )(dilation_shift, y, yt, e0, m0, e1, m1, gs, ds)
    (returning,) = call(
        return_kernel,
        [((slots, slide_width), BF)],
        [
            pltpu.VMEM((144, BLK), F32),
            pltpu.VMEM((slots, slide_width), BF),
            dma((4,)),
        ],
        n_smem=1,
        n_hbm_out=1,
        limit=6,
    )(dilation_shift, dall, own, dq2, *back, *grads, table_col)
    returned = exchange(returning)
    turned_rest = turned_weights(weights[2:], returning)
    parts = [parts[0]] + [swap(parts[d], d, seq_count) for d in range(1, 4)]

    tile_grad, slide_out = call(
        backward_mlp_kernel,
        [((rows, width), BF), ((192, BLK), BF)],
        [
            pltpu.VMEM((device_count, rows), I32),
            pltpu.VMEM((rows, width), BF),
            pltpu.VMEM((rows, slide_width), BF),
            pltpu.VMEM((rows, ff), BF),
            pltpu.VMEM((rows, ff), BF),
        ]
        + [pltpu.VMEM(w.shape[::-1], BF) for w in weights]
        + [
            pltpu.VMEM((rows, 3 * slide_width), BF),
            pltpu.VMEM((rows, slide_width), BF),
            pltpu.VMEM((192, BLK), BF),
            dma((26,)),
        ],
        n_any=4,
        n_hbm=10,
        limit=48,
    )(
        returned.reshape(8, 16 * SLOTS, slide_width),
        *parts,
        all_pos,
        tile_features,
        x,
        a1,
        a2,
        *turned_ff,
        *turned_rest,
    )
    return (slide_out.T, tile_grad)


def solution(mesh):
    placed = (P(("seq", "tile"), None), P(), P(), P(), P(), P(), P(), P(), P("seq", "tile"))
    return jax.shard_map(
        on_device,
        mesh=mesh,
        in_specs=placed,
        out_specs=(P("seq", "tile"), P(("seq", "tile"), None)),
        check_vma=False,
    )
```

```python
import functools

import jax
import jax.numpy as jnp
from jax import lax
from jax.experimental import pallas as pl
from jax.experimental.pallas import tpu as pltpu
from jax.sharding import PartitionSpec as P

HEADS = 16
HD = 48
EPSILON = 1e-06
SOFT_CAP = 50.0
SCALE = HD**-0.5
LOG2_E = 1.4426950408889634
BLK = 512
SLOTS = 8
BF = jnp.bfloat16
F32 = jnp.float32
I32 = jnp.int32

NN = (((1,), (0,)), ((), ()))
NT = (((1,), (1,)), ((), ()))
TN = (((0,), (0,)), ((), ()))


def mm(a, b, dims=NN):
    return lax.dot_general(a, b, dims, preferred_element_type=F32)


def iota(shape, dim):
    return lax.broadcasted_iota(I32, shape, dim)


def class_order(row):
    return (row & 3) * 128 + ((row >> 2) & 3) * 32 + (row >> 4)


def order_matrix():
    return jnp.where(class_order(iota((BLK, BLK), 0)) == iota((BLK, BLK), 1), 1.0, 0.0).astype(BF)


def normalize(values):
    centred = values - jnp.mean(values, axis=-1, keepdims=True)
    inv_std = lax.rsqrt(jnp.mean(centred * centred, axis=-1, keepdims=True) + EPSILON)
    return (centred * inv_std, inv_std)


def norm_back(normed, inv_std, grads):
    mean_grad = jnp.mean(grads, axis=-1, keepdims=True)
    mean_cross = jnp.mean(grads * normed, axis=-1, keepdims=True)
    return (grads - mean_grad - normed * mean_cross) * inv_std


def call(kernel, outs, scratch=(), n_smem=0, n_any=0, n_hbm=0, n_hbm_out=0, limit=4):
    def run(*args):
        n_vmem = len(args) - n_smem - n_any - n_hbm
        specs = [pl.BlockSpec(memory_space=pltpu.SMEM)] * n_smem
        specs += [pl.BlockSpec(memory_space=pltpu.VMEM)] * n_vmem
        specs += [pl.BlockSpec(memory_space=pl.ANY)] * n_any
        specs += [pl.BlockSpec(memory_space=pltpu.HBM)] * n_hbm
        out_specs = [pl.BlockSpec(memory_space=pltpu.HBM)] * n_hbm_out
        out_specs += [pl.BlockSpec(memory_space=pltpu.VMEM)] * (len(outs) - n_hbm_out)
        shapes = [pltpu.HBM(shape, kind) for shape, kind in outs[:n_hbm_out]]
        shapes += [jax.ShapeDtypeStruct(shape, kind) for shape, kind in outs[n_hbm_out:]]
        cut = len(args) - n_hbm
        held = [pltpu.with_memory_space_constraint(x, pltpu.HBM) for x in args[cut:]]
        return pl.pallas_call(
            kernel,
            out_shape=shapes,
            in_specs=specs,
            out_specs=out_specs,
            scratch_shapes=list(scratch),
            compiler_params=pltpu.CompilerParams(vmem_limit_bytes=limit * 1024 * 1024),
        )(*args[:cut], *held)

    return run


def started(copies):
    for copy in copies:
        copy.start()
    return copies


def finish(copies):
    for copy in copies:
        copy.wait()


def order_kernel(grad_ref, g0_ref, g1_ref, g2_ref, g3_ref, tmp_ref):
    j = lax.axis_index("seq") & 3
    tmp_ref[...] = mm(grad_ref[...], order_matrix()).astype(BF)
    for d, out_ref in enumerate((g0_ref, g1_ref, g2_ref, g3_ref)):
        out_ref[...] = tmp_ref[pl.ds(pl.multiple_of((j ^ d) * HD, 16), HD), :]


def offsets(shift_ref):
    head = 4 * lax.axis_index("tile") + (lax.axis_index("seq") & 3)
    o1 = shift_ref[0, head]
    o2 = shift_ref[1, head]
    return (o1 * 128, (o2 & 3) * 128, o2 >> 2)


def table_kernel(pos_ref, row_ref, col_ref):
    s = lax.axis_index("seq")
    pos = pos_ref[...].T
    n = pos.shape[0]
    block = pos >> 9
    seat = class_order(pos & (BLK - 1)) + 1
    lower = jnp.where(iota((n, n), 1) < iota((n, n), 0), 1.0, 0.0).astype(BF)
    high, low = [], []
    for d in range(4):
        owned = block == (s ^ d)
        rank = mm(lower, jnp.where(owned, 1.0, 0.0).astype(BF)).astype(I32)
        held = jnp.where(owned, seat, 0)
        for k in range(SLOTS):
            found = jnp.sum(jnp.where(rank == k, held, 0), axis=0, keepdims=True)
            high.append(found >> 4)
            low.append(found & 15)
    digits = jnp.concatenate(high + low, axis=0).astype(F32).astype(BF)
    lanes = n * SLOTS
    spread = jnp.where(iota((n, lanes), 0) == iota((n, lanes), 1) >> 3, 1.0, 0.0).astype(BF)
    wide = mm(digits, spread)
    wide = 16.0 * wide[0:32] + wide[32:64]
    own = iota((8, lanes), 0) == (iota((8, lanes), 1) & 7)
    rows = [
        jnp.sum(jnp.where(own, wide[8 * d : 8 * d + 8], 0.0), axis=0, keepdims=True)
        for d in range(4)
    ]
    table = jnp.concatenate(rows + rows, axis=0) - 1.0
    row_ref[...] = table.astype(I32)
    col_ref[...] = table.T.astype(I32)


def forward_mlp_kernel(
    feat_hbm,
    pos_hbm,
    gate_hbm,
    up_hbm,
    down_hbm,
    proj_hbm,
    qkvw_hbm,
    out_hbm,
    x_hbm,
    a1_hbm,
    a2_hbm,
    feat_ref,
    pos_ref,
    wg_ref,
    wu_ref,
    wd_ref,
    wp_ref,
    wq_ref,
    x_ref,
    a1_ref,
    a2_ref,
    heads_ref,
    picker_ref,
    tmp_ref,
    sems,
    out_sems,
):
    ff = gate_hbm.shape[1]
    width = HEADS * HD
    step = 512
    chunks = ff // step
    first = started(
        [
            pltpu.make_async_copy(feat_hbm, feat_ref, sems.at[3 * chunks]),
            pltpu.make_async_copy(pos_hbm, pos_ref, sems.at[3 * chunks + 1]),
        ]
    )
    waits = []
    for c in range(chunks):
        at = pl.ds(c * step, step)
        waits.append(
            started(
                [
                    pltpu.make_async_copy(gate_hbm.at[:, at], wg_ref.at[:, at], sems.at[3 * c]),
                    pltpu.make_async_copy(up_hbm.at[:, at], wu_ref.at[:, at], sems.at[3 * c + 1]),
                    pltpu.make_async_copy(down_hbm.at[at, :], wd_ref.at[at, :], sems.at[3 * c + 2]),
                ]
            )
        )
    last = started(
        [
            pltpu.make_async_copy(proj_hbm, wp_ref, sems.at[3 * chunks + 2]),
        ]
        + [
            pltpu.make_async_copy(qkvw_hbm.at[:, at], wq_ref.at[:, at], sems.at[3 * chunks + 3 + i])
            for i, at in enumerate(pl.ds(width * part, width) for part in range(3))
        ]
    )
    finish(first)

    me = lax.axis_index("seq") * 4 + lax.axis_index("tile")
    brow = pos_ref[pl.ds(me, 1), :] >> 9
    n = brow.shape[1]
    bcol = jnp.broadcast_to(brow, (n, n)).T
    before = iota((n, n), 0) < iota((n, n), 1)
    rank = jnp.sum(jnp.where((bcol == brow) & before, 1, 0), axis=0, keepdims=True)
    code = brow * SLOTS + rank
    code = jnp.concatenate([code, code + 4096], axis=1)
    seat = iota((BLK, 2 * n), 0)
    want = (((seat >> 4) & 7) * 4 + (seat >> 7)) * SLOTS + (seat & 7) + 4096 * ((seat >> 3) & 1)
    picker_ref[...] = jnp.where(code == want, 1.0, 0.0).astype(BF)

    feats = feat_ref[...].astype(F32)
    normed = normalize(feats)[0].astype(BF)
    total = feats
    outs = []
    for c in range(chunks):
        at = slice(c * step, c * step + step)
        waits[c][0].wait()
        gate = mm(normed, wg_ref[:, at])
        waits[c][1].wait()
        up = mm(normed, wu_ref[:, at])
        sig = jax.nn.sigmoid(gate)
        silu = gate * sig
        hidden = (silu * up).astype(BF)
        a1_ref[:, at] = (up * (sig + silu * (1.0 - sig))).astype(BF)
        a2_ref[:, at] = silu.astype(BF)
        waits[c][2].wait()
        total = total + mm(hidden, wd_ref[at, :])
    outs += started(
        [
            pltpu.make_async_copy(a1_ref, a1_hbm, out_sems.at[0]),
            pltpu.make_async_copy(a2_ref, a2_hbm, out_sems.at[1]),
        ]
    )
    last[0].wait()
    x = mm(total.astype(BF), wp_ref[...]).astype(BF)
    x_ref[...] = x
    outs += started([pltpu.make_async_copy(x_ref, x_hbm, out_sems.at[2])])
    slide_norm = normalize(x.astype(F32))[0].astype(BF)

    def deal(values, part):
        for h in range(HEADS):
            t, j = h // 4, h % 4
            heads_ref[2 * j + t // 2, n * (t % 2) : n * (t % 2) + n, HD * part : HD * part + HD] = (
                values[:, h * HD : h * HD + HD]
            )

    deal(x, 3)
    for part in range(3):
        last[1 + part].wait()
        at = slice(width * part, width * part + width)
        deal(mm(slide_norm, wq_ref[:, at]).astype(BF), part)
    for pair in range(HEADS // 2):
        j = pair // 2
        rows = mm(picker_ref[...], heads_ref[pair]).astype(BF)
        at = slice(16 * pair, 16 * pair + 16)
        for block in range(4):
            lane = (j ^ block) * 192
            tmp_ref[:, at, lane : lane + 192] = rows[128 * block : 128 * block + 128].reshape(
                8, 16, 192
            )
        outs += started(
            [
                pltpu.make_async_copy(
                    tmp_ref.at[:, at, :], out_hbm.at[:, at, :], out_sems.at[3 + pair]
                )
            ]
        )
    finish(outs)


def turn_steps(shapes):
    steps = []
    for which, (rows, columns) in enumerate(shapes):
        band = 384 if columns == 2048 else 512 if columns == 1536 else 256 if columns == 2304 else 768
        steps += [(which, at, band) for at in range(0, rows, band)]
    return steps


def turn_kernel(shapes, *refs):
    count = len(shapes)
    given = refs[:count]
    made = refs[count + 1 : 2 * count + 1]
    in_ref, out_ref, in_sems, out_sems = refs[2 * count + 1 :]
    steps = turn_steps(shapes)

    def load(i):
        which, at, band = steps[i]
        columns = shapes[which][1]
        return pltpu.make_async_copy(
            given[which].at[pl.ds(at, band), :],
            in_ref.at[i % 2, pl.ds(0, band), pl.ds(0, columns)],
            in_sems.at[i % 2],
        )

    def store(i):
        which, at, band = steps[i]
        columns = shapes[which][1]
        return pltpu.make_async_copy(
            out_ref.at[i % 2, pl.ds(0, columns), pl.ds(0, band)],
            made[which].at[:, pl.ds(at, band)],
            out_sems.at[i % 2],
        )

    load(0).start()
    for i, (which, _, band) in enumerate(steps):
        columns = shapes[which][1]
        if i + 1 < len(steps):
            load(i + 1).start()
        load(i).wait()
        if i >= 2:
            store(i - 2).wait()
        out_ref[i % 2, 0:columns, 0:band] = in_ref[i % 2, 0:band, 0:columns].T
        store(i).start()
    for i in range(max(len(steps) - 2, 0), len(steps)):
        store(i).wait()


def turned_weights(weights, after):
    shapes = [w.shape for w in weights]
    bands = [band for _, _, band in turn_steps(shapes)]
    widest = max(columns for _, columns in shapes)
    return call(
        functools.partial(turn_kernel, shapes),
        [((columns, rows), BF) for rows, columns in shapes],
        [
            pltpu.VMEM((2, max(bands), widest), BF),
            pltpu.VMEM((2, widest, max(bands)), BF),
            pltpu.SemaphoreType.DMA((2,)),
            pltpu.SemaphoreType.DMA((2,)),
        ],
        n_hbm=len(shapes) + 1,
        n_hbm_out=len(shapes),
        limit=20,
    )(*weights, after)


def fold_kernel(
    down_hbm,
    proj_hbm,
    qkvw_hbm,
    _after_hbm,
    fold_hbm,
    projt_hbm,
    qkvt_hbm,
    wd_ref,
    wp_ref,
    wq_ref,
    fold_ref,
    projt_ref,
    qkvt_ref,
    sems,
    out_sems,
):
    step = 512
    chunks = down_hbm.shape[0] // step
    loads = started(
        [
            pltpu.make_async_copy(qkvw_hbm, wq_ref, sems.at[0]),
            pltpu.make_async_copy(proj_hbm, wp_ref, sems.at[1]),
        ]
        + [
            pltpu.make_async_copy(
                down_hbm.at[pl.ds(step * c, step), :],
                wd_ref.at[pl.ds(step * c, step), :],
                sems.at[2 + c],
            )
            for c in range(chunks)
        ]
    )
    loads[0].wait()
    qkvt_ref[...] = wq_ref[...].T
    outs = started([pltpu.make_async_copy(qkvt_ref, qkvt_hbm, out_sems.at[0])])
    loads[1].wait()
    projt_ref[...] = wp_ref[...].T
    outs += started([pltpu.make_async_copy(projt_ref, projt_hbm, out_sems.at[1])])
    for c in range(chunks):
        loads[2 + c].wait()
        at = slice(step * c, step * c + step)
        fold_ref[:, at] = mm(wd_ref[at, :], wp_ref[...]).astype(BF).T
        outs += started(
            [
                pltpu.make_async_copy(
                    fold_ref.at[:, pl.ds(step * c, step)],
                    fold_hbm.at[:, pl.ds(step * c, step)],
                    out_sems.at[2 + c],
                )
            ]
        )
    finish(outs)


def backward_mlp_kernel(
    ret_ref,
    s0_any,
    s1_any,
    s2_any,
    s3_any,
    pos_hbm,
    feat_hbm,
    x_hbm,
    a1_hbm,
    a2_hbm,
    gate_hbm,
    up_hbm,
    fold_hbm,
    proj_hbm,
    qkvw_hbm,
    out_ref,
    slide_ref,
    pos_ref,
    feat_ref,
    x_ref,
    a1_ref,
    a2_ref,
    wg_ref,
    wu_ref,
    fold_ref,
    wp_ref,
    wq_ref,
    dqkv_ref,
    grad_ref,
    tmp_ref,
    sems,
):
    ff = gate_hbm.shape[0]
    cuts = [(at, 512) for at in range(0, ff - 512, 512)] + [(ff - 512, 256), (ff - 256, 256)]
    chunks = len(cuts)
    pairs = (
        (pos_hbm, pos_ref),
        (x_hbm, x_ref),
        (qkvw_hbm, wq_ref),
        (proj_hbm, wp_ref),
        (a1_hbm, a1_ref),
        (a2_hbm, a2_ref),
        (feat_hbm, feat_ref),
    )
    first = started(
        [
            pltpu.make_async_copy(here, there, sems.at[3 * chunks + i])
            for i, (here, there) in enumerate(pairs)
        ]
    )
    waits = []
    for c, (start, size) in enumerate(cuts):
        at = pl.ds(start, size)
        waits.append(
            started(
                [
                    pltpu.make_async_copy(fold_hbm.at[:, at], fold_ref.at[:, at], sems.at[3 * c]),
                    pltpu.make_async_copy(gate_hbm.at[at, :], wg_ref.at[at, :], sems.at[3 * c + 1]),
                    pltpu.make_async_copy(up_hbm.at[at, :], wu_ref.at[at, :], sems.at[3 * c + 2]),
                ]
            )
        )
    j = lax.axis_index("seq") & 3
    pieces = started(
        [
            pltpu.make_async_copy(
                so,
                tmp_ref.at[pl.ds(pl.multiple_of((j ^ d) * HD, 16), HD), :],
                sems.at[3 * chunks + len(pairs) + d],
            )
            for d, so in enumerate((s0_any, s1_any, s2_any, s3_any))
        ]
    )
    first[0].wait()
    me = lax.axis_index("seq") * 4 + lax.axis_index("tile")
    brow = pos_ref[pl.ds(me, 1), :] >> 9
    n = brow.shape[1]
    bcol = jnp.broadcast_to(brow, (n, n)).T
    before = iota((n, n), 1) < iota((n, n), 0)
    rank = jnp.sum(jnp.where((bcol == brow) & before, 1, 0), axis=1, keepdims=True)
    code = bcol[:, 0:1] * SLOTS + rank
    code = jnp.concatenate([code, code + 4096], axis=0)
    seat = iota((2 * n, BLK), 1)
    want = (((seat >> 4) & 7) * 4 + (seat >> 7)) * SLOTS + (seat & 7) + 4096 * ((seat >> 3) & 1)
    picker = jnp.where(code == want, 1.0, 0.0).astype(BF)
    width = HEADS * HD
    for pair in range(HEADS // 2):
        j, t = pair // 2, 2 * (pair % 2)
        tile = ret_ref[:, 16 * pair : 16 * pair + 16, :].reshape(128, 768)
        stacked = jnp.concatenate(
            [tile[:, (j ^ b) * 192 : (j ^ b) * 192 + 192] for b in range(4)], axis=0
        )
        got = mm(picker, stacked).astype(BF)
        for tp in range(2):
            h = 4 * (t + tp) + j
            mine = got[n * tp : n * tp + n]
            for part in range(3):
                dqkv_ref[:, part * width + h * HD : part * width + h * HD + HD] = mine[
                    :, HD * part : HD * part + HD
                ]
            grad_ref[:, h * HD : h * HD + HD] = mine[:, 144:192]
    first[1].wait()
    slide_norm, slide_inv = normalize(x_ref[...].astype(F32))
    first[2].wait()
    dnorm = mm(dqkv_ref[...], wq_ref[...])
    dslide = (grad_ref[...].astype(F32) + norm_back(slide_norm, slide_inv, dnorm)).astype(BF)
    first[3].wait()
    dembed = mm(dslide, wp_ref[...]).astype(BF)
    finish(first[4:])
    normed, inv = normalize(feat_ref[...].astype(F32))
    finish(pieces)
    slide_ref[...] = mm(tmp_ref[...], order_matrix(), NT).astype(BF)
    dfeat = jnp.zeros(feat_ref.shape, F32)
    for c, (start, size) in enumerate(cuts):
        at = slice(start, start + size)
        waits[c][0].wait()
        dhidden = mm(dslide, fold_ref[:, at])
        dgate = (dhidden * a1_ref[:, at].astype(F32)).astype(BF)
        dup = (dhidden * a2_ref[:, at].astype(F32)).astype(BF)
        waits[c][1].wait()
        dfeat = dfeat + mm(dgate, wg_ref[at, :])
        waits[c][2].wait()
        dfeat = dfeat + mm(dup, wu_ref[at, :])
    out_ref[...] = (dembed.astype(F32) + norm_back(normed, inv, dfeat)).astype(BF)


def place_kernel(shift_ref, recv_ref, tab_ref, _after_hbm, y_ref, yt_ref, y2_ref):
    _, base, part = offsets(shift_ref)
    o2 = pl.multiple_of(base + 32 * part, 32)
    for d in range(4):
        tab = tab_ref[d : d + 1, :]
        onehot = jnp.where(iota((BLK, tab.shape[1]), 0) == tab, 1.0, 0.0).astype(BF)
        y = mm(onehot, recv_ref[:, 192 * d : 192 * d + 192])
        y = y.astype(BF)
        y_ref[d] = y
        yt_ref[d] = y.T
        y2_ref[32 * d : 32 * d + 32, :] = y_ref[d, pl.ds(o2, 32), :]


def score_rows(keys, queries_t, e_store, m_store):
    count, width = keys.shape[0], queries_t.shape[1]
    total = jnp.zeros((8, width), F32)
    step = 128
    for c in range(0, count, step):
        t = jnp.tanh(mm(keys[c : c + step], queries_t) * (SCALE / SOFT_CAP))
        e = jnp.exp2((SOFT_CAP * LOG2_E) * t)
        total = total + jnp.sum(e.reshape(step // 8, 8, width), axis=0)
        e_store(c, step, e.astype(BF))
        m_store(c, step, (e - e * (t * t)).astype(BF))
    return jnp.sum(total, axis=0, keepdims=True)


def forward_kernel(shift_ref, y_ref, yt_ref, e0_ref, m0_ref, e1_ref, m1_ref, u_ref, l_ref):
    o1 = pl.multiple_of(offsets(shift_ref)[0], 128)

    def block(d):
        def e_store(c, n, v):
            e0_ref[d, c : c + n, :] = v

        def m_store(c, n, v):
            m0_ref[d, c : c + n, :] = v

        l_ref[d] = score_rows(y_ref[d, :, 48:96], yt_ref[d, 0:48, :], e_store, m_store)
        u_ref[d] = mm(yt_ref[d, 96:144, :], e0_ref[d])

    for d in range(4):
        block(d)

    def e_store(c, n, v):
        e1_ref[c : c + n, :] = v

    def m_store(c, n, v):
        m1_ref[c : c + n, :] = v

    keys = jnp.concatenate([y_ref[d, pl.ds(o1, 128), 48:96] for d in range(4)], axis=0)
    queries = jnp.concatenate([yt_ref[d, 0:48, pl.ds(o1, 128)] for d in range(4)], axis=1)
    values = jnp.concatenate([yt_ref[d, 96:144, pl.ds(o1, 128)] for d in range(4)], axis=1)
    l1 = score_rows(keys, queries, e_store, m_store)
    u1 = mm(values, e1_ref[...])
    for d in range(4):
        u_ref[d, :, pl.ds(o1, 128)] += u1[:, 128 * d : 128 * d + 128]
        l_ref[d, :, pl.ds(o1, 128)] += l1[:, 128 * d : 128 * d + 128]


def turned(value, shift):
    return pltpu.roll(value, shift & 127, 1)


def wide_kernel(
    shift_ref,
    yt_ref,
    a0_ref,
    a1_ref,
    a2_ref,
    a3_ref,
    u_ref,
    l_ref,
    g0_ref,
    g1_ref,
    g2_ref,
    g3_ref,
    so0_hbm,
    so1_hbm,
    so2_hbm,
    so3_hbm,
    gs_ref,
    ds_ref,
    own_ref,
    send1_ref,
    send2_ref,
    send3_ref,
    dq_ref,
    e2_ref,
    m2_ref,
    usum_ref,
    lsum_ref,
    so_ref,
    so_sems,
):
    outs = []
    _, base, part = offsets(shift_ref)
    base = pl.multiple_of(base, 128)
    y2 = jnp.concatenate([a0_ref[...], a1_ref[...], a2_ref[...], a3_ref[...]], axis=0)
    keys, values = y2[:, 48:96], y2[:, 96:144]
    both_t = y2[:, 48:144].astype(F32).T.astype(BF)
    query_t = a0_ref[:, 0:48].astype(F32).T.astype(BF)

    def e_store(c, n, v):
        e2_ref[c : c + n, :] = v

    def m_store(c, n, v):
        m2_ref[c : c + n, :] = v

    l2 = score_rows(keys, query_t, e_store, m_store)
    u2 = mm(both_t[48:96], e2_ref[...])
    l2w = jnp.broadcast_to(l2, (8, 128))
    lane = iota((1, 128), 1) >> 5
    gs2 = jnp.zeros((48, 128), F32)
    ds2 = jnp.zeros((8, 128), F32)
    for d in range(4):
        here = lane == part
        shift = 32 * (part - d)
        usum_ref[...] = u_ref[d]
        lsum_ref[...] = l_ref[d]
        usum_ref[:, pl.ds(base, 128)] += jnp.where(here, turned(u2, shift), 0.0)
        lsum_ref[:, pl.ds(base, 128)] += jnp.where(here, turned(l2w, shift), 0.0)[0:1]
        inv = 1.0 / lsum_ref[...]
        att = usum_ref[...] * inv
        so_ref[d] = (yt_ref[d, 144:192, :].astype(F32) + att).astype(BF)
        so = (so0_hbm, so1_hbm, so2_hbm, so3_hbm)[d]
        outs += started([pltpu.make_async_copy(so_ref.at[d], so, so_sems.at[d])])
        grad_ref = (g0_ref, g1_ref, g2_ref, g3_ref)[d]
        gs = (grad_ref[...].astype(F32) * inv).astype(BF)
        gs_ref[d] = gs
        ds_ref[d] = jnp.sum(gs.astype(F32) * att, axis=0, keepdims=True)
        gs_wide = gs_ref[d, :, pl.ds(base, 128)].astype(F32)
        ds_wide = jnp.broadcast_to(ds_ref[d, :, pl.ds(base, 128)], (8, 128))
        gs2 = jnp.where(lane == d, turned(gs_wide, -shift), gs2)
        ds2 = jnp.where(lane == d, turned(ds_wide, -shift), ds2)
    gs2 = gs2.astype(BF)
    dp = mm(values, gs2)
    dscore = (m2_ref[...].astype(F32) * (dp - ds2[0:1])).astype(BF)
    dq_ref[...] = mm(both_t[0:48], dscore) * SCALE
    dk = mm(query_t, dscore, NT) * SCALE
    dv = mm(gs2, e2_ref[...], NT)
    dkv = jnp.concatenate([dk, dv], axis=0)
    own_ref[...] = dkv[:, 0:128]
    for e, send_ref in enumerate((send1_ref, send2_ref, send3_ref)):
        send_ref[...] = dkv[:, 128 * e + 128 : 128 * e + 256].astype(BF)
    finish(outs)


def dscores(values, gs, ds, m_load, store):
    dp = mm(values, gs)
    step = 64
    for c in range(0, dp.shape[0], step):
        store(c, step, (m_load(c, step).astype(F32) * (dp[c : c + step] - ds)).astype(BF))


def backward_kernel(
    shift_ref, y_ref, yt_ref, e0_ref, m0_ref, e1_ref, m1_ref, gs_ref, ds_ref, out_ref, tmp_ref
):
    o1 = pl.multiple_of(offsets(shift_ref)[0], 128)

    def store(c, n, v):
        tmp_ref[c : c + n, :] = v

    def block(d):
        gs = gs_ref[d]
        dscores(y_ref[d, :, 96:144], gs, ds_ref[d], lambda c, n: m0_ref[d, c : c + n, :], store)
        dscore = tmp_ref[...]
        out_ref[d, 0:48, :] = mm(yt_ref[d, 48:96, :], dscore) * SCALE
        out_ref[d, 48:96, :] = mm(yt_ref[d, 0:48, :], dscore, NT) * SCALE
        out_ref[d, 96:144, :] = mm(gs, e0_ref[d], NT)

    for d in range(4):
        block(d)
    values = jnp.concatenate([y_ref[d, pl.ds(o1, 128), 96:144] for d in range(4)], axis=0)
    queries = jnp.concatenate([yt_ref[d, 0:48, pl.ds(o1, 128)] for d in range(4)], axis=1)
    keys = jnp.concatenate([yt_ref[d, 48:96, pl.ds(o1, 128)] for d in range(4)], axis=1)
    gs = jnp.concatenate([gs_ref[d, :, pl.ds(o1, 128)] for d in range(4)], axis=1)
    ds = jnp.concatenate([ds_ref[d, :, pl.ds(o1, 128)] for d in range(4)], axis=1)
    dscores(values, gs, ds, lambda c, n: m1_ref[c : c + n, :], store)
    dscore = tmp_ref[...]
    dq = mm(keys, dscore) * SCALE
    dk = mm(queries, dscore, NT) * SCALE
    dv = mm(gs, e1_ref[...], NT)
    dall = jnp.concatenate([dq, dk, dv], axis=0)
    for d in range(4):
        out_ref[d, :, pl.ds(o1, 128)] += dall[:, 128 * d : 128 * d + 128]


def return_kernel(
    shift_ref,
    dall_ref,
    own_ref,
    dq_ref,
    r1_ref,
    r2_ref,
    r3_ref,
    g0_ref,
    g1_ref,
    g2_ref,
    g3_ref,
    tab_ref,
    out_hbm,
    sum_ref,
    out_ref,
    sems,
):
    _, base, part = offsets(shift_ref)
    base = pl.multiple_of(base, 128)
    dkv = (
        own_ref[...]
        + r1_ref[...].astype(F32)
        + r2_ref[...].astype(F32)
        + r3_ref[...].astype(F32)
    )
    extra = jnp.concatenate([dq_ref[...], dkv], axis=0)
    lane = iota((1, 128), 1) >> 5
    rows = tab_ref.shape[0]
    step = rows // 8
    outs, parts = [], []
    for d in range(4):
        grad_ref = (g0_ref, g1_ref, g2_ref, g3_ref)[d]
        sum_ref[...] = dall_ref[d]
        sum_ref[:, pl.ds(base, 128)] += jnp.where(
            lane == part, turned(extra, 32 * (part - d)), 0.0
        )
        parts.append(jnp.concatenate([sum_ref[...].astype(BF), grad_ref[...]], axis=0).T)
    for c in range(8):
        at = slice(step * c, step * c + step)
        for d in range(4):
            onehot = jnp.where(tab_ref[at, d : d + 1] == iota((step, BLK), 1), 1.0, 0.0)
            out_ref[at, 192 * d : 192 * d + 192] = mm(onehot.astype(BF), parts[d]).astype(BF)
        outs += started([pltpu.make_async_copy(out_ref.at[at, :], out_hbm.at[at, :], sems.at[c])])
    finish(outs)


def swap(value, distance, count):
    return lax.ppermute(value, "seq", [(i, i ^ distance) for i in range(count)])


def on_device(
    tile_features,
    gate_weight,
    up_weight,
    down_weight,
    input_projection_weight,
    query_key_value_weight,
    positions,
    dilation_shift,
    slide_output_gradient,
):
    seq_count = lax.axis_size("seq")
    device_count = seq_count * lax.axis_size("tile")
    rows, width = tile_features.shape
    ff = gate_weight.shape[1]
    slide_width = input_projection_weight.shape[1]
    all_pos = positions.reshape(device_count, rows)
    routed = ((8, 16 * SLOTS, slide_width), BF)
    weights = (gate_weight, up_weight, down_weight, input_projection_weight, query_key_value_weight)

    def exchange(block):
        return lax.all_to_all(
            block.reshape(device_count, SLOTS, slide_width),
            ("seq", "tile"),
            split_axis=0,
            concat_axis=0,
            tiled=True,
        ).reshape(device_count * SLOTS, slide_width)

    stored = [
        pltpu.VMEM((width, ff), BF),
        pltpu.VMEM((width, ff), BF),
        pltpu.VMEM((ff, width), BF),
        pltpu.VMEM((width, slide_width), BF),
        pltpu.VMEM((slide_width, 3 * slide_width), BF),
    ]
    dma = pltpu.SemaphoreType.DMA
    outgoing, x, a1, a2 = call(
        forward_mlp_kernel,
        [routed, ((rows, slide_width), BF), ((rows, ff), BF), ((rows, ff), BF)],
        [pltpu.VMEM((rows, width), BF), pltpu.VMEM((device_count, rows), I32)]
        + stored
        + [
            pltpu.VMEM((rows, slide_width), BF),
            pltpu.VMEM((rows, ff), BF),
            pltpu.VMEM((rows, ff), BF),
            pltpu.VMEM((HEADS // 2, 2 * rows, 192), BF),
            pltpu.VMEM((BLK, 2 * rows), BF),
            pltpu.VMEM((8, 16 * SLOTS, slide_width), BF),
            dma((18,)),
            dma((3 + HEADS // 2,)),
        ],
        n_hbm=7,
        n_hbm_out=4,
        limit=48,
    )(tile_features, all_pos, *weights)
    arrived = exchange(outgoing)
    turned_ff = turned_weights(weights[:2], x)

    grads = call(
        order_kernel,
        [((HD, BLK), BF)] * 4,
        [pltpu.VMEM((192, BLK), BF)],
    )(slide_output_gradient.T)
    grads = [grads[0]] + [swap(grads[d], d, seq_count) for d in range(1, 4)]
    slots = device_count * SLOTS
    table, table_col = call(
        table_kernel,
        [((8, slots), I32), ((slots, 8), I32)],
    )(all_pos)

    y, yt, y2 = call(
        place_kernel,
        [((4, BLK, 192), BF), ((4, 192, BLK), BF), ((128, 192), BF)],
        n_smem=1,
        n_hbm=1,
    )(dilation_shift, arrived, table, turned_ff[0])
    y2_in = [swap(y2, 4 * e, seq_count) for e in range(1, 4)]
    e0, m0, e1, m1, u, l = call(
        forward_kernel,
        [
            ((4, BLK, BLK), BF),
            ((4, BLK, BLK), BF),
            ((BLK, BLK), BF),
            ((BLK, BLK), BF),
            ((4, HD, BLK), F32),
            ((4, 1, BLK), F32),
        ],
        n_smem=1,
    )(dilation_shift, y, yt)
    *parts, gs, ds, own, send1, send2, send3, dq2 = call(
        wide_kernel,
        [((HD, BLK), BF)] * 4
        + [((4, HD, BLK), BF), ((4, 1, BLK), F32), ((96, 128), F32)]
        + [((96, 128), BF)] * 3
        + [((HD, 128), F32)],
        [
            pltpu.VMEM((BLK, 128), BF),
            pltpu.VMEM((BLK, 128), BF),
            pltpu.VMEM((HD, BLK), F32),
            pltpu.VMEM((1, BLK), F32),
            pltpu.VMEM((4, HD, BLK), BF),
            dma((4,)),
        ],
        n_smem=1,
        n_hbm_out=4,
    )(dilation_shift, yt, y2, *y2_in, u, l, *grads)
    back = [swap(send, 4 * e, seq_count) for e, send in ((1, send1), (2, send2), (3, send3))]
    (dall,) = call(
        backward_kernel,
        [((4, 144, BLK), F32)],
        [pltpu.VMEM((BLK, BLK), BF)],
        n_smem=1,
    )(dilation_shift, y, yt, e0, m0, e1, m1, gs, ds)
    (returning,) = call(
        return_kernel,
        [((slots, slide_width), BF)],
        [
            pltpu.VMEM((144, BLK), F32),
            pltpu.VMEM((slots, slide_width), BF),
            dma((8,)),
        ],
        n_smem=1,
        n_hbm_out=1,
        limit=6,
    )(dilation_shift, dall, own, dq2, *back, *grads, table_col)
    returned = exchange(returning)
    folded = call(
        fold_kernel,
        [
            ((slide_width, ff), BF),
            ((slide_width, width), BF),
            ((3 * slide_width, slide_width), BF),
        ],
        stored[2:]
        + [
            pltpu.VMEM((slide_width, ff), BF),
            pltpu.VMEM((slide_width, width), BF),
            pltpu.VMEM((3 * slide_width, slide_width), BF),
            dma((6,)),
            dma((6,)),
        ],
        n_hbm=4,
        n_hbm_out=3,
        limit=32,
    )(*weights[2:], returning)
    parts = [parts[0]] + [swap(parts[d], d, seq_count) for d in range(1, 4)]

    tile_grad, slide_out = call(
        backward_mlp_kernel,
        [((rows, width), BF), ((192, BLK), BF)],
        [
            pltpu.VMEM((device_count, rows), I32),
            pltpu.VMEM((rows, width), BF),
            pltpu.VMEM((rows, slide_width), BF),
            pltpu.VMEM((rows, ff), BF),
            pltpu.VMEM((rows, ff), BF),
        ]
        + [pltpu.VMEM(w.shape, BF) for w in (*turned_ff, *folded)]
        + [
            pltpu.VMEM((rows, 3 * slide_width), BF),
            pltpu.VMEM((rows, slide_width), BF),
            pltpu.VMEM((192, BLK), BF),
            dma((26,)),
        ],
        n_any=4,
        n_hbm=10,
        limit=48,
    )(
        returned.reshape(8, 16 * SLOTS, slide_width),
        *parts,
        all_pos,
        tile_features,
        x,
        a1,
        a2,
        *turned_ff,
        *folded,
    )
    return (slide_out.T, tile_grad)


def solution(mesh):
    placed = (P(("seq", "tile"), None), P(), P(), P(), P(), P(), P(), P(), P("seq", "tile"))
    return jax.shard_map(
        on_device,
        mesh=mesh,
        in_specs=placed,
        out_specs=(P("seq", "tile"), P(("seq", "tile"), None)),
        check_vma=False,
    )
```

```python
import jax
import jax.numpy as jnp
from jax import lax
from jax.experimental import pallas as pl
from jax.experimental.pallas import tpu as pltpu
from jax.sharding import PartitionSpec as P

HEADS = 16
HD = 48
EPSILON = 1e-06
SOFT_CAP = 50.0
SCALE = HD**-0.5
LOG2_E = 1.4426950408889634
BLK = 512
SLOTS = 8
BF = jnp.bfloat16
F32 = jnp.float32
I32 = jnp.int32

NN = (((1,), (0,)), ((), ()))
NT = (((1,), (1,)), ((), ()))
TN = (((0,), (0,)), ((), ()))


def mm(a, b, dims=NN):
    return lax.dot_general(a, b, dims, preferred_element_type=F32)


def iota(shape, dim):
    return lax.broadcasted_iota(I32, shape, dim)


def class_order(row):
    return (row & 3) * 128 + ((row >> 2) & 3) * 32 + (row >> 4)


def order_matrix():
    return jnp.where(class_order(iota((BLK, BLK), 0)) == iota((BLK, BLK), 1), 1.0, 0.0).astype(BF)


def normalize(values):
    centred = values - jnp.mean(values, axis=-1, keepdims=True)
    inv_std = lax.rsqrt(jnp.mean(centred * centred, axis=-1, keepdims=True) + EPSILON)
    return (centred * inv_std, inv_std)


def norm_back(normed, inv_std, grads):
    mean_grad = jnp.mean(grads, axis=-1, keepdims=True)
    mean_cross = jnp.mean(grads * normed, axis=-1, keepdims=True)
    return (grads - mean_grad - normed * mean_cross) * inv_std


def call(kernel, outs, scratch=(), n_smem=0, n_any=0, n_hbm=0, n_hbm_out=0, limit=4):
    def run(*args):
        n_vmem = len(args) - n_smem - n_any - n_hbm
        specs = [pl.BlockSpec(memory_space=pltpu.SMEM)] * n_smem
        specs += [pl.BlockSpec(memory_space=pltpu.VMEM)] * n_vmem
        specs += [pl.BlockSpec(memory_space=pl.ANY)] * n_any
        specs += [pl.BlockSpec(memory_space=pltpu.HBM)] * n_hbm
        out_specs = [pl.BlockSpec(memory_space=pltpu.HBM)] * n_hbm_out
        out_specs += [pl.BlockSpec(memory_space=pltpu.VMEM)] * (len(outs) - n_hbm_out)
        shapes = [pltpu.HBM(shape, kind) for shape, kind in outs[:n_hbm_out]]
        shapes += [jax.ShapeDtypeStruct(shape, kind) for shape, kind in outs[n_hbm_out:]]
        cut = len(args) - n_hbm
        held = [pltpu.with_memory_space_constraint(x, pltpu.HBM) for x in args[cut:]]
        return pl.pallas_call(
            kernel,
            out_shape=shapes,
            in_specs=specs,
            out_specs=out_specs,
            scratch_shapes=list(scratch),
            compiler_params=pltpu.CompilerParams(vmem_limit_bytes=limit * 1024 * 1024),
        )(*args[:cut], *held)

    return run


def started(copies):
    for copy in copies:
        copy.start()
    return copies


def finish(copies):
    for copy in copies:
        copy.wait()


def order_kernel(grad_ref, g0_ref, g1_ref, g2_ref, g3_ref, tmp_ref):
    j = lax.axis_index("seq") & 3
    tmp_ref[...] = mm(grad_ref[...], order_matrix()).astype(BF)
    for d, out_ref in enumerate((g0_ref, g1_ref, g2_ref, g3_ref)):
        out_ref[...] = tmp_ref[pl.ds(pl.multiple_of((j ^ d) * HD, 16), HD), :]


def offsets(shift_ref):
    head = 4 * lax.axis_index("tile") + (lax.axis_index("seq") & 3)
    o1 = shift_ref[0, head]
    o2 = shift_ref[1, head]
    return (o1 * 128, (o2 & 3) * 128, o2 >> 2)


def table_kernel(pos_ref, row_ref, col_ref):
    s = lax.axis_index("seq")
    pos = pos_ref[...].T
    n = pos.shape[0]
    block = pos >> 9
    seat = class_order(pos & (BLK - 1)) + 1
    lower = jnp.where(iota((n, n), 1) < iota((n, n), 0), 1.0, 0.0).astype(BF)
    high, low = [], []
    for d in range(4):
        owned = block == (s ^ d)
        rank = mm(lower, jnp.where(owned, 1.0, 0.0).astype(BF)).astype(I32)
        held = jnp.where(owned, seat, 0)
        for k in range(SLOTS):
            found = jnp.sum(jnp.where(rank == k, held, 0), axis=0, keepdims=True)
            high.append(found >> 4)
            low.append(found & 15)
    digits = jnp.concatenate(high + low, axis=0).astype(F32).astype(BF)
    lanes = n * SLOTS
    spread = jnp.where(iota((n, lanes), 0) == iota((n, lanes), 1) >> 3, 1.0, 0.0).astype(BF)
    wide = mm(digits, spread)
    wide = 16.0 * wide[0:32] + wide[32:64]
    own = iota((8, lanes), 0) == (iota((8, lanes), 1) & 7)
    rows = [
        jnp.sum(jnp.where(own, wide[8 * d : 8 * d + 8], 0.0), axis=0, keepdims=True)
        for d in range(4)
    ]
    table = jnp.concatenate(rows + rows, axis=0) - 1.0
    row_ref[...] = table.astype(I32)
    col_ref[...] = table.T.astype(I32)


def forward_mlp_kernel(
    feat_hbm,
    pos_hbm,
    gate_hbm,
    up_hbm,
    down_hbm,
    proj_hbm,
    qkvw_hbm,
    out_hbm,
    x_hbm,
    a1_hbm,
    a2_hbm,
    feat_ref,
    pos_ref,
    wg_ref,
    wu_ref,
    wd_ref,
    wp_ref,
    wq_ref,
    x_ref,
    a1_ref,
    a2_ref,
    heads_ref,
    picker_ref,
    tmp_ref,
    sems,
    out_sems,
):
    ff = gate_hbm.shape[1]
    width = HEADS * HD
    step = 512
    chunks = ff // step
    first = started(
        [
            pltpu.make_async_copy(feat_hbm, feat_ref, sems.at[3 * chunks]),
            pltpu.make_async_copy(pos_hbm, pos_ref, sems.at[3 * chunks + 1]),
        ]
    )
    waits = []
    for c in range(chunks):
        at = pl.ds(c * step, step)
        waits.append(
            started(
                [
                    pltpu.make_async_copy(gate_hbm.at[:, at], wg_ref.at[:, at], sems.at[3 * c]),
                    pltpu.make_async_copy(up_hbm.at[:, at], wu_ref.at[:, at], sems.at[3 * c + 1]),
                    pltpu.make_async_copy(down_hbm.at[at, :], wd_ref.at[at, :], sems.at[3 * c + 2]),
                ]
            )
        )
    last = started(
        [
            pltpu.make_async_copy(proj_hbm, wp_ref, sems.at[3 * chunks + 2]),
        ]
        + [
            pltpu.make_async_copy(qkvw_hbm.at[:, at], wq_ref.at[:, at], sems.at[3 * chunks + 3 + i])
            for i, at in enumerate(pl.ds(width * part, width) for part in range(3))
        ]
    )
    finish(first)

    me = lax.axis_index("seq") * 4 + lax.axis_index("tile")
    brow = pos_ref[pl.ds(me, 1), :] >> 9
    n = brow.shape[1]
    bcol = jnp.broadcast_to(brow, (n, n)).T
    before = iota((n, n), 0) < iota((n, n), 1)
    rank = jnp.sum(jnp.where((bcol == brow) & before, 1, 0), axis=0, keepdims=True)
    code = brow * SLOTS + rank
    code = jnp.concatenate([code, code + 4096], axis=1)
    seat = iota((BLK, 2 * n), 0)
    want = (((seat >> 4) & 7) * 4 + (seat >> 7)) * SLOTS + (seat & 7) + 4096 * ((seat >> 3) & 1)
    picker_ref[...] = jnp.where(code == want, 1.0, 0.0).astype(BF)

    feats = feat_ref[...].astype(F32)
    normed = normalize(feats)[0].astype(BF)
    total = feats
    outs = []
    for c in range(chunks):
        at = slice(c * step, c * step + step)
        waits[c][0].wait()
        gate = mm(normed, wg_ref[:, at])
        waits[c][1].wait()
        up = mm(normed, wu_ref[:, at])
        sig = jax.nn.sigmoid(gate)
        silu = gate * sig
        hidden = (silu * up).astype(BF)
        a1_ref[:, at] = (up * (sig + silu * (1.0 - sig))).astype(BF)
        a2_ref[:, at] = silu.astype(BF)
        waits[c][2].wait()
        total = total + mm(hidden, wd_ref[at, :])
    outs += started(
        [
            pltpu.make_async_copy(a1_ref, a1_hbm, out_sems.at[0]),
            pltpu.make_async_copy(a2_ref, a2_hbm, out_sems.at[1]),
        ]
    )
    last[0].wait()
    x = mm(total.astype(BF), wp_ref[...]).astype(BF)
    x_ref[...] = x
    outs += started([pltpu.make_async_copy(x_ref, x_hbm, out_sems.at[2])])
    slide_norm = normalize(x.astype(F32))[0].astype(BF)

    def deal(values, part):
        for h in range(HEADS):
            t, j = h // 4, h % 4
            heads_ref[2 * j + t // 2, n * (t % 2) : n * (t % 2) + n, HD * part : HD * part + HD] = (
                values[:, h * HD : h * HD + HD]
            )

    deal(x, 3)
    for part in range(3):
        last[1 + part].wait()
        at = slice(width * part, width * part + width)
        deal(mm(slide_norm, wq_ref[:, at]).astype(BF), part)
    for pair in range(HEADS // 2):
        j = pair // 2
        rows = mm(picker_ref[...], heads_ref[pair]).astype(BF)
        at = slice(16 * pair, 16 * pair + 16)
        for block in range(4):
            lane = (j ^ block) * 192
            tmp_ref[:, at, lane : lane + 192] = rows[128 * block : 128 * block + 128].reshape(
                8, 16, 192
            )
        outs += started(
            [
                pltpu.make_async_copy(
                    tmp_ref.at[:, at, :], out_hbm.at[:, at, :], out_sems.at[3 + pair]
                )
            ]
        )
    finish(outs)


BAND = 256


def band(i):
    return pl.ds(pl.multiple_of(i * BAND, BAND), BAND)


def turn_kernel(
    gate_hbm, up_hbm, _after_hbm, gatet_hbm, upt_hbm, in_ref, out_ref, sems, out_sems
):
    count = gate_hbm.shape[0] // BAND
    given, made = (gate_hbm, up_hbm), (gatet_hbm, upt_hbm)

    def load(which, i):
        return pltpu.make_async_copy(
            given[which].at[band(i), :], in_ref.at[which, band(i), :], sems.at[which, i]
        )

    def store(which, i):
        return pltpu.make_async_copy(
            out_ref.at[which, :, band(i)], made[which].at[:, band(i)], out_sems.at[which, i]
        )

    for which in range(2):
        for i in range(count):
            load(which, i).start()
    for which in range(2):

        def step(i, carry):
            load(which, i).wait()
            out_ref[which, :, band(i)] = in_ref[which, band(i), :].T
            store(which, i).start()
            return carry

        lax.fori_loop(0, count, step, 0)
    for which in range(2):
        for i in range(count):
            store(which, i).wait()


def fold_kernel(
    down_hbm,
    proj_hbm,
    qkvw_hbm,
    _after_hbm,
    fold_hbm,
    projt_hbm,
    qkvt_hbm,
    wd_ref,
    wp_ref,
    wq_ref,
    fold_ref,
    projt_ref,
    qkvt_ref,
    sems,
    out_sems,
):
    count = down_hbm.shape[0] // BAND
    loads = started(
        [
            pltpu.make_async_copy(qkvw_hbm, wq_ref, sems.at[count]),
            pltpu.make_async_copy(proj_hbm, wp_ref, sems.at[count + 1]),
        ]
    )

    def load(i):
        return pltpu.make_async_copy(down_hbm.at[band(i), :], wd_ref.at[band(i), :], sems.at[i])

    def store(i):
        return pltpu.make_async_copy(
            fold_ref.at[:, band(i)], fold_hbm.at[:, band(i)], out_sems.at[i]
        )

    def turn(from_ref, to_ref):
        def step(i, carry):
            to_ref[:, band(i)] = from_ref[band(i), :].T
            return carry

        lax.fori_loop(0, from_ref.shape[0] // BAND, step, 0)

    for i in range(count):
        load(i).start()
    loads[0].wait()
    turn(wq_ref, qkvt_ref)
    outs = started([pltpu.make_async_copy(qkvt_ref, qkvt_hbm, out_sems.at[count])])
    loads[1].wait()
    turn(wp_ref, projt_ref)
    outs += started([pltpu.make_async_copy(projt_ref, projt_hbm, out_sems.at[count + 1])])

    def step(i, carry):
        load(i).wait()
        fold_ref[:, band(i)] = mm(wd_ref[band(i), :], wp_ref[...]).astype(BF).T
        store(i).start()
        return carry

    lax.fori_loop(0, count, step, 0)
    for i in range(count):
        store(i).wait()
    finish(outs)


def backward_mlp_kernel(
    ret_ref,
    s0_any,
    s1_any,
    s2_any,
    s3_any,
    pos_hbm,
    feat_hbm,
    x_hbm,
    a1_hbm,
    a2_hbm,
    gate_hbm,
    up_hbm,
    fold_hbm,
    proj_hbm,
    qkvw_hbm,
    out_ref,
    slide_ref,
    pos_ref,
    feat_ref,
    x_ref,
    a1_ref,
    a2_ref,
    wg_ref,
    wu_ref,
    fold_ref,
    wp_ref,
    wq_ref,
    dqkv_ref,
    grad_ref,
    tmp_ref,
    sems,
):
    ff = gate_hbm.shape[0]
    cuts = [(at, 512) for at in range(0, ff - 512, 512)] + [(ff - 512, 256), (ff - 256, 256)]
    chunks = len(cuts)
    pairs = (
        (pos_hbm, pos_ref),
        (x_hbm, x_ref),
        (qkvw_hbm, wq_ref),
        (proj_hbm, wp_ref),
        (a1_hbm, a1_ref),
        (a2_hbm, a2_ref),
        (feat_hbm, feat_ref),
    )
    first = started(
        [
            pltpu.make_async_copy(here, there, sems.at[3 * chunks + i])
            for i, (here, there) in enumerate(pairs)
        ]
    )
    waits = []
    for c, (start, size) in enumerate(cuts):
        at = pl.ds(start, size)
        waits.append(
            started(
                [
                    pltpu.make_async_copy(fold_hbm.at[:, at], fold_ref.at[:, at], sems.at[3 * c]),
                    pltpu.make_async_copy(gate_hbm.at[at, :], wg_ref.at[at, :], sems.at[3 * c + 1]),
                    pltpu.make_async_copy(up_hbm.at[at, :], wu_ref.at[at, :], sems.at[3 * c + 2]),
                ]
            )
        )
    j = lax.axis_index("seq") & 3
    pieces = started(
        [
            pltpu.make_async_copy(
                so,
                tmp_ref.at[pl.ds(pl.multiple_of((j ^ d) * HD, 16), HD), :],
                sems.at[3 * chunks + len(pairs) + d],
            )
            for d, so in enumerate((s0_any, s1_any, s2_any, s3_any))
        ]
    )
    first[0].wait()
    me = lax.axis_index("seq") * 4 + lax.axis_index("tile")
    brow = pos_ref[pl.ds(me, 1), :] >> 9
    n = brow.shape[1]
    bcol = jnp.broadcast_to(brow, (n, n)).T
    before = iota((n, n), 1) < iota((n, n), 0)
    rank = jnp.sum(jnp.where((bcol == brow) & before, 1, 0), axis=1, keepdims=True)
    code = bcol[:, 0:1] * SLOTS + rank
    code = jnp.concatenate([code, code + 4096], axis=0)
    seat = iota((2 * n, BLK), 1)
    want = (((seat >> 4) & 7) * 4 + (seat >> 7)) * SLOTS + (seat & 7) + 4096 * ((seat >> 3) & 1)
    picker = jnp.where(code == want, 1.0, 0.0).astype(BF)
    width = HEADS * HD
    for pair in range(HEADS // 2):
        j, t = pair // 2, 2 * (pair % 2)
        tile = ret_ref[:, 16 * pair : 16 * pair + 16, :].reshape(128, 768)
        stacked = jnp.concatenate(
            [tile[:, (j ^ b) * 192 : (j ^ b) * 192 + 192] for b in range(4)], axis=0
        )
        got = mm(picker, stacked).astype(BF)
        for tp in range(2):
            h = 4 * (t + tp) + j
            mine = got[n * tp : n * tp + n]
            for part in range(3):
                dqkv_ref[:, part * width + h * HD : part * width + h * HD + HD] = mine[
                    :, HD * part : HD * part + HD
                ]
            grad_ref[:, h * HD : h * HD + HD] = mine[:, 144:192]
    first[1].wait()
    slide_norm, slide_inv = normalize(x_ref[...].astype(F32))
    first[2].wait()
    dnorm = mm(dqkv_ref[...], wq_ref[...])
    dslide = (grad_ref[...].astype(F32) + norm_back(slide_norm, slide_inv, dnorm)).astype(BF)
    first[3].wait()
    dembed = mm(dslide, wp_ref[...]).astype(BF)
    finish(first[4:])
    normed, inv = normalize(feat_ref[...].astype(F32))
    finish(pieces)
    slide_ref[...] = mm(tmp_ref[...], order_matrix(), NT).astype(BF)
    dfeat = jnp.zeros(feat_ref.shape, F32)
    for c, (start, size) in enumerate(cuts):
        at = slice(start, start + size)
        waits[c][0].wait()
        dhidden = mm(dslide, fold_ref[:, at])
        dgate = (dhidden * a1_ref[:, at].astype(F32)).astype(BF)
        dup = (dhidden * a2_ref[:, at].astype(F32)).astype(BF)
        waits[c][1].wait()
        dfeat = dfeat + mm(dgate, wg_ref[at, :])
        waits[c][2].wait()
        dfeat = dfeat + mm(dup, wu_ref[at, :])
    out_ref[...] = (dembed.astype(F32) + norm_back(normed, inv, dfeat)).astype(BF)


def place_kernel(shift_ref, recv_ref, tab_ref, _after_hbm, y_ref, yt_ref, y2_ref):
    _, base, part = offsets(shift_ref)
    o2 = pl.multiple_of(base + 32 * part, 32)
    for d in range(4):
        tab = tab_ref[d : d + 1, :]
        onehot = jnp.where(iota((BLK, tab.shape[1]), 0) == tab, 1.0, 0.0).astype(BF)
        y = mm(onehot, recv_ref[:, 192 * d : 192 * d + 192])
        y = y.astype(BF)
        y_ref[d] = y
        yt_ref[d] = y.T
        y2_ref[32 * d : 32 * d + 32, :] = y_ref[d, pl.ds(o2, 32), :]


def score_rows(keys, queries_t, e_store, m_store):
    count, width = keys.shape[0], queries_t.shape[1]
    total = jnp.zeros((8, width), F32)
    step = 128
    for c in range(0, count, step):
        t = jnp.tanh(mm(keys[c : c + step], queries_t) * (SCALE / SOFT_CAP))
        e = jnp.exp2((SOFT_CAP * LOG2_E) * t)
        total = total + jnp.sum(e.reshape(step // 8, 8, width), axis=0)
        e_store(c, step, e.astype(BF))
        m_store(c, step, (e - e * (t * t)).astype(BF))
    return jnp.sum(total, axis=0, keepdims=True)


def forward_kernel(shift_ref, y_ref, yt_ref, e0_ref, m0_ref, e1_ref, m1_ref, u_ref, l_ref):
    o1 = pl.multiple_of(offsets(shift_ref)[0], 128)

    def block(d):
        def e_store(c, n, v):
            e0_ref[d, c : c + n, :] = v

        def m_store(c, n, v):
            m0_ref[d, c : c + n, :] = v

        l_ref[d] = score_rows(y_ref[d, :, 48:96], yt_ref[d, 0:48, :], e_store, m_store)
        u_ref[d] = mm(yt_ref[d, 96:144, :], e0_ref[d])

    for d in range(4):
        block(d)

    def e_store(c, n, v):
        e1_ref[c : c + n, :] = v

    def m_store(c, n, v):
        m1_ref[c : c + n, :] = v

    keys = jnp.concatenate([y_ref[d, pl.ds(o1, 128), 48:96] for d in range(4)], axis=0)
    queries = jnp.concatenate([yt_ref[d, 0:48, pl.ds(o1, 128)] for d in range(4)], axis=1)
    values = jnp.concatenate([yt_ref[d, 96:144, pl.ds(o1, 128)] for d in range(4)], axis=1)
    l1 = score_rows(keys, queries, e_store, m_store)
    u1 = mm(values, e1_ref[...])
    for d in range(4):
        u_ref[d, :, pl.ds(o1, 128)] += u1[:, 128 * d : 128 * d + 128]
        l_ref[d, :, pl.ds(o1, 128)] += l1[:, 128 * d : 128 * d + 128]


def turned(value, shift):
    return pltpu.roll(value, shift & 127, 1)


def wide_kernel(
    shift_ref,
    yt_ref,
    a0_ref,
    a1_ref,
    a2_ref,
    a3_ref,
    u_ref,
    l_ref,
    g0_ref,
    g1_ref,
    g2_ref,
    g3_ref,
    so0_hbm,
    so1_hbm,
    so2_hbm,
    so3_hbm,
    gs_ref,
    ds_ref,
    own_ref,
    send1_ref,
    send2_ref,
    send3_ref,
    dq_ref,
    e2_ref,
    m2_ref,
    usum_ref,
    lsum_ref,
    so_ref,
    so_sems,
):
    outs = []
    _, base, part = offsets(shift_ref)
    base = pl.multiple_of(base, 128)
    y2 = jnp.concatenate([a0_ref[...], a1_ref[...], a2_ref[...], a3_ref[...]], axis=0)
    keys, values = y2[:, 48:96], y2[:, 96:144]
    both_t = y2[:, 48:144].astype(F32).T.astype(BF)
    query_t = a0_ref[:, 0:48].astype(F32).T.astype(BF)

    def e_store(c, n, v):
        e2_ref[c : c + n, :] = v

    def m_store(c, n, v):
        m2_ref[c : c + n, :] = v

    l2 = score_rows(keys, query_t, e_store, m_store)
    u2 = mm(both_t[48:96], e2_ref[...])
    l2w = jnp.broadcast_to(l2, (8, 128))
    lane = iota((1, 128), 1) >> 5
    gs2 = jnp.zeros((48, 128), F32)
    ds2 = jnp.zeros((8, 128), F32)
    for d in range(4):
        here = lane == part
        shift = 32 * (part - d)
        usum_ref[...] = u_ref[d]
        lsum_ref[...] = l_ref[d]
        usum_ref[:, pl.ds(base, 128)] += jnp.where(here, turned(u2, shift), 0.0)
        lsum_ref[:, pl.ds(base, 128)] += jnp.where(here, turned(l2w, shift), 0.0)[0:1]
        inv = 1.0 / lsum_ref[...]
        att = usum_ref[...] * inv
        so_ref[d] = (yt_ref[d, 144:192, :].astype(F32) + att).astype(BF)
        so = (so0_hbm, so1_hbm, so2_hbm, so3_hbm)[d]
        outs += started([pltpu.make_async_copy(so_ref.at[d], so, so_sems.at[d])])
        grad_ref = (g0_ref, g1_ref, g2_ref, g3_ref)[d]
        gs = (grad_ref[...].astype(F32) * inv).astype(BF)
        gs_ref[d] = gs
        ds_ref[d] = jnp.sum(gs.astype(F32) * att, axis=0, keepdims=True)
        gs_wide = gs_ref[d, :, pl.ds(base, 128)].astype(F32)
        ds_wide = jnp.broadcast_to(ds_ref[d, :, pl.ds(base, 128)], (8, 128))
        gs2 = jnp.where(lane == d, turned(gs_wide, -shift), gs2)
        ds2 = jnp.where(lane == d, turned(ds_wide, -shift), ds2)
    gs2 = gs2.astype(BF)
    dp = mm(values, gs2)
    dscore = (m2_ref[...].astype(F32) * (dp - ds2[0:1])).astype(BF)
    dq_ref[...] = mm(both_t[0:48], dscore) * SCALE
    dk = mm(query_t, dscore, NT) * SCALE
    dv = mm(gs2, e2_ref[...], NT)
    dkv = jnp.concatenate([dk, dv], axis=0)
    own_ref[...] = dkv[:, 0:128]
    for e, send_ref in enumerate((send1_ref, send2_ref, send3_ref)):
        send_ref[...] = dkv[:, 128 * e + 128 : 128 * e + 256].astype(BF)
    finish(outs)


def dscores(values, gs, ds, m_load, store):
    dp = mm(values, gs)
    step = 64
    for c in range(0, dp.shape[0], step):
        store(c, step, (m_load(c, step).astype(F32) * (dp[c : c + step] - ds)).astype(BF))


def backward_kernel(
    shift_ref, y_ref, yt_ref, e0_ref, m0_ref, e1_ref, m1_ref, gs_ref, ds_ref, out_ref, tmp_ref
):
    o1 = pl.multiple_of(offsets(shift_ref)[0], 128)

    def store(c, n, v):
        tmp_ref[c : c + n, :] = v

    def block(d):
        gs = gs_ref[d]
        dscores(y_ref[d, :, 96:144], gs, ds_ref[d], lambda c, n: m0_ref[d, c : c + n, :], store)
        dscore = tmp_ref[...]
        out_ref[d, 0:48, :] = mm(yt_ref[d, 48:96, :], dscore) * SCALE
        out_ref[d, 48:96, :] = mm(yt_ref[d, 0:48, :], dscore, NT) * SCALE
        out_ref[d, 96:144, :] = mm(gs, e0_ref[d], NT)

    for d in range(4):
        block(d)
    values = jnp.concatenate([y_ref[d, pl.ds(o1, 128), 96:144] for d in range(4)], axis=0)
    queries = jnp.concatenate([yt_ref[d, 0:48, pl.ds(o1, 128)] for d in range(4)], axis=1)
    keys = jnp.concatenate([yt_ref[d, 48:96, pl.ds(o1, 128)] for d in range(4)], axis=1)
    gs = jnp.concatenate([gs_ref[d, :, pl.ds(o1, 128)] for d in range(4)], axis=1)
    ds = jnp.concatenate([ds_ref[d, :, pl.ds(o1, 128)] for d in range(4)], axis=1)
    dscores(values, gs, ds, lambda c, n: m1_ref[c : c + n, :], store)
    dscore = tmp_ref[...]
    dq = mm(keys, dscore) * SCALE
    dk = mm(queries, dscore, NT) * SCALE
    dv = mm(gs, e1_ref[...], NT)
    dall = jnp.concatenate([dq, dk, dv], axis=0)
    for d in range(4):
        out_ref[d, :, pl.ds(o1, 128)] += dall[:, 128 * d : 128 * d + 128]


def return_kernel(
    shift_ref,
    dall_ref,
    own_ref,
    dq_ref,
    r1_ref,
    r2_ref,
    r3_ref,
    g0_ref,
    g1_ref,
    g2_ref,
    g3_ref,
    tab_ref,
    out_hbm,
    sum_ref,
    out_ref,
    sems,
):
    _, base, part = offsets(shift_ref)
    base = pl.multiple_of(base, 128)
    dkv = (
        own_ref[...]
        + r1_ref[...].astype(F32)
        + r2_ref[...].astype(F32)
        + r3_ref[...].astype(F32)
    )
    extra = jnp.concatenate([dq_ref[...], dkv], axis=0)
    lane = iota((1, 128), 1) >> 5
    rows = tab_ref.shape[0]
    step = rows // 4
    outs, parts = [], []
    for d in range(4):
        grad_ref = (g0_ref, g1_ref, g2_ref, g3_ref)[d]
        sum_ref[...] = dall_ref[d]
        sum_ref[:, pl.ds(base, 128)] += jnp.where(
            lane == part, turned(extra, 32 * (part - d)), 0.0
        )
        parts.append(jnp.concatenate([sum_ref[...].astype(BF), grad_ref[...]], axis=0).T)
    for c in range(4):
        at = slice(step * c, step * c + step)
        for d in range(4):
            onehot = jnp.where(tab_ref[at, d : d + 1] == iota((step, BLK), 1), 1.0, 0.0)
            out_ref[at, 192 * d : 192 * d + 192] = mm(onehot.astype(BF), parts[d]).astype(BF)
        outs += started([pltpu.make_async_copy(out_ref.at[at, :], out_hbm.at[at, :], sems.at[c])])
    finish(outs)


def swap(value, distance, count):
    return lax.ppermute(value, "seq", [(i, i ^ distance) for i in range(count)])


def on_device(
    tile_features,
    gate_weight,
    up_weight,
    down_weight,
    input_projection_weight,
    query_key_value_weight,
    positions,
    dilation_shift,
    slide_output_gradient,
):
    seq_count = lax.axis_size("seq")
    device_count = seq_count * lax.axis_size("tile")
    rows, width = tile_features.shape
    ff = gate_weight.shape[1]
    slide_width = input_projection_weight.shape[1]
    all_pos = positions.reshape(device_count, rows)
    routed = ((8, 16 * SLOTS, slide_width), BF)
    weights = (gate_weight, up_weight, down_weight, input_projection_weight, query_key_value_weight)

    def exchange(block):
        return lax.all_to_all(
            block.reshape(device_count, SLOTS, slide_width),
            ("seq", "tile"),
            split_axis=0,
            concat_axis=0,
            tiled=True,
        ).reshape(device_count * SLOTS, slide_width)

    stored = [
        pltpu.VMEM((width, ff), BF),
        pltpu.VMEM((width, ff), BF),
        pltpu.VMEM((ff, width), BF),
        pltpu.VMEM((width, slide_width), BF),
        pltpu.VMEM((slide_width, 3 * slide_width), BF),
    ]
    dma = pltpu.SemaphoreType.DMA
    outgoing, x, a1, a2 = call(
        forward_mlp_kernel,
        [routed, ((rows, slide_width), BF), ((rows, ff), BF), ((rows, ff), BF)],
        [pltpu.VMEM((rows, width), BF), pltpu.VMEM((device_count, rows), I32)]
        + stored
        + [
            pltpu.VMEM((rows, slide_width), BF),
            pltpu.VMEM((rows, ff), BF),
            pltpu.VMEM((rows, ff), BF),
            pltpu.VMEM((HEADS // 2, 2 * rows, 192), BF),
            pltpu.VMEM((BLK, 2 * rows), BF),
            pltpu.VMEM((8, 16 * SLOTS, slide_width), BF),
            dma((18,)),
            dma((3 + HEADS // 2,)),
        ],
        n_hbm=7,
        n_hbm_out=4,
        limit=48,
    )(tile_features, all_pos, *weights)
    arrived = exchange(outgoing)
    turned_ff = call(
        turn_kernel,
        [((ff, width), BF)] * 2,
        [
            pltpu.VMEM((2, width, ff), BF),
            pltpu.VMEM((2, ff, width), BF),
            dma((2, width // BAND)),
            dma((2, width // BAND)),
        ],
        n_hbm=3,
        n_hbm_out=2,
        limit=32,
    )(gate_weight, up_weight, x)

    grads = call(
        order_kernel,
        [((HD, BLK), BF)] * 4,
        [pltpu.VMEM((192, BLK), BF)],
    )(slide_output_gradient.T)
    grads = [grads[0]] + [swap(grads[d], d, seq_count) for d in range(1, 4)]
    slots = device_count * SLOTS
    table, table_col = call(
        table_kernel,
        [((8, slots), I32), ((slots, 8), I32)],
    )(all_pos)

    y, yt, y2 = call(
        place_kernel,
        [((4, BLK, 192), BF), ((4, 192, BLK), BF), ((128, 192), BF)],
        n_smem=1,
        n_hbm=1,
    )(dilation_shift, arrived, table, turned_ff[0])
    y2_in = [swap(y2, 4 * e, seq_count) for e in range(1, 4)]
    e0, m0, e1, m1, u, l = call(
        forward_kernel,
        [
            ((4, BLK, BLK), BF),
            ((4, BLK, BLK), BF),
            ((BLK, BLK), BF),
            ((BLK, BLK), BF),
            ((4, HD, BLK), F32),
            ((4, 1, BLK), F32),
        ],
        n_smem=1,
    )(dilation_shift, y, yt)
    *parts, gs, ds, own, send1, send2, send3, dq2 = call(
        wide_kernel,
        [((HD, BLK), BF)] * 4
        + [((4, HD, BLK), BF), ((4, 1, BLK), F32), ((96, 128), F32)]
        + [((96, 128), BF)] * 3
        + [((HD, 128), F32)],
        [
            pltpu.VMEM((BLK, 128), BF),
            pltpu.VMEM((BLK, 128), BF),
            pltpu.VMEM((HD, BLK), F32),
            pltpu.VMEM((1, BLK), F32),
            pltpu.VMEM((4, HD, BLK), BF),
            dma((4,)),
        ],
        n_smem=1,
        n_hbm_out=4,
    )(dilation_shift, yt, y2, *y2_in, u, l, *grads)
    back = [swap(send, 4 * e, seq_count) for e, send in ((1, send1), (2, send2), (3, send3))]
    (dall,) = call(
        backward_kernel,
        [((4, 144, BLK), F32)],
        [pltpu.VMEM((BLK, BLK), BF)],
        n_smem=1,
    )(dilation_shift, y, yt, e0, m0, e1, m1, gs, ds)
    (returning,) = call(
        return_kernel,
        [((slots, slide_width), BF)],
        [
            pltpu.VMEM((144, BLK), F32),
            pltpu.VMEM((slots, slide_width), BF),
            dma((4,)),
        ],
        n_smem=1,
        n_hbm_out=1,
        limit=6,
    )(dilation_shift, dall, own, dq2, *back, *grads, table_col)
    returned = exchange(returning)
    folded = call(
        fold_kernel,
        [
            ((slide_width, ff), BF),
            ((slide_width, width), BF),
            ((3 * slide_width, slide_width), BF),
        ],
        stored[2:]
        + [
            pltpu.VMEM((slide_width, ff), BF),
            pltpu.VMEM((slide_width, width), BF),
            pltpu.VMEM((3 * slide_width, slide_width), BF),
            dma((ff // BAND + 2,)),
            dma((ff // BAND + 2,)),
        ],
        n_hbm=4,
        n_hbm_out=3,
        limit=32,
    )(*weights[2:], returning)
    parts = [parts[0]] + [swap(parts[d], d, seq_count) for d in range(1, 4)]

    tile_grad, slide_out = call(
        backward_mlp_kernel,
        [((rows, width), BF), ((192, BLK), BF)],
        [
            pltpu.VMEM((device_count, rows), I32),
            pltpu.VMEM((rows, width), BF),
            pltpu.VMEM((rows, slide_width), BF),
            pltpu.VMEM((rows, ff), BF),
            pltpu.VMEM((rows, ff), BF),
        ]
        + [pltpu.VMEM(w.shape, BF) for w in (*turned_ff, *folded)]
        + [
            pltpu.VMEM((rows, 3 * slide_width), BF),
            pltpu.VMEM((rows, slide_width), BF),
            pltpu.VMEM((192, BLK), BF),
            dma((26,)),
        ],
        n_any=4,
        n_hbm=10,
        limit=48,
    )(
        returned.reshape(8, 16 * SLOTS, slide_width),
        *parts,
        all_pos,
        tile_features,
        x,
        a1,
        a2,
        *turned_ff,
        *folded,
    )
    return (slide_out.T, tile_grad)


def solution(mesh):
    placed = (P(("seq", "tile"), None), P(), P(), P(), P(), P(), P(), P(), P("seq", "tile"))
    return jax.shard_map(
        on_device,
        mesh=mesh,
        in_specs=placed,
        out_specs=(P("seq", "tile"), P(("seq", "tile"), None)),
        check_vma=False,
    )
```

```python
import jax
import jax.numpy as jnp
from jax import lax
from jax.experimental import pallas as pl
from jax.experimental.pallas import tpu as pltpu
from jax.sharding import PartitionSpec as P

HEADS = 16
HD = 48
EPSILON = 1e-06
SOFT_CAP = 50.0
SCALE = HD**-0.5
LOG2_E = 1.4426950408889634
BLK = 512
SLOTS = 8
BF = jnp.bfloat16
F32 = jnp.float32
I32 = jnp.int32

NN = (((1,), (0,)), ((), ()))
NT = (((1,), (1,)), ((), ()))
TN = (((0,), (0,)), ((), ()))


def mm(a, b, dims=NN):
    return lax.dot_general(a, b, dims, preferred_element_type=F32)


def iota(shape, dim):
    return lax.broadcasted_iota(I32, shape, dim)


def class_order(row):
    return (row & 3) * 128 + ((row >> 2) & 3) * 32 + (row >> 4)


def order_matrix():
    return jnp.where(class_order(iota((BLK, BLK), 0)) == iota((BLK, BLK), 1), 1.0, 0.0).astype(BF)


def normalize(values):
    centred = values - jnp.mean(values, axis=-1, keepdims=True)
    inv_std = lax.rsqrt(jnp.mean(centred * centred, axis=-1, keepdims=True) + EPSILON)
    return (centred * inv_std, inv_std)


def norm_back(normed, inv_std, grads):
    mean_grad = jnp.mean(grads, axis=-1, keepdims=True)
    mean_cross = jnp.mean(grads * normed, axis=-1, keepdims=True)
    return (grads - mean_grad - normed * mean_cross) * inv_std


def call(
    kernel, outs, scratch=(), n_smem=0, n_any=0, n_hbm=0, n_hbm_out=0, limit=4, aliases=None
):
    def run(*args):
        n_vmem = len(args) - n_smem - n_any - n_hbm
        specs = [pl.BlockSpec(memory_space=pltpu.SMEM)] * n_smem
        specs += [pl.BlockSpec(memory_space=pltpu.VMEM)] * n_vmem
        specs += [pl.BlockSpec(memory_space=pl.ANY)] * n_any
        specs += [pl.BlockSpec(memory_space=pltpu.HBM)] * n_hbm
        out_specs = [pl.BlockSpec(memory_space=pltpu.HBM)] * n_hbm_out
        out_specs += [pl.BlockSpec(memory_space=pltpu.VMEM)] * (len(outs) - n_hbm_out)
        shapes = [pltpu.HBM(shape, kind) for shape, kind in outs[:n_hbm_out]]
        shapes += [jax.ShapeDtypeStruct(shape, kind) for shape, kind in outs[n_hbm_out:]]
        cut = len(args) - n_hbm
        held = [pltpu.with_memory_space_constraint(x, pltpu.HBM) for x in args[cut:]]
        return pl.pallas_call(
            kernel,
            out_shape=shapes,
            in_specs=specs,
            out_specs=out_specs,
            scratch_shapes=list(scratch),
            input_output_aliases=aliases or {},
            compiler_params=pltpu.CompilerParams(vmem_limit_bytes=limit * 1024 * 1024),
        )(*args[:cut], *held)

    return run


def started(copies):
    for copy in copies:
        copy.start()
    return copies


def finish(copies):
    for copy in copies:
        copy.wait()


def order_kernel(grad_ref, _after_hbm, g0_ref, g1_ref, g2_ref, g3_ref, tmp_ref):
    j = lax.axis_index("seq") & 3
    tmp_ref[...] = mm(grad_ref[...], order_matrix()).astype(BF)
    for d, out_ref in enumerate((g0_ref, g1_ref, g2_ref, g3_ref)):
        out_ref[...] = tmp_ref[pl.ds(pl.multiple_of((j ^ d) * HD, 16), HD), :]


def offsets(shift_ref):
    head = 4 * lax.axis_index("tile") + (lax.axis_index("seq") & 3)
    o1 = shift_ref[0, head]
    o2 = shift_ref[1, head]
    return (o1 * 128, (o2 & 3) * 128, o2 >> 2)


def table_kernel(pos_ref, row_ref, col_ref):
    s = lax.axis_index("seq")
    pos = pos_ref[...].T
    n = pos.shape[0]
    block = pos >> 9
    seat = class_order(pos & (BLK - 1)) + 1
    lower = jnp.where(iota((n, n), 1) < iota((n, n), 0), 1.0, 0.0).astype(BF)
    high, low = [], []
    for d in range(4):
        owned = block == (s ^ d)
        rank = mm(lower, jnp.where(owned, 1.0, 0.0).astype(BF)).astype(I32)
        held = jnp.where(owned, seat, 0)
        for k in range(SLOTS):
            found = jnp.sum(jnp.where(rank == k, held, 0), axis=0, keepdims=True)
            high.append(found >> 4)
            low.append(found & 15)
    digits = jnp.concatenate(high + low, axis=0).astype(F32).astype(BF)
    lanes = n * SLOTS
    spread = jnp.where(iota((n, lanes), 0) == iota((n, lanes), 1) >> 3, 1.0, 0.0).astype(BF)
    wide = mm(digits, spread)
    wide = 16.0 * wide[0:32] + wide[32:64]
    own = iota((8, lanes), 0) == (iota((8, lanes), 1) & 7)
    rows = [
        jnp.sum(jnp.where(own, wide[8 * d : 8 * d + 8], 0.0), axis=0, keepdims=True)
        for d in range(4)
    ]
    table = jnp.concatenate(rows + rows, axis=0) - 1.0
    row_ref[...] = table.astype(I32)
    col_ref[...] = table.T.astype(I32)


def forward_mlp_kernel(
    feat_hbm,
    pos_hbm,
    gate_hbm,
    up_hbm,
    down_hbm,
    proj_hbm,
    qkvw_hbm,
    out_hbm,
    x_hbm,
    feat_ref,
    pos_ref,
    wg_ref,
    wu_ref,
    wd_ref,
    wp_ref,
    wq_ref,
    x_ref,
    heads_ref,
    picker_ref,
    tmp_ref,
    sems,
    out_sems,
):
    ff = gate_hbm.shape[1]
    width = HEADS * HD
    step = 512
    chunks = ff // step
    first = started(
        [
            pltpu.make_async_copy(feat_hbm, feat_ref, sems.at[3 * chunks]),
            pltpu.make_async_copy(pos_hbm, pos_ref, sems.at[3 * chunks + 1]),
        ]
    )
    waits = []
    for c in range(chunks):
        at = pl.ds(c * step, step)
        waits.append(
            started(
                [
                    pltpu.make_async_copy(gate_hbm.at[:, at], wg_ref.at[:, at], sems.at[3 * c]),
                    pltpu.make_async_copy(up_hbm.at[:, at], wu_ref.at[:, at], sems.at[3 * c + 1]),
                    pltpu.make_async_copy(down_hbm.at[at, :], wd_ref.at[at, :], sems.at[3 * c + 2]),
                ]
            )
        )
    last = started(
        [
            pltpu.make_async_copy(proj_hbm, wp_ref, sems.at[3 * chunks + 2]),
        ]
        + [
            pltpu.make_async_copy(qkvw_hbm.at[:, at], wq_ref.at[:, at], sems.at[3 * chunks + 3 + i])
            for i, at in enumerate(pl.ds(width * part, width) for part in range(3))
        ]
    )
    finish(first)

    me = lax.axis_index("seq") * 4 + lax.axis_index("tile")
    brow = pos_ref[pl.ds(me, 1), :] >> 9
    n = brow.shape[1]
    bcol = jnp.broadcast_to(brow, (n, n)).T
    before = iota((n, n), 0) < iota((n, n), 1)
    rank = jnp.sum(jnp.where((bcol == brow) & before, 1, 0), axis=0, keepdims=True)
    code = brow * SLOTS + rank
    code = jnp.concatenate([code, code + 4096], axis=1)
    seat = iota((BLK, 2 * n), 0)
    want = (((seat >> 4) & 7) * 4 + (seat >> 7)) * SLOTS + (seat & 7) + 4096 * ((seat >> 3) & 1)
    picker_ref[...] = jnp.where(code == want, 1.0, 0.0).astype(BF)

    feats = feat_ref[...].astype(F32)
    normed = normalize(feats)[0].astype(BF)
    total = feats
    outs = []
    for c in range(chunks):
        at = slice(c * step, c * step + step)
        waits[c][0].wait()
        gate = mm(normed, wg_ref[:, at])
        waits[c][1].wait()
        up = mm(normed, wu_ref[:, at])
        sig = jax.nn.sigmoid(gate)
        silu = gate * sig
        hidden = (silu * up).astype(BF)
        waits[c][2].wait()
        total = total + mm(hidden, wd_ref[at, :])
    last[0].wait()
    x = mm(total.astype(BF), wp_ref[...]).astype(BF)
    x_ref[...] = x
    outs += started([pltpu.make_async_copy(x_ref, x_hbm, out_sems.at[0])])
    slide_norm = normalize(x.astype(F32))[0].astype(BF)

    def deal(values, part):
        for h in range(HEADS):
            t, j = h // 4, h % 4
            heads_ref[2 * j + t // 2, n * (t % 2) : n * (t % 2) + n, HD * part : HD * part + HD] = (
                values[:, h * HD : h * HD + HD]
            )

    deal(x, 3)
    for part in range(3):
        last[1 + part].wait()
        at = slice(width * part, width * part + width)
        deal(mm(slide_norm, wq_ref[:, at]).astype(BF), part)
    for pair in range(HEADS // 2):
        j = pair // 2
        rows = mm(picker_ref[...], heads_ref[pair]).astype(BF)
        at = slice(16 * pair, 16 * pair + 16)
        for block in range(4):
            lane = (j ^ block) * 192
            tmp_ref[:, at, lane : lane + 192] = rows[128 * block : 128 * block + 128].reshape(
                8, 16, 192
            )
        outs += started(
            [
                pltpu.make_async_copy(
                    tmp_ref.at[:, at, :], out_hbm.at[:, at, :], out_sems.at[1 + pair]
                )
            ]
        )
    finish(outs)


BAND = 256


def band(i):
    return pl.ds(pl.multiple_of(i * BAND, BAND), BAND)


def turn_kernel(
    feat_hbm,
    gate_hbm,
    up_hbm,
    _after_hbm,
    gatet_hbm,
    upt_hbm,
    a1_hbm,
    a2_hbm,
    feat_ref,
    in_ref,
    out_ref,
    a1_ref,
    a2_ref,
    sems,
    out_sems,
    own_sems,
):
    count = gate_hbm.shape[0] // BAND
    given, made = (gate_hbm, up_hbm), (gatet_hbm, upt_hbm)

    def load(which, i):
        return pltpu.make_async_copy(
            given[which].at[band(i), :], in_ref.at[which, band(i), :], sems.at[which, i]
        )

    def store(which, i):
        return pltpu.make_async_copy(
            out_ref.at[which, :, band(i)], made[which].at[:, band(i)], out_sems.at[which, i]
        )

    feats = started([pltpu.make_async_copy(feat_hbm, feat_ref, own_sems.at[0])])
    for which in range(2):
        for i in range(count):
            load(which, i).start()
    finish(feats)
    normed = normalize(feat_ref[...].astype(F32))[0].astype(BF)
    for which in range(2):

        def step(i, carry):
            load(which, i).wait()
            out_ref[which, :, band(i)] = in_ref[which, band(i), :].T
            store(which, i).start()
            return carry

        lax.fori_loop(0, count, step, 0)
    size = 512
    for c in range(0, gate_hbm.shape[1], size):
        at = slice(c, c + size)
        gate = mm(normed, in_ref[0, :, at])
        up = mm(normed, in_ref[1, :, at])
        sig = jax.nn.sigmoid(gate)
        silu = gate * sig
        a1_ref[:, at] = (up * (sig + silu * (1.0 - sig))).astype(BF)
        a2_ref[:, at] = silu.astype(BF)
    outs = started(
        [
            pltpu.make_async_copy(a1_ref, a1_hbm, own_sems.at[1]),
            pltpu.make_async_copy(a2_ref, a2_hbm, own_sems.at[2]),
        ]
    )
    finish(outs)
    for which in range(2):
        for i in range(count):
            store(which, i).wait()


def fold_kernel(
    down_hbm,
    proj_hbm,
    qkvw_hbm,
    _after_hbm,
    _in1_hbm,
    _in2_hbm,
    _in3_hbm,
    fold_hbm,
    projt_hbm,
    qkvt_hbm,
    _out1_hbm,
    _out2_hbm,
    _out3_hbm,
    wd_ref,
    wp_ref,
    wq_ref,
    fold_ref,
    projt_ref,
    qkvt_ref,
    sems,
    out_sems,
):
    count = down_hbm.shape[0] // BAND
    loads = started(
        [
            pltpu.make_async_copy(qkvw_hbm, wq_ref, sems.at[count]),
            pltpu.make_async_copy(proj_hbm, wp_ref, sems.at[count + 1]),
        ]
    )

    def load(i):
        return pltpu.make_async_copy(down_hbm.at[band(i), :], wd_ref.at[band(i), :], sems.at[i])

    def store(i):
        return pltpu.make_async_copy(
            fold_ref.at[:, band(i)], fold_hbm.at[:, band(i)], out_sems.at[i]
        )

    def turn(from_ref, to_ref):
        def step(i, carry):
            to_ref[:, band(i)] = from_ref[band(i), :].T
            return carry

        lax.fori_loop(0, from_ref.shape[0] // BAND, step, 0)

    for i in range(count):
        load(i).start()
    loads[0].wait()
    turn(wq_ref, qkvt_ref)
    outs = started([pltpu.make_async_copy(qkvt_ref, qkvt_hbm, out_sems.at[count])])
    loads[1].wait()
    turn(wp_ref, projt_ref)
    outs += started([pltpu.make_async_copy(projt_ref, projt_hbm, out_sems.at[count + 1])])

    def step(i, carry):
        load(i).wait()
        fold_ref[:, band(i)] = mm(wd_ref[band(i), :], wp_ref[...]).astype(BF).T
        store(i).start()
        return carry

    lax.fori_loop(0, count, step, 0)
    for i in range(count):
        store(i).wait()
    finish(outs)


def backward_mlp_kernel(
    ret_ref,
    s0_any,
    s1_any,
    s2_any,
    s3_any,
    pos_hbm,
    feat_hbm,
    x_hbm,
    a1_hbm,
    a2_hbm,
    gate_hbm,
    up_hbm,
    fold_hbm,
    proj_hbm,
    qkvw_hbm,
    out_ref,
    slide_ref,
    pos_ref,
    feat_ref,
    x_ref,
    a1_ref,
    a2_ref,
    wg_ref,
    wu_ref,
    fold_ref,
    wp_ref,
    wq_ref,
    dqkv_ref,
    grad_ref,
    tmp_ref,
    sems,
):
    ff = gate_hbm.shape[0]
    cuts = [(at, 512) for at in range(0, ff - 512, 512)] + [(ff - 512, 256), (ff - 256, 256)]
    chunks = len(cuts)
    pairs = (
        (pos_hbm, pos_ref),
        (x_hbm, x_ref),
        (qkvw_hbm, wq_ref),
        (proj_hbm, wp_ref),
        (a1_hbm, a1_ref),
        (a2_hbm, a2_ref),
        (feat_hbm, feat_ref),
    )
    first = started(
        [
            pltpu.make_async_copy(here, there, sems.at[3 * chunks + i])
            for i, (here, there) in enumerate(pairs)
        ]
    )
    waits = []
    for c, (start, size) in enumerate(cuts):
        at = pl.ds(start, size)
        waits.append(
            started(
                [
                    pltpu.make_async_copy(fold_hbm.at[:, at], fold_ref.at[:, at], sems.at[3 * c]),
                    pltpu.make_async_copy(gate_hbm.at[at, :], wg_ref.at[at, :], sems.at[3 * c + 1]),
                    pltpu.make_async_copy(up_hbm.at[at, :], wu_ref.at[at, :], sems.at[3 * c + 2]),
                ]
            )
        )
    j = lax.axis_index("seq") & 3
    pieces = started(
        [
            pltpu.make_async_copy(
                so,
                tmp_ref.at[pl.ds(pl.multiple_of((j ^ d) * HD, 16), HD), :],
                sems.at[3 * chunks + len(pairs) + d],
            )
            for d, so in enumerate((s0_any, s1_any, s2_any, s3_any))
        ]
    )
    first[0].wait()
    me = lax.axis_index("seq") * 4 + lax.axis_index("tile")
    brow = pos_ref[pl.ds(me, 1), :] >> 9
    n = brow.shape[1]
    bcol = jnp.broadcast_to(brow, (n, n)).T
    before = iota((n, n), 1) < iota((n, n), 0)
    rank = jnp.sum(jnp.where((bcol == brow) & before, 1, 0), axis=1, keepdims=True)
    code = bcol[:, 0:1] * SLOTS + rank
    code = jnp.concatenate([code, code + 4096], axis=0)
    seat = iota((2 * n, BLK), 1)
    want = (((seat >> 4) & 7) * 4 + (seat >> 7)) * SLOTS + (seat & 7) + 4096 * ((seat >> 3) & 1)
    picker = jnp.where(code == want, 1.0, 0.0).astype(BF)
    width = HEADS * HD
    for pair in range(HEADS // 2):
        j, t = pair // 2, 2 * (pair % 2)
        tile = ret_ref[:, 16 * pair : 16 * pair + 16, :].reshape(128, 768)
        stacked = jnp.concatenate(
            [tile[:, (j ^ b) * 192 : (j ^ b) * 192 + 192] for b in range(4)], axis=0
        )
        got = mm(picker, stacked).astype(BF)
        for tp in range(2):
            h = 4 * (t + tp) + j
            mine = got[n * tp : n * tp + n]
            for part in range(3):
                dqkv_ref[:, part * width + h * HD : part * width + h * HD + HD] = mine[
                    :, HD * part : HD * part + HD
                ]
            grad_ref[:, h * HD : h * HD + HD] = mine[:, 144:192]
    first[1].wait()
    slide_norm, slide_inv = normalize(x_ref[...].astype(F32))
    first[2].wait()
    dnorm = mm(dqkv_ref[...], wq_ref[...])
    dslide = (grad_ref[...].astype(F32) + norm_back(slide_norm, slide_inv, dnorm)).astype(BF)
    first[3].wait()
    dembed = mm(dslide, wp_ref[...]).astype(BF)
    finish(first[4:])
    normed, inv = normalize(feat_ref[...].astype(F32))
    finish(pieces)
    slide_ref[...] = mm(tmp_ref[...], order_matrix(), NT).astype(BF)
    dfeat = jnp.zeros(feat_ref.shape, F32)
    for c, (start, size) in enumerate(cuts):
        at = slice(start, start + size)
        waits[c][0].wait()
        dhidden = mm(dslide, fold_ref[:, at])
        dgate = (dhidden * a1_ref[:, at].astype(F32)).astype(BF)
        dup = (dhidden * a2_ref[:, at].astype(F32)).astype(BF)
        waits[c][1].wait()
        dfeat = dfeat + mm(dgate, wg_ref[at, :])
        waits[c][2].wait()
        dfeat = dfeat + mm(dup, wu_ref[at, :])
    out_ref[...] = (dembed.astype(F32) + norm_back(normed, inv, dfeat)).astype(BF)


def place_kernel(shift_ref, recv_ref, tab_ref, _after_hbm, y_ref, yt_ref, y2_ref):
    _, base, part = offsets(shift_ref)
    o2 = pl.multiple_of(base + 32 * part, 32)
    for d in range(4):
        tab = tab_ref[d : d + 1, :]
        onehot = jnp.where(iota((BLK, tab.shape[1]), 0) == tab, 1.0, 0.0).astype(BF)
        y = mm(onehot, recv_ref[:, 192 * d : 192 * d + 192])
        y = y.astype(BF)
        y_ref[d] = y
        yt_ref[d] = y.T
        y2_ref[32 * d : 32 * d + 32, :] = y_ref[d, pl.ds(o2, 32), :]


def score_rows(keys, queries_t, e_store, m_store):
    count, width = keys.shape[0], queries_t.shape[1]
    total = jnp.zeros((8, width), F32)
    step = 128
    for c in range(0, count, step):
        t = jnp.tanh(mm(keys[c : c + step], queries_t) * (SCALE / SOFT_CAP))
        e = jnp.exp2((SOFT_CAP * LOG2_E) * t)
        total = total + jnp.sum(e.reshape(step // 8, 8, width), axis=0)
        e_store(c, step, e.astype(BF))
        m_store(c, step, (e - e * (t * t)).astype(BF))
    return jnp.sum(total, axis=0, keepdims=True)


def forward_kernel(shift_ref, y_ref, yt_ref, e0_ref, m0_ref, e1_ref, m1_ref, u_ref, l_ref):
    o1 = pl.multiple_of(offsets(shift_ref)[0], 128)

    def block(d):
        def e_store(c, n, v):
            e0_ref[d, c : c + n, :] = v

        def m_store(c, n, v):
            m0_ref[d, c : c + n, :] = v

        l_ref[d] = score_rows(y_ref[d, :, 48:96], yt_ref[d, 0:48, :], e_store, m_store)
        u_ref[d] = mm(yt_ref[d, 96:144, :], e0_ref[d])

    for d in range(4):
        block(d)

    def e_store(c, n, v):
        e1_ref[c : c + n, :] = v

    def m_store(c, n, v):
        m1_ref[c : c + n, :] = v

    keys = jnp.concatenate([y_ref[d, pl.ds(o1, 128), 48:96] for d in range(4)], axis=0)
    queries = jnp.concatenate([yt_ref[d, 0:48, pl.ds(o1, 128)] for d in range(4)], axis=1)
    values = jnp.concatenate([yt_ref[d, 96:144, pl.ds(o1, 128)] for d in range(4)], axis=1)
    l1 = score_rows(keys, queries, e_store, m_store)
    u1 = mm(values, e1_ref[...])
    for d in range(4):
        u_ref[d, :, pl.ds(o1, 128)] += u1[:, 128 * d : 128 * d + 128]
        l_ref[d, :, pl.ds(o1, 128)] += l1[:, 128 * d : 128 * d + 128]


def turned(value, shift):
    return pltpu.roll(value, shift & 127, 1)


def wide_kernel(
    shift_ref,
    yt_ref,
    a0_ref,
    a1_ref,
    a2_ref,
    a3_ref,
    u_ref,
    l_ref,
    g0_ref,
    g1_ref,
    g2_ref,
    g3_ref,
    so0_hbm,
    so1_hbm,
    so2_hbm,
    so3_hbm,
    gs_ref,
    ds_ref,
    own_ref,
    send1_ref,
    send2_ref,
    send3_ref,
    dq_ref,
    e2_ref,
    m2_ref,
    usum_ref,
    lsum_ref,
    so_ref,
    so_sems,
):
    outs = []
    _, base, part = offsets(shift_ref)
    base = pl.multiple_of(base, 128)
    y2 = jnp.concatenate([a0_ref[...], a1_ref[...], a2_ref[...], a3_ref[...]], axis=0)
    keys, values = y2[:, 48:96], y2[:, 96:144]
    both_t = y2[:, 48:144].astype(F32).T.astype(BF)
    query_t = a0_ref[:, 0:48].astype(F32).T.astype(BF)

    def e_store(c, n, v):
        e2_ref[c : c + n, :] = v

    def m_store(c, n, v):
        m2_ref[c : c + n, :] = v

    l2 = score_rows(keys, query_t, e_store, m_store)
    u2 = mm(both_t[48:96], e2_ref[...])
    l2w = jnp.broadcast_to(l2, (8, 128))
    lane = iota((1, 128), 1) >> 5
    gs2 = jnp.zeros((48, 128), F32)
    ds2 = jnp.zeros((8, 128), F32)
    for d in range(4):
        here = lane == part
        shift = 32 * (part - d)
        usum_ref[...] = u_ref[d]
        lsum_ref[...] = l_ref[d]
        usum_ref[:, pl.ds(base, 128)] += jnp.where(here, turned(u2, shift), 0.0)
        lsum_ref[:, pl.ds(base, 128)] += jnp.where(here, turned(l2w, shift), 0.0)[0:1]
        inv = 1.0 / lsum_ref[...]
        att = usum_ref[...] * inv
        so_ref[d] = (yt_ref[d, 144:192, :].astype(F32) + att).astype(BF)
        so = (so0_hbm, so1_hbm, so2_hbm, so3_hbm)[d]
        outs += started([pltpu.make_async_copy(so_ref.at[d], so, so_sems.at[d])])
        grad_ref = (g0_ref, g1_ref, g2_ref, g3_ref)[d]
        gs = (grad_ref[...].astype(F32) * inv).astype(BF)
        gs_ref[d] = gs
        ds_ref[d] = jnp.sum(gs.astype(F32) * att, axis=0, keepdims=True)
        gs_wide = gs_ref[d, :, pl.ds(base, 128)].astype(F32)
        ds_wide = jnp.broadcast_to(ds_ref[d, :, pl.ds(base, 128)], (8, 128))
        gs2 = jnp.where(lane == d, turned(gs_wide, -shift), gs2)
        ds2 = jnp.where(lane == d, turned(ds_wide, -shift), ds2)
    gs2 = gs2.astype(BF)
    dp = mm(values, gs2)
    dscore = (m2_ref[...].astype(F32) * (dp - ds2[0:1])).astype(BF)
    dq_ref[...] = mm(both_t[0:48], dscore) * SCALE
    dk = mm(query_t, dscore, NT) * SCALE
    dv = mm(gs2, e2_ref[...], NT)
    dkv = jnp.concatenate([dk, dv], axis=0)
    own_ref[...] = dkv[:, 0:128]
    for e, send_ref in enumerate((send1_ref, send2_ref, send3_ref)):
        send_ref[...] = dkv[:, 128 * e + 128 : 128 * e + 256].astype(BF)
    finish(outs)


def dscores(values, gs, ds, m_load, store):
    dp = mm(values, gs)
    step = 64
    for c in range(0, dp.shape[0], step):
        store(c, step, (m_load(c, step).astype(F32) * (dp[c : c + step] - ds)).astype(BF))


def backward_kernel(
    shift_ref, y_ref, yt_ref, e0_ref, m0_ref, e1_ref, m1_ref, gs_ref, ds_ref, out_ref, tmp_ref
):
    o1 = pl.multiple_of(offsets(shift_ref)[0], 128)

    def store(c, n, v):
        tmp_ref[c : c + n, :] = v

    def block(d):
        gs = gs_ref[d]
        dscores(y_ref[d, :, 96:144], gs, ds_ref[d], lambda c, n: m0_ref[d, c : c + n, :], store)
        dscore = tmp_ref[...]
        out_ref[d, 0:48, :] = mm(yt_ref[d, 48:96, :], dscore) * SCALE
        out_ref[d, 48:96, :] = mm(yt_ref[d, 0:48, :], dscore, NT) * SCALE
        out_ref[d, 96:144, :] = mm(gs, e0_ref[d], NT)

    for d in range(4):
        block(d)
    values = jnp.concatenate([y_ref[d, pl.ds(o1, 128), 96:144] for d in range(4)], axis=0)
    queries = jnp.concatenate([yt_ref[d, 0:48, pl.ds(o1, 128)] for d in range(4)], axis=1)
    keys = jnp.concatenate([yt_ref[d, 48:96, pl.ds(o1, 128)] for d in range(4)], axis=1)
    gs = jnp.concatenate([gs_ref[d, :, pl.ds(o1, 128)] for d in range(4)], axis=1)
    ds = jnp.concatenate([ds_ref[d, :, pl.ds(o1, 128)] for d in range(4)], axis=1)
    dscores(values, gs, ds, lambda c, n: m1_ref[c : c + n, :], store)
    dscore = tmp_ref[...]
    dq = mm(keys, dscore) * SCALE
    dk = mm(queries, dscore, NT) * SCALE
    dv = mm(gs, e1_ref[...], NT)
    dall = jnp.concatenate([dq, dk, dv], axis=0)
    for d in range(4):
        out_ref[d, :, pl.ds(o1, 128)] += dall[:, 128 * d : 128 * d + 128]


def return_kernel(
    shift_ref,
    dall_ref,
    own_ref,
    dq_ref,
    r1_ref,
    r2_ref,
    r3_ref,
    g0_ref,
    g1_ref,
    g2_ref,
    g3_ref,
    tab_ref,
    out_hbm,
    sum_ref,
    out_ref,
    sems,
):
    _, base, part = offsets(shift_ref)
    base = pl.multiple_of(base, 128)
    dkv = (
        own_ref[...]
        + r1_ref[...].astype(F32)
        + r2_ref[...].astype(F32)
        + r3_ref[...].astype(F32)
    )
    extra = jnp.concatenate([dq_ref[...], dkv], axis=0)
    lane = iota((1, 128), 1) >> 5
    rows = tab_ref.shape[0]
    step = rows // 4
    outs, parts = [], []
    for d in range(4):
        grad_ref = (g0_ref, g1_ref, g2_ref, g3_ref)[d]
        sum_ref[...] = dall_ref[d]
        sum_ref[:, pl.ds(base, 128)] += jnp.where(
            lane == part, turned(extra, 32 * (part - d)), 0.0
        )
        parts.append(jnp.concatenate([sum_ref[...].astype(BF), grad_ref[...]], axis=0).T)
    for c in range(4):
        at = slice(step * c, step * c + step)
        for d in range(4):
            onehot = jnp.where(tab_ref[at, d : d + 1] == iota((step, BLK), 1), 1.0, 0.0)
            out_ref[at, 192 * d : 192 * d + 192] = mm(onehot.astype(BF), parts[d]).astype(BF)
        outs += started([pltpu.make_async_copy(out_ref.at[at, :], out_hbm.at[at, :], sems.at[c])])
    finish(outs)


def swap(value, distance, count):
    return lax.ppermute(value, "seq", [(i, i ^ distance) for i in range(count)])


def on_device(
    tile_features,
    gate_weight,
    up_weight,
    down_weight,
    input_projection_weight,
    query_key_value_weight,
    positions,
    dilation_shift,
    slide_output_gradient,
):
    seq_count = lax.axis_size("seq")
    device_count = seq_count * lax.axis_size("tile")
    rows, width = tile_features.shape
    ff = gate_weight.shape[1]
    slide_width = input_projection_weight.shape[1]
    all_pos = positions.reshape(device_count, rows)
    routed = ((8, 16 * SLOTS, slide_width), BF)
    weights = (gate_weight, up_weight, down_weight, input_projection_weight, query_key_value_weight)

    def exchange(block):
        return lax.all_to_all(
            block.reshape(device_count, SLOTS, slide_width),
            ("seq", "tile"),
            split_axis=0,
            concat_axis=0,
            tiled=True,
        ).reshape(device_count * SLOTS, slide_width)

    stored = [
        pltpu.VMEM((width, ff), BF),
        pltpu.VMEM((width, ff), BF),
        pltpu.VMEM((ff, width), BF),
        pltpu.VMEM((width, slide_width), BF),
        pltpu.VMEM((slide_width, 3 * slide_width), BF),
    ]
    dma = pltpu.SemaphoreType.DMA
    outgoing, x = call(
        forward_mlp_kernel,
        [routed, ((rows, slide_width), BF)],
        [pltpu.VMEM((rows, width), BF), pltpu.VMEM((device_count, rows), I32)]
        + stored
        + [
            pltpu.VMEM((rows, slide_width), BF),
            pltpu.VMEM((HEADS // 2, 2 * rows, 192), BF),
            pltpu.VMEM((BLK, 2 * rows), BF),
            pltpu.VMEM((8, 16 * SLOTS, slide_width), BF),
            dma((18,)),
            dma((1 + HEADS // 2,)),
        ],
        n_hbm=7,
        n_hbm_out=2,
        limit=48,
    )(tile_features, all_pos, *weights)
    arrived = exchange(outgoing)
    *turned_ff, a1, a2 = call(
        turn_kernel,
        [((ff, width), BF)] * 2 + [((rows, ff), BF)] * 2,
        [
            pltpu.VMEM((rows, width), BF),
            pltpu.VMEM((2, width, ff), BF),
            pltpu.VMEM((2, ff, width), BF),
            pltpu.VMEM((rows, ff), BF),
            pltpu.VMEM((rows, ff), BF),
            dma((2, width // BAND)),
            dma((2, width // BAND)),
            dma((3,)),
        ],
        n_hbm=4,
        n_hbm_out=4,
        limit=36,
    )(tile_features, gate_weight, up_weight, x)

    grads = call(
        order_kernel,
        [((HD, BLK), BF)] * 4,
        [pltpu.VMEM((192, BLK), BF)],
        n_hbm=1,
    )(slide_output_gradient.T, turned_ff[0])
    grads = [grads[0]] + [swap(grads[d], d, seq_count) for d in range(1, 4)]
    slots = device_count * SLOTS
    table, table_col = call(
        table_kernel,
        [((8, slots), I32), ((slots, 8), I32)],
    )(all_pos)

    y, yt, y2 = call(
        place_kernel,
        [((4, BLK, 192), BF), ((4, 192, BLK), BF), ((128, 192), BF)],
        n_smem=1,
        n_hbm=1,
    )(dilation_shift, arrived, table, turned_ff[0])
    y2_in = [swap(y2, 4 * e, seq_count) for e in range(1, 4)]
    e0, m0, e1, m1, u, l = call(
        forward_kernel,
        [
            ((4, BLK, BLK), BF),
            ((4, BLK, BLK), BF),
            ((BLK, BLK), BF),
            ((BLK, BLK), BF),
            ((4, HD, BLK), F32),
            ((4, 1, BLK), F32),
        ],
        n_smem=1,
    )(dilation_shift, y, yt)
    *parts, gs, ds, own, send1, send2, send3, dq2 = call(
        wide_kernel,
        [((HD, BLK), BF)] * 4
        + [((4, HD, BLK), BF), ((4, 1, BLK), F32), ((96, 128), F32)]
        + [((96, 128), BF)] * 3
        + [((HD, 128), F32)],
        [
            pltpu.VMEM((BLK, 128), BF),
            pltpu.VMEM((BLK, 128), BF),
            pltpu.VMEM((HD, BLK), F32),
            pltpu.VMEM((1, BLK), F32),
            pltpu.VMEM((4, HD, BLK), BF),
            dma((4,)),
        ],
        n_smem=1,
        n_hbm_out=4,
    )(dilation_shift, yt, y2, *y2_in, u, l, *grads)
    back = [swap(send, 4 * e, seq_count) for e, send in ((1, send1), (2, send2), (3, send3))]
    (dall,) = call(
        backward_kernel,
        [((4, 144, BLK), F32)],
        [pltpu.VMEM((BLK, BLK), BF)],
        n_smem=1,
    )(dilation_shift, y, yt, e0, m0, e1, m1, gs, ds)
    (returning,) = call(
        return_kernel,
        [((slots, slide_width), BF)],
        [
            pltpu.VMEM((144, BLK), F32),
            pltpu.VMEM((slots, slide_width), BF),
            dma((4,)),
        ],
        n_smem=1,
        n_hbm_out=1,
        limit=6,
    )(dilation_shift, dall, own, dq2, *back, *grads, table_col)
    returned = exchange(returning)
    *folded, part1, part2, part3 = call(
        fold_kernel,
        [
            ((slide_width, ff), BF),
            ((slide_width, width), BF),
            ((3 * slide_width, slide_width), BF),
        ]
        + [((HD, BLK), BF)] * 3,
        stored[2:]
        + [
            pltpu.VMEM((slide_width, ff), BF),
            pltpu.VMEM((slide_width, width), BF),
            pltpu.VMEM((3 * slide_width, slide_width), BF),
            dma((ff // BAND + 2,)),
            dma((ff // BAND + 2,)),
        ],
        n_hbm=7,
        n_hbm_out=6,
        limit=32,
        aliases={4: 3, 5: 4, 6: 5},
    )(*weights[2:], returning, *parts[1:])
    *folded, part1, part2, part3 = call(
        fold_kernel,
        [
            ((slide_width, ff), BF),
            ((slide_width, width), BF),
            ((3 * slide_width, slide_width), BF),
        ]
        + [((HD, BLK), BF)] * 3,
        stored[2:]
        + [
            pltpu.VMEM((slide_width, ff), BF),
            pltpu.VMEM((slide_width, width), BF),
            pltpu.VMEM((3 * slide_width, slide_width), BF),
            dma((ff // BAND + 2,)),
            dma((ff // BAND + 2,)),
        ],
        n_hbm=7,
        n_hbm_out=6,
        limit=32,
        aliases={4: 3, 5: 4, 6: 5},
    )(*weights[2:], returning, *parts[1:])
    late = enumerate((part1, part2, part3), 1)
    parts = [parts[0]] + [swap(piece, d, seq_count) for d, piece in late]


    tile_grad, slide_out = call(
        backward_mlp_kernel,
        [((rows, width), BF), ((192, BLK), BF)],
        [
            pltpu.VMEM((device_count, rows), I32),
            pltpu.VMEM((rows, width), BF),
            pltpu.VMEM((rows, slide_width), BF),
            pltpu.VMEM((rows, ff), BF),
            pltpu.VMEM((rows, ff), BF),
        ]
        + [pltpu.VMEM(w.shape, BF) for w in (*turned_ff, *folded)]
        + [
            pltpu.VMEM((rows, 3 * slide_width), BF),
            pltpu.VMEM((rows, slide_width), BF),
            pltpu.VMEM((192, BLK), BF),
            dma((26,)),
        ],
        n_any=4,
        n_hbm=10,
        limit=48,
    )(
        returned.reshape(8, 16 * SLOTS, slide_width),
        *parts,
        all_pos,
        tile_features,
        x,
        a1,
        a2,
        *turned_ff,
        *folded,
    )
    return (slide_out.T, tile_grad)


def solution(mesh):
    placed = (P(("seq", "tile"), None), P(), P(), P(), P(), P(), P(), P(), P("seq", "tile"))
    return jax.shard_map(
        on_device,
        mesh=mesh,
        in_specs=placed,
        out_specs=(P("seq", "tile"), P(("seq", "tile"), None)),
        check_vma=False,
    )
```

```python
import jax
import jax.numpy as jnp
from jax import lax
from jax.experimental import pallas as pl
from jax.experimental.pallas import tpu as pltpu
from jax.sharding import PartitionSpec as P

HEADS = 16
HD = 48
EPSILON = 1e-06
SOFT_CAP = 50.0
SCALE = HD**-0.5
LOG2_E = 1.4426950408889634
BLK = 512
SLOTS = 8
BF = jnp.bfloat16
F32 = jnp.float32
I32 = jnp.int32

NN = (((1,), (0,)), ((), ()))
NT = (((1,), (1,)), ((), ()))
TN = (((0,), (0,)), ((), ()))


def mm(a, b, dims=NN):
    return lax.dot_general(a, b, dims, preferred_element_type=F32)


def iota(shape, dim):
    return lax.broadcasted_iota(I32, shape, dim)


def class_order(row):
    return (row & 3) * 128 + ((row >> 2) & 3) * 32 + (row >> 4)


def order_matrix():
    return jnp.where(class_order(iota((BLK, BLK), 0)) == iota((BLK, BLK), 1), 1.0, 0.0).astype(BF)


def normalize(values):
    centred = values - jnp.mean(values, axis=-1, keepdims=True)
    inv_std = lax.rsqrt(jnp.mean(centred * centred, axis=-1, keepdims=True) + EPSILON)
    return (centred * inv_std, inv_std)


def norm_back(normed, inv_std, grads):
    mean_grad = jnp.mean(grads, axis=-1, keepdims=True)
    mean_cross = jnp.mean(grads * normed, axis=-1, keepdims=True)
    return (grads - mean_grad - normed * mean_cross) * inv_std


def call(kernel, outs, scratch=(), n_smem=0, n_any=0, n_hbm=0, n_hbm_out=0, limit=4):
    def run(*args):
        n_vmem = len(args) - n_smem - n_any - n_hbm
        specs = [pl.BlockSpec(memory_space=pltpu.SMEM)] * n_smem
        specs += [pl.BlockSpec(memory_space=pltpu.VMEM)] * n_vmem
        specs += [pl.BlockSpec(memory_space=pl.ANY)] * n_any
        specs += [pl.BlockSpec(memory_space=pltpu.HBM)] * n_hbm
        out_specs = [pl.BlockSpec(memory_space=pltpu.HBM)] * n_hbm_out
        out_specs += [pl.BlockSpec(memory_space=pltpu.VMEM)] * (len(outs) - n_hbm_out)
        shapes = [pltpu.HBM(shape, kind) for shape, kind in outs[:n_hbm_out]]
        shapes += [jax.ShapeDtypeStruct(shape, kind) for shape, kind in outs[n_hbm_out:]]
        cut = len(args) - n_hbm
        held = [pltpu.with_memory_space_constraint(x, pltpu.HBM) for x in args[cut:]]
        return pl.pallas_call(
            kernel,
            out_shape=shapes,
            in_specs=specs,
            out_specs=out_specs,
            scratch_shapes=list(scratch),
            compiler_params=pltpu.CompilerParams(vmem_limit_bytes=limit * 1024 * 1024),
        )(*args[:cut], *held)

    return run


def started(copies):
    for copy in copies:
        copy.start()
    return copies


def finish(copies):
    for copy in copies:
        copy.wait()


def order_kernel(grad_ref, g0_ref, g1_ref, g2_ref, g3_ref, tmp_ref):
    j = lax.axis_index("seq") & 3
    tmp_ref[...] = mm(grad_ref[...], order_matrix()).astype(BF)
    for d, out_ref in enumerate((g0_ref, g1_ref, g2_ref, g3_ref)):
        out_ref[...] = tmp_ref[pl.ds(pl.multiple_of((j ^ d) * HD, 16), HD), :]


def offsets(shift_ref):
    head = 4 * lax.axis_index("tile") + (lax.axis_index("seq") & 3)
    o1 = shift_ref[0, head]
    o2 = shift_ref[1, head]
    return (o1 * 128, (o2 & 3) * 128, o2 >> 2)


def table_kernel(pos_ref, row_ref, col_ref):
    s = lax.axis_index("seq")
    pos = pos_ref[...].T
    n = pos.shape[0]
    block = pos >> 9
    seat = class_order(pos & (BLK - 1)) + 1
    lower = jnp.where(iota((n, n), 1) < iota((n, n), 0), 1.0, 0.0).astype(BF)
    high, low = [], []
    for d in range(4):
        owned = block == (s ^ d)
        rank = mm(lower, jnp.where(owned, 1.0, 0.0).astype(BF)).astype(I32)
        held = jnp.where(owned, seat, 0)
        for k in range(SLOTS):
            found = jnp.sum(jnp.where(rank == k, held, 0), axis=0, keepdims=True)
            high.append(found >> 4)
            low.append(found & 15)
    digits = jnp.concatenate(high + low, axis=0).astype(F32).astype(BF)
    lanes = n * SLOTS
    spread = jnp.where(iota((n, lanes), 0) == iota((n, lanes), 1) >> 3, 1.0, 0.0).astype(BF)
    wide = mm(digits, spread)
    wide = 16.0 * wide[0:32] + wide[32:64]
    own = iota((8, lanes), 0) == (iota((8, lanes), 1) & 7)
    rows = [
        jnp.sum(jnp.where(own, wide[8 * d : 8 * d + 8], 0.0), axis=0, keepdims=True)
        for d in range(4)
    ]
    table = jnp.concatenate(rows + rows, axis=0) - 1.0
    row_ref[...] = table.astype(I32)
    col_ref[...] = table.T.astype(I32)


def forward_mlp_kernel(
    feat_hbm,
    pos_hbm,
    gate_hbm,
    up_hbm,
    down_hbm,
    proj_hbm,
    qkvw_hbm,
    out_hbm,
    x_hbm,
    a1_hbm,
    a2_hbm,
    feat_ref,
    pos_ref,
    wg_ref,
    wu_ref,
    wd_ref,
    wp_ref,
    wq_ref,
    x_ref,
    a1_ref,
    a2_ref,
    heads_ref,
    picker_ref,
    tmp_ref,
    sems,
    out_sems,
):
    ff = gate_hbm.shape[1]
    width = HEADS * HD
    step = 512
    chunks = ff // step
    first = started(
        [
            pltpu.make_async_copy(feat_hbm, feat_ref, sems.at[3 * chunks]),
            pltpu.make_async_copy(pos_hbm, pos_ref, sems.at[3 * chunks + 1]),
        ]
    )
    waits = []
    for c in range(chunks):
        at = pl.ds(c * step, step)
        waits.append(
            started(
                [
                    pltpu.make_async_copy(gate_hbm.at[:, at], wg_ref.at[:, at], sems.at[3 * c]),
                    pltpu.make_async_copy(up_hbm.at[:, at], wu_ref.at[:, at], sems.at[3 * c + 1]),
                    pltpu.make_async_copy(down_hbm.at[at, :], wd_ref.at[at, :], sems.at[3 * c + 2]),
                ]
            )
        )
    last = started(
        [
            pltpu.make_async_copy(proj_hbm, wp_ref, sems.at[3 * chunks + 2]),
        ]
        + [
            pltpu.make_async_copy(qkvw_hbm.at[:, at], wq_ref.at[:, at], sems.at[3 * chunks + 3 + i])
            for i, at in enumerate(pl.ds(width * part, width) for part in range(3))
        ]
    )
    finish(first)

    me = lax.axis_index("seq") * 4 + lax.axis_index("tile")
    brow = pos_ref[pl.ds(me, 1), :] >> 9
    n = brow.shape[1]
    bcol = jnp.broadcast_to(brow, (n, n)).T
    before = iota((n, n), 0) < iota((n, n), 1)
    rank = jnp.sum(jnp.where((bcol == brow) & before, 1, 0), axis=0, keepdims=True)
    code = brow * SLOTS + rank
    code = jnp.concatenate([code, code + 4096], axis=1)
    seat = iota((BLK, 2 * n), 0)
    want = (((seat >> 4) & 7) * 4 + (seat >> 7)) * SLOTS + (seat & 7) + 4096 * ((seat >> 3) & 1)
    picker_ref[...] = jnp.where(code == want, 1.0, 0.0).astype(BF)

    feats = feat_ref[...].astype(F32)
    normed = normalize(feats)[0].astype(BF)
    total = feats
    outs = []
    for c in range(chunks):
        at = slice(c * step, c * step + step)
        waits[c][0].wait()
        gate = mm(normed, wg_ref[:, at])
        waits[c][1].wait()
        up = mm(normed, wu_ref[:, at])
        sig = jax.nn.sigmoid(gate)
        silu = gate * sig
        hidden = (silu * up).astype(BF)
        a1_ref[:, at] = (up * (sig + silu * (1.0 - sig))).astype(BF)
        a2_ref[:, at] = silu.astype(BF)
        waits[c][2].wait()
        total = total + mm(hidden, wd_ref[at, :])
    outs += started(
        [
            pltpu.make_async_copy(a1_ref, a1_hbm, out_sems.at[0]),
            pltpu.make_async_copy(a2_ref, a2_hbm, out_sems.at[1]),
        ]
    )
    last[0].wait()
    x = mm(total.astype(BF), wp_ref[...]).astype(BF)
    x_ref[...] = x
    outs += started([pltpu.make_async_copy(x_ref, x_hbm, out_sems.at[2])])
    slide_norm = normalize(x.astype(F32))[0].astype(BF)

    def deal(values, part):
        for h in range(HEADS):
            t, j = h // 4, h % 4
            heads_ref[2 * j + t // 2, n * (t % 2) : n * (t % 2) + n, HD * part : HD * part + HD] = (
                values[:, h * HD : h * HD + HD]
            )

    deal(x, 3)
    for part in range(3):
        last[1 + part].wait()
        at = slice(width * part, width * part + width)
        deal(mm(slide_norm, wq_ref[:, at]).astype(BF), part)
    for pair in range(HEADS // 2):
        j = pair // 2
        rows = mm(picker_ref[...], heads_ref[pair]).astype(BF)
        at = slice(16 * pair, 16 * pair + 16)
        for block in range(4):
            lane = (j ^ block) * 192
            tmp_ref[:, at, lane : lane + 192] = rows[128 * block : 128 * block + 128].reshape(
                8, 16, 192
            )
        outs += started(
            [
                pltpu.make_async_copy(
                    tmp_ref.at[:, at, :], out_hbm.at[:, at, :], out_sems.at[3 + pair]
                )
            ]
        )
    finish(outs)


BAND = 256


def band(i):
    return pl.ds(pl.multiple_of(i * BAND, BAND), BAND)


def turn_kernel(
    gate_hbm, up_hbm, _after_hbm, gatet_hbm, upt_hbm, in_ref, out_ref, sems, out_sems
):
    count = gate_hbm.shape[0] // BAND
    given, made = (gate_hbm, up_hbm), (gatet_hbm, upt_hbm)

    def load(which, i):
        return pltpu.make_async_copy(
            given[which].at[band(i), :], in_ref.at[which, band(i), :], sems.at[which, i]
        )

    def store(which, i):
        return pltpu.make_async_copy(
            out_ref.at[which, :, band(i)], made[which].at[:, band(i)], out_sems.at[which, i]
        )

    for which in range(2):
        for i in range(count):
            load(which, i).start()
    for which in range(2):

        def step(i, carry):
            load(which, i).wait()
            out_ref[which, :, band(i)] = in_ref[which, band(i), :].T
            store(which, i).start()
            return carry

        lax.fori_loop(0, count, step, 0)
    for which in range(2):
        for i in range(count):
            store(which, i).wait()


def fold_kernel(
    down_hbm,
    proj_hbm,
    qkvw_hbm,
    _after_hbm,
    fold_hbm,
    projt_hbm,
    qkvt_hbm,
    wd_ref,
    wp_ref,
    wq_ref,
    fold_ref,
    projt_ref,
    qkvt_ref,
    sems,
    out_sems,
):
    count = down_hbm.shape[0] // BAND
    loads = started(
        [
            pltpu.make_async_copy(qkvw_hbm, wq_ref, sems.at[count]),
            pltpu.make_async_copy(proj_hbm, wp_ref, sems.at[count + 1]),
        ]
    )

    def load(i):
        return pltpu.make_async_copy(down_hbm.at[band(i), :], wd_ref.at[band(i), :], sems.at[i])

    def store(i):
        return pltpu.make_async_copy(
            fold_ref.at[:, band(i)], fold_hbm.at[:, band(i)], out_sems.at[i]
        )

    def turn(from_ref, to_ref):
        def step(i, carry):
            to_ref[:, band(i)] = from_ref[band(i), :].T
            return carry

        lax.fori_loop(0, from_ref.shape[0] // BAND, step, 0)

    for i in range(count):
        load(i).start()
    loads[0].wait()
    turn(wq_ref, qkvt_ref)
    outs = started([pltpu.make_async_copy(qkvt_ref, qkvt_hbm, out_sems.at[count])])
    loads[1].wait()
    turn(wp_ref, projt_ref)
    outs += started([pltpu.make_async_copy(projt_ref, projt_hbm, out_sems.at[count + 1])])

    def step(i, carry):
        load(i).wait()
        fold_ref[:, band(i)] = mm(wd_ref[band(i), :], wp_ref[...]).astype(BF).T
        store(i).start()
        return carry

    lax.fori_loop(0, count, step, 0)
    for i in range(count):
        store(i).wait()
    finish(outs)


def backward_mlp_kernel(
    ret_ref,
    s0_any,
    s1_any,
    s2_any,
    s3_any,
    pos_hbm,
    feat_hbm,
    x_hbm,
    a1_hbm,
    a2_hbm,
    gate_hbm,
    up_hbm,
    fold_hbm,
    proj_hbm,
    qkvw_hbm,
    out_ref,
    slide_ref,
    pos_ref,
    feat_ref,
    x_ref,
    a1_ref,
    a2_ref,
    wg_ref,
    wu_ref,
    fold_ref,
    wp_ref,
    wq_ref,
    dqkv_ref,
    grad_ref,
    tmp_ref,
    sems,
):
    ff = gate_hbm.shape[0]
    cuts = [(at, 512) for at in range(0, ff - 512, 512)] + [(ff - 512, 256), (ff - 256, 256)]
    chunks = len(cuts)
    pairs = (
        (pos_hbm, pos_ref),
        (x_hbm, x_ref),
        (qkvw_hbm, wq_ref),
        (proj_hbm, wp_ref),
        (a1_hbm, a1_ref),
        (a2_hbm, a2_ref),
        (feat_hbm, feat_ref),
    )
    first = started(
        [
            pltpu.make_async_copy(here, there, sems.at[3 * chunks + i])
            for i, (here, there) in enumerate(pairs)
        ]
    )
    waits = []
    for c, (start, size) in enumerate(cuts):
        at = pl.ds(start, size)
        waits.append(
            started(
                [
                    pltpu.make_async_copy(fold_hbm.at[:, at], fold_ref.at[:, at], sems.at[3 * c]),
                    pltpu.make_async_copy(gate_hbm.at[at, :], wg_ref.at[at, :], sems.at[3 * c + 1]),
                    pltpu.make_async_copy(up_hbm.at[at, :], wu_ref.at[at, :], sems.at[3 * c + 2]),
                ]
            )
        )
    j = lax.axis_index("seq") & 3
    pieces = started(
        [
            pltpu.make_async_copy(
                so,
                tmp_ref.at[pl.ds(pl.multiple_of((j ^ d) * HD, 16), HD), :],
                sems.at[3 * chunks + len(pairs) + d],
            )
            for d, so in enumerate((s0_any, s1_any, s2_any, s3_any))
        ]
    )
    first[0].wait()
    me = lax.axis_index("seq") * 4 + lax.axis_index("tile")
    brow = pos_ref[pl.ds(me, 1), :] >> 9
    n = brow.shape[1]
    bcol = jnp.broadcast_to(brow, (n, n)).T
    before = iota((n, n), 1) < iota((n, n), 0)
    rank = jnp.sum(jnp.where((bcol == brow) & before, 1, 0), axis=1, keepdims=True)
    code = bcol[:, 0:1] * SLOTS + rank
    code = jnp.concatenate([code, code + 4096], axis=0)
    seat = iota((2 * n, BLK), 1)
    want = (((seat >> 4) & 7) * 4 + (seat >> 7)) * SLOTS + (seat & 7) + 4096 * ((seat >> 3) & 1)
    picker = jnp.where(code == want, 1.0, 0.0).astype(BF)
    width = HEADS * HD
    for pair in range(HEADS // 2):
        j, t = pair // 2, 2 * (pair % 2)
        tile = ret_ref[:, 16 * pair : 16 * pair + 16, :].reshape(128, 768)
        stacked = jnp.concatenate(
            [tile[:, (j ^ b) * 192 : (j ^ b) * 192 + 192] for b in range(4)], axis=0
        )
        got = mm(picker, stacked).astype(BF)
        for tp in range(2):
            h = 4 * (t + tp) + j
            mine = got[n * tp : n * tp + n]
            for part in range(3):
                dqkv_ref[:, part * width + h * HD : part * width + h * HD + HD] = mine[
                    :, HD * part : HD * part + HD
                ]
            grad_ref[:, h * HD : h * HD + HD] = mine[:, 144:192]
    first[1].wait()
    slide_norm, slide_inv = normalize(x_ref[...].astype(F32))
    first[2].wait()
    dnorm = mm(dqkv_ref[...], wq_ref[...])
    dslide = (grad_ref[...].astype(F32) + norm_back(slide_norm, slide_inv, dnorm)).astype(BF)
    first[3].wait()
    dembed = mm(dslide, wp_ref[...]).astype(BF)
    finish(first[4:])
    normed, inv = normalize(feat_ref[...].astype(F32))
    finish(pieces)
    slide_ref[...] = mm(tmp_ref[...], order_matrix(), NT).astype(BF)
    dfeat = jnp.zeros(feat_ref.shape, F32)
    for c, (start, size) in enumerate(cuts):
        at = slice(start, start + size)
        waits[c][0].wait()
        dhidden = mm(dslide, fold_ref[:, at])
        dgate = (dhidden * a1_ref[:, at].astype(F32)).astype(BF)
        dup = (dhidden * a2_ref[:, at].astype(F32)).astype(BF)
        waits[c][1].wait()
        dfeat = dfeat + mm(dgate, wg_ref[at, :])
        waits[c][2].wait()
        dfeat = dfeat + mm(dup, wu_ref[at, :])
    out_ref[...] = (dembed.astype(F32) + norm_back(normed, inv, dfeat)).astype(BF)


def place_kernel(shift_ref, recv_ref, tab_ref, _after_hbm, y_ref, yt_ref, y2_ref):
    _, base, part = offsets(shift_ref)
    o2 = pl.multiple_of(base + 32 * part, 32)
    for d in range(4):
        tab = tab_ref[d : d + 1, :]
        onehot = jnp.where(iota((BLK, tab.shape[1]), 0) == tab, 1.0, 0.0).astype(BF)
        y = mm(onehot, recv_ref[:, 192 * d : 192 * d + 192])
        y = y.astype(BF)
        y_ref[d] = y
        yt_ref[d] = y.T
        y2_ref[32 * d : 32 * d + 32, :] = y_ref[d, pl.ds(o2, 32), :]


def score_rows(keys, queries_t, e_store, m_store):
    count, width = keys.shape[0], queries_t.shape[1]
    total = jnp.zeros((8, width), F32)
    step = 128
    for c in range(0, count, step):
        t = jnp.tanh(mm(keys[c : c + step], queries_t) * (SCALE / SOFT_CAP))
        e = jnp.exp2((SOFT_CAP * LOG2_E) * t)
        total = total + jnp.sum(e.reshape(step // 8, 8, width), axis=0)
        e_store(c, step, e.astype(BF))
        m_store(c, step, (e - e * (t * t)).astype(BF))
    return jnp.sum(total, axis=0, keepdims=True)


def forward_kernel(shift_ref, y_ref, yt_ref, e0_ref, m0_ref, e1_ref, m1_ref, u_ref, l_ref):
    o1 = pl.multiple_of(offsets(shift_ref)[0], 128)

    def block(d):
        def e_store(c, n, v):
            e0_ref[d, c : c + n, :] = v

        def m_store(c, n, v):
            m0_ref[d, c : c + n, :] = v

        l_ref[d] = score_rows(y_ref[d, :, 48:96], yt_ref[d, 0:48, :], e_store, m_store)
        u_ref[d] = mm(yt_ref[d, 96:144, :], e0_ref[d])

    for d in range(4):
        block(d)

    def e_store(c, n, v):
        e1_ref[c : c + n, :] = v

    def m_store(c, n, v):
        m1_ref[c : c + n, :] = v

    keys = jnp.concatenate([y_ref[d, pl.ds(o1, 128), 48:96] for d in range(4)], axis=0)
    queries = jnp.concatenate([yt_ref[d, 0:48, pl.ds(o1, 128)] for d in range(4)], axis=1)
    values = jnp.concatenate([yt_ref[d, 96:144, pl.ds(o1, 128)] for d in range(4)], axis=1)
    l1 = score_rows(keys, queries, e_store, m_store)
    u1 = mm(values, e1_ref[...])
    for d in range(4):
        u_ref[d, :, pl.ds(o1, 128)] += u1[:, 128 * d : 128 * d + 128]
        l_ref[d, :, pl.ds(o1, 128)] += l1[:, 128 * d : 128 * d + 128]


def turned(value, shift):
    return pltpu.roll(value, shift & 127, 1)


def wide_kernel(
    shift_ref,
    yt_ref,
    a0_ref,
    a1_ref,
    a2_ref,
    a3_ref,
    u_ref,
    l_ref,
    g0_ref,
    g1_ref,
    g2_ref,
    g3_ref,
    so0_ref,
    so1_ref,
    so2_ref,
    so3_ref,
    gs_ref,
    ds_ref,
    own_ref,
    send1_ref,
    send2_ref,
    send3_ref,
    dq_ref,
    e2_ref,
    m2_ref,
    usum_ref,
    lsum_ref,
):
    _, base, part = offsets(shift_ref)
    base = pl.multiple_of(base, 128)
    y2 = jnp.concatenate([a0_ref[...], a1_ref[...], a2_ref[...], a3_ref[...]], axis=0)
    keys, values = y2[:, 48:96], y2[:, 96:144]
    both_t = y2[:, 48:144].astype(F32).T.astype(BF)
    query_t = a0_ref[:, 0:48].astype(F32).T.astype(BF)

    def e_store(c, n, v):
        e2_ref[c : c + n, :] = v

    def m_store(c, n, v):
        m2_ref[c : c + n, :] = v

    l2 = score_rows(keys, query_t, e_store, m_store)
    u2 = mm(both_t[48:96], e2_ref[...])
    l2w = jnp.broadcast_to(l2, (8, 128))
    lane = iota((1, 128), 1) >> 5
    gs2 = jnp.zeros((48, 128), F32)
    ds2 = jnp.zeros((8, 128), F32)
    for d in range(4):
        here = lane == part
        shift = 32 * (part - d)
        usum_ref[...] = u_ref[d]
        lsum_ref[...] = l_ref[d]
        usum_ref[:, pl.ds(base, 128)] += jnp.where(here, turned(u2, shift), 0.0)
        lsum_ref[:, pl.ds(base, 128)] += jnp.where(here, turned(l2w, shift), 0.0)[0:1]
        inv = 1.0 / lsum_ref[...]
        att = usum_ref[...] * inv
        so_ref = (so0_ref, so1_ref, so2_ref, so3_ref)[d]
        so_ref[...] = (yt_ref[d, 144:192, :].astype(F32) + att).astype(BF)
        grad_ref = (g0_ref, g1_ref, g2_ref, g3_ref)[d]
        gs = (grad_ref[...].astype(F32) * inv).astype(BF)
        gs_ref[d] = gs
        ds_ref[d] = jnp.sum(gs.astype(F32) * att, axis=0, keepdims=True)
        gs_wide = gs_ref[d, :, pl.ds(base, 128)].astype(F32)
        ds_wide = jnp.broadcast_to(ds_ref[d, :, pl.ds(base, 128)], (8, 128))
        gs2 = jnp.where(lane == d, turned(gs_wide, -shift), gs2)
        ds2 = jnp.where(lane == d, turned(ds_wide, -shift), ds2)
    gs2 = gs2.astype(BF)
    dp = mm(values, gs2)
    dscore = (m2_ref[...].astype(F32) * (dp - ds2[0:1])).astype(BF)
    dq_ref[...] = mm(both_t[0:48], dscore) * SCALE
    dk = mm(query_t, dscore, NT) * SCALE
    dv = mm(gs2, e2_ref[...], NT)
    dkv = jnp.concatenate([dk, dv], axis=0)
    own_ref[...] = dkv[:, 0:128]
    for e, send_ref in enumerate((send1_ref, send2_ref, send3_ref)):
        send_ref[...] = dkv[:, 128 * e + 128 : 128 * e + 256].astype(BF)


def dscores(values, gs, ds, m_load, store):
    dp = mm(values, gs)
    step = 64
    for c in range(0, dp.shape[0], step):
        store(c, step, (m_load(c, step).astype(F32) * (dp[c : c + step] - ds)).astype(BF))


def backward_kernel(
    shift_ref,
    y_ref,
    yt_ref,
    e0_ref,
    m0_ref,
    e1_ref,
    m1_ref,
    gs_ref,
    ds_ref,
    so0_ref,
    so1_ref,
    so2_ref,
    so3_ref,
    so0_hbm,
    so1_hbm,
    so2_hbm,
    so3_hbm,
    out_ref,
    tmp_ref,
    sems,
):
    pairs = ((so0_ref, so0_hbm), (so1_ref, so1_hbm), (so2_ref, so2_hbm), (so3_ref, so3_hbm))
    outs = started(
        [pltpu.make_async_copy(here, there, sems.at[d]) for d, (here, there) in enumerate(pairs)]
    )
    o1 = pl.multiple_of(offsets(shift_ref)[0], 128)

    def store(c, n, v):
        tmp_ref[c : c + n, :] = v

    def block(d):
        gs = gs_ref[d]
        dscores(y_ref[d, :, 96:144], gs, ds_ref[d], lambda c, n: m0_ref[d, c : c + n, :], store)
        dscore = tmp_ref[...]
        out_ref[d, 0:48, :] = mm(yt_ref[d, 48:96, :], dscore) * SCALE
        out_ref[d, 48:96, :] = mm(yt_ref[d, 0:48, :], dscore, NT) * SCALE
        out_ref[d, 96:144, :] = mm(gs, e0_ref[d], NT)

    for d in range(4):
        block(d)
    values = jnp.concatenate([y_ref[d, pl.ds(o1, 128), 96:144] for d in range(4)], axis=0)
    queries = jnp.concatenate([yt_ref[d, 0:48, pl.ds(o1, 128)] for d in range(4)], axis=1)
    keys = jnp.concatenate([yt_ref[d, 48:96, pl.ds(o1, 128)] for d in range(4)], axis=1)
    gs = jnp.concatenate([gs_ref[d, :, pl.ds(o1, 128)] for d in range(4)], axis=1)
    ds = jnp.concatenate([ds_ref[d, :, pl.ds(o1, 128)] for d in range(4)], axis=1)
    dscores(values, gs, ds, lambda c, n: m1_ref[c : c + n, :], store)
    dscore = tmp_ref[...]
    dq = mm(keys, dscore) * SCALE
    dk = mm(queries, dscore, NT) * SCALE
    dv = mm(gs, e1_ref[...], NT)
    dall = jnp.concatenate([dq, dk, dv], axis=0)
    for d in range(4):
        out_ref[d, :, pl.ds(o1, 128)] += dall[:, 128 * d : 128 * d + 128]
    finish(outs)


def return_kernel(
    shift_ref,
    dall_ref,
    own_ref,
    dq_ref,
    r1_ref,
    r2_ref,
    r3_ref,
    g0_ref,
    g1_ref,
    g2_ref,
    g3_ref,
    tab_ref,
    out_hbm,
    sum_ref,
    out_ref,
    sems,
):
    _, base, part = offsets(shift_ref)
    base = pl.multiple_of(base, 128)
    dkv = (
        own_ref[...]
        + r1_ref[...].astype(F32)
        + r2_ref[...].astype(F32)
        + r3_ref[...].astype(F32)
    )
    extra = jnp.concatenate([dq_ref[...], dkv], axis=0)
    lane = iota((1, 128), 1) >> 5
    outs, parts = [], []
    for d in range(4):
        grad_ref = (g0_ref, g1_ref, g2_ref, g3_ref)[d]
        sum_ref[...] = dall_ref[d]
        sum_ref[:, pl.ds(base, 128)] += jnp.where(
            lane == part, turned(extra, 32 * (part - d)), 0.0
        )
        parts.append(jnp.concatenate([sum_ref[...].astype(BF), grad_ref[...]], axis=0).T)
    for c, (first, step) in enumerate(((0, 384), (384, 384), (768, 192), (960, 64))):
        at = slice(first, first + step)
        for d in range(4):
            onehot = jnp.where(tab_ref[at, d : d + 1] == iota((step, BLK), 1), 1.0, 0.0)
            out_ref[at, 192 * d : 192 * d + 192] = mm(onehot.astype(BF), parts[d]).astype(BF)
        outs += started([pltpu.make_async_copy(out_ref.at[at, :], out_hbm.at[at, :], sems.at[c])])
    finish(outs)


def swap(value, distance, count):
    return lax.ppermute(value, "seq", [(i, i ^ distance) for i in range(count)])


def on_device(
    tile_features,
    gate_weight,
    up_weight,
    down_weight,
    input_projection_weight,
    query_key_value_weight,
    positions,
    dilation_shift,
    slide_output_gradient,
):
    seq_count = lax.axis_size("seq")
    device_count = seq_count * lax.axis_size("tile")
    rows, width = tile_features.shape
    ff = gate_weight.shape[1]
    slide_width = input_projection_weight.shape[1]
    all_pos = positions.reshape(device_count, rows)
    routed = ((8, 16 * SLOTS, slide_width), BF)
    weights = (gate_weight, up_weight, down_weight, input_projection_weight, query_key_value_weight)

    def exchange(block):
        return lax.all_to_all(
            block.reshape(device_count, SLOTS, slide_width),
            ("seq", "tile"),
            split_axis=0,
            concat_axis=0,
            tiled=True,
        ).reshape(device_count * SLOTS, slide_width)

    stored = [
        pltpu.VMEM((width, ff), BF),
        pltpu.VMEM((width, ff), BF),
        pltpu.VMEM((ff, width), BF),
        pltpu.VMEM((width, slide_width), BF),
        pltpu.VMEM((slide_width, 3 * slide_width), BF),
    ]
    dma = pltpu.SemaphoreType.DMA
    outgoing, x, a1, a2 = call(
        forward_mlp_kernel,
        [routed, ((rows, slide_width), BF), ((rows, ff), BF), ((rows, ff), BF)],
        [pltpu.VMEM((rows, width), BF), pltpu.VMEM((device_count, rows), I32)]
        + stored
        + [
            pltpu.VMEM((rows, slide_width), BF),
            pltpu.VMEM((rows, ff), BF),
            pltpu.VMEM((rows, ff), BF),
            pltpu.VMEM((HEADS // 2, 2 * rows, 192), BF),
            pltpu.VMEM((BLK, 2 * rows), BF),
            pltpu.VMEM((8, 16 * SLOTS, slide_width), BF),
            dma((18,)),
            dma((3 + HEADS // 2,)),
        ],
        n_hbm=7,
        n_hbm_out=4,
        limit=48,
    )(tile_features, all_pos, *weights)
    arrived = exchange(outgoing)
    turned_ff = call(
        turn_kernel,
        [((ff, width), BF)] * 2,
        [
            pltpu.VMEM((2, width, ff), BF),
            pltpu.VMEM((2, ff, width), BF),
            dma((2, width // BAND)),
            dma((2, width // BAND)),
        ],
        n_hbm=3,
        n_hbm_out=2,
        limit=32,
    )(gate_weight, up_weight, x)

    grads = call(
        order_kernel,
        [((HD, BLK), BF)] * 4,
        [pltpu.VMEM((192, BLK), BF)],
    )(slide_output_gradient.T)
    grads = [grads[0]] + [swap(grads[d], d, seq_count) for d in range(1, 4)]
    slots = device_count * SLOTS
    table, table_col = call(
        table_kernel,
        [((8, slots), I32), ((slots, 8), I32)],
    )(all_pos)

    y, yt, y2 = call(
        place_kernel,
        [((4, BLK, 192), BF), ((4, 192, BLK), BF), ((128, 192), BF)],
        n_smem=1,
        n_hbm=1,
    )(dilation_shift, arrived, table, turned_ff[0])
    y2_in = [swap(y2, 4 * e, seq_count) for e in range(1, 4)]
    e0, m0, e1, m1, u, l = call(
        forward_kernel,
        [
            ((4, BLK, BLK), BF),
            ((4, BLK, BLK), BF),
            ((BLK, BLK), BF),
            ((BLK, BLK), BF),
            ((4, HD, BLK), F32),
            ((4, 1, BLK), F32),
        ],
        n_smem=1,
    )(dilation_shift, y, yt)
    *parts, gs, ds, own, send1, send2, send3, dq2 = call(
        wide_kernel,
        [((HD, BLK), BF)] * 4
        + [((4, HD, BLK), BF), ((4, 1, BLK), F32), ((96, 128), F32)]
        + [((96, 128), BF)] * 3
        + [((HD, 128), F32)],
        [
            pltpu.VMEM((BLK, 128), BF),
            pltpu.VMEM((BLK, 128), BF),
            pltpu.VMEM((HD, BLK), F32),
            pltpu.VMEM((1, BLK), F32),
        ],
        n_smem=1,
    )(dilation_shift, yt, y2, *y2_in, u, l, *grads)
    back = [swap(send, 4 * e, seq_count) for e, send in ((3, send3), (2, send2), (1, send1))]
    *parts, dall = call(
        backward_kernel,
        [((HD, BLK), BF)] * 4 + [((4, 144, BLK), F32)],
        [pltpu.VMEM((BLK, BLK), BF), dma((4,))],
        n_smem=1,
        n_hbm_out=4,
    )(dilation_shift, y, yt, e0, m0, e1, m1, gs, ds, *parts)
    (returning,) = call(
        return_kernel,
        [((slots, slide_width), BF)],
        [
            pltpu.VMEM((144, BLK), F32),
            pltpu.VMEM((slots, slide_width), BF),
            dma((4,)),
        ],
        n_smem=1,
        n_hbm_out=1,
        limit=6,
    )(dilation_shift, dall, own, dq2, *back, *grads, table_col)
    returned = exchange(returning)
    folded = call(
        fold_kernel,
        [
            ((slide_width, ff), BF),
            ((slide_width, width), BF),
            ((3 * slide_width, slide_width), BF),
        ],
        stored[2:]
        + [
            pltpu.VMEM((slide_width, ff), BF),
            pltpu.VMEM((slide_width, width), BF),
            pltpu.VMEM((3 * slide_width, slide_width), BF),
            dma((ff // BAND + 2,)),
            dma((ff // BAND + 2,)),
        ],
        n_hbm=4,
        n_hbm_out=3,
        limit=32,
    )(*weights[2:], returning)
    parts = [parts[0]] + [swap(parts[d], d, seq_count) for d in range(1, 4)]

    tile_grad, slide_out = call(
        backward_mlp_kernel,
        [((rows, width), BF), ((192, BLK), BF)],
        [
            pltpu.VMEM((device_count, rows), I32),
            pltpu.VMEM((rows, width), BF),
            pltpu.VMEM((rows, slide_width), BF),
            pltpu.VMEM((rows, ff), BF),
            pltpu.VMEM((rows, ff), BF),
        ]
        + [pltpu.VMEM(w.shape, BF) for w in (*turned_ff, *folded)]
        + [
            pltpu.VMEM((rows, 3 * slide_width), BF),
            pltpu.VMEM((rows, slide_width), BF),
            pltpu.VMEM((192, BLK), BF),
            dma((26,)),
        ],
        n_any=4,
        n_hbm=10,
        limit=48,
    )(
        returned.reshape(8, 16 * SLOTS, slide_width),
        *parts,
        all_pos,
        tile_features,
        x,
        a1,
        a2,
        *turned_ff,
        *folded,
    )
    return (slide_out.T, tile_grad)


def solution(mesh):
    placed = (P(("seq", "tile"), None), P(), P(), P(), P(), P(), P(), P(), P("seq", "tile"))
    return jax.shard_map(
        on_device,
        mesh=mesh,
        in_specs=placed,
        out_specs=(P("seq", "tile"), P(("seq", "tile"), None)),
        check_vma=False,
    )
```

```python
import jax
import jax.numpy as jnp
from jax import lax
from jax.experimental import pallas as pl
from jax.experimental.pallas import tpu as pltpu
from jax.sharding import PartitionSpec as P

HEADS = 16
HD = 48
EPSILON = 1e-06
SOFT_CAP = 50.0
SCALE = HD**-0.5
LOG2_E = 1.4426950408889634
BLK = 512
SLOTS = 8
BF = jnp.bfloat16
F32 = jnp.float32
I32 = jnp.int32

NN = (((1,), (0,)), ((), ()))
NT = (((1,), (1,)), ((), ()))
TN = (((0,), (0,)), ((), ()))


def mm(a, b, dims=NN):
    return lax.dot_general(a, b, dims, preferred_element_type=F32)


def iota(shape, dim):
    return lax.broadcasted_iota(I32, shape, dim)


def class_order(row):
    return (row & 3) * 128 + ((row >> 2) & 3) * 32 + (row >> 4)


def order_matrix():
    return jnp.where(class_order(iota((BLK, BLK), 0)) == iota((BLK, BLK), 1), 1.0, 0.0).astype(BF)


def normalize(values):
    centred = values - jnp.mean(values, axis=-1, keepdims=True)
    inv_std = lax.rsqrt(jnp.mean(centred * centred, axis=-1, keepdims=True) + EPSILON)
    return (centred * inv_std, inv_std)


def norm_back(normed, inv_std, grads):
    mean_grad = jnp.mean(grads, axis=-1, keepdims=True)
    mean_cross = jnp.mean(grads * normed, axis=-1, keepdims=True)
    return (grads - mean_grad - normed * mean_cross) * inv_std


def call(kernel, outs, scratch=(), n_smem=0, n_any=0, n_hbm=0, n_hbm_out=0, limit=4):
    def run(*args):
        n_vmem = len(args) - n_smem - n_any - n_hbm
        specs = [pl.BlockSpec(memory_space=pltpu.SMEM)] * n_smem
        specs += [pl.BlockSpec(memory_space=pltpu.VMEM)] * n_vmem
        specs += [pl.BlockSpec(memory_space=pl.ANY)] * n_any
        specs += [pl.BlockSpec(memory_space=pltpu.HBM)] * n_hbm
        out_specs = [pl.BlockSpec(memory_space=pltpu.HBM)] * n_hbm_out
        out_specs += [pl.BlockSpec(memory_space=pltpu.VMEM)] * (len(outs) - n_hbm_out)
        shapes = [pltpu.HBM(shape, kind) for shape, kind in outs[:n_hbm_out]]
        shapes += [jax.ShapeDtypeStruct(shape, kind) for shape, kind in outs[n_hbm_out:]]
        cut = len(args) - n_hbm
        held = [pltpu.with_memory_space_constraint(x, pltpu.HBM) for x in args[cut:]]
        return pl.pallas_call(
            kernel,
            out_shape=shapes,
            in_specs=specs,
            out_specs=out_specs,
            scratch_shapes=list(scratch),
            compiler_params=pltpu.CompilerParams(vmem_limit_bytes=limit * 1024 * 1024),
        )(*args[:cut], *held)

    return run


def started(copies):
    for copy in copies:
        copy.start()
    return copies


def finish(copies):
    for copy in copies:
        copy.wait()


def order_kernel(grad_ref, g0_ref, g1_ref, g2_ref, g3_ref, tmp_ref):
    j = lax.axis_index("seq") & 3
    tmp_ref[...] = mm(grad_ref[...], order_matrix()).astype(BF)
    for d, out_ref in enumerate((g0_ref, g1_ref, g2_ref, g3_ref)):
        out_ref[...] = tmp_ref[pl.ds(pl.multiple_of((j ^ d) * HD, 16), HD), :]


def offsets(shift_ref):
    head = 4 * lax.axis_index("tile") + (lax.axis_index("seq") & 3)
    o1 = shift_ref[0, head]
    o2 = shift_ref[1, head]
    return (o1 * 128, (o2 & 3) * 128, o2 >> 2)


def table_kernel(pos_ref, row_ref, col_ref):
    s = lax.axis_index("seq")
    pos = pos_ref[...].T
    n = pos.shape[0]
    block = pos >> 9
    seat = class_order(pos & (BLK - 1)) + 1
    lower = jnp.where(iota((n, n), 1) < iota((n, n), 0), 1.0, 0.0).astype(BF)
    high, low = [], []
    for d in range(4):
        owned = block == (s ^ d)
        rank = mm(lower, jnp.where(owned, 1.0, 0.0).astype(BF)).astype(I32)
        held = jnp.where(owned, seat, 0)
        for k in range(SLOTS):
            found = jnp.sum(jnp.where(rank == k, held, 0), axis=0, keepdims=True)
            high.append(found >> 4)
            low.append(found & 15)
    digits = jnp.concatenate(high + low, axis=0).astype(F32).astype(BF)
    lanes = n * SLOTS
    spread = jnp.where(iota((n, lanes), 0) == iota((n, lanes), 1) >> 3, 1.0, 0.0).astype(BF)
    wide = mm(digits, spread)
    wide = 16.0 * wide[0:32] + wide[32:64]
    own = iota((8, lanes), 0) == (iota((8, lanes), 1) & 7)
    rows = [
        jnp.sum(jnp.where(own, wide[8 * d : 8 * d + 8], 0.0), axis=0, keepdims=True)
        for d in range(4)
    ]
    table = jnp.concatenate(rows + rows, axis=0) - 1.0
    row_ref[...] = table.astype(I32)
    col_ref[...] = table.T.astype(I32)


def forward_mlp_kernel(
    feat_hbm,
    pos_hbm,
    gate_hbm,
    up_hbm,
    down_hbm,
    proj_hbm,
    qkvw_hbm,
    out_hbm,
    x_hbm,
    a1_hbm,
    a2_hbm,
    feat_ref,
    pos_ref,
    wg_ref,
    wu_ref,
    wd_ref,
    wp_ref,
    wq_ref,
    x_ref,
    a1_ref,
    a2_ref,
    heads_ref,
    picker_ref,
    tmp_ref,
    sems,
    out_sems,
):
    ff = gate_hbm.shape[1]
    width = HEADS * HD
    step = 512
    chunks = ff // step
    first = started(
        [
            pltpu.make_async_copy(feat_hbm, feat_ref, sems.at[3 * chunks]),
            pltpu.make_async_copy(pos_hbm, pos_ref, sems.at[3 * chunks + 1]),
        ]
    )
    waits = []
    for c in range(chunks):
        at = pl.ds(c * step, step)
        waits.append(
            started(
                [
                    pltpu.make_async_copy(gate_hbm.at[:, at], wg_ref.at[:, at], sems.at[3 * c]),
                    pltpu.make_async_copy(up_hbm.at[:, at], wu_ref.at[:, at], sems.at[3 * c + 1]),
                    pltpu.make_async_copy(down_hbm.at[at, :], wd_ref.at[at, :], sems.at[3 * c + 2]),
                ]
            )
        )
    last = started(
        [
            pltpu.make_async_copy(proj_hbm, wp_ref, sems.at[3 * chunks + 2]),
        ]
        + [
            pltpu.make_async_copy(qkvw_hbm.at[:, at], wq_ref.at[:, at], sems.at[3 * chunks + 3 + i])
            for i, at in enumerate(pl.ds(width * part, width) for part in range(3))
        ]
    )
    finish(first)

    me = lax.axis_index("seq") * 4 + lax.axis_index("tile")
    brow = pos_ref[pl.ds(me, 1), :] >> 9
    n = brow.shape[1]
    bcol = jnp.broadcast_to(brow, (n, n)).T
    before = iota((n, n), 0) < iota((n, n), 1)
    rank = jnp.sum(jnp.where((bcol == brow) & before, 1, 0), axis=0, keepdims=True)
    code = brow * SLOTS + rank
    code = jnp.concatenate([code, code + 4096], axis=1)
    seat = iota((BLK, 2 * n), 0)
    want = (((seat >> 4) & 7) * 4 + (seat >> 7)) * SLOTS + (seat & 7) + 4096 * ((seat >> 3) & 1)
    picker_ref[...] = jnp.where(code == want, 1.0, 0.0).astype(BF)

    feats = feat_ref[...].astype(F32)
    normed = normalize(feats)[0].astype(BF)
    total = feats
    outs = []
    for c in range(chunks):
        at = slice(c * step, c * step + step)
        waits[c][0].wait()
        gate = mm(normed, wg_ref[:, at])
        waits[c][1].wait()
        up = mm(normed, wu_ref[:, at])
        sig = jax.nn.sigmoid(gate)
        silu = gate * sig
        hidden = (silu * up).astype(BF)
        a1_ref[:, at] = (up * (sig + silu * (1.0 - sig))).astype(BF)
        a2_ref[:, at] = silu.astype(BF)
        waits[c][2].wait()
        total = total + mm(hidden, wd_ref[at, :])
    outs += started(
        [
            pltpu.make_async_copy(a1_ref, a1_hbm, out_sems.at[0]),
            pltpu.make_async_copy(a2_ref, a2_hbm, out_sems.at[1]),
        ]
    )
    last[0].wait()
    x = mm(total.astype(BF), wp_ref[...]).astype(BF)
    x_ref[...] = x
    outs += started([pltpu.make_async_copy(x_ref, x_hbm, out_sems.at[2])])
    slide_norm = normalize(x.astype(F32))[0].astype(BF)

    def deal(values, part):
        for h in range(HEADS):
            t, j = h // 4, h % 4
            heads_ref[2 * j + t // 2, n * (t % 2) : n * (t % 2) + n, HD * part : HD * part + HD] = (
                values[:, h * HD : h * HD + HD]
            )

    deal(x, 3)
    for part in range(3):
        last[1 + part].wait()
        at = slice(width * part, width * part + width)
        deal(mm(slide_norm, wq_ref[:, at]).astype(BF), part)
    for pair in range(HEADS // 2):
        j = pair // 2
        rows = mm(picker_ref[...], heads_ref[pair]).astype(BF)
        at = slice(16 * pair, 16 * pair + 16)
        for block in range(4):
            lane = (j ^ block) * 192
            tmp_ref[:, at, lane : lane + 192] = rows[128 * block : 128 * block + 128].reshape(
                8, 16, 192
            )
        outs += started(
            [
                pltpu.make_async_copy(
                    tmp_ref.at[:, at, :], out_hbm.at[:, at, :], out_sems.at[3 + pair]
                )
            ]
        )
    finish(outs)


BAND = 256


def band(i):
    return pl.ds(pl.multiple_of(i * BAND, BAND), BAND)


def turn_kernel(
    gate_hbm, up_hbm, _after_hbm, gatet_hbm, upt_hbm, in_ref, out_ref, sems, out_sems
):
    count = gate_hbm.shape[0] // BAND
    given, made = (gate_hbm, up_hbm), (gatet_hbm, upt_hbm)

    def load(which, i):
        return pltpu.make_async_copy(
            given[which].at[band(i), :], in_ref.at[which, band(i), :], sems.at[which, i]
        )

    def store(which, i):
        return pltpu.make_async_copy(
            out_ref.at[which, :, band(i)], made[which].at[:, band(i)], out_sems.at[which, i]
        )

    for which in range(2):
        for i in range(count):
            load(which, i).start()
    for which in range(2):

        def step(i, carry):
            load(which, i).wait()
            out_ref[which, :, band(i)] = in_ref[which, band(i), :].T
            store(which, i).start()
            return carry

        lax.fori_loop(0, count, step, 0)
    for which in range(2):
        for i in range(count):
            store(which, i).wait()


def fold_kernel(
    down_hbm,
    proj_hbm,
    qkvw_hbm,
    _after_hbm,
    fold_hbm,
    projt_hbm,
    qkvt_hbm,
    wd_ref,
    wp_ref,
    wq_ref,
    fold_ref,
    projt_ref,
    qkvt_ref,
    sems,
    out_sems,
):
    count = down_hbm.shape[0] // BAND
    loads = started(
        [
            pltpu.make_async_copy(qkvw_hbm, wq_ref, sems.at[count]),
            pltpu.make_async_copy(proj_hbm, wp_ref, sems.at[count + 1]),
        ]
    )

    def load(i):
        return pltpu.make_async_copy(down_hbm.at[band(i), :], wd_ref.at[band(i), :], sems.at[i])

    def store(i):
        return pltpu.make_async_copy(
            fold_ref.at[:, band(i)], fold_hbm.at[:, band(i)], out_sems.at[i]
        )

    def turn(from_ref, to_ref):
        def step(i, carry):
            to_ref[:, band(i)] = from_ref[band(i), :].T
            return carry

        lax.fori_loop(0, from_ref.shape[0] // BAND, step, 0)

    for i in range(count):
        load(i).start()
    loads[0].wait()
    turn(wq_ref, qkvt_ref)
    outs = started([pltpu.make_async_copy(qkvt_ref, qkvt_hbm, out_sems.at[count])])
    loads[1].wait()
    turn(wp_ref, projt_ref)
    outs += started([pltpu.make_async_copy(projt_ref, projt_hbm, out_sems.at[count + 1])])

    def step(i, carry):
        load(i).wait()
        fold_ref[:, band(i)] = mm(wd_ref[band(i), :], wp_ref[...]).astype(BF).T
        store(i).start()
        return carry

    lax.fori_loop(0, count, step, 0)
    for i in range(count):
        store(i).wait()
    finish(outs)


def backward_mlp_kernel(
    ret_ref,
    s0_any,
    s1_any,
    s2_any,
    s3_any,
    pos_hbm,
    feat_hbm,
    x_hbm,
    a1_hbm,
    a2_hbm,
    gate_hbm,
    up_hbm,
    fold_hbm,
    proj_hbm,
    qkvw_hbm,
    out_ref,
    slide_ref,
    pos_ref,
    feat_ref,
    x_ref,
    a1_ref,
    a2_ref,
    wg_ref,
    wu_ref,
    fold_ref,
    wp_ref,
    wq_ref,
    dqkv_ref,
    grad_ref,
    tmp_ref,
    sems,
):
    ff = gate_hbm.shape[0]
    cuts = [(at, 512) for at in range(0, ff - 512, 512)] + [(ff - 512, 256), (ff - 256, 256)]
    chunks = len(cuts)
    pairs = (
        (pos_hbm, pos_ref),
        (x_hbm, x_ref),
        (qkvw_hbm, wq_ref),
        (proj_hbm, wp_ref),
        (a1_hbm, a1_ref),
        (a2_hbm, a2_ref),
        (feat_hbm, feat_ref),
    )
    first = started(
        [
            pltpu.make_async_copy(here, there, sems.at[3 * chunks + i])
            for i, (here, there) in enumerate(pairs)
        ]
    )
    waits = []
    for c, (start, size) in enumerate(cuts):
        at = pl.ds(start, size)
        waits.append(
            started(
                [
                    pltpu.make_async_copy(fold_hbm.at[:, at], fold_ref.at[:, at], sems.at[3 * c]),
                    pltpu.make_async_copy(gate_hbm.at[at, :], wg_ref.at[at, :], sems.at[3 * c + 1]),
                    pltpu.make_async_copy(up_hbm.at[at, :], wu_ref.at[at, :], sems.at[3 * c + 2]),
                ]
            )
        )
    j = lax.axis_index("seq") & 3
    pieces = started(
        [
            pltpu.make_async_copy(
                so,
                tmp_ref.at[pl.ds(pl.multiple_of((j ^ d) * HD, 16), HD), :],
                sems.at[3 * chunks + len(pairs) + d],
            )
            for d, so in enumerate((s0_any, s1_any, s2_any, s3_any))
        ]
    )
    first[0].wait()
    me = lax.axis_index("seq") * 4 + lax.axis_index("tile")
    brow = pos_ref[pl.ds(me, 1), :] >> 9
    n = brow.shape[1]
    bcol = jnp.broadcast_to(brow, (n, n)).T
    before = iota((n, n), 1) < iota((n, n), 0)
    rank = jnp.sum(jnp.where((bcol == brow) & before, 1, 0), axis=1, keepdims=True)
    code = bcol[:, 0:1] * SLOTS + rank
    code = jnp.concatenate([code, code + 4096], axis=0)
    seat = iota((2 * n, BLK), 1)
    want = (((seat >> 4) & 7) * 4 + (seat >> 7)) * SLOTS + (seat & 7) + 4096 * ((seat >> 3) & 1)
    picker = jnp.where(code == want, 1.0, 0.0).astype(BF)
    width = HEADS * HD
    for pair in range(HEADS // 2):
        j, t = pair // 2, 2 * (pair % 2)
        tile = ret_ref[:, 16 * pair : 16 * pair + 16, :].reshape(128, 768)
        stacked = jnp.concatenate(
            [tile[:, (j ^ b) * 192 : (j ^ b) * 192 + 192] for b in range(4)], axis=0
        )
        got = mm(picker, stacked).astype(BF)
        for tp in range(2):
            h = 4 * (t + tp) + j
            mine = got[n * tp : n * tp + n]
            for part in range(3):
                dqkv_ref[:, part * width + h * HD : part * width + h * HD + HD] = mine[
                    :, HD * part : HD * part + HD
                ]
            grad_ref[:, h * HD : h * HD + HD] = mine[:, 144:192]
    first[1].wait()
    slide_norm, slide_inv = normalize(x_ref[...].astype(F32))
    first[2].wait()
    dnorm = mm(dqkv_ref[...], wq_ref[...])
    dslide = (grad_ref[...].astype(F32) + norm_back(slide_norm, slide_inv, dnorm)).astype(BF)
    first[3].wait()
    dembed = mm(dslide, wp_ref[...]).astype(BF)
    finish(first[4:])
    normed, inv = normalize(feat_ref[...].astype(F32))
    finish(pieces)
    slide_ref[...] = mm(tmp_ref[...], order_matrix(), NT).astype(BF)
    dfeat = jnp.zeros(feat_ref.shape, F32)
    for c, (start, size) in enumerate(cuts):
        at = slice(start, start + size)
        waits[c][0].wait()
        dhidden = mm(dslide, fold_ref[:, at])
        dgate = (dhidden * a1_ref[:, at].astype(F32)).astype(BF)
        dup = (dhidden * a2_ref[:, at].astype(F32)).astype(BF)
        waits[c][1].wait()
        dfeat = dfeat + mm(dgate, wg_ref[at, :])
        waits[c][2].wait()
        dfeat = dfeat + mm(dup, wu_ref[at, :])
    out_ref[...] = (dembed.astype(F32) + norm_back(normed, inv, dfeat)).astype(BF)


def place_kernel(shift_ref, recv_ref, tab_ref, _after_hbm, y_ref, yt_ref, y2_ref):
    _, base, part = offsets(shift_ref)
    o2 = pl.multiple_of(base + 32 * part, 32)
    for d in range(4):
        tab = tab_ref[d : d + 1, :]
        onehot = jnp.where(iota((BLK, tab.shape[1]), 0) == tab, 1.0, 0.0).astype(BF)
        y = mm(onehot, recv_ref[:, 192 * d : 192 * d + 192])
        y = y.astype(BF)
        y_ref[d] = y
        yt_ref[d] = y.T
        y2_ref[32 * d : 32 * d + 32, :] = y_ref[d, pl.ds(o2, 32), :]


def score_rows(keys, queries_t, e_store, m_store):
    count, width = keys.shape[0], queries_t.shape[1]
    total = jnp.zeros((8, width), F32)
    step = 128
    for c in range(0, count, step):
        t = jnp.tanh(mm(keys[c : c + step], queries_t) * (SCALE / SOFT_CAP))
        e = jnp.exp2((SOFT_CAP * LOG2_E) * t - 17.0)
        total = total + jnp.sum(e.reshape(step // 8, 8, width), axis=0)
        e_store(c, step, e.astype(BF))
        m_store(c, step, (e - e * (t * t)).astype(BF))
    return jnp.sum(total, axis=0, keepdims=True)


def forward_kernel(shift_ref, y_ref, yt_ref, e0_ref, m0_ref, e1_ref, m1_ref, u_ref, l_ref):
    o1 = pl.multiple_of(offsets(shift_ref)[0], 128)

    def block(d):
        def e_store(c, n, v):
            e0_ref[d, c : c + n, :] = v

        def m_store(c, n, v):
            m0_ref[d, c : c + n, :] = v

        l_ref[d] = score_rows(y_ref[d, :, 48:96], yt_ref[d, 0:48, :], e_store, m_store)
        u_ref[d] = mm(yt_ref[d, 96:144, :], e0_ref[d])

    for d in range(4):
        block(d)

    def e_store(c, n, v):
        e1_ref[c : c + n, :] = v

    def m_store(c, n, v):
        m1_ref[c : c + n, :] = v

    keys = jnp.concatenate([y_ref[d, pl.ds(o1, 128), 48:96] for d in range(4)], axis=0)
    queries = jnp.concatenate([yt_ref[d, 0:48, pl.ds(o1, 128)] for d in range(4)], axis=1)
    values = jnp.concatenate([yt_ref[d, 96:144, pl.ds(o1, 128)] for d in range(4)], axis=1)
    l1 = score_rows(keys, queries, e_store, m_store)
    u1 = mm(values, e1_ref[...])
    for d in range(4):
        u_ref[d, :, pl.ds(o1, 128)] += u1[:, 128 * d : 128 * d + 128]
        l_ref[d, :, pl.ds(o1, 128)] += l1[:, 128 * d : 128 * d + 128]


def turned(value, shift):
    return pltpu.roll(value, shift & 127, 1)


def wide_kernel(
    shift_ref,
    yt_ref,
    a0_ref,
    a1_ref,
    a2_ref,
    a3_ref,
    u_ref,
    l_ref,
    g0_ref,
    g1_ref,
    g2_ref,
    g3_ref,
    so0_ref,
    so1_ref,
    so2_ref,
    so3_ref,
    gs_ref,
    ds_ref,
    own_ref,
    send1_ref,
    send2_ref,
    send3_ref,
    dq_ref,
    e2_ref,
    m2_ref,
    usum_ref,
    lsum_ref,
):
    _, base, part = offsets(shift_ref)
    base = pl.multiple_of(base, 128)
    y2 = jnp.concatenate([a0_ref[...], a1_ref[...], a2_ref[...], a3_ref[...]], axis=0)
    keys, values = y2[:, 48:96], y2[:, 96:144]
    both_t = y2[:, 48:144].astype(F32).T.astype(BF)
    query_t = a0_ref[:, 0:48].astype(F32).T.astype(BF)

    def e_store(c, n, v):
        e2_ref[c : c + n, :] = v

    def m_store(c, n, v):
        m2_ref[c : c + n, :] = v

    l2 = score_rows(keys, query_t, e_store, m_store)
    u2 = mm(both_t[48:96], e2_ref[...])
    l2w = jnp.broadcast_to(l2, (8, 128))
    lane = iota((1, 128), 1) >> 5
    gs2 = jnp.zeros((48, 128), F32)
    ds2 = jnp.zeros((8, 128), F32)
    for d in range(4):
        here = lane == part
        shift = 32 * (part - d)
        usum_ref[...] = u_ref[d]
        lsum_ref[...] = l_ref[d]
        usum_ref[:, pl.ds(base, 128)] += jnp.where(here, turned(u2, shift), 0.0)
        lsum_ref[:, pl.ds(base, 128)] += jnp.where(here, turned(l2w, shift), 0.0)[0:1]
        inv = 1.0 / lsum_ref[...]
        att = usum_ref[...] * inv
        so_ref = (so0_ref, so1_ref, so2_ref, so3_ref)[d]
        so_ref[...] = (yt_ref[d, 144:192, :].astype(F32) + att).astype(BF)
        grad_ref = (g0_ref, g1_ref, g2_ref, g3_ref)[d]
        gs = (grad_ref[...].astype(F32) * inv).astype(BF)
        gs_ref[d] = gs
        ds_ref[d] = jnp.sum(gs.astype(F32) * att, axis=0, keepdims=True)
        gs_wide = gs_ref[d, :, pl.ds(base, 128)].astype(F32)
        ds_wide = jnp.broadcast_to(ds_ref[d, :, pl.ds(base, 128)], (8, 128))
        gs2 = jnp.where(lane == d, turned(gs_wide, -shift), gs2)
        ds2 = jnp.where(lane == d, turned(ds_wide, -shift), ds2)
    gs2 = gs2.astype(BF)
    dp = mm(values, gs2)
    dscore = (m2_ref[...].astype(F32) * (dp - ds2[0:1])).astype(BF)
    dq_ref[...] = mm(both_t[0:48], dscore) * SCALE
    dk = mm(query_t, dscore, NT) * SCALE
    dv = mm(gs2, e2_ref[...], NT)
    dkv = jnp.concatenate([dk, dv], axis=0)
    own_ref[...] = dkv[:, 0:128]
    for e, send_ref in enumerate((send1_ref, send2_ref, send3_ref)):
        send_ref[...] = dkv[:, 128 * e + 128 : 128 * e + 256].astype(BF)


def dscores(values, gs, ds, m_load, store):
    dp = mm(values, gs)
    step = 64
    for c in range(0, dp.shape[0], step):
        store(c, step, (m_load(c, step).astype(F32) * (dp[c : c + step] - ds)).astype(BF))


def backward_kernel(
    shift_ref,
    y_ref,
    yt_ref,
    e0_ref,
    m0_ref,
    e1_ref,
    m1_ref,
    gs_ref,
    ds_ref,
    so0_ref,
    so1_ref,
    so2_ref,
    so3_ref,
    so0_hbm,
    so1_hbm,
    so2_hbm,
    so3_hbm,
    out_ref,
    tmp_ref,
    sems,
):
    pairs = ((so0_ref, so0_hbm), (so1_ref, so1_hbm), (so2_ref, so2_hbm), (so3_ref, so3_hbm))
    outs = started(
        [pltpu.make_async_copy(here, there, sems.at[d]) for d, (here, there) in enumerate(pairs)]
    )
    o1 = pl.multiple_of(offsets(shift_ref)[0], 128)

    def store(c, n, v):
        tmp_ref[c : c + n, :] = v

    def block(d):
        gs = gs_ref[d]
        dscores(y_ref[d, :, 96:144], gs, ds_ref[d], lambda c, n: m0_ref[d, c : c + n, :], store)
        dscore = tmp_ref[...]
        out_ref[d, 0:48, :] = mm(yt_ref[d, 48:96, :], dscore) * SCALE
        out_ref[d, 48:96, :] = mm(yt_ref[d, 0:48, :], dscore, NT) * SCALE
        out_ref[d, 96:144, :] = mm(gs, e0_ref[d], NT)

    for d in range(4):
        block(d)
    values = jnp.concatenate([y_ref[d, pl.ds(o1, 128), 96:144] for d in range(4)], axis=0)
    queries = jnp.concatenate([yt_ref[d, 0:48, pl.ds(o1, 128)] for d in range(4)], axis=1)
    keys = jnp.concatenate([yt_ref[d, 48:96, pl.ds(o1, 128)] for d in range(4)], axis=1)
    gs = jnp.concatenate([gs_ref[d, :, pl.ds(o1, 128)] for d in range(4)], axis=1)
    ds = jnp.concatenate([ds_ref[d, :, pl.ds(o1, 128)] for d in range(4)], axis=1)
    dscores(values, gs, ds, lambda c, n: m1_ref[c : c + n, :], store)
    dscore = tmp_ref[...]
    dq = mm(keys, dscore) * SCALE
    dk = mm(queries, dscore, NT) * SCALE
    dv = mm(gs, e1_ref[...], NT)
    dall = jnp.concatenate([dq, dk, dv], axis=0)
    for d in range(4):
        out_ref[d, :, pl.ds(o1, 128)] += dall[:, 128 * d : 128 * d + 128]
    finish(outs)


def return_kernel(
    shift_ref,
    dall_ref,
    own_ref,
    dq_ref,
    r1_ref,
    r2_ref,
    r3_ref,
    g0_ref,
    g1_ref,
    g2_ref,
    g3_ref,
    tab_ref,
    out_hbm,
    sum_ref,
    out_ref,
    sems,
):
    _, base, part = offsets(shift_ref)
    base = pl.multiple_of(base, 128)
    dkv = (
        own_ref[...]
        + r1_ref[...].astype(F32)
        + r2_ref[...].astype(F32)
        + r3_ref[...].astype(F32)
    )
    extra = jnp.concatenate([dq_ref[...], dkv], axis=0)
    lane = iota((1, 128), 1) >> 5
    outs, parts = [], []
    for d in range(4):
        grad_ref = (g0_ref, g1_ref, g2_ref, g3_ref)[d]
        sum_ref[...] = dall_ref[d]
        sum_ref[:, pl.ds(base, 128)] += jnp.where(
            lane == part, turned(extra, 32 * (part - d)), 0.0
        )
        parts.append(jnp.concatenate([sum_ref[...].astype(BF), grad_ref[...]], axis=0).T)
    for c, (first, step) in enumerate(((0, 384), (384, 384), (768, 192), (960, 64))):
        at = slice(first, first + step)
        for d in range(4):
            onehot = jnp.where(tab_ref[at, d : d + 1] == iota((step, BLK), 1), 1.0, 0.0)
            out_ref[at, 192 * d : 192 * d + 192] = mm(onehot.astype(BF), parts[d]).astype(BF)
        outs += started([pltpu.make_async_copy(out_ref.at[at, :], out_hbm.at[at, :], sems.at[c])])
    finish(outs)


def swap(value, distance, count):
    return lax.ppermute(value, "seq", [(i, i ^ distance) for i in range(count)])


def on_device(
    tile_features,
    gate_weight,
    up_weight,
    down_weight,
    input_projection_weight,
    query_key_value_weight,
    positions,
    dilation_shift,
    slide_output_gradient,
):
    seq_count = lax.axis_size("seq")
    device_count = seq_count * lax.axis_size("tile")
    rows, width = tile_features.shape
    ff = gate_weight.shape[1]
    slide_width = input_projection_weight.shape[1]
    all_pos = positions.reshape(device_count, rows)
    routed = ((8, 16 * SLOTS, slide_width), BF)
    weights = (gate_weight, up_weight, down_weight, input_projection_weight, query_key_value_weight)

    def exchange(block):
        return lax.all_to_all(
            block.reshape(device_count, SLOTS, slide_width),
            ("seq", "tile"),
            split_axis=0,
            concat_axis=0,
            tiled=True,
        ).reshape(device_count * SLOTS, slide_width)

    stored = [
        pltpu.VMEM((width, ff), BF),
        pltpu.VMEM((width, ff), BF),
        pltpu.VMEM((ff, width), BF),
        pltpu.VMEM((width, slide_width), BF),
        pltpu.VMEM((slide_width, 3 * slide_width), BF),
    ]
    dma = pltpu.SemaphoreType.DMA
    outgoing, x, a1, a2 = call(
        forward_mlp_kernel,
        [routed, ((rows, slide_width), BF), ((rows, ff), BF), ((rows, ff), BF)],
        [pltpu.VMEM((rows, width), BF), pltpu.VMEM((device_count, rows), I32)]
        + stored
        + [
            pltpu.VMEM((rows, slide_width), BF),
            pltpu.VMEM((rows, ff), BF),
            pltpu.VMEM((rows, ff), BF),
            pltpu.VMEM((HEADS // 2, 2 * rows, 192), BF),
            pltpu.VMEM((BLK, 2 * rows), BF),
            pltpu.VMEM((8, 16 * SLOTS, slide_width), BF),
            dma((18,)),
            dma((3 + HEADS // 2,)),
        ],
        n_hbm=7,
        n_hbm_out=4,
        limit=48,
    )(tile_features, all_pos, *weights)
    arrived = exchange(outgoing)
    turned_ff = call(
        turn_kernel,
        [((ff, width), BF)] * 2,
        [
            pltpu.VMEM((2, width, ff), BF),
            pltpu.VMEM((2, ff, width), BF),
            dma((2, width // BAND)),
            dma((2, width // BAND)),
        ],
        n_hbm=3,
        n_hbm_out=2,
        limit=32,
    )(gate_weight, up_weight, x)

    grads = call(
        order_kernel,
        [((HD, BLK), BF)] * 4,
        [pltpu.VMEM((192, BLK), BF)],
    )(slide_output_gradient.T)
    grads = [grads[0]] + [swap(grads[d], d, seq_count) for d in range(1, 4)]
    slots = device_count * SLOTS
    table, table_col = call(
        table_kernel,
        [((8, slots), I32), ((slots, 8), I32)],
    )(all_pos)

    y, yt, y2 = call(
        place_kernel,
        [((4, BLK, 192), BF), ((4, 192, BLK), BF), ((128, 192), BF)],
        n_smem=1,
        n_hbm=1,
    )(dilation_shift, arrived, table, turned_ff[0])
    y2_in = [swap(y2, 4 * e, seq_count) for e in range(1, 4)]
    e0, m0, e1, m1, u, l = call(
        forward_kernel,
        [
            ((4, BLK, BLK), BF),
            ((4, BLK, BLK), BF),
            ((BLK, BLK), BF),
            ((BLK, BLK), BF),
            ((4, HD, BLK), F32),
            ((4, 1, BLK), F32),
        ],
        n_smem=1,
    )(dilation_shift, y, yt)
    *parts, gs, ds, own, send1, send2, send3, dq2 = call(
        wide_kernel,
        [((HD, BLK), BF)] * 4
        + [((4, HD, BLK), BF), ((4, 1, BLK), F32), ((96, 128), F32)]
        + [((96, 128), BF)] * 3
        + [((HD, 128), F32)],
        [
            pltpu.VMEM((BLK, 128), BF),
            pltpu.VMEM((BLK, 128), BF),
            pltpu.VMEM((HD, BLK), F32),
            pltpu.VMEM((1, BLK), F32),
        ],
        n_smem=1,
    )(dilation_shift, yt, y2, *y2_in, u, l, *grads)
    back = [swap(send, 4 * e, seq_count) for e, send in ((3, send3), (2, send2), (1, send1))]
    *parts, dall = call(
        backward_kernel,
        [((HD, BLK), BF)] * 4 + [((4, 144, BLK), F32)],
        [pltpu.VMEM((BLK, BLK), BF), dma((4,))],
        n_smem=1,
        n_hbm_out=4,
    )(dilation_shift, y, yt, e0, m0, e1, m1, gs, ds, *parts)
    (returning,) = call(
        return_kernel,
        [((slots, slide_width), BF)],
        [
            pltpu.VMEM((144, BLK), F32),
            pltpu.VMEM((slots, slide_width), BF),
            dma((4,)),
        ],
        n_smem=1,
        n_hbm_out=1,
        limit=6,
    )(dilation_shift, dall, own, dq2, *back, *grads, table_col)
    returned = exchange(returning)
    folded = call(
        fold_kernel,
        [
            ((slide_width, ff), BF),
            ((slide_width, width), BF),
            ((3 * slide_width, slide_width), BF),
        ],
        stored[2:]
        + [
            pltpu.VMEM((slide_width, ff), BF),
            pltpu.VMEM((slide_width, width), BF),
            pltpu.VMEM((3 * slide_width, slide_width), BF),
            dma((ff // BAND + 2,)),
            dma((ff // BAND + 2,)),
        ],
        n_hbm=4,
        n_hbm_out=3,
        limit=32,
    )(*weights[2:], returning)
    parts = [parts[0]] + [swap(parts[d], d, seq_count) for d in range(1, 4)]

    tile_grad, slide_out = call(
        backward_mlp_kernel,
        [((rows, width), BF), ((192, BLK), BF)],
        [
            pltpu.VMEM((device_count, rows), I32),
            pltpu.VMEM((rows, width), BF),
            pltpu.VMEM((rows, slide_width), BF),
            pltpu.VMEM((rows, ff), BF),
            pltpu.VMEM((rows, ff), BF),
        ]
        + [pltpu.VMEM(w.shape, BF) for w in (*turned_ff, *folded)]
        + [
            pltpu.VMEM((rows, 3 * slide_width), BF),
            pltpu.VMEM((rows, slide_width), BF),
            pltpu.VMEM((192, BLK), BF),
            dma((26,)),
        ],
        n_any=4,
        n_hbm=10,
        limit=48,
    )(
        returned.reshape(8, 16 * SLOTS, slide_width),
        *parts,
        all_pos,
        tile_features,
        x,
        a1,
        a2,
        *turned_ff,
        *folded,
    )
    return (slide_out.T, tile_grad)


def solution(mesh):
    placed = (P(("seq", "tile"), None), P(), P(), P(), P(), P(), P(), P(), P("seq", "tile"))
    return jax.shard_map(
        on_device,
        mesh=mesh,
        in_specs=placed,
        out_specs=(P("seq", "tile"), P(("seq", "tile"), None)),
        check_vma=False,
    )
```

```python
import jax
import jax.numpy as jnp
from jax import lax
from jax.experimental import pallas as pl
from jax.experimental.pallas import tpu as pltpu
from jax.sharding import PartitionSpec as P

HEADS = 16
HD = 48
EPSILON = 1e-06
SOFT_CAP = 50.0
SCALE = HD**-0.5
LOG2_E = 1.4426950408889634
BLK = 512
SLOTS = 8
BF = jnp.bfloat16
F32 = jnp.float32
I32 = jnp.int32

NN = (((1,), (0,)), ((), ()))
NT = (((1,), (1,)), ((), ()))
TN = (((0,), (0,)), ((), ()))


def mm(a, b, dims=NN):
    return lax.dot_general(a, b, dims, preferred_element_type=F32)


def iota(shape, dim):
    return lax.broadcasted_iota(I32, shape, dim)


def class_order(row):
    return (row & 3) * 128 + ((row >> 2) & 3) * 32 + (row >> 4)


def order_matrix():
    return jnp.where(class_order(iota((BLK, BLK), 0)) == iota((BLK, BLK), 1), 1.0, 0.0).astype(BF)


def normalize(values):
    centred = values - jnp.mean(values, axis=-1, keepdims=True)
    inv_std = lax.rsqrt(jnp.mean(centred * centred, axis=-1, keepdims=True) + EPSILON)
    return (centred * inv_std, inv_std)


def norm_back(normed, inv_std, grads):
    mean_grad = jnp.mean(grads, axis=-1, keepdims=True)
    mean_cross = jnp.mean(grads * normed, axis=-1, keepdims=True)
    return (grads - mean_grad - normed * mean_cross) * inv_std


def call(kernel, outs, scratch=(), n_smem=0, n_any=0, n_hbm=0, n_hbm_out=0, limit=4):
    def run(*args):
        n_vmem = len(args) - n_smem - n_any - n_hbm
        specs = [pl.BlockSpec(memory_space=pltpu.SMEM)] * n_smem
        specs += [pl.BlockSpec(memory_space=pltpu.VMEM)] * n_vmem
        specs += [pl.BlockSpec(memory_space=pl.ANY)] * n_any
        specs += [pl.BlockSpec(memory_space=pltpu.HBM)] * n_hbm
        out_specs = [pl.BlockSpec(memory_space=pltpu.HBM)] * n_hbm_out
        out_specs += [pl.BlockSpec(memory_space=pltpu.VMEM)] * (len(outs) - n_hbm_out)
        shapes = [pltpu.HBM(shape, kind) for shape, kind in outs[:n_hbm_out]]
        shapes += [jax.ShapeDtypeStruct(shape, kind) for shape, kind in outs[n_hbm_out:]]
        cut = len(args) - n_hbm
        held = [pltpu.with_memory_space_constraint(x, pltpu.HBM) for x in args[cut:]]
        return pl.pallas_call(
            kernel,
            out_shape=shapes,
            in_specs=specs,
            out_specs=out_specs,
            scratch_shapes=list(scratch),
            compiler_params=pltpu.CompilerParams(vmem_limit_bytes=limit * 1024 * 1024),
        )(*args[:cut], *held)

    return run


def started(copies):
    for copy in copies:
        copy.start()
    return copies


def finish(copies):
    for copy in copies:
        copy.wait()


def order_kernel(grad_ref, g0_ref, g1_ref, g2_ref, g3_ref, tmp_ref):
    j = lax.axis_index("seq") & 3
    tmp_ref[...] = mm(grad_ref[...], order_matrix()).astype(BF)
    for d, out_ref in enumerate((g0_ref, g1_ref, g2_ref, g3_ref)):
        out_ref[...] = tmp_ref[pl.ds(pl.multiple_of((j ^ d) * HD, 16), HD), :]


def offsets(shift_ref):
    head = 4 * lax.axis_index("tile") + (lax.axis_index("seq") & 3)
    o1 = shift_ref[0, head]
    o2 = shift_ref[1, head]
    return (o1 * 128, (o2 & 3) * 128, o2 >> 2)


def table_kernel(pos_ref, row_ref, col_ref):
    s = lax.axis_index("seq")
    pos = pos_ref[...].T
    n = pos.shape[0]
    block = pos >> 9
    seat = class_order(pos & (BLK - 1)) + 1
    lower = jnp.where(iota((n, n), 1) < iota((n, n), 0), 1.0, 0.0).astype(BF)
    high, low = [], []
    for d in range(4):
        owned = block == (s ^ d)
        rank = mm(lower, jnp.where(owned, 1.0, 0.0).astype(BF)).astype(I32)
        held = jnp.where(owned, seat, 0)
        for k in range(SLOTS):
            found = jnp.sum(jnp.where(rank == k, held, 0), axis=0, keepdims=True)
            high.append(found >> 4)
            low.append(found & 15)
    digits = jnp.concatenate(high + low, axis=0).astype(F32).astype(BF)
    lanes = n * SLOTS
    spread = jnp.where(iota((n, lanes), 0) == iota((n, lanes), 1) >> 3, 1.0, 0.0).astype(BF)
    wide = mm(digits, spread)
    wide = 16.0 * wide[0:32] + wide[32:64]
    own = iota((8, lanes), 0) == (iota((8, lanes), 1) & 7)
    rows = [
        jnp.sum(jnp.where(own, wide[8 * d : 8 * d + 8], 0.0), axis=0, keepdims=True)
        for d in range(4)
    ]
    table = jnp.concatenate(rows + rows, axis=0) - 1.0
    row_ref[...] = table.astype(I32)
    col_ref[...] = table.T.astype(I32)


def forward_mlp_kernel(
    feat_hbm,
    pos_hbm,
    gate_hbm,
    up_hbm,
    down_hbm,
    proj_hbm,
    qkvw_hbm,
    out_hbm,
    x_hbm,
    a1_hbm,
    a2_hbm,
    feat_ref,
    pos_ref,
    wg_ref,
    wu_ref,
    wd_ref,
    wp_ref,
    wq_ref,
    x_ref,
    a1_ref,
    a2_ref,
    heads_ref,
    picker_ref,
    tmp_ref,
    sems,
    out_sems,
):
    ff = gate_hbm.shape[1]
    width = HEADS * HD
    step = 1024
    chunks = ff // step
    first = started(
        [
            pltpu.make_async_copy(feat_hbm, feat_ref, sems.at[3 * chunks]),
            pltpu.make_async_copy(pos_hbm, pos_ref, sems.at[3 * chunks + 1]),
        ]
    )
    waits = []
    for c in range(chunks):
        at = pl.ds(c * step, step)
        waits.append(
            started(
                [
                    pltpu.make_async_copy(gate_hbm.at[:, at], wg_ref.at[:, at], sems.at[3 * c]),
                    pltpu.make_async_copy(up_hbm.at[:, at], wu_ref.at[:, at], sems.at[3 * c + 1]),
                    pltpu.make_async_copy(down_hbm.at[at, :], wd_ref.at[at, :], sems.at[3 * c + 2]),
                ]
            )
        )
    last = started(
        [
            pltpu.make_async_copy(proj_hbm, wp_ref, sems.at[3 * chunks + 2]),
        ]
        + [
            pltpu.make_async_copy(qkvw_hbm.at[:, at], wq_ref.at[:, at], sems.at[3 * chunks + 3 + i])
            for i, at in enumerate(pl.ds(width * part, width) for part in range(3))
        ]
    )
    finish(first)

    me = lax.axis_index("seq") * 4 + lax.axis_index("tile")
    brow = pos_ref[pl.ds(me, 1), :] >> 9
    n = brow.shape[1]
    bcol = jnp.broadcast_to(brow, (n, n)).T
    before = iota((n, n), 0) < iota((n, n), 1)
    rank = jnp.sum(jnp.where((bcol == brow) & before, 1, 0), axis=0, keepdims=True)
    code = brow * SLOTS + rank
    code = jnp.concatenate([code, code + 4096], axis=1)
    seat = iota((BLK, 2 * n), 0)
    want = (((seat >> 4) & 7) * 4 + (seat >> 7)) * SLOTS + (seat & 7) + 4096 * ((seat >> 3) & 1)
    picker_ref[...] = jnp.where(code == want, 1.0, 0.0).astype(BF)

    feats = feat_ref[...].astype(F32)
    normed = normalize(feats)[0].astype(BF)
    total = feats
    outs = []
    for c in range(chunks):
        at = slice(c * step, c * step + step)
        waits[c][0].wait()
        gate = mm(normed, wg_ref[:, at])
        waits[c][1].wait()
        up = mm(normed, wu_ref[:, at])
        sig = jax.nn.sigmoid(gate)
        silu = gate * sig
        hidden = (silu * up).astype(BF)
        a1_ref[:, at] = (up * (sig + silu * (1.0 - sig))).astype(BF)
        a2_ref[:, at] = silu.astype(BF)
        waits[c][2].wait()
        total = total + mm(hidden, wd_ref[at, :])
    outs += started(
        [
            pltpu.make_async_copy(a1_ref, a1_hbm, out_sems.at[0]),
            pltpu.make_async_copy(a2_ref, a2_hbm, out_sems.at[1]),
        ]
    )
    last[0].wait()
    x = mm(total.astype(BF), wp_ref[...]).astype(BF)
    x_ref[...] = x
    outs += started([pltpu.make_async_copy(x_ref, x_hbm, out_sems.at[2])])
    slide_norm = normalize(x.astype(F32))[0].astype(BF)

    def deal(values, part):
        for h in range(HEADS):
            t, j = h // 4, h % 4
            heads_ref[2 * j + t // 2, n * (t % 2) : n * (t % 2) + n, HD * part : HD * part + HD] = (
                values[:, h * HD : h * HD + HD]
            )

    deal(x, 3)
    for part in range(3):
        last[1 + part].wait()
        at = slice(width * part, width * part + width)
        deal(mm(slide_norm, wq_ref[:, at]).astype(BF), part)
    for pair in range(HEADS // 2):
        j = pair // 2
        rows = mm(picker_ref[...], heads_ref[pair]).astype(BF)
        at = slice(16 * pair, 16 * pair + 16)
        for block in range(4):
            lane = (j ^ block) * 192
            tmp_ref[:, at, lane : lane + 192] = rows[128 * block : 128 * block + 128].reshape(
                8, 16, 192
            )
        outs += started(
            [
                pltpu.make_async_copy(
                    tmp_ref.at[:, at, :], out_hbm.at[:, at, :], out_sems.at[3 + pair]
                )
            ]
        )
    finish(outs)


BAND = 256


def band(i):
    return pl.ds(pl.multiple_of(i * BAND, BAND), BAND)


def turn_kernel(
    gate_hbm, up_hbm, _after_hbm, gatet_hbm, upt_hbm, in_ref, out_ref, sems, out_sems
):
    count = gate_hbm.shape[0] // BAND
    given, made = (gate_hbm, up_hbm), (gatet_hbm, upt_hbm)

    def load(which, i):
        return pltpu.make_async_copy(
            given[which].at[band(i), :], in_ref.at[which, band(i), :], sems.at[which, i]
        )

    def store(which, i):
        return pltpu.make_async_copy(
            out_ref.at[which, :, band(i)], made[which].at[:, band(i)], out_sems.at[which, i]
        )

    for which in range(2):
        for i in range(count):
            load(which, i).start()
    for which in range(2):

        def step(i, carry):
            load(which, i).wait()
            out_ref[which, :, band(i)] = in_ref[which, band(i), :].T
            store(which, i).start()
            return carry

        lax.fori_loop(0, count, step, 0)
    for which in range(2):
        for i in range(count):
            store(which, i).wait()


def fold_kernel(
    down_hbm,
    proj_hbm,
    qkvw_hbm,
    _after_hbm,
    fold_hbm,
    projt_hbm,
    qkvt_hbm,
    wd_ref,
    wp_ref,
    wq_ref,
    fold_ref,
    projt_ref,
    qkvt_ref,
    sems,
    out_sems,
):
    count = down_hbm.shape[0] // BAND
    loads = started(
        [
            pltpu.make_async_copy(qkvw_hbm, wq_ref, sems.at[count]),
            pltpu.make_async_copy(proj_hbm, wp_ref, sems.at[count + 1]),
        ]
    )

    def load(i):
        return pltpu.make_async_copy(down_hbm.at[band(i), :], wd_ref.at[band(i), :], sems.at[i])

    def store(i):
        return pltpu.make_async_copy(
            fold_ref.at[:, band(i)], fold_hbm.at[:, band(i)], out_sems.at[i]
        )

    def turn(from_ref, to_ref):
        def step(i, carry):
            to_ref[:, band(i)] = from_ref[band(i), :].T
            return carry

        lax.fori_loop(0, from_ref.shape[0] // BAND, step, 0)

    for i in range(count):
        load(i).start()
    loads[0].wait()
    turn(wq_ref, qkvt_ref)
    outs = started([pltpu.make_async_copy(qkvt_ref, qkvt_hbm, out_sems.at[count])])
    loads[1].wait()
    turn(wp_ref, projt_ref)
    outs += started([pltpu.make_async_copy(projt_ref, projt_hbm, out_sems.at[count + 1])])

    def step(i, carry):
        load(i).wait()
        fold_ref[:, band(i)] = mm(wd_ref[band(i), :], wp_ref[...]).astype(BF).T
        store(i).start()
        return carry

    lax.fori_loop(0, count, step, 0)
    for i in range(count):
        store(i).wait()
    finish(outs)


def backward_mlp_kernel(
    ret_ref,
    s0_any,
    s1_any,
    s2_any,
    s3_any,
    pos_hbm,
    feat_hbm,
    x_hbm,
    a1_hbm,
    a2_hbm,
    gate_hbm,
    up_hbm,
    fold_hbm,
    proj_hbm,
    qkvw_hbm,
    out_ref,
    slide_ref,
    pos_ref,
    feat_ref,
    x_ref,
    a1_ref,
    a2_ref,
    wg_ref,
    wu_ref,
    fold_ref,
    wp_ref,
    wq_ref,
    dqkv_ref,
    grad_ref,
    tmp_ref,
    sems,
):
    ff = gate_hbm.shape[0]
    cuts = [(at, 512) for at in range(0, ff - 512, 512)] + [(ff - 512, 256), (ff - 256, 256)]
    chunks = len(cuts)
    pairs = (
        (pos_hbm, pos_ref),
        (x_hbm, x_ref),
        (qkvw_hbm, wq_ref),
        (proj_hbm, wp_ref),
        (a1_hbm, a1_ref),
        (a2_hbm, a2_ref),
        (feat_hbm, feat_ref),
    )
    first = started(
        [
            pltpu.make_async_copy(here, there, sems.at[3 * chunks + i])
            for i, (here, there) in enumerate(pairs)
        ]
    )
    waits = []
    for c, (start, size) in enumerate(cuts):
        at = pl.ds(start, size)
        waits.append(
            started(
                [
                    pltpu.make_async_copy(fold_hbm.at[:, at], fold_ref.at[:, at], sems.at[3 * c]),
                    pltpu.make_async_copy(gate_hbm.at[at, :], wg_ref.at[at, :], sems.at[3 * c + 1]),
                    pltpu.make_async_copy(up_hbm.at[at, :], wu_ref.at[at, :], sems.at[3 * c + 2]),
                ]
            )
        )
    j = lax.axis_index("seq") & 3
    pieces = started(
        [
            pltpu.make_async_copy(
                so,
                tmp_ref.at[pl.ds(pl.multiple_of((j ^ d) * HD, 16), HD), :],
                sems.at[3 * chunks + len(pairs) + d],
            )
            for d, so in enumerate((s0_any, s1_any, s2_any, s3_any))
        ]
    )
    first[0].wait()
    me = lax.axis_index("seq") * 4 + lax.axis_index("tile")
    brow = pos_ref[pl.ds(me, 1), :] >> 9
    n = brow.shape[1]
    bcol = jnp.broadcast_to(brow, (n, n)).T
    before = iota((n, n), 1) < iota((n, n), 0)
    rank = jnp.sum(jnp.where((bcol == brow) & before, 1, 0), axis=1, keepdims=True)
    code = bcol[:, 0:1] * SLOTS + rank
    code = jnp.concatenate([code, code + 4096], axis=0)
    seat = iota((2 * n, BLK), 1)
    want = (((seat >> 4) & 7) * 4 + (seat >> 7)) * SLOTS + (seat & 7) + 4096 * ((seat >> 3) & 1)
    picker = jnp.where(code == want, 1.0, 0.0).astype(BF)
    width = HEADS * HD
    for pair in range(HEADS // 2):
        j, t = pair // 2, 2 * (pair % 2)
        tile = ret_ref[:, 16 * pair : 16 * pair + 16, :].reshape(128, 768)
        stacked = jnp.concatenate(
            [tile[:, (j ^ b) * 192 : (j ^ b) * 192 + 192] for b in range(4)], axis=0
        )
        got = mm(picker, stacked).astype(BF)
        for tp in range(2):
            h = 4 * (t + tp) + j
            mine = got[n * tp : n * tp + n]
            for part in range(3):
                dqkv_ref[:, part * width + h * HD : part * width + h * HD + HD] = mine[
                    :, HD * part : HD * part + HD
                ]
            grad_ref[:, h * HD : h * HD + HD] = mine[:, 144:192]
    first[1].wait()
    slide_norm, slide_inv = normalize(x_ref[...].astype(F32))
    first[2].wait()
    dnorm = mm(dqkv_ref[...], wq_ref[...])
    dslide = (grad_ref[...].astype(F32) + norm_back(slide_norm, slide_inv, dnorm)).astype(BF)
    first[3].wait()
    dembed = mm(dslide, wp_ref[...]).astype(BF)
    finish(first[4:])
    normed, inv = normalize(feat_ref[...].astype(F32))
    finish(pieces)
    slide_ref[...] = mm(tmp_ref[...], order_matrix(), NT).astype(BF)
    dfeat = jnp.zeros(feat_ref.shape, F32)
    for c, (start, size) in enumerate(cuts):
        at = slice(start, start + size)
        waits[c][0].wait()
        dhidden = mm(dslide, fold_ref[:, at])
        dgate = (dhidden * a1_ref[:, at].astype(F32)).astype(BF)
        dup = (dhidden * a2_ref[:, at].astype(F32)).astype(BF)
        waits[c][1].wait()
        dfeat = dfeat + mm(dgate, wg_ref[at, :])
        waits[c][2].wait()
        dfeat = dfeat + mm(dup, wu_ref[at, :])
    out_ref[...] = (dembed.astype(F32) + norm_back(normed, inv, dfeat)).astype(BF)


def place_kernel(shift_ref, recv_ref, tab_ref, _after_hbm, y_ref, yt_ref, y2_ref):
    _, base, part = offsets(shift_ref)
    o2 = pl.multiple_of(base + 32 * part, 32)
    for d in range(4):
        tab = tab_ref[d : d + 1, :]
        onehot = jnp.where(iota((BLK, tab.shape[1]), 0) == tab, 1.0, 0.0).astype(BF)
        y = mm(onehot, recv_ref[:, 192 * d : 192 * d + 192])
        y = y.astype(BF)
        y_ref[d] = y
        yt_ref[d] = y.T
        y2_ref[32 * d : 32 * d + 32, :] = y_ref[d, pl.ds(o2, 32), :]


def score_rows(keys, queries_t, e_store, m_store):
    count, width = keys.shape[0], queries_t.shape[1]
    total = jnp.zeros((8, width), F32)
    step = 128
    for c in range(0, count, step):
        t = jnp.tanh(mm(keys[c : c + step], queries_t) * (SCALE / SOFT_CAP))
        e = jnp.exp2((SOFT_CAP * LOG2_E) * t - 17.0)
        total = total + jnp.sum(e.reshape(step // 8, 8, width), axis=0)
        e_store(c, step, e.astype(BF))
        m_store(c, step, (e - e * (t * t)).astype(BF))
    return jnp.sum(total, axis=0, keepdims=True)


def forward_kernel(shift_ref, y_ref, yt_ref, e0_ref, m0_ref, e1_ref, m1_ref, u_ref, l_ref):
    o1 = pl.multiple_of(offsets(shift_ref)[0], 128)

    def block(d):
        def e_store(c, n, v):
            e0_ref[d, c : c + n, :] = v

        def m_store(c, n, v):
            m0_ref[d, c : c + n, :] = v

        l_ref[d] = score_rows(y_ref[d, :, 48:96], yt_ref[d, 0:48, :], e_store, m_store)
        u_ref[d] = mm(yt_ref[d, 96:144, :], e0_ref[d])

    for d in range(4):
        block(d)

    def e_store(c, n, v):
        e1_ref[c : c + n, :] = v

    def m_store(c, n, v):
        m1_ref[c : c + n, :] = v

    keys = jnp.concatenate([y_ref[d, pl.ds(o1, 128), 48:96] for d in range(4)], axis=0)
    queries = jnp.concatenate([yt_ref[d, 0:48, pl.ds(o1, 128)] for d in range(4)], axis=1)
    values = jnp.concatenate([yt_ref[d, 96:144, pl.ds(o1, 128)] for d in range(4)], axis=1)
    l1 = score_rows(keys, queries, e_store, m_store)
    u1 = mm(values, e1_ref[...])
    for d in range(4):
        u_ref[d, :, pl.ds(o1, 128)] += u1[:, 128 * d : 128 * d + 128]
        l_ref[d, :, pl.ds(o1, 128)] += l1[:, 128 * d : 128 * d + 128]


def turned(value, shift):
    return pltpu.roll(value, shift & 127, 1)


def wide_kernel(
    shift_ref,
    yt_ref,
    a0_ref,
    a1_ref,
    a2_ref,
    a3_ref,
    u_ref,
    l_ref,
    g0_ref,
    g1_ref,
    g2_ref,
    g3_ref,
    so0_ref,
    so1_ref,
    so2_ref,
    so3_ref,
    gs_ref,
    ds_ref,
    own_ref,
    send1_ref,
    send2_ref,
    send3_ref,
    dq_ref,
    e2_ref,
    m2_ref,
    usum_ref,
    lsum_ref,
):
    _, base, part = offsets(shift_ref)
    base = pl.multiple_of(base, 128)
    y2 = jnp.concatenate([a0_ref[...], a1_ref[...], a2_ref[...], a3_ref[...]], axis=0)
    keys, values = y2[:, 48:96], y2[:, 96:144]
    both_t = y2[:, 48:144].astype(F32).T.astype(BF)
    query_t = a0_ref[:, 0:48].astype(F32).T.astype(BF)

    def e_store(c, n, v):
        e2_ref[c : c + n, :] = v

    def m_store(c, n, v):
        m2_ref[c : c + n, :] = v

    l2 = score_rows(keys, query_t, e_store, m_store)
    u2 = mm(both_t[48:96], e2_ref[...])
    l2w = jnp.broadcast_to(l2, (8, 128))
    lane = iota((1, 128), 1) >> 5
    gs2 = jnp.zeros((48, 128), F32)
    ds2 = jnp.zeros((8, 128), F32)
    for d in range(4):
        here = lane == part
        shift = 32 * (part - d)
        usum_ref[...] = u_ref[d]
        lsum_ref[...] = l_ref[d]
        usum_ref[:, pl.ds(base, 128)] += jnp.where(here, turned(u2, shift), 0.0)
        lsum_ref[:, pl.ds(base, 128)] += jnp.where(here, turned(l2w, shift), 0.0)[0:1]
        inv = 1.0 / lsum_ref[...]
        att = usum_ref[...] * inv
        so_ref = (so0_ref, so1_ref, so2_ref, so3_ref)[d]
        so_ref[...] = (yt_ref[d, 144:192, :].astype(F32) + att).astype(BF)
        grad_ref = (g0_ref, g1_ref, g2_ref, g3_ref)[d]
        gs = (grad_ref[...].astype(F32) * inv).astype(BF)
        gs_ref[d] = gs
        ds_ref[d] = jnp.sum(gs.astype(F32) * att, axis=0, keepdims=True)
        gs_wide = gs_ref[d, :, pl.ds(base, 128)].astype(F32)
        ds_wide = jnp.broadcast_to(ds_ref[d, :, pl.ds(base, 128)], (8, 128))
        gs2 = jnp.where(lane == d, turned(gs_wide, -shift), gs2)
        ds2 = jnp.where(lane == d, turned(ds_wide, -shift), ds2)
    gs2 = gs2.astype(BF)
    dp = mm(values, gs2)
    dscore = (m2_ref[...].astype(F32) * (dp - ds2[0:1])).astype(BF)
    dq_ref[...] = mm(both_t[0:48], dscore) * SCALE
    dk = mm(query_t, dscore, NT) * SCALE
    dv = mm(gs2, e2_ref[...], NT)
    dkv = jnp.concatenate([dk, dv], axis=0)
    own_ref[...] = dkv[:, 0:128]
    for e, send_ref in enumerate((send1_ref, send2_ref, send3_ref)):
        send_ref[...] = dkv[:, 128 * e + 128 : 128 * e + 256].astype(BF)


def dscores(values, gs, ds, m_load, store):
    dp = mm(values, gs)
    step = 64
    for c in range(0, dp.shape[0], step):
        store(c, step, (m_load(c, step).astype(F32) * (dp[c : c + step] - ds)).astype(BF))


def backward_kernel(
    shift_ref,
    y_ref,
    yt_ref,
    e0_ref,
    m0_ref,
    e1_ref,
    m1_ref,
    gs_ref,
    ds_ref,
    so0_ref,
    so1_ref,
    so2_ref,
    so3_ref,
    so0_hbm,
    so1_hbm,
    so2_hbm,
    so3_hbm,
    out_ref,
    tmp_ref,
    sems,
):
    pairs = ((so0_ref, so0_hbm), (so1_ref, so1_hbm), (so2_ref, so2_hbm), (so3_ref, so3_hbm))
    outs = started(
        [pltpu.make_async_copy(here, there, sems.at[d]) for d, (here, there) in enumerate(pairs)]
    )
    o1 = pl.multiple_of(offsets(shift_ref)[0], 128)

    def store(c, n, v):
        tmp_ref[c : c + n, :] = v

    def block(d):
        gs = gs_ref[d]
        dscores(y_ref[d, :, 96:144], gs, ds_ref[d], lambda c, n: m0_ref[d, c : c + n, :], store)
        dscore = tmp_ref[...]
        out_ref[d, 0:48, :] = mm(yt_ref[d, 48:96, :], dscore) * SCALE
        out_ref[d, 48:96, :] = mm(yt_ref[d, 0:48, :], dscore, NT) * SCALE
        out_ref[d, 96:144, :] = mm(gs, e0_ref[d], NT)

    for d in range(4):
        block(d)
    values = jnp.concatenate([y_ref[d, pl.ds(o1, 128), 96:144] for d in range(4)], axis=0)
    queries = jnp.concatenate([yt_ref[d, 0:48, pl.ds(o1, 128)] for d in range(4)], axis=1)
    keys = jnp.concatenate([yt_ref[d, 48:96, pl.ds(o1, 128)] for d in range(4)], axis=1)
    gs = jnp.concatenate([gs_ref[d, :, pl.ds(o1, 128)] for d in range(4)], axis=1)
    ds = jnp.concatenate([ds_ref[d, :, pl.ds(o1, 128)] for d in range(4)], axis=1)
    dscores(values, gs, ds, lambda c, n: m1_ref[c : c + n, :], store)
    dscore = tmp_ref[...]
    dq = mm(keys, dscore) * SCALE
    dk = mm(queries, dscore, NT) * SCALE
    dv = mm(gs, e1_ref[...], NT)
    dall = jnp.concatenate([dq, dk, dv], axis=0)
    for d in range(4):
        out_ref[d, :, pl.ds(o1, 128)] += dall[:, 128 * d : 128 * d + 128]
    finish(outs)


def return_kernel(
    shift_ref,
    dall_ref,
    own_ref,
    dq_ref,
    r1_ref,
    r2_ref,
    r3_ref,
    g0_ref,
    g1_ref,
    g2_ref,
    g3_ref,
    tab_ref,
    out_hbm,
    sum_ref,
    out_ref,
    sems,
):
    _, base, part = offsets(shift_ref)
    base = pl.multiple_of(base, 128)
    dkv = (
        own_ref[...]
        + r1_ref[...].astype(F32)
        + r2_ref[...].astype(F32)
        + r3_ref[...].astype(F32)
    )
    extra = jnp.concatenate([dq_ref[...], dkv], axis=0)
    lane = iota((1, 128), 1) >> 5
    outs, parts = [], []
    for d in range(4):
        grad_ref = (g0_ref, g1_ref, g2_ref, g3_ref)[d]
        sum_ref[...] = dall_ref[d]
        sum_ref[:, pl.ds(base, 128)] += jnp.where(
            lane == part, turned(extra, 32 * (part - d)), 0.0
        )
        parts.append(jnp.concatenate([sum_ref[...].astype(BF), grad_ref[...]], axis=0).T)
    for c, (first, step) in enumerate(((0, 384), (384, 384), (768, 192), (960, 64))):
        at = slice(first, first + step)
        for d in range(4):
            onehot = jnp.where(tab_ref[at, d : d + 1] == iota((step, BLK), 1), 1.0, 0.0)
            out_ref[at, 192 * d : 192 * d + 192] = mm(onehot.astype(BF), parts[d]).astype(BF)
        outs += started([pltpu.make_async_copy(out_ref.at[at, :], out_hbm.at[at, :], sems.at[c])])
    finish(outs)


def swap(value, distance, count):
    return lax.ppermute(value, "seq", [(i, i ^ distance) for i in range(count)])


def on_device(
    tile_features,
    gate_weight,
    up_weight,
    down_weight,
    input_projection_weight,
    query_key_value_weight,
    positions,
    dilation_shift,
    slide_output_gradient,
):
    seq_count = lax.axis_size("seq")
    device_count = seq_count * lax.axis_size("tile")
    rows, width = tile_features.shape
    ff = gate_weight.shape[1]
    slide_width = input_projection_weight.shape[1]
    all_pos = positions.reshape(device_count, rows)
    routed = ((8, 16 * SLOTS, slide_width), BF)
    weights = (gate_weight, up_weight, down_weight, input_projection_weight, query_key_value_weight)

    def exchange(block):
        return lax.all_to_all(
            block.reshape(device_count, SLOTS, slide_width),
            ("seq", "tile"),
            split_axis=0,
            concat_axis=0,
            tiled=True,
        ).reshape(device_count * SLOTS, slide_width)

    stored = [
        pltpu.VMEM((width, ff), BF),
        pltpu.VMEM((width, ff), BF),
        pltpu.VMEM((ff, width), BF),
        pltpu.VMEM((width, slide_width), BF),
        pltpu.VMEM((slide_width, 3 * slide_width), BF),
    ]
    dma = pltpu.SemaphoreType.DMA
    outgoing, x, a1, a2 = call(
        forward_mlp_kernel,
        [routed, ((rows, slide_width), BF), ((rows, ff), BF), ((rows, ff), BF)],
        [pltpu.VMEM((rows, width), BF), pltpu.VMEM((device_count, rows), I32)]
        + stored
        + [
            pltpu.VMEM((rows, slide_width), BF),
            pltpu.VMEM((rows, ff), BF),
            pltpu.VMEM((rows, ff), BF),
            pltpu.VMEM((HEADS // 2, 2 * rows, 192), BF),
            pltpu.VMEM((BLK, 2 * rows), BF),
            pltpu.VMEM((8, 16 * SLOTS, slide_width), BF),
            dma((18,)),
            dma((3 + HEADS // 2,)),
        ],
        n_hbm=7,
        n_hbm_out=4,
        limit=48,
    )(tile_features, all_pos, *weights)
    arrived = exchange(outgoing)
    turned_ff = call(
        turn_kernel,
        [((ff, width), BF)] * 2,
        [
            pltpu.VMEM((2, width, ff), BF),
            pltpu.VMEM((2, ff, width), BF),
            dma((2, width // BAND)),
            dma((2, width // BAND)),
        ],
        n_hbm=3,
        n_hbm_out=2,
        limit=32,
    )(gate_weight, up_weight, x)

    grads = call(
        order_kernel,
        [((HD, BLK), BF)] * 4,
        [pltpu.VMEM((192, BLK), BF)],
    )(slide_output_gradient.T)
    grads = [grads[0]] + [swap(grads[d], d, seq_count) for d in range(1, 4)]
    slots = device_count * SLOTS
    table, table_col = call(
        table_kernel,
        [((8, slots), I32), ((slots, 8), I32)],
    )(all_pos)

    y, yt, y2 = call(
        place_kernel,
        [((4, BLK, 192), BF), ((4, 192, BLK), BF), ((128, 192), BF)],
        n_smem=1,
        n_hbm=1,
    )(dilation_shift, arrived, table, turned_ff[0])
    y2_in = [swap(y2, 4 * e, seq_count) for e in range(1, 4)]
    e0, m0, e1, m1, u, l = call(
        forward_kernel,
        [
            ((4, BLK, BLK), BF),
            ((4, BLK, BLK), BF),
            ((BLK, BLK), BF),
            ((BLK, BLK), BF),
            ((4, HD, BLK), F32),
            ((4, 1, BLK), F32),
        ],
        n_smem=1,
    )(dilation_shift, y, yt)
    *parts, gs, ds, own, send1, send2, send3, dq2 = call(
        wide_kernel,
        [((HD, BLK), BF)] * 4
        + [((4, HD, BLK), BF), ((4, 1, BLK), F32), ((96, 128), F32)]
        + [((96, 128), BF)] * 3
        + [((HD, 128), F32)],
        [
            pltpu.VMEM((BLK, 128), BF),
            pltpu.VMEM((BLK, 128), BF),
            pltpu.VMEM((HD, BLK), F32),
            pltpu.VMEM((1, BLK), F32),
        ],
        n_smem=1,
    )(dilation_shift, yt, y2, *y2_in, u, l, *grads)
    back = [swap(send, 4 * e, seq_count) for e, send in ((3, send3), (2, send2), (1, send1))]
    *parts, dall = call(
        backward_kernel,
        [((HD, BLK), BF)] * 4 + [((4, 144, BLK), F32)],
        [pltpu.VMEM((BLK, BLK), BF), dma((4,))],
        n_smem=1,
        n_hbm_out=4,
    )(dilation_shift, y, yt, e0, m0, e1, m1, gs, ds, *parts)
    (returning,) = call(
        return_kernel,
        [((slots, slide_width), BF)],
        [
            pltpu.VMEM((144, BLK), F32),
            pltpu.VMEM((slots, slide_width), BF),
            dma((4,)),
        ],
        n_smem=1,
        n_hbm_out=1,
        limit=6,
    )(dilation_shift, dall, own, dq2, *back, *grads, table_col)
    returned = exchange(returning)
    folded = call(
        fold_kernel,
        [
            ((slide_width, ff), BF),
            ((slide_width, width), BF),
            ((3 * slide_width, slide_width), BF),
        ],
        stored[2:]
        + [
            pltpu.VMEM((slide_width, ff), BF),
            pltpu.VMEM((slide_width, width), BF),
            pltpu.VMEM((3 * slide_width, slide_width), BF),
            dma((ff // BAND + 2,)),
            dma((ff // BAND + 2,)),
        ],
        n_hbm=4,
        n_hbm_out=3,
        limit=32,
    )(*weights[2:], returning)
    parts = [parts[0]] + [swap(parts[d], d, seq_count) for d in range(1, 4)]

    tile_grad, slide_out = call(
        backward_mlp_kernel,
        [((rows, width), BF), ((192, BLK), BF)],
        [
            pltpu.VMEM((device_count, rows), I32),
            pltpu.VMEM((rows, width), BF),
            pltpu.VMEM((rows, slide_width), BF),
            pltpu.VMEM((rows, ff), BF),
            pltpu.VMEM((rows, ff), BF),
        ]
        + [pltpu.VMEM(w.shape, BF) for w in (*turned_ff, *folded)]
        + [
            pltpu.VMEM((rows, 3 * slide_width), BF),
            pltpu.VMEM((rows, slide_width), BF),
            pltpu.VMEM((192, BLK), BF),
            dma((26,)),
        ],
        n_any=4,
        n_hbm=10,
        limit=48,
    )(
        returned.reshape(8, 16 * SLOTS, slide_width),
        *parts,
        all_pos,
        tile_features,
        x,
        a1,
        a2,
        *turned_ff,
        *folded,
    )
    return (slide_out.T, tile_grad)


def solution(mesh):
    placed = (P(("seq", "tile"), None), P(), P(), P(), P(), P(), P(), P(), P("seq", "tile"))
    return jax.shard_map(
        on_device,
        mesh=mesh,
        in_specs=placed,
        out_specs=(P("seq", "tile"), P(("seq", "tile"), None)),
        check_vma=False,
    )
```
